32 devices in a mesh: wide: 8 (over z, y), narrow: 4 (over x, core).
Axes of the slice: x: 2, y: 2, z: 4, core: 2. Of those that a mesh axis runs over, the one named last changes fastest.
Arguments:
- inputs: bfloat16 [2, 4096, 2048], P(None, 'wide', 'narrow'), may hold values from -6 to 6
- lengths: int32 [2, 8, 4], P(None, 'wide'), may hold values from 1 to 384, 512 in all within a row
- hidden_counts: int32 [4], replicated, may hold values from 1 to 1536, 5461 in all
- w_qkv: bfloat16 [3, 2048, 2048], P(None, 'wide', 'narrow'), may hold values from -0.1875 to 0.1875
- w_out: bfloat16 [2048, 2048], P('narrow', 'wide'), may hold values from -0.75 to 0.75
- w_gate_up: bfloat16 [2, 2048, 6144], P(None, 'wide', 'narrow'), may hold values from -0.125 to 0.125
- w_down: bfloat16 [6144, 2048], P('narrow', 'wide'), may hold values from -0.078125 to 0.078125
- norm1_gain: bfloat16 [2048], P('wide'), may hold values from 0.5 to 1.5
- norm1_bias: bfloat16 [2048], P('wide'), may hold values from -3 to 3
- norm2_gain: bfloat16 [2048], P('wide'), may hold values from 0.5 to 1.5
- norm2_bias: bfloat16 [2048], P('wide'), may hold values from -3 to 3
- out_cotangent: bfloat16 [2, 4096, 2048], P(None, 'wide', 'narrow'), may hold values from -6 to 6
Outputs:
- layer_out: bfloat16 [2, 4096, 2048], P(None, 'wide', 'narrow')
- input_grad: bfloat16 [2, 4096, 2048], P(None, 'wide', 'narrow')
- qkv_grad: float32 [3, 2048, 2048], P(None, 'wide', 'narrow')
- out_proj_grad: float32 [2048, 2048], P('narrow', 'wide')
- gate_up_grad: float32 [2, 2048, 6144], P(None, 'wide', 'narrow')
- down_grad: float32 [6144, 2048], P('narrow', 'wide')
- norm1_gain_grad: float32 [2048], P('wide')
- norm1_bias_grad: float32 [2048], P('wide')
- norm2_gain_grad: float32 [2048], P('wide')
- norm2_bias_grad: float32 [2048], P('wide')
The draws below stay inside these ranges and needn't reach their ends.
Inputs may be any that keep to these rules, and one draw needn't show every extreme that they name: Protein lengths of each block of 512 rows, in order; each block's sum to 512 and the longest of each block is exactly 384. `hidden_counts`: hidden units used in each column block of 1536 slots; they sum to 5461 and the largest is exactly 1536.
All inputs are finite; a program needn't handle non-finite values.
Results may differ from the reference program's by a relative error of at most 0.014.
The reference program's roundings to bfloat16 on the way count: a program that leaves them out, or rounds other values in their place, can miss the bound.
Values may be sent and summed in bfloat16 or wider, within the bound.
A program may use at most 320 MiB of HBM per device.

```python
import math
import jax
import jax.numpy as jnp
import numpy as np
from jax import lax

D = 2048
HEAD_DIM = 128
FF = 5461
MICRO = 2
SEQS = 4
TOK_W = 512
TOKENS = 4096
MAX_LEN = 384
FF_SLOT = 1536
HID_SLOTS = 6144
N_WIDE = 8
N_NARROW = 4


def strengthened(values, key, source, target, shards_of, factor):
    owner, partner = [(jnp.arange(values.shape[position]) // (values.shape[position] // shards_of)).reshape([-1 if axis == position else 1 for axis in range(values.ndim)]) for position in (source, target)]
    chosen = jax.random.permutation(key, shards_of)[partner]
    strong = (owner == chosen) | (owner == (partner + shards_of // 2) % shards_of)
    return jnp.where(strong, factor * values, values)


def levels(stream_key, extent, split, least, top_value):
    level, own = 1.0, jax.random.fold_in(stream_key, 6)
    for axis_at, parts in split:
        steps = jnp.exp(jax.random.uniform(jax.random.fold_in(own, axis_at), (parts,), jnp.float32, least / len(split), top_value / len(split)))
        level = level * jnp.repeat(steps, extent[axis_at] // parts).reshape([-1 if axis == axis_at else 1 for axis in range(len(extent))])
    return level


def profile(number_of, total, limit, skew):
    portions = [(1 << 20) // math.isqrt(rank ** skew) + 1 for rank in range(2, number_of + 1)]
    spare, counts = total - limit - (number_of - 1), [1] * (number_of - 1)
    while spare > 0:
        candidates = [i for i in range(number_of - 1) if counts[i] < limit]
        whole, budget = sum([portions[i] for i in candidates]), spare
        for i in candidates:
            extra = min(limit - counts[i], max(1, budget * portions[i] // whole), spare)
            counts[i] = counts[i] + extra
            spare = spare - extra
    return np.array([limit] + counts)


def ragged_sizes(own_key, number_of, total, limit, lean):
    if number_of == 2:
        one = jax.random.randint(own_key, (), max(1, total - limit), min(limit, total - 1) + 1)
        return jnp.stack([one, total - one])
    tallies = jnp.asarray(profile(number_of, total, limit, lean), jnp.int32)
    pairs = (number_of - 1) // 2
    giver, sink = tallies[1:1 + 2 * pairs:2], tallies[2:2 + 2 * pairs:2]
    slack = jnp.minimum(giver - 1, limit - sink)
    moved = jax.random.randint(jax.random.fold_in(own_key, 1), (pairs,), 0, 1 << 20) % (slack + 1)
    tallies = tallies.at[1:1 + 2 * pairs:2].set(giver - moved).at[2:2 + 2 * pairs:2].set(sink + moved)
    return tallies[jax.random.permutation(jax.random.fold_in(own_key, 2), number_of)]


def gaussian(rng, dims, width, limit, split=(), kind=jnp.bfloat16):
    values = jax.random.normal(rng, dims, jnp.float32) * width
    if len(split) > 0:
        values = levels(rng, dims, split, -0.22, 0.18) * values
    return jnp.clip(values, min=-limit, max=limit).astype(kind)


def bell_draw_with(stream_key, extent, scale, bound, shards, heavy, held_as=jnp.bfloat16):
    drawn = scale * jax.random.normal(stream_key, extent, jnp.float32)
    if shards:
        drawn = drawn * levels(stream_key, extent, shards, -0.22, 0.18)
    return jnp.clip(strengthened(drawn, jax.random.fold_in(stream_key, 3), *heavy), -bound, bound).astype(held_as)


def setup_inputs(seed: int = 0) -> dict:
    seeds = jax.random.split(jax.random.key(seed), 13)
    return {
        "inputs": gaussian(seeds[0], (MICRO, TOKENS, D), 1.0, 6.0, ((1, 8), (2, 4))),
        "lengths": jax.vmap(lambda own: ragged_sizes(own, SEQS, TOK_W, MAX_LEN, 2))(jax.random.split(seeds[1], MICRO * N_WIDE)).reshape((MICRO, N_WIDE, SEQS)).astype(jnp.int32),
        "hidden_counts": ragged_sizes(seeds[2], N_NARROW, FF, FF_SLOT, 1).astype(jnp.int32),
        "w_qkv": gaussian(seeds[3], (3, D, D), (D // 2) ** -0.5, 0.1875, ((1, 8), (2, 4))),
        "w_out": gaussian(seeds[4], (D, D), (D // 32) ** -0.5, 0.75, ((0, 4), (1, 8))),
        "w_gate_up": gaussian(seeds[5], (2, D, HID_SLOTS), D ** -0.5, 0.125, ((1, 8), (2, 4))),
        "w_down": gaussian(seeds[6], (HID_SLOTS, D), FF ** -0.5, 0.078125, ((0, 4), (1, 8))),
        "norm1_gain": jnp.clip(1.0 + 0.1 * jax.random.normal(seeds[7], (D,), jnp.float32), 0.5, 1.5).astype(jnp.bfloat16),
        "norm1_bias": gaussian(seeds[8], (D,), 0.3, 3.0, ((0, 8),)),
        "norm2_gain": jnp.clip(1.0 + 0.1 * jax.random.normal(seeds[9], (D,), jnp.float32), 0.5, 1.5).astype(jnp.bfloat16),
        "norm2_bias": gaussian(seeds[10], (D,), 0.3, 3.0, ((0, 8),)),
        "out_cotangent": bell_draw_with(seeds[11], (MICRO, TOKENS, D), 1.0, 6.0, ((1, 8), (2, 4)), (1, 2, 8, 2.0)),
    }


eps = 1e-05
precise = lax.Precision.HIGHEST

@jax.custom_vjp
def low(v):
    return lax.optimization_barrier(v.astype(jnp.bfloat16)).astype(jnp.float32)

@jax.custom_vjp
def low_back(v):
    return v

def low_keep(v):
    return (low(v), None)

def low_pass(kept, grad):
    return (grad,)

def back_keep(v):
    return (v, None)

def back_low(kept, grad):
    return (low(grad),)
low.defvjp(low_keep, low_pass)
low_back.defvjp(back_keep, back_low)

def layer_norm(values, gain, shift):
    average = lax.optimization_barrier(jnp.mean(values, axis=-1, keepdims=True))
    centred = values - average
    spread = lax.optimization_barrier(jnp.mean(centred * centred, axis=-1, keepdims=True))
    return centred * lax.rsqrt(spread + eps) * gain + shift

def protein_layout(length_row, row_count):
    seq_ends = jnp.cumsum(length_row).astype(jnp.int32)
    seq_starts = (seq_ends - length_row).astype(jnp.int32)
    places = jnp.arange(row_count, dtype=jnp.int32)
    protein_id = lax.optimization_barrier(jnp.sum((places[:, None] >= seq_ends[None, :]).astype(jnp.int32), axis=1)).astype(jnp.int32)
    onehot = protein_id[:, None] == jnp.arange(length_row.shape[0], dtype=jnp.int32)[None, :]
    positions = places - lax.optimization_barrier(jnp.sum(jnp.where(onehot, seq_starts[None, :], 0), axis=1)).astype(jnp.int32)
    return (protein_id, positions)

def rotary_tables(positions):
    half_dim = HEAD_DIM // 2
    frequency = 10000.0 ** (-jnp.arange(half_dim, dtype=jnp.float32) / half_dim)
    angles = positions.astype(jnp.float32)[:, None] * frequency[None, :]
    return (jnp.cos(angles)[:, None, :], jnp.sin(angles)[:, None, :])

def rotate(values, cosine_table, sine_table):
    half_dim = values.shape[-1] // 2
    first_half = values[..., :half_dim]
    second_half = values[..., half_dim:]
    return jnp.concatenate([first_half * cosine_table - second_half * sine_table, second_half * cosine_table + first_half * sine_table], axis=-1)

def attend_block(block_data):
    queries, key_rows, value_rows, protein_id = block_data
    scores = jnp.einsum('thd,shd->hts', queries, key_rows, precision=precise) * HEAD_DIM ** (-0.5)
    scores = low_back(scores)
    same_protein = protein_id[:, None] == protein_id[None, :]
    scores = jnp.where(same_protein[None], scores, -1e+30)
    top_score = lax.optimization_barrier(jnp.max(scores, axis=-1, keepdims=True))
    exp_scores = jnp.exp(scores - top_score)
    attention_probs = exp_scores / lax.optimization_barrier(jnp.sum(exp_scores, axis=-1, keepdims=True))
    return jnp.einsum('hts,shd->thd', low(attention_probs), value_rows, precision=precise)

def forward(inputs, w_qkv, w_out, w_gate_up, w_down, gain_one, shift_one, gain_two, shift_two, protein_id, cosine_table, sine_table, column_mask):
    micro_count, token_count, model_width = inputs.shape
    head_count = model_width // HEAD_DIM
    normed_one = low(layer_norm(inputs, gain_one, shift_one))
    projected_qkv = low_back(jnp.einsum('mtd,cde->cmte', normed_one, w_qkv, precision=precise))
    shaped = projected_qkv.reshape(3, micro_count, token_count, head_count, HEAD_DIM)
    queries = low(rotate(shaped[0], cosine_table, sine_table))
    key_rows = low(rotate(shaped[1], cosine_table, sine_table))
    value_rows = low(shaped[2])
    blocks = micro_count * token_count // TOK_W

    def to_blocks(tensor):
        return tensor.reshape(blocks, TOK_W, head_count, HEAD_DIM)
    attended = lax.map(jax.checkpoint(attend_block), (to_blocks(queries), to_blocks(key_rows), to_blocks(value_rows), protein_id))
    attended = low(low_back(attended.reshape(micro_count, token_count, model_width)))
    branch = low_back(jnp.einsum('mte,ed->mtd', attended, w_out, precision=precise))
    middle = inputs + branch
    normed_two = low(layer_norm(middle, gain_two, shift_two))
    gate_up = low_back(jnp.einsum('mtd,cdf->cmtf', normed_two, w_gate_up, precision=precise))
    hidden = low(jax.nn.gelu(gate_up[0], approximate=False) * gate_up[1] * column_mask)
    return middle + low_back(jnp.einsum('mtf,fd->mtd', hidden, w_down, precision=precise))

def reference(inputs, lengths, hidden_counts, w_qkv, w_out, w_gate_up, w_down, norm1_gain, norm1_bias, norm2_gain, norm2_bias, out_cotangent):
    flat_lengths = lengths.reshape(-1, lengths.shape[-1]).astype(jnp.int32)
    protein_id, positions = jax.vmap(lambda length_row: protein_layout(length_row, TOK_W))(flat_lengths)
    cosine_table, sine_table = rotary_tables(positions.reshape(-1))
    half_dim = HEAD_DIM // 2
    cosine_table = cosine_table.reshape(MICRO, TOKENS, 1, half_dim)
    sine_table = sine_table.reshape(MICRO, TOKENS, 1, half_dim)
    slot_index = jnp.arange(N_NARROW * FF_SLOT, dtype=jnp.int32)
    slot_owner = (slot_index // FF_SLOT).astype(jnp.int32)
    owner_count = lax.optimization_barrier(jnp.sum(jnp.where(slot_owner[:, None] == jnp.arange(N_NARROW, dtype=jnp.int32)[None, :], hidden_counts.astype(jnp.int32)[None, :], 0), axis=1))
    column_mask = (slot_index % FF_SLOT < owner_count).astype(jnp.float32)
    float_args = (inputs.astype(jnp.float32), w_qkv.astype(jnp.float32), w_out.astype(jnp.float32), w_gate_up.astype(jnp.float32), w_down.astype(jnp.float32), norm1_gain.astype(jnp.float32), norm1_bias.astype(jnp.float32), norm2_gain.astype(jnp.float32), norm2_bias.astype(jnp.float32))

    def wrapped(*values):
        return forward(*values, protein_id, cosine_table, sine_table, column_mask)
    result, pullback = jax.vjp(wrapped, *float_args)
    grads = pullback(out_cotangent.astype(jnp.float32))
    return (result.astype(jnp.bfloat16), grads[0].astype(jnp.bfloat16), grads[1], grads[2], grads[3], grads[4], grads[5], grads[6], grads[7], grads[8])
```

```python
import functools

import jax
import jax.numpy as jnp
from jax import lax
from jax.experimental import pallas as pl
from jax.experimental.pallas import tpu as pltpu
from jax.sharding import Mesh
from jax.sharding import PartitionSpec as P

HEAD_DIM = 128
EPS = 1e-05
BF = jnp.bfloat16
F32 = jnp.float32
MESH = pl.DeviceIdType.MESH
VMEM_BYTES = 60 * 2**20
SWAP = [(0, 1), (1, 0)]
ANY = pl.BlockSpec(memory_space=pl.ANY)
VMEM = pl.BlockSpec(memory_space=pltpu.VMEM)
SMEM = pl.BlockSpec(memory_space=pltpu.SMEM)


def dot(a, b):
    return jnp.dot(a, b, preferred_element_type=F32)


def dot_nt(a, b):
    return lax.dot_general(a, b, (((1,), (1,)), ((), ())), preferred_element_type=F32)


def dot_tn(a, b):
    return lax.dot_general(a, b, (((0,), (0,)), ((), ())), preferred_element_type=F32)


def normalise(v):
    centred = v - jnp.mean(v, axis=-1, keepdims=True)
    rstd = lax.rsqrt(jnp.mean(centred * centred, axis=-1, keepdims=True) + EPS)
    return centred * rstd, rstd


def norm_back(xhat, rstd, grad, gain):
    dx = grad * gain
    a = jnp.mean(dx, axis=-1, keepdims=True)
    b = jnp.mean(dx * xhat, axis=-1, keepdims=True)
    return rstd * (dx - a - xhat * b)


def cost(us, sent=0):
    return pl.CostEstimate(flops=int(us * 1e9), bytes_accessed=int(us * 3.2e6), transcendentals=0)


class Place:
    def __init__(self):
        self.y = lax.axis_index("y")
        self.n = lax.axis_index("n")
        self.x = self.n // 2
        self.c = self.n % 2
        self.ns = self.n + 1 - 2 * self.c
        self.nx = (self.n + 2) % 4
        self.nd = (self.ns + 2) % 4
        self.sib = {"n": self.ns}
        self.xn = {"n": self.nx}
        self.yn = {"y": 1 - self.y}
        self.xs = {"n": self.nd}


def meet(devices):
    barrier = pltpu.get_barrier_semaphore()
    for d in devices:
        pl.semaphore_signal(barrier, inc=1, device_id=d, device_id_type=MESH)
    pl.semaphore_wait(barrier, len(devices))


class Wire:
    def __init__(self, send_sems, recv_sems, first=0):
        self.ss, self.rs, self.at, self.sent = send_sems, recv_sems, first, []

    def make(self, src, dst, device):
        k = self.at
        self.at += 1
        copy = pltpu.make_async_remote_copy(
            src_ref=src, dst_ref=dst, send_sem=self.ss.at[k], recv_sem=self.rs.at[k],
            device_id=device, device_id_type=MESH,
        )
        self.sent.append(copy)
        return copy

    def finish(self):
        for copy in self.sent:
            copy.wait_send()


SPREAD = 9


class Spread:
    def __init__(self, wire, at, src, slot):
        y, n, nx = at.y, at.n, at.nx
        self.first = [
            wire.make(src, slot(y, n, None), at.xn),
            wire.make(src, slot(y, n, None), at.yn),
            wire.make(src, slot(y, n, None), at.sib),
        ]
        self.on_x = [
            wire.make(slot(y, nx, 0), slot(y, nx, 0), at.yn),
            wire.make(slot(y, nx, None), slot(y, nx, None), at.sib),
        ]
        self.on_y = [
            wire.make(slot(1 - y, n, 1), slot(1 - y, n, 1), at.xn),
            wire.make(slot(1 - y, n, None), slot(1 - y, n, None), at.sib),
        ]
        self.last = [
            wire.make(slot(1 - y, nx, 0), slot(1 - y, nx, 0), at.sib),
            wire.make(slot(1 - y, nx, 1), slot(1 - y, nx, 1), at.sib),
        ]

    def begin(self):
        for copy in self.first:
            copy.start()

    def forward(self):
        self.first[0].wait_recv()
        for copy in self.on_x:
            copy.start()
        self.first[1].wait_recv()
        for copy in self.on_y:
            copy.start()

    def forward_last(self):
        self.on_x[0].wait_recv()
        self.last[0].start()
        self.on_y[0].wait_recv()
        self.last[1].start()

    def end(self):
        self.first[2].wait_recv()
        self.on_x[1].wait_recv()
        self.on_y[1].wait_recv()
        self.last[0].wait_recv()
        self.last[1].wait_recv()


REDUCE = 10


def reduce_scratch(micro, tok, sub, width):
    half = sub // 2
    return [
        pltpu.VMEM((micro, 2, tok, width), BF),
        pltpu.VMEM((micro, 2, 2, sub, width), BF),
        pltpu.VMEM((micro, sub, width), BF),
        pltpu.VMEM((micro, sub, width), BF),
        pltpu.VMEM((micro, sub, width), BF),
        pltpu.VMEM((micro, 2, half, width), BF),
        pltpu.VMEM((micro, sub, width), BF),
        pltpu.VMEM((micro, sub, width), BF),
    ]


def reduce_rows(wire, at, scratch, compute, finish):
    part, ra, sb, sx, sy, rb, rcx, rcy = scratch
    micro, sub = sb.shape[0], sb.shape[1]
    half = sub // 2
    y, x, c, n = at.y, at.x, at.c, at.n

    def rows(core, xx, lo=0, size=sub):
        return pl.ds(pl.multiple_of((2 * xx + core) * sub, sub) + lo, size)

    a = {}
    for m in range(micro):
        for yk, yy in ((1, 1 - y), (0, y)):
            compute(m, yy)
            for xk, xx in ((1, 1 - x), (0, x)):
                copy = wire.make(part.at[m, yy, rows(1 - c, xx)], ra.at[m, yy, xx], at.sib)
                copy.start()
                a[m, yk, xk] = copy

    def summed(m, yy, xx, lo, size):
        return part[m, yy, rows(c, xx, lo, size), :].astype(F32) + ra[m, yy, xx, lo : lo + size, :].astype(F32)

    b = {}
    for m in range(micro):
        a[m, 1, 1].wait_recv()
        sb[m] = summed(m, 1 - y, 1 - x, 0, sub).astype(BF)
        b[m, 0] = wire.make(sb.at[m, 0:half], rb.at[m, 0], at.xn)
        b[m, 1] = wire.make(sb.at[m, half:sub], rb.at[m, 1], at.yn)
        b[m, 0].start()
        b[m, 1].start()
    d = {}
    for m in range(micro):
        a[m, 1, 0].wait_recv()
        sy[m, half:sub] = summed(m, 1 - y, x, half, half).astype(BF)
        d[m, 0] = wire.make(sy.at[m, half:sub], rcy.at[m, half:sub], at.yn)
        d[m, 0].start()
        a[m, 0, 1].wait_recv()
        sx[m, 0:half] = summed(m, y, 1 - x, 0, half).astype(BF)
        d[m, 1] = wire.make(sx.at[m, 0:half], rcx.at[m, 0:half], at.xn)
        d[m, 1].start()
        b[m, 0].wait_recv()
        sy[m, 0:half] = (summed(m, 1 - y, x, 0, half) + rb[m, 0].astype(F32)).astype(BF)
        d[m, 2] = wire.make(sy.at[m, 0:half], rcy.at[m, 0:half], at.yn)
        d[m, 2].start()
        b[m, 1].wait_recv()
        sx[m, half:sub] = (summed(m, y, 1 - x, half, half) + rb[m, 1].astype(F32)).astype(BF)
        d[m, 3] = wire.make(sx.at[m, half:sub], rcx.at[m, half:sub], at.xn)
        d[m, 3].start()
    for m in range(micro):
        a[m, 0, 0].wait_recv()
        for k in range(4):
            d[m, k].wait_recv()
        finish(m, lambda lo, size, m=m: summed(m, y, x, lo, size) + rcx[m, lo : lo + size, :].astype(F32) + rcy[m, lo : lo + size, :].astype(F32))


def blockwise(part, m, yy, fn, tile=256):
    tok = part.shape[2]

    def step(i, carry):
        lo = pl.multiple_of(i * tile, tile)
        fn(lo, tile)
        return carry

    lax.fori_loop(0, tok // tile, step, 0)


def gather_kernel(zn, x_in, d_in, v_in, x_out, d_out, v_out, ss, rs, ls):
    at = Place()
    z = lax.axis_index("z")
    micro, tok, feat = x_in.shape
    ring = [(dz, dy) for dz in range(zn) for dy in range(2) if dz or dy]
    others = [{"z": (z + dz) % zn, "y": (at.y + dy) % 2} for dz, dy in ring]
    meet([at.sib, at.xn] + others)
    wire = Wire(ss, rs)
    half = tok // 2
    spreads, local = [], []
    for src, out in ((x_in, x_out), (d_in, d_out)):
        for m in range(micro):

            def slot(yy, nn, part, m=m, out=out):
                lo, size = (0, tok) if part is None else (part * half, half)
                return out.at[m, yy, pl.ds(lo, size), pl.ds(pl.multiple_of(nn * feat, feat), feat)]

            spreads.append(Spread(wire, at, src.at[m], slot))
            local.append(pltpu.make_async_copy(src.at[m], slot(at.y, at.n, None), ls.at[len(local)]))
    local.append(pltpu.make_async_copy(v_in, v_out.at[z, at.y], ls.at[len(local)]))
    small = [wire.make(v_in, v_out.at[z, at.y], d) for d in others]
    for copy in small:
        copy.start()
    for s in spreads:
        s.begin()
    for copy in local:
        copy.start()
    for s in spreads:
        s.forward()
    for s in spreads:
        s.forward_last()
    for s in spreads:
        s.end()
    for copy in small:
        copy.wait_recv()
    wire.finish()
    for copy in local:
        copy.wait()


def gather_all(x, d, v, zn):
    micro, tok, feat = x.shape
    whole = jax.ShapeDtypeStruct((micro, 2, tok, 4 * feat), BF)
    count = SPREAD * 2 * micro + 2 * zn - 1
    return pl.pallas_call(
        functools.partial(gather_kernel, zn),
        out_shape=(whole, whole, jax.ShapeDtypeStruct((zn, 2) + v.shape, F32)),
        in_specs=[ANY] * 3,
        out_specs=(ANY,) * 3,
        scratch_shapes=[
            pltpu.SemaphoreType.DMA((count,)),
            pltpu.SemaphoreType.DMA((count,)),
            pltpu.SemaphoreType.DMA((2 * micro + 1,)),
        ],
        compiler_params=pltpu.CompilerParams(collective_id=0, has_side_effects=True, vmem_limit_bytes=VMEM_BYTES),
        cost_estimate=cost(45),
        name="gather_all",
    )(x, d, v)


def row_slot(out, m, sub):
    half = sub // 2

    def slot(yy, nn, part):
        ref = out.at[m, yy, nn]
        return ref if part is None else ref.at[pl.ds(part * half, half)]

    return slot


def run_spreads(spreads, local):
    for s in spreads:
        s.forward()
    for s in spreads:
        s.forward_last()
    for s in spreads:
        s.end()
    for copy in local:
        copy.wait()


def attn_out_kernel(att, wo, x_all, gain, shift, middle, n2, *scratch):
    *red, xb, nb, ss, rs, ls = scratch
    at = Place()
    micro, sub, width = middle.shape
    zn, _, dz = wo.shape
    tok = red[0].shape[2]
    meet([at.sib, at.xn, at.yn])
    wire = Wire(ss, rs)
    own = [pltpu.make_async_copy(x_all.at[m, at.y, pl.ds(at.n * sub, sub)], xb.at[m], ls.at[m]) for m in range(micro)]
    for copy in own:
        copy.start()

    def compute(m, yy):
        def tile(lo, size):
            a = att[pl.ds(pl.multiple_of((m * 2 + yy) * tok, tok) + lo, size), :]
            for k in range(zn):
                red[0][m, yy, pl.ds(lo, size), k * dz : (k + 1) * dz] = dot(a, wo[k]).astype(BF)

        blockwise(red[0], m, yy, tile)

    spreads, local = [], []

    def finish(m, total):
        own[m].wait()
        step = sub // 2
        for lo in range(0, sub, step):
            mid = xb[m, lo : lo + step, :].astype(F32) + total(lo, step)
            middle[m, lo : lo + step, :] = mid
            xhat, _ = normalise(mid)
            nb[m, lo : lo + step, :] = (xhat * gain[...] + shift[...]).astype(BF)
        slot = row_slot(n2, m, sub)
        spreads.append(Spread(wire, at, nb.at[m], slot))
        spreads[-1].begin()
        local.append(pltpu.make_async_copy(nb.at[m], slot(at.y, at.n, None), ls.at[micro + m]))
        local[-1].start()

    reduce_rows(wire, at, red, compute, finish)
    run_spreads(spreads, local)
    wire.finish()


def attn_out(att, wo, x_all, gain, shift):
    micro, _, tok, width = x_all.shape
    sub = tok // 4
    count = (REDUCE + SPREAD) * micro
    return pl.pallas_call(
        attn_out_kernel,
        out_shape=(
            jax.ShapeDtypeStruct((micro, sub, width), F32),
            jax.ShapeDtypeStruct((micro, 2, 4, sub, width), BF),
        ),
        in_specs=[VMEM, VMEM, ANY, VMEM, VMEM],
        out_specs=(VMEM, ANY),
        scratch_shapes=reduce_scratch(micro, tok, sub, width)
        + [
            pltpu.VMEM((micro, sub, width), BF),
            pltpu.VMEM((micro, sub, width), BF),
            pltpu.SemaphoreType.DMA((count,)),
            pltpu.SemaphoreType.DMA((count,)),
            pltpu.SemaphoreType.DMA((2 * micro,)),
        ],
        compiler_params=pltpu.CompilerParams(collective_id=1, has_side_effects=True, vmem_limit_bytes=VMEM_BYTES),
        cost_estimate=cost(85),
        name="attn_out",
    )(att, wo, x_all, gain, shift)


def nt_compute(part, low, w):
    zn, dz, _ = w.shape
    tok = part.shape[2]

    def compute(m, yy):
        def tile(lo, size):
            a = low[pl.ds(pl.multiple_of((m * 2 + yy) * tok, tok) + lo, size), :]
            for k in range(zn):
                part[m, yy, pl.ds(lo, size), k * dz : (k + 1) * dz] = dot_nt(a, w[k]).astype(BF)

        blockwise(part, m, yy, tile)

    return compute


def ffn_back_kernel(gul, wgu, d_all, middle, gain, mid_grad, branch, vec, *scratch):
    *red, db, nb, ss, rs, ls = scratch
    at = Place()
    micro, sub, width = middle.shape
    meet([at.sib, at.xn, at.yn])
    wire = Wire(ss, rs)
    own = [pltpu.make_async_copy(d_all.at[m, at.y, pl.ds(at.n * sub, sub)], db.at[m], ls.at[m]) for m in range(micro)]
    for copy in own:
        copy.start()
    vec[...] = jnp.zeros_like(vec)
    spreads, local = [], []

    def finish(m, total):
        own[m].wait()
        step = sub // 2
        for lo in range(0, sub, step):
            grad = total(lo, step)
            xhat, rstd = normalise(middle[m, lo : lo + step, :])
            vec[0:1, :] += jnp.sum(grad * xhat, axis=0, keepdims=True)
            vec[1:2, :] += jnp.sum(grad, axis=0, keepdims=True)
            mg = db[m, lo : lo + step, :].astype(F32) + norm_back(xhat, rstd, grad, gain[...])
            mid_grad[m, lo : lo + step, :] = mg
            nb[m, lo : lo + step, :] = mg.astype(BF)
        slot = row_slot(branch, m, sub)
        spreads.append(Spread(wire, at, nb.at[m], slot))
        spreads[-1].begin()
        local.append(pltpu.make_async_copy(nb.at[m], slot(at.y, at.n, None), ls.at[micro + m]))
        local[-1].start()

    reduce_rows(wire, at, red, nt_compute(red[0], gul, wgu), finish)
    run_spreads(spreads, local)
    wire.finish()


def ffn_back(gul, wgu, d_all, middle, gain):
    micro, _, tok, width = d_all.shape
    sub = tok // 4
    count = (REDUCE + SPREAD) * micro
    return pl.pallas_call(
        ffn_back_kernel,
        out_shape=(
            jax.ShapeDtypeStruct((micro, sub, width), F32),
            jax.ShapeDtypeStruct((micro, 2, 4, sub, width), BF),
            jax.ShapeDtypeStruct((8, width), F32),
        ),
        in_specs=[VMEM, VMEM, ANY, VMEM, VMEM],
        out_specs=(VMEM, ANY, VMEM),
        scratch_shapes=reduce_scratch(micro, tok, sub, width)
        + [
            pltpu.VMEM((micro, sub, width), BF),
            pltpu.VMEM((micro, sub, width), BF),
            pltpu.SemaphoreType.DMA((count,)),
            pltpu.SemaphoreType.DMA((count,)),
            pltpu.SemaphoreType.DMA((2 * micro,)),
        ],
        compiler_params=pltpu.CompilerParams(collective_id=2, has_side_effects=True, vmem_limit_bytes=VMEM_BYTES),
        cost_estimate=cost(95),
        name="ffn_back",
    )(gul, wgu, d_all, middle, gain)


class Deal:
    def __init__(self, wire, at, rows, out, m, sems, k):
        sub, width = rows.shape[1], rows.shape[2]
        feat = width // 4

        def cols(nn):
            return rows.at[m, :, pl.ds(pl.multiple_of(nn * feat, feat), feat)]

        place = out.at[m, pl.ds(pl.multiple_of(at.n * sub, sub), sub)]
        self.local = pltpu.make_async_copy(cols(at.n), place, sems.at[k])
        self.copies = [
            wire.make(cols(at.nx), place, at.xn),
            wire.make(cols(at.nd), place, at.xs),
            wire.make(cols(at.ns), place, at.sib),
        ]

    def begin(self):
        for copy in self.copies:
            copy.start()
        self.local.start()

    def end(self):
        for copy in self.copies:
            copy.wait_recv()
        self.local.wait()


def attn_back_kernel(low, w, x_all, mid_grad, gain, out, vec, *scratch):
    *red, xb, ob, ss, rs, ls = scratch
    at = Place()
    micro, sub, width = mid_grad.shape
    meet([at.sib, at.xn, at.yn, at.xs])
    wire = Wire(ss, rs)
    own = [pltpu.make_async_copy(x_all.at[m, at.y, pl.ds(at.n * sub, sub)], xb.at[m], ls.at[m]) for m in range(micro)]
    for copy in own:
        copy.start()
    vec[...] = jnp.zeros_like(vec)
    deals = []

    def finish(m, total):
        own[m].wait()
        step = sub // 2
        for lo in range(0, sub, step):
            grad = total(lo, step)
            xhat, rstd = normalise(xb[m, lo : lo + step, :].astype(F32))
            vec[0:1, :] += jnp.sum(grad * xhat, axis=0, keepdims=True)
            vec[1:2, :] += jnp.sum(grad, axis=0, keepdims=True)
            ob[m, lo : lo + step, :] = (
                mid_grad[m, lo : lo + step, :] + norm_back(xhat, rstd, grad, gain[...])
            ).astype(BF)
        deals.append(Deal(wire, at, ob, out, m, ls, micro + m))
        deals[-1].begin()

    reduce_rows(wire, at, red, nt_compute(red[0], low, w), finish)
    for deal in deals:
        deal.end()
    wire.finish()


def attn_back(low, w, x_all, mid_grad, gain):
    micro, _, tok, width = x_all.shape
    sub = tok // 4
    count = (REDUCE + 3) * micro
    return pl.pallas_call(
        attn_back_kernel,
        out_shape=(
            jax.ShapeDtypeStruct((micro, tok, width // 4), BF),
            jax.ShapeDtypeStruct((8, width), F32),
        ),
        in_specs=[VMEM, VMEM, ANY, VMEM, VMEM],
        out_specs=(ANY, VMEM),
        scratch_shapes=reduce_scratch(micro, tok, sub, width)
        + [
            pltpu.VMEM((micro, sub, width), BF),
            pltpu.VMEM((micro, sub, width), BF),
            pltpu.SemaphoreType.DMA((count,)),
            pltpu.SemaphoreType.DMA((count,)),
            pltpu.SemaphoreType.DMA((2 * micro,)),
        ],
        compiler_params=pltpu.CompilerParams(collective_id=3, has_side_effects=True, vmem_limit_bytes=VMEM_BYTES),
        cost_estimate=cost(55),
        name="attn_back",
    )(low, w, x_all, mid_grad, gain)


def ffn_out_kernel(hidden, wd, middle, out, *scratch):
    *red, ob, ss, rs, ls = scratch
    at = Place()
    micro, sub, width = middle.shape
    zn, _, dz = wd.shape
    tok = red[0].shape[2]
    meet([at.sib, at.xn, at.yn, at.xs])
    wire = Wire(ss, rs)

    def compute(m, yy):
        def tile(lo, size):
            a = hidden[pl.ds(pl.multiple_of((m * 2 + yy) * tok, tok) + lo, size), :]
            for k in range(zn):
                red[0][m, yy, pl.ds(lo, size), k * dz : (k + 1) * dz] = dot(a, wd[k]).astype(BF)

        blockwise(red[0], m, yy, tile)

    deals = []

    def finish(m, total):
        step = sub // 2
        for lo in range(0, sub, step):
            ob[m, lo : lo + step, :] = (middle[m, lo : lo + step, :] + total(lo, step)).astype(BF)
        deals.append(Deal(wire, at, ob, out, m, ls, m))
        deals[-1].begin()

    reduce_rows(wire, at, red, compute, finish)
    for deal in deals:
        deal.end()
    wire.finish()


def ffn_out(hidden, wd, middle, tok):
    micro, sub, width = middle.shape
    count = (REDUCE + 3) * micro
    return pl.pallas_call(
        ffn_out_kernel,
        out_shape=jax.ShapeDtypeStruct((micro, tok, width // 4), BF),
        in_specs=[VMEM, VMEM, VMEM],
        out_specs=ANY,
        scratch_shapes=reduce_scratch(micro, tok, sub, width)
        + [
            pltpu.VMEM((micro, sub, width), BF),
            pltpu.SemaphoreType.DMA((count,)),
            pltpu.SemaphoreType.DMA((count,)),
            pltpu.SemaphoreType.DMA((micro,)),
        ],
        compiler_params=pltpu.CompilerParams(collective_id=4, has_side_effects=True, vmem_limit_bytes=VMEM_BYTES),
        cost_estimate=cost(55),
        name="ffn_out",
    )(hidden, wd, middle)


def local_call(body, grid, ins, in_specs, outs, out_specs, us, name, scratch=()):
    return pl.pallas_call(
        body,
        grid=grid,
        in_specs=in_specs,
        out_specs=out_specs,
        out_shape=outs,
        scratch_shapes=list(scratch),
        compiler_params=pltpu.CompilerParams(vmem_limit_bytes=VMEM_BYTES),
        cost_estimate=cost(us),
        name=name,
    )(*ins)


def tiles(rows, cols):
    return pl.BlockSpec((rows, cols), lambda i: (i, 0))


def first_norm_body(x, gain, shift, out):
    xhat, _ = normalise(x[...].astype(F32))
    out[...] = (xhat * gain[...] + shift[...]).astype(BF)


def first_norm(x, gain, shift):
    rows, width = x.shape
    tile = 256
    return local_call(
        first_norm_body, (rows // tile,), (x, gain, shift), [tiles(tile, width), VMEM, VMEM],
        jax.ShapeDtypeStruct((rows, width), BF), tiles(tile, width), 8, "first_norm",
    )


def same_protein(ends, b, tok, count):
    col = lax.broadcasted_iota(jnp.int32, (tok, 1), 0)
    row = lax.broadcasted_iota(jnp.int32, (1, tok), 1)
    pc, pr = jnp.zeros_like(col), jnp.zeros_like(row)
    for k in range(count):
        end = ends[b, k]
        pc = pc + (col >= end).astype(jnp.int32)
        pr = pr + (row >= end).astype(jnp.int32)
    return pc == pr


def turn(v, cos, sin):
    return v * cos + pltpu.roll(v, HEAD_DIM // 2, 1) * sin


def attention_body(ends, n1, w, cos, sin, qkv, att):
    zn, dz, cols = w.shape
    tok = n1.shape[0]
    heads = cols // 3 // HEAD_DIM
    span = heads * HEAD_DIM
    acc = dot(n1[:, 0:dz], w[0])
    for k in range(1, zn):
        acc = acc + dot(n1[:, k * dz : (k + 1) * dz], w[k])
    same = same_protein(ends, pl.program_id(0), tok, ends.shape[1])
    scale = HEAD_DIM ** (-0.5)
    for h in range(heads):
        lo = h * HEAD_DIM
        q = turn(acc[:, lo : lo + HEAD_DIM], cos[...], sin[...]).astype(BF)
        k = turn(acc[:, span + lo : span + lo + HEAD_DIM], cos[...], sin[...]).astype(BF)
        v = acc[:, 2 * span + lo : 2 * span + lo + HEAD_DIM].astype(BF)
        qkv[:, lo : lo + HEAD_DIM] = q
        qkv[:, span + lo : span + lo + HEAD_DIM] = k
        qkv[:, 2 * span + lo : 2 * span + lo + HEAD_DIM] = v
        s = jnp.where(same, dot_nt(q, k) * scale, -1e30)
        e = jnp.exp(s - jnp.max(s, axis=-1, keepdims=True))
        p = (e / jnp.sum(e, axis=-1, keepdims=True)).astype(BF)
        att[:, lo : lo + HEAD_DIM] = dot(p, v).astype(BF)


def attention(ends, n1, w, cos, sin):
    rows, width = n1.shape
    zn, dz, cols = w.shape
    tok = rows // ends.shape[0]
    return local_call(
        attention_body, (rows // tok,), (ends, n1, w, cos, sin),
        [SMEM, tiles(tok, width), VMEM, tiles(tok, HEAD_DIM), tiles(tok, HEAD_DIM)],
        (jax.ShapeDtypeStruct((rows, cols), BF), jax.ShapeDtypeStruct((rows, cols // 3), BF)),
        (tiles(tok, cols), tiles(tok, cols // 3)), 20, "attention",
    )


def attention_back_body(ends, branch, wo, qkv, cos, sin, low):
    zn, span, dz = wo.shape
    tok = branch.shape[0]
    heads = span // HEAD_DIM
    acc = dot_nt(branch[:, 0:dz], wo[0])
    for k in range(1, zn):
        acc = acc + dot_nt(branch[:, k * dz : (k + 1) * dz], wo[k])
    same = same_protein(ends, pl.program_id(0), tok, ends.shape[1])
    scale = HEAD_DIM ** (-0.5)
    for h in range(heads):
        lo = h * HEAD_DIM
        ag = acc[:, lo : lo + HEAD_DIM].astype(BF)
        q = qkv[:, lo : lo + HEAD_DIM]
        k = qkv[:, span + lo : span + lo + HEAD_DIM]
        v = qkv[:, 2 * span + lo : 2 * span + lo + HEAD_DIM]
        s = jnp.where(same, dot_nt(q, k) * scale, -1e30)
        e = jnp.exp(s - jnp.max(s, axis=-1, keepdims=True))
        p = e / jnp.sum(e, axis=-1, keepdims=True)
        pg = dot_nt(ag, v)
        vg = dot_tn(p.astype(BF), ag)
        rd = jnp.sum(p * pg, axis=-1, keepdims=True)
        sg = (p * (pg - rd)).astype(BF)
        qg = dot(sg, k) * scale
        kg = dot_tn(sg, q) * scale
        low[:, lo : lo + HEAD_DIM] = turn(qg, cos[...], -sin[...]).astype(BF)
        low[:, span + lo : span + lo + HEAD_DIM] = turn(kg, cos[...], -sin[...]).astype(BF)
        low[:, 2 * span + lo : 2 * span + lo + HEAD_DIM] = vg.astype(BF)


def attention_back(ends, branch, wo, qkv, cos, sin):
    rows, width = branch.shape
    cols = qkv.shape[1]
    tok = rows // ends.shape[0]
    return local_call(
        attention_back_body, (rows // tok,), (ends, branch, wo, qkv, cos, sin),
        [SMEM, tiles(tok, width), VMEM, tiles(tok, cols), tiles(tok, HEAD_DIM), tiles(tok, HEAD_DIM)],
        jax.ShapeDtypeStruct((rows, cols), BF), tiles(tok, cols), 25, "attention_back",
    )


def gate_up_body(n2, w, mask, gu, hidden):
    zn, dz, cols = w.shape
    half = cols // 2
    acc = dot(n2[:, 0:dz], w[0])
    for k in range(1, zn):
        acc = acc + dot(n2[:, k * dz : (k + 1) * dz], w[k])
    gu[...] = acc
    g, u = acc[:, :half], acc[:, half:]
    hidden[...] = (g * (0.5 * (1.0 + lax.erf(g * (0.5**0.5)))) * u * mask[...]).astype(BF)


def gate_up(n2, w, mask):
    rows, width = n2.shape
    cols = w.shape[2]
    tile = 256
    return local_call(
        gate_up_body, (rows // tile,), (n2, w, mask), [tiles(tile, width), VMEM, VMEM],
        (jax.ShapeDtypeStruct((rows, cols), F32), jax.ShapeDtypeStruct((rows, cols // 2), BF)),
        (tiles(tile, cols), tiles(tile, cols // 2)), 20, "gate_up",
    )


def hidden_back_body(dy, w, gu, mask, low):
    zn, half, dz = w.shape
    hg = dot_nt(dy[:, 0:dz], w[0])
    for k in range(1, zn):
        hg = hg + dot_nt(dy[:, k * dz : (k + 1) * dz], w[k])
    hg = hg * mask[...]
    g, u = gu[:, :half], gu[:, half:]
    phi = 0.5 * (1.0 + lax.erf(g * (0.5**0.5)))
    slope = phi + g * jnp.exp(-0.5 * g * g) * 0.3989422804014327
    low[:, :half] = (hg * u * slope).astype(BF)
    low[:, half:] = (hg * (g * phi)).astype(BF)


def hidden_back(dy, w, gu, mask):
    rows, width = dy.shape
    cols = gu.shape[1]
    tile = 256
    return local_call(
        hidden_back_body, (rows // tile,), (dy, w, gu, mask),
        [tiles(tile, width), VMEM, tiles(tile, cols), VMEM],
        jax.ShapeDtypeStruct((rows, cols), BF), tiles(tile, cols), 15, "hidden_back",
    )


def pick(w, index, axis):
    half = w.shape[axis] // 2
    return lax.dynamic_slice_in_dim(w, index * half, half, axis)


def ordered(y, keep, got, axis):
    return jnp.concatenate([jnp.where(y == 0, keep, got), jnp.where(y == 0, got, keep)], axis=axis)


def on_device(inputs, lengths, counts, w_qkv, w_out, w_gu, w_down, g1, b1, g2, b2, dy_in):
    z = lax.axis_index("z")
    y = lax.axis_index("y")
    n = lax.axis_index("n")
    zn = lax.axis_size("z")
    micro, tok, feat = inputs.shape
    width = feat * lax.axis_size("n")
    rows = micro * 2 * tok
    blocks = micro * 2

    def columns(w):
        parts, depth, cols = w.shape
        cut = lambda i: pick(w, i, 2).transpose(1, 0, 2).reshape(depth, parts * cols // 2)
        return ordered(y, cut(y), lax.ppermute(cut(1 - y), "y", SWAP), 0)

    def lines(w):
        return ordered(y, pick(w, y, 0), lax.ppermute(pick(w, 1 - y, 0), "y", SWAP), 1)

    def gather_z(w):
        return lax.all_gather(w, "z", axis=0, tiled=False)

    wq = gather_z(columns(w_qkv))
    wo = gather_z(lines(w_out))
    wgu = gather_z(columns(w_gu))
    wd = gather_z(lines(w_down))

    vecs = jnp.stack([g1, b1, g2, b2]).astype(F32)
    vecs = jnp.pad(vecs, ((0, 4), (0, 0)))
    x_all, d_all, norms = gather_all(inputs, dy_in, vecs, zn)
    norms = norms.transpose(2, 0, 1, 3).reshape(8, width)
    gain1, shift1, gain2, shift2 = (norms[i : i + 1] for i in range(4))

    half_slots = wgu.shape[2] // 2
    own = jnp.sum(jnp.where(jnp.arange(counts.shape[0]) == n, counts, 0))
    mask = (y * half_slots + jnp.arange(half_slots) < own).astype(F32)[None]

    other = lax.ppermute(lengths, "y", SWAP)
    both = ordered(y, lengths, other, 1).reshape(blocks, -1)
    count = both.shape[1]
    upto = jnp.arange(count)[:, None] >= jnp.arange(count)[None, :]
    ends = jnp.sum(jnp.where(upto[None], both[:, None, :], 0), axis=2)
    places = jnp.arange(tok, dtype=jnp.int32)
    before = places[None, :, None] >= ends[:, None, :]
    position = places[None] - jnp.max(jnp.where(before, ends[:, None, :], 0), axis=2)
    half_dim = HEAD_DIM // 2
    frequency = 10000.0 ** (-jnp.arange(half_dim, dtype=F32) / half_dim)
    angles = position.reshape(rows, 1).astype(F32) * frequency[None]
    cos, sin = jnp.cos(angles), jnp.sin(angles)
    cos = jnp.concatenate([cos, cos], 1)
    sin = jnp.concatenate([-sin, sin], 1)

    n1 = first_norm(x_all.reshape(rows, width), gain1, shift1)
    qkv, att = attention(ends, n1, wq, cos, sin)
    middle, n2 = attn_out(att, wo, x_all, gain2, shift2)
    n2 = n2.reshape(rows, width)
    gu, hidden = gate_up(n2, wgu, mask)
    dy = d_all.reshape(rows, width)

    def weight_grad(a, b):
        return jnp.einsum("ta,tb->ab", a, b, preferred_element_type=F32).astype(BF)

    def scatter_z(g, axis):
        return lax.psum_scatter(g, "z", scatter_dimension=axis, tiled=True)

    down_s = scatter_z(weight_grad(hidden, dy), 1)
    gul = hidden_back(dy, wd, gu, mask)
    gu_s = scatter_z(weight_grad(n2, gul), 0)
    mid_grad, branch, vec2 = ffn_back(gul, wgu, d_all, middle, gain2)
    branch = branch.reshape(rows, width)
    out_s = scatter_z(weight_grad(att, branch), 1)
    low = attention_back(ends, branch, wo, qkv, cos, sin)
    qkv_s = scatter_z(weight_grad(n1, low), 0)
    in_grad, vec1 = attn_back(low, wq, x_all, mid_grad, gain1)
    layer_out = ffn_out(hidden, wd, middle, tok)

    def columns_back(r, parts):
        depth, cols = r.shape[0] // 2, r.shape[1] // parts
        cut = lambda i: pick(r, i, 0)
        full = ordered(y, cut(y).reshape(depth, parts, cols), lax.ppermute(cut(1 - y), "y", SWAP).reshape(depth, parts, cols), 2)
        return full.transpose(1, 0, 2).astype(F32)

    def lines_back(r):
        return ordered(y, pick(r, y, 1), lax.ppermute(pick(r, 1 - y, 1), "y", SWAP), 0).astype(F32)

    sums = jnp.concatenate([vec1[0:2], vec2[0:2]], axis=0)
    sums = lax.psum(sums, ("z", "y", "n"))
    mine = lax.dynamic_slice_in_dim(sums, (z * 2 + y) * g1.shape[0], g1.shape[0], 1)
    return (
        layer_out,
        in_grad,
        columns_back(qkv_s, w_qkv.shape[0]),
        lines_back(out_s),
        columns_back(gu_s, w_gu.shape[0]),
        lines_back(down_s),
        mine[0],
        mine[1],
        mine[2],
        mine[3],
    )


def solution(mesh):
    wide, narrow = mesh.shape["wide"], mesh.shape["narrow"]
    grid = Mesh(mesh.devices.reshape(wide // 2, 2, narrow), ("z", "y", "n"))
    w = ("z", "y")
    tokens, depth, lines, vector = P(None, w, "n"), P(None, w, "n"), P("n", w), P(w)
    return jax.shard_map(
        on_device,
        mesh=grid,
        in_specs=(
            tokens, P(None, w, None), P(), depth, lines, depth, lines,
            vector, vector, vector, vector, tokens,
        ),
        out_specs=(
            tokens, tokens, depth, lines, depth, lines, vector, vector, vector, vector,
        ),
        check_vma=False,
    )
```

```python
import functools

import jax
import jax.numpy as jnp
from jax import lax
from jax.experimental import pallas as pl
from jax.experimental.pallas import tpu as pltpu
from jax.sharding import Mesh
from jax.sharding import PartitionSpec as P

HEAD_DIM = 128
EPS = 1e-05
BF = jnp.bfloat16
F32 = jnp.float32
MESH = pl.DeviceIdType.MESH
VMEM_BYTES = 60 * 2**20
SWAP = [(0, 1), (1, 0)]
ANY = pl.BlockSpec(memory_space=pl.ANY)
VMEM = pl.BlockSpec(memory_space=pltpu.VMEM)
SMEM = pl.BlockSpec(memory_space=pltpu.SMEM)


def dot(a, b):
    return jnp.dot(a, b, preferred_element_type=F32)


def dot_nt(a, b):
    return lax.dot_general(a, b, (((1,), (1,)), ((), ())), preferred_element_type=F32)


def dot_tn(a, b):
    return lax.dot_general(a, b, (((0,), (0,)), ((), ())), preferred_element_type=F32)


def normalise(v):
    centred = v - jnp.mean(v, axis=-1, keepdims=True)
    rstd = lax.rsqrt(jnp.mean(centred * centred, axis=-1, keepdims=True) + EPS)
    return centred * rstd, rstd


def norm_back(xhat, rstd, grad, gain):
    dx = grad * gain
    a = jnp.mean(dx, axis=-1, keepdims=True)
    b = jnp.mean(dx * xhat, axis=-1, keepdims=True)
    return rstd * (dx - a - xhat * b)


def cost(us, sent=0):
    return pl.CostEstimate(flops=int(us * 1e9), bytes_accessed=int(us * 3.2e6), transcendentals=0)


def without(body, ins, extra):
    def run(*refs):
        return body(*refs[:ins], *refs[ins + extra :])

    return run


def kernel(body, ins, in_specs, outs, out_specs, us, name, scratch=(), first=(), grid=(), talk=None, aliases=None):
    extra = len(first)
    return pl.pallas_call(
        without(body, len(ins), extra),
        grid=grid,
        in_specs=list(in_specs) + [ANY] * extra,
        out_specs=out_specs,
        out_shape=outs,
        scratch_shapes=list(scratch),
        input_output_aliases=aliases or {},
        compiler_params=pltpu.CompilerParams(
            vmem_limit_bytes=VMEM_BYTES, collective_id=talk, has_side_effects=talk is not None
        ),
        cost_estimate=cost(us),
        name=name,
    )(*ins, *first)


def sems(*counts):
    return [pltpu.SemaphoreType.DMA((k,)) for k in counts]


def shaped(shape, dtype=BF):
    return jax.ShapeDtypeStruct(tuple(shape), dtype)


class Place:
    def __init__(self):
        self.y = lax.axis_index("y")
        self.n = lax.axis_index("n")
        self.x = self.n // 2
        self.c = self.n % 2
        self.ns = self.n + 1 - 2 * self.c
        self.nx = (self.n + 2) % 4
        self.nd = (self.ns + 2) % 4
        self.sib = {"n": self.ns}
        self.xn = {"n": self.nx}
        self.yn = {"y": 1 - self.y}
        self.xs = {"n": self.nd}


def meet(devices):
    barrier = pltpu.get_barrier_semaphore()
    for d in devices:
        pl.semaphore_signal(barrier, inc=1, device_id=d, device_id_type=MESH)
    pl.semaphore_wait(barrier, len(devices))


class Wire:
    def __init__(self, send_sems, recv_sems, first=0):
        self.ss, self.rs, self.at, self.sent = send_sems, recv_sems, first, []

    def make(self, src, dst, device, keep=True, again=False):
        self.at += not again
        k = self.at - 1
        copy = pltpu.make_async_remote_copy(
            src_ref=src, dst_ref=dst, send_sem=self.ss.at[k], recv_sem=self.rs.at[k],
            device_id=device, device_id_type=MESH,
        )
        if keep:
            self.sent.append(copy)
        return copy

    def finish(self):
        for copy in self.sent:
            copy.wait_send()


SPREAD = 9


class Spread:
    def __init__(self, wire, at, src, slot):
        y, n, nx = at.y, at.n, at.nx
        self.first = [
            wire.make(src, slot(y, n, None), at.xn),
            wire.make(src, slot(y, n, None), at.yn),
            wire.make(src, slot(y, n, None), at.sib),
        ]
        self.on_x = [
            wire.make(slot(y, nx, 0), slot(y, nx, 0), at.yn),
            wire.make(slot(y, nx, None), slot(y, nx, None), at.sib),
        ]
        self.on_y = [
            wire.make(slot(1 - y, n, 1), slot(1 - y, n, 1), at.xn),
            wire.make(slot(1 - y, n, None), slot(1 - y, n, None), at.sib),
        ]
        self.last = [
            wire.make(slot(1 - y, nx, 0), slot(1 - y, nx, 0), at.sib),
            wire.make(slot(1 - y, nx, 1), slot(1 - y, nx, 1), at.sib),
        ]

    def begin(self):
        for copy in self.first:
            copy.start()

    def forward(self):
        self.first[0].wait_recv()
        for copy in self.on_x:
            copy.start()
        self.first[1].wait_recv()
        for copy in self.on_y:
            copy.start()

    def forward_last(self):
        self.on_x[0].wait_recv()
        self.last[0].start()
        self.on_y[0].wait_recv()
        self.last[1].start()

    def end(self):
        self.first[2].wait_recv()
        self.on_x[1].wait_recv()
        self.on_y[1].wait_recv()
        self.last[0].wait_recv()
        self.last[1].wait_recv()


REDUCE = 10


def reduce_scratch(micro, tok, sub, width):
    half = sub // 2
    return [
        pltpu.VMEM((micro, 2, tok, width), BF),
        pltpu.VMEM((micro, 2, 2, sub, width), BF),
        pltpu.VMEM((micro, sub, width), BF),
        pltpu.VMEM((micro, sub, width), BF),
        pltpu.VMEM((micro, sub, width), BF),
        pltpu.VMEM((micro, 2, half, width), BF),
        pltpu.VMEM((micro, sub, width), BF),
        pltpu.VMEM((micro, sub, width), BF),
    ]


class Reduce:
    def __init__(self, wire, at, scratch, compute):
        self.part, self.ra, self.sb, self.sx, self.sy, self.rb, self.rcx, self.rcy = scratch
        self.wire, self.at, self.compute = wire, at, compute
        self.micro, self.sub = self.sb.shape[0], self.sb.shape[1]
        self.a, self.b, self.d = {}, {}, {}
        self.released = False

    def rows(self, core, xx, lo=0, size=None):
        return pl.ds(pl.multiple_of((2 * xx + core) * self.sub, self.sub) + lo, size or self.sub)

    def summed(self, m, yy, xx, lo, size):
        mine = self.part[m, yy, self.rows(self.at.c, xx, lo, size), :].astype(F32)
        return mine + self.ra[m, yy, xx, lo : lo + size, :].astype(F32)

    def cores(self, m):
        at = self.at
        for yk, yy in ((1, 1 - at.y), (0, at.y)):
            self.compute(m, yy)
            for xk, xx in ((1, 1 - at.x), (0, at.x)):
                copy = self.wire.make(self.part.at[m, yy, self.rows(1 - at.c, xx)], self.ra.at[m, yy, xx], at.sib)
                copy.start()
                self.a[m, yk, xk] = copy

    def diagonal(self, m):
        at, sub, half = self.at, self.sub, self.sub // 2
        self.a[m, 1, 1].wait_recv()
        self.sb[m] = self.summed(m, 1 - at.y, 1 - at.x, 0, sub).astype(BF)
        self.b[m, 0] = self.wire.make(self.sb.at[m, 0:half], self.rb.at[m, 0], at.xn)
        self.b[m, 1] = self.wire.make(self.sb.at[m, half:sub], self.rb.at[m, 1], at.yn)
        self.b[m, 0].start()
        self.b[m, 1].start()

    def sides(self, m):
        at, sub, half = self.at, self.sub, self.sub // 2
        sx, sy, rb, rcx, rcy = self.sx, self.sy, self.rb, self.rcx, self.rcy
        self.a[m, 1, 0].wait_recv()
        sy[m, half:sub] = self.summed(m, 1 - at.y, at.x, half, half).astype(BF)
        self.d[m, 0] = self.wire.make(sy.at[m, half:sub], rcy.at[m, half:sub], at.yn)
        self.d[m, 0].start()
        self.a[m, 0, 1].wait_recv()
        sx[m, 0:half] = self.summed(m, at.y, 1 - at.x, 0, half).astype(BF)
        self.d[m, 1] = self.wire.make(sx.at[m, 0:half], rcx.at[m, 0:half], at.xn)
        self.d[m, 1].start()
        self.b[m, 0].wait_recv()
        sy[m, 0:half] = (self.summed(m, 1 - at.y, at.x, 0, half) + rb[m, 0].astype(F32)).astype(BF)
        self.d[m, 2] = self.wire.make(sy.at[m, 0:half], rcy.at[m, 0:half], at.yn)
        self.d[m, 2].start()
        self.b[m, 1].wait_recv()
        sx[m, half:sub] = (self.summed(m, at.y, 1 - at.x, half, half) + rb[m, 1].astype(F32)).astype(BF)
        self.d[m, 3] = self.wire.make(sx.at[m, half:sub], rcx.at[m, half:sub], at.xn)
        self.d[m, 3].start()

    def release(self, m):
        at = self.at
        self.a[m, 0, 0].wait_recv()
        self.ra[m, at.y, at.x] = self.summed(m, at.y, at.x, 0, self.sub).astype(BF)
        for yk in (1, 0):
            for xk in (1, 0):
                copy = self.a[m, yk, xk]
                copy.wait_send()
                self.wire.sent = [other for other in self.wire.sent if other is not copy]
        self.released = True

    def arrived(self, m):
        if not self.released:
            self.a[m, 0, 0].wait_recv()
        for k in range(4):
            self.d[m, k].wait_recv()

    def total(self, m, lo, size):
        if self.released:
            own = self.ra[m, self.at.y, self.at.x, lo : lo + size, :].astype(F32)
        else:
            own = self.summed(m, self.at.y, self.at.x, lo, size)
        return own + self.rcx[m, lo : lo + size, :].astype(F32) + self.rcy[m, lo : lo + size, :].astype(F32)


def nothing():
    pass


def reduce_rows(wire, at, scratch, compute, finish, tick=nothing):
    red = Reduce(wire, at, scratch, compute)
    for m in range(red.micro):
        red.cores(m)
        red.diagonal(m)
    tick()
    for m in range(red.micro):
        red.sides(m)
    tick()
    for m in range(red.micro):
        red.arrived(m)
        finish(m, lambda lo, size, m=m: red.total(m, lo, size))
    tick()


class Step:
    def __init__(self, wire, z, zn, s, g, prev, got, bufs, load, k):
        rows, cols = got[0].shape
        far, cap = zn - 1 - s, min(s, zn - 2)
        self.bufs, self.cols, self.ways = bufs, cols, []
        for d, (place, sign) in enumerate(((z, 1), (zn - 1 - z, -1))):
            group = (z + sign * far + zn) % zn
            here = bufs.at[d, 0, :, pl.ds(0, cols)]
            own = pltpu.make_async_copy(
                g.at[pl.ds(pl.multiple_of(group * rows, rows), rows)], here, load.at[k + 2 * d]
            )
            came = bufs.at[d, 1, :, pl.ds(0, cols)]
            carry = pltpu.make_async_copy(prev[d], came, load.at[k + 2 * d + 1]) if s else None
            peer = {"z": (z + sign + zn) % zn}
            away = wire.make(here, got[d], peer, keep=False)
            last = d * (zn - 1 - far) + (1 - d) * far
            straight = wire.make(g.at[pl.ds(last * rows, rows)], got[d], peer, keep=False, again=True)
            gets = jnp.logical_and(place >= 1, place <= cap + 1)
            adds = jnp.logical_and(place <= cap, place >= 1)
            self.ways.append((place <= cap, adds, gets, own, carry, away, place == 0, straight))

    def begin(self):
        for *_, end, straight in self.ways:
            pl.when(end)(straight.start)

    def go(self):
        for _, adds, _, own, carry, *_ in self.ways:
            if carry is not None:
                pl.when(adds)(own.start)
                pl.when(adds)(carry.start)
        for d, (_, adds, _, own, carry, away, *_) in enumerate(self.ways):
            if carry is not None:

                def add(d=d, own=own, carry=carry, away=away):
                    own.wait()
                    carry.wait()
                    cols = pl.ds(0, self.cols)
                    both = self.bufs[d, 0, :, cols].astype(F32) + self.bufs[d, 1, :, cols].astype(F32)
                    self.bufs[d, 0, :, cols] = both.astype(BF)
                    away.start()

                pl.when(adds)(add)

    def wait(self):
        for sends, _, gets, _, _, away, *_ in self.ways:
            pl.when(gets)(away.wait_recv)
            pl.when(sends)(away.wait_send)


class Host:
    def __init__(self, wire, zn, jobs, bufs, load):
        z = lax.axis_index("z")
        self.steps, self.now, self.count, self.then, k = [], None, 0, {}, 0
        for g, prev, first, outs in jobs:
            for i in range(len(outs) // 2):
                got = outs[2 * i : 2 * i + 2]
                self.steps.append(Step(wire, z, zn, first + i, g, prev, got, bufs, load, k))
                prev = got
                k += 4

    def begin(self):
        for step in self.steps:
            step.begin()
        self.next()

    def next(self):
        if self.now is not None:
            self.now.wait()
            self.count += 1
            done, self.now = self.then.pop(self.count, None), None
            if self.steps:
                self.now = self.steps.pop(0)
                self.now.go()
            if done is not None:
                done()
        elif self.steps:
            self.now = self.steps.pop(0)
            self.now.go()

    def end(self):
        while self.steps or self.now is not None:
            self.next()


class Settle:
    def __init__(self, wire, at, zn, g, got, keep, theirs, bufs, load):
        z = lax.axis_index("z")
        _, self.rows, self.cols = bufs.shape[0], keep.shape[0] * 2, keep.shape[1]
        rows, half = self.rows, keep.shape[0]
        self.bufs, self.has = bufs, (None, z >= 1, z <= zn - 2)
        view = [bufs.at[k, :, pl.ds(0, self.cols)] for k in range(3)]
        mine = g.at[pl.ds(pl.multiple_of(z * rows, rows), rows)]
        self.loads = [pltpu.make_async_copy(src, view[k], load.at[k]) for k, src in enumerate((mine, got[0], got[1]))]

        def part(i):
            return bufs.at[0, pl.ds(pl.multiple_of(i * half, half), half), pl.ds(0, self.cols)]

        self.away = wire.make(part(1 - at.y), theirs, at.yn, keep=False)
        self.here = pltpu.make_async_copy(part(at.y), keep, load.at[3])

    def go(self):
        cols = pl.ds(0, self.cols)
        self.loads[0].start()
        for k in (1, 2):
            pl.when(self.has[k])(self.loads[k].start)
        self.loads[0].wait()
        for k in (1, 2):
            pl.when(self.has[k])(self.loads[k].wait)

            def none(k=k):
                self.bufs[k, :, cols] = jnp.zeros((self.rows, self.cols), BF)

            pl.when(jnp.logical_not(self.has[k]))(none)
        total = self.bufs[0, :, cols].astype(F32)
        for k in (1, 2):
            total = total + self.bufs[k, :, cols].astype(F32)
        self.bufs[0, :, cols] = total.astype(BF)
        self.away.start()
        self.here.start()

    def wait(self):
        self.away.wait_recv()
        self.away.wait_send()
        self.here.wait()


def z_partners(zn):
    z = lax.axis_index("z")
    return [{"z": (z + 1) % zn}, {"z": (z + zn - 1) % zn}]


class Jobs:
    def __init__(self, plan, zn):
        self.plan, self.zn = plan, zn
        self.ins, self.outs = [], []
        for g, prev, first, steps in plan:
            self.ins += [g] + (list(prev) if prev is not None else [])
            self.outs += [shaped((g.shape[0] // zn, g.shape[1]))] * (2 * steps)
        self.steps = sum(p[3] for p in plan)
        wide = max([p[0].shape[1] for p in plan], default=0)
        rows = plan[0][0].shape[0] // zn if plan else 0
        self.scratch = [pltpu.VMEM((2, 2, rows, wide), BF)] + sems(4 * self.steps) if plan else []

    def host(self, wire, ins, outs, scratch):
        jobs, i, o = [], 0, 0
        for _, prev, first, steps in self.plan:
            took = 1 if prev is None else 3
            jobs.append((ins[i], None if prev is None else ins[i + 1 : i + 3], first, outs[o : o + 2 * steps]))
            i, o = i + took, o + 2 * steps
        return Host(wire, self.zn, jobs, *scratch)


def blockwise(part, m, yy, fn, tile=256):
    tok = part.shape[2]

    def step(i, carry):
        lo = pl.multiple_of(i * tile, tile)
        fn(lo, tile)
        return carry

    lax.fori_loop(0, tok // tile, step, 0)


def token_spreads(wire, at, src, out, sem, first, cut):
    micro, tok, feat = src.shape
    spreads, local = [], []
    for m in range(micro):

        def slot(yy, nn, part, m=m):
            lo, size = {None: (0, tok), 0: (0, cut), 1: (cut, tok - cut)}[part]
            return out.at[m, yy, pl.ds(lo, size), pl.ds(pl.multiple_of(nn * feat, feat), feat)]

        spreads.append(Spread(wire, at, src.at[m], slot))
        local.append(pltpu.make_async_copy(src.at[m], slot(at.y, at.n, None), sem.at[first + m]))
    return spreads, local


def attn_cut(w_qkv, w_out, i, buf):
    parts, _, cols = w_qkv.shape
    half = cols // 2
    at = pl.ds(pl.multiple_of(i * half, half), half)
    for p in range(parts):
        buf[:, p * half : (p + 1) * half] = w_qkv[p, :, at]
    buf[:, parts * half :] = w_out[at, :].astype(F32).T.astype(BF)


def chunk_cut(w_gu, w_down, i, c, one, buf):
    half = w_gu.shape[2] // 2
    at = pl.ds(pl.multiple_of(i * half, half) + c * one, one)
    buf[:, :one] = w_gu[0, :, at]
    buf[:, one : 2 * one] = w_gu[1, :, at]
    buf[:, 2 * one :] = w_down[at, :].astype(F32).T.astype(BF)


class Swap:
    def __init__(self, wire, at, bufs, out, sem):
        depth = bufs.shape[1]
        place = out.at[pl.ds(pl.multiple_of(at.y * depth, depth), depth)]
        self.away = wire.make(bufs.at[0], place, at.yn)
        self.here = pltpu.make_async_copy(bufs.at[1], place, sem)

    def end(self):
        self.away.wait_recv()
        self.here.wait()


def swap_attn_kernel(w_qkv, w_out, out, bufs, ss, rs, ls):
    at = Place()
    meet([at.yn])
    wire = Wire(ss, rs)
    swap = Swap(wire, at, bufs, out, ls.at[0])
    attn_cut(w_qkv, w_out, 1 - at.y, bufs.at[0])
    swap.away.start()
    attn_cut(w_qkv, w_out, at.y, bufs.at[1])
    swap.here.start()
    swap.end()
    wire.finish()


def swap_attn(w_qkv, w_out):
    parts, depth, cols = w_qkv.shape
    size = (parts + 1) * cols // 2
    return kernel(
        swap_attn_kernel, (w_qkv, w_out), [VMEM, VMEM], shaped((2 * depth, size)), ANY, 14, "swap_attn",
        [pltpu.VMEM((2, depth, size), BF)] + sems(1, 1, 1), talk=6,
    )


def swap_chunks(wire, at, w_gu, w_down, which, one, bufs, outs, ls):
    swaps = []
    for k, (c, out) in enumerate(zip(which, outs)):
        swap = Swap(wire, at, bufs.at[k], out, ls.at[k])
        chunk_cut(w_gu, w_down, 1 - at.y, c, one, bufs.at[k, 0])
        swap.away.start()
        chunk_cut(w_gu, w_down, at.y, c, one, bufs.at[k, 1])
        swap.here.start()
        swaps.append(swap)
    return swaps


def gather_x_kernel(zn, which, count, x_in, v_in, lens, freq, w_gu, w_down, x_out, v_out, lens_all, cos, sin, own, *scratch):
    bufs, ss, rs, ls = scratch
    at = Place()
    z = lax.axis_index("z")
    one = own.shape[2] // 3
    ring = [(dz, dy) for dz in range(zn) for dy in range(2) if dz or dy]
    others = [{"z": (z + dz) % zn, "y": (at.y + dy) % 2} for dz, dy in ring]
    meet([at.sib, at.xn] + others)
    wire = Wire(ss, rs)
    there = wire.make(lens, lens_all.at[at.y], at.yn)
    there.start()
    spreads, local = token_spreads(wire, at, x_in, x_out, ls, len(which) + 1, x_in.shape[1] // 8)
    local.append(pltpu.make_async_copy(v_in, v_out.at[z, at.y], ls.at[len(which)]))
    small = [wire.make(v_in, v_out.at[z, at.y], d) for d in others]
    for s in spreads:
        s.begin()
    for copy in small + local:
        copy.start()
    swaps = swap_chunks(wire, at, w_gu, w_down, which, one, bufs, [own.at[k] for k in range(len(which))], ls)
    lens_all[at.y] = lens[...]
    there.wait_recv()
    tok = x_in.shape[1]
    row = lax.broadcasted_iota(jnp.int32, (tok, 1), 0)
    flip = jnp.where(lax.broadcasted_iota(jnp.int32, (1, HEAD_DIM), 1) < HEAD_DIM // 2, -1.0, 1.0)

    def table(b, carry):
        m, yy = b // 2, b % 2
        line = lens_all[yy, pl.ds(m, 1), :]
        end = jnp.zeros((1, 1), jnp.int32)
        start = jnp.zeros_like(row)
        for k in range(count):
            end = end + line[:, k : k + 1]
            start = jnp.where(row >= end, end, start)
        angle = (row - start).astype(F32) * freq[...]
        place = pl.ds(pl.multiple_of(b * tok, tok), tok)
        cos[place, :] = jnp.cos(angle)
        sin[place, :] = jnp.sin(angle) * flip
        return carry

    lax.fori_loop(0, x_in.shape[0] * 2, table, 0)
    run_spreads(spreads, local)
    for copy in small:
        copy.wait_recv()
    for swap in swaps:
        swap.end()
    wire.finish()


def gather_x(x, v, lens, freq, w_gu, w_down, zn, which, one, count, first):
    micro, tok, feat = x.shape
    depth = w_gu.shape[1]
    rows = micro * 2 * tok
    links = SPREAD * micro + 2 * zn - 1 + len(which) + 1
    return kernel(
        functools.partial(gather_x_kernel, zn, which, count), (x, v, lens, freq, w_gu, w_down),
        [ANY, ANY, VMEM, VMEM, VMEM, VMEM],
        (
            shaped((micro, 2, tok, 4 * feat)), shaped((zn, 2) + v.shape, F32), shaped((2,) + lens.shape, jnp.int32),
            shaped((rows, HEAD_DIM), F32), shaped((rows, HEAD_DIM), F32), shaped((len(which), 2 * depth, 3 * one)),
        ),
        (ANY, ANY, VMEM, VMEM, VMEM, ANY), 48, "gather_x",
        [pltpu.VMEM((len(which), 2, depth, 3 * one), BF)] + sems(links, links, micro + 1 + len(which)),
        first, talk=0,
    )


def gather_d_kernel(which, one, d_in, x_all, gain, shift, w_gu, w_down, d_out, n1, *refs):
    outs, (bufs, xin, nout, ss, rs, ls, load) = refs[: len(which)], refs[len(which) :]
    at = Place()
    micro, _, tok, _ = x_all.shape
    meet([at.sib, at.xn, at.yn])
    wire = Wire(ss, rs)
    spreads, local = token_spreads(wire, at, d_in, d_out, ls, len(which), d_in.shape[1] // 16 * 5)

    def bring(b):
        return pltpu.make_async_copy(x_all.at[b // 2, b % 2], xin.at[b % 2], load.at[b])

    def put(b):
        return pltpu.make_async_copy(nout.at[b % 2], n1.at[pl.ds(b * tok, tok)], load.at[2 * micro + b])

    bring(0).start()
    bring(1).start()
    for s in spreads:
        s.begin()
    for copy in local:
        copy.start()
    swaps = swap_chunks(wire, at, w_gu, w_down, which, one, bufs, outs, ls)
    for b in range(2 * micro):
        bring(b).wait()
        if b >= 2:
            put(b - 2).wait()

        def tile(i, carry, b=b):
            place = pl.ds(pl.multiple_of(i * 128, 128), 128)
            xhat, _ = normalise(xin[b % 2, place, :].astype(F32))
            nout[b % 2, place, :] = (xhat * gain[...] + shift[...]).astype(BF)
            return carry

        lax.fori_loop(0, tok // 128, tile, 0)
        put(b).start()
        if b + 2 < 2 * micro:
            bring(b + 2).start()
        if b % 2:
            spreads[b // 2].forward()
    put(2 * micro - 2).wait()
    put(2 * micro - 1).wait()
    for s in spreads:
        s.forward_last()
    for s in spreads:
        s.end()
    for copy in local:
        copy.wait()
    for swap in swaps:
        swap.end()
    wire.finish()


def gather_d(d, x_all, gain, shift, w_gu, w_down, which, one):
    micro, tok, feat = d.shape
    depth = w_gu.shape[1]
    count = SPREAD * micro + len(which)
    return kernel(
        functools.partial(gather_d_kernel, which, one), (d, x_all, gain, shift, w_gu, w_down),
        [ANY, ANY, VMEM, VMEM, VMEM, VMEM],
        (shaped((micro, 2, tok, 4 * feat)), shaped((micro * 2 * tok, 4 * feat))) + (shaped((2 * depth, 3 * one)),) * len(which),
        (ANY,) * (2 + len(which)), 48, "gather_d",
        [pltpu.VMEM((len(which), 2, depth, 3 * one), BF)] + [pltpu.VMEM((2, tok, 4 * feat), BF)] * 2
        + sems(count, count, micro + len(which), 4 * micro),
        talk=5,
    )


def row_slot(out, m, sub):
    half = sub // 2

    def slot(yy, nn, part):
        ref = out.at[m, yy, nn]
        return ref if part is None else ref.at[pl.ds(part * half, half)]

    return slot


def run_spreads(spreads, local):
    for s in spreads:
        s.forward()
    for s in spreads:
        s.forward_last()
    for s in spreads:
        s.end()
    for copy in local:
        copy.wait()


def attn_out_kernel(att, wo, x_all, gain, shift, middle, n2, *scratch):
    *red, xb, nb, ss, rs, ls = scratch
    at = Place()
    micro, sub, width = middle.shape
    zn, dz, cols = wo.shape
    span = att.shape[1]
    tok = red[0].shape[2]
    meet([at.sib, at.xn, at.yn])
    wire = Wire(ss, rs)
    own = [pltpu.make_async_copy(x_all.at[m, at.y, pl.ds(at.n * sub, sub)], xb.at[m], ls.at[m]) for m in range(micro)]
    for copy in own:
        copy.start()

    def compute(m, yy):
        def tile(lo, size):
            a = att[pl.ds(pl.multiple_of((m * 2 + yy) * tok, tok) + lo, size), :]
            for k in range(zn):
                red[0][m, yy, pl.ds(lo, size), k * dz : (k + 1) * dz] = dot_nt(a, wo[k, :, cols - span :]).astype(BF)

        blockwise(red[0], m, yy, tile)

    spreads, local = [], []

    def finish(m, total):
        own[m].wait()
        step = sub // 2
        for lo in range(0, sub, step):
            mid = xb[m, lo : lo + step, :].astype(F32) + total(lo, step)
            middle[m, lo : lo + step, :] = mid
            xhat, _ = normalise(mid)
            nb[m, lo : lo + step, :] = (xhat * gain[...] + shift[...]).astype(BF)
        slot = row_slot(n2, m, sub)
        spreads.append(Spread(wire, at, nb.at[m], slot))
        spreads[-1].begin()
        local.append(pltpu.make_async_copy(nb.at[m], slot(at.y, at.n, None), ls.at[micro + m]))
        local[-1].start()

    reduce_rows(wire, at, red, compute, finish)
    run_spreads(spreads, local)
    wire.finish()


def attn_out(att, wo, x_all, gain, shift):
    micro, _, tok, width = x_all.shape
    sub = tok // 4
    count = (REDUCE + SPREAD) * micro
    return kernel(
        attn_out_kernel, (att, wo, x_all, gain, shift), [VMEM, VMEM, ANY, VMEM, VMEM],
        (shaped((micro, sub, width), F32), shaped((micro, 2, 4, sub, width))), (VMEM, ANY), 85, "attn_out",
        reduce_scratch(micro, tok, sub, width) + [pltpu.VMEM((micro, sub, width), BF)] * 2 + sems(count, count, 2 * micro),
        talk=1,
    )


def nt_compute(part, lows, ws, first, each=0):
    zn, dz, _ = ws[0].shape
    tok = part.shape[2]
    span = lows[0].shape[1]

    def compute(m, yy):
        def tile(lo, size):
            at = pl.multiple_of((m * 2 + yy) * tok, tok) + lo
            for k in range(zn):
                acc = None
                for i, (low, w) in enumerate(zip(lows, ws)):
                    lo_col = first + i * each
                    term = dot_nt(low[pl.ds(at, size), :], w[k, :, lo_col : lo_col + span])
                    acc = term if acc is None else acc + term
                part[m, yy, pl.ds(lo, size), k * dz : (k + 1) * dz] = acc.astype(BF)

        blockwise(part, m, yy, tile)

    return compute


class Columns:
    def __init__(self, groups, cols, bufs, load):
        self.copies = [
            pltpu.make_async_copy(src.at[:, :, cols], bufs.at[k], load.at[k]) for k, src in enumerate(groups)
        ]
        for copy in self.copies:
            copy.start()

    def wait(self):
        for copy in self.copies:
            copy.wait()


def chunk_refs(pair, last):
    return [pair.at[:, k] for k in range(pair.shape[1])] + [last]


def ffn_back_kernel(jobs, parts, *refs):
    guls = refs[:parts]
    pair, last, d_all, middle, gain, *refs = refs[parts:]
    zin, (mid_grad, branch, vec), refs = refs[: len(jobs.ins)], refs[len(jobs.ins) :][:3], refs[len(jobs.ins) + 3 :]
    zout, refs = refs[: len(jobs.outs)], refs[len(jobs.outs) :]
    *red, db, nb, wv, ss, rs, ls, lw, zb, zl = refs
    at = Place()
    micro, sub, width = middle.shape
    span = guls[0].shape[1]
    weights = Columns(chunk_refs(pair, last), pl.ds(0, span), wv, lw)
    own = [pltpu.make_async_copy(d_all.at[m, at.y, pl.ds(at.n * sub, sub)], db.at[m], ls.at[m]) for m in range(micro)]
    for copy in own:
        copy.start()
    meet([at.sib, at.xn, at.yn] + z_partners(jobs.zn))
    wire = Wire(ss, rs)
    host = jobs.host(wire, zin, zout, (zb, zl))
    host.begin()
    vec[...] = jnp.zeros_like(vec)
    spreads, local = [], []

    def finish(m, total):
        own[m].wait()
        step = sub // 2
        for lo in range(0, sub, step):
            grad = total(lo, step)
            xhat, rstd = normalise(middle[m, lo : lo + step, :])
            vec[0:1, :] += jnp.sum(grad * xhat, axis=0, keepdims=True)
            vec[1:2, :] += jnp.sum(grad, axis=0, keepdims=True)
            mg = db[m, lo : lo + step, :].astype(F32) + norm_back(xhat, rstd, grad, gain[...])
            mid_grad[m, lo : lo + step, :] = mg
            nb[m, lo : lo + step, :] = mg.astype(BF)
        slot = row_slot(branch, m, sub)
        spreads.append(Spread(wire, at, nb.at[m], slot))
        spreads[-1].begin()
        local.append(pltpu.make_async_copy(nb.at[m], slot(at.y, at.n, None), ls.at[micro + m]))
        local[-1].start()

    weights.wait()
    reduce_rows(wire, at, red, nt_compute(red[0], guls, [wv.at[k] for k in range(parts)], 0), finish, host.next)
    run_spreads(spreads, local)
    host.end()
    wire.finish()


def ffn_back(guls, pair, last, d_all, middle, gain, plan, zn, first):
    parts = len(guls)
    micro, _, tok, width = d_all.shape
    sub = tok // 4
    jobs = Jobs(plan, zn)
    count = (REDUCE + SPREAD) * micro + 2 * jobs.steps
    span = guls[0].shape[1]
    return kernel(
        functools.partial(ffn_back_kernel, jobs, parts), (*guls, pair, last, d_all, middle, gain, *jobs.ins),
        [VMEM] * parts + [ANY, ANY, ANY, VMEM, VMEM] + [ANY] * len(jobs.ins),
        (shaped((micro, sub, width), F32), shaped((micro, 2, 4, sub, width)), shaped((8, width), F32), *jobs.outs),
        (VMEM, ANY, VMEM) + (ANY,) * len(jobs.outs), 90, "ffn_back",
        reduce_scratch(micro, tok, sub, width) + [pltpu.VMEM((micro, sub, width), BF)] * 2
        + [pltpu.VMEM((parts, zn, width // zn, span), BF)] + sems(count, count, 2 * micro, parts) + jobs.scratch,
        first, talk=2,
    )


def host_kernel(jobs, *refs):
    zin, zout, (ss, rs, zb, zl) = refs[: len(jobs.ins)], refs[len(jobs.ins) :][: len(jobs.outs)], refs[-4:]
    meet(z_partners(jobs.zn))
    host = jobs.host(Wire(ss, rs), zin, zout, (zb, zl))
    host.begin()
    host.end()


def host_only(plan, zn, first):
    jobs = Jobs(plan, zn)
    return kernel(
        functools.partial(host_kernel, jobs), jobs.ins, [ANY] * len(jobs.ins), tuple(jobs.outs), (ANY,) * len(jobs.outs),
        20 * jobs.steps, "along_z", sems(2 * jobs.steps, 2 * jobs.steps) + jobs.scratch, first, talk=8,
    )


class Deal:
    def __init__(self, wire, at, rows, out, m, sems, k):
        sub, width = rows.shape[1], rows.shape[2]
        feat = width // 4

        def cols(nn):
            return rows.at[m, :, pl.ds(pl.multiple_of(nn * feat, feat), feat)]

        place = out.at[m, pl.ds(pl.multiple_of(at.n * sub, sub), sub)]
        self.local = pltpu.make_async_copy(cols(at.n), place, sems.at[k])
        self.copies = [
            wire.make(cols(at.nx), place, at.xn),
            wire.make(cols(at.nd), place, at.xs),
            wire.make(cols(at.ns), place, at.sib),
        ]

    def begin(self):
        for copy in self.copies:
            copy.start()
        self.local.start()

    def end(self):
        for copy in self.copies:
            copy.wait_recv()
        self.local.wait()


def last_kernel(jobs, zn, *refs):
    low, wa, x_all, mid_grad, gain, vec2, g1, got1, got2, *refs = refs
    zin, refs = refs[: len(jobs.ins)], refs[len(jobs.ins) :]
    in_grad, sums, *refs = refs
    settled, zout, refs = refs[:6], refs[6:][: len(jobs.outs)], refs[6 + len(jobs.outs) :]
    red, refs = refs[:8], refs[8:]
    xb, ob, w1, mine, plane, summed, lines, yb, yl, ss, rs, ls, *talk = refs
    at = Place()
    z = lax.axis_index("z")
    micro, sub, width = mid_grad.shape
    qkv = pltpu.make_async_copy(wa.at[:, :, pl.ds(0, low.shape[1])], w1, ls.at[2 * micro])
    qkv.start()
    own = [pltpu.make_async_copy(x_all.at[m, at.y, pl.ds(at.n * sub, sub)], xb.at[m], ls.at[m]) for m in range(micro)]
    for copy in own:
        copy.start()
    flips = [(dy, dn) for dy in range(2) for dn in range(4) if dy or dn]
    peers = [{"y": (at.y + dy) % 2, "n": (at.n + dn) % 4} for dy, dn in flips]
    along = [{"z": (z + dz) % zn} for dz in range(1, zn)]
    meet(peers + along)
    wire = Wire(ss, rs)
    host = jobs.host(wire, zin, zout, talk)
    host.begin()
    g2, ga = zin[0], zin[3]
    settles = [
        Settle(wire, at, zn, g1, (got1, got2), settled[0], settled[1], yb, yl),
        Settle(wire, at, zn, g2, zout[0:2], settled[2], settled[3], yb, yl),
        Settle(wire, at, zn, ga, zout[-2:], settled[4], settled[5], yb, yl),
    ]

    def settle(k):
        def run():
            if k:
                settles[k - 1].wait()
            settles[k].go()

        return run

    host.then = {1: settle(1), zn: settle(2)}
    mine[...] = jnp.zeros_like(mine)
    mine[2:4] = vec2[0:2]
    qkv.wait()
    total = Reduce(wire, at, red, nt_compute(red[0], [low], [w1], 0))
    for m in range(micro):
        total.cores(m)
        total.diagonal(m)
    settle(0)()
    host.next()
    for m in range(micro):
        total.sides(m)
    step = sub // 2
    deals = []
    for m in range(micro):
        total.arrived(m)
        own[m].wait()
        for lo in range(0, sub, step):
            grad = total.total(m, lo, step)
            xhat, rstd = normalise(xb[m, lo : lo + step, :].astype(F32))
            mine[0:1, :] += jnp.sum(grad * xhat, axis=0, keepdims=True)
            mine[1:2, :] += jnp.sum(grad, axis=0, keepdims=True)
            back = norm_back(xhat, rstd, grad, gain[...])
            ob[m, lo : lo + step, :] = (mid_grad[m, lo : lo + step, :] + back).astype(BF)
        deals.append(Deal(wire, at, ob, in_grad, m, ls, micro + m))
        deals[-1].begin()
    near = [wire.make(mine, plane.at[k], d) for k, d in enumerate(peers)]
    for copy in near:
        copy.start()
    host.next()
    for copy in near:
        copy.wait_recv()
    both = mine[...]
    for k in range(len(peers)):
        both = both + plane[k]
    summed[...] = both
    far = [wire.make(summed, lines.at[k], d) for k, d in enumerate(along)]
    for copy in far:
        copy.start()
    host.next()
    for copy in far:
        copy.wait_recv()
    both = summed[...]
    for k in range(len(along)):
        both = both + lines[k]
    sums[...] = both
    for deal in deals:
        deal.end()
    host.end()
    settles[-1].wait()
    wire.finish()


def last_sums(low, wa, x_all, mid_grad, gain, vec2, g1, got, plan, zn):
    micro, _, tok, width = x_all.shape
    sub = tok // 4
    dz, cols = width // zn, low.shape[1]
    jobs = Jobs(plan, zn)
    count = (REDUCE + 3) * micro + 7 + zn - 1 + 2 * jobs.steps + 3
    size = vec2.shape
    rows = pltpu.VMEM((micro, sub, width), BF)
    chunk_cols, big = g1.shape[1], plan[-1][0].shape[1]
    halves = [shaped((dz // 2, k)) for k in (chunk_cols,) * 4 + (big, big)]
    return kernel(
        functools.partial(last_kernel, jobs, zn),
        (low, wa, x_all, mid_grad, gain, vec2, g1, *got, *jobs.ins),
        [VMEM, ANY, ANY, VMEM, VMEM, VMEM] + [ANY] * (3 + len(jobs.ins)),
        (shaped((micro, tok, width // 4)), shaped(size, F32), *halves, *jobs.outs),
        (ANY, VMEM) + (ANY,) * (6 + len(jobs.outs)), 100, "last_sums",
        reduce_scratch(micro, tok, sub, width) + [rows] * 2 + [pltpu.VMEM((zn, dz, cols), BF)]
        + [pltpu.VMEM(size, F32), pltpu.VMEM((7,) + size, F32), pltpu.VMEM(size, F32), pltpu.VMEM((zn - 1,) + size, F32)]
        + [pltpu.VMEM((3, dz, big), BF)] + sems(4, count, count, 2 * micro + 1) + jobs.scratch,
        talk=3,
    )


def tiles(rows, cols):
    return pl.BlockSpec((rows, cols), lambda i: (i, 0))


def same_protein(lens, b, tok, count):
    col = lax.broadcasted_iota(jnp.int32, (tok, 1), 0)
    row = lax.broadcasted_iota(jnp.int32, (1, tok), 1)
    pc, pr = jnp.zeros_like(col), jnp.zeros_like(row)
    end = jnp.int32(0)
    for k in range(count):
        end = end + lens[b % 2, b // 2, k]
        pc = pc + (col >= end).astype(jnp.int32)
        pr = pr + (row >= end).astype(jnp.int32)
    return pc == pr


def turn(v, cos, sin):
    return v * cos + pltpu.roll(v, HEAD_DIM // 2, 1) * sin


def attention_body(count, ends, n1, w, cos, sin, qkv, att):
    zn, dz, _ = w.shape
    cols = qkv.shape[1]
    tok = n1.shape[0]
    heads = cols // 3 // HEAD_DIM
    span = heads * HEAD_DIM
    acc = dot(n1[:, 0:dz], w[0, :, :cols])
    for k in range(1, zn):
        acc = acc + dot(n1[:, k * dz : (k + 1) * dz], w[k, :, :cols])
    same = same_protein(ends, pl.program_id(0), tok, count)
    scale = HEAD_DIM ** (-0.5)
    for h in range(heads):
        lo = h * HEAD_DIM
        q = turn(acc[:, lo : lo + HEAD_DIM], cos[...], sin[...]).astype(BF)
        k = turn(acc[:, span + lo : span + lo + HEAD_DIM], cos[...], sin[...]).astype(BF)
        v = acc[:, 2 * span + lo : 2 * span + lo + HEAD_DIM].astype(BF)
        qkv[:, lo : lo + HEAD_DIM] = q
        qkv[:, span + lo : span + lo + HEAD_DIM] = k
        qkv[:, 2 * span + lo : 2 * span + lo + HEAD_DIM] = v
        s = jnp.where(same, dot_nt(q, k) * scale, -1e30)
        e = jnp.exp(s - jnp.max(s, axis=-1, keepdims=True))
        p = (e / jnp.sum(e, axis=-1, keepdims=True)).astype(BF)
        att[:, lo : lo + HEAD_DIM] = dot(p, v).astype(BF)


def attention(count, ends, n1, w, cos, sin, passed, tok):
    rows, width = n1.shape
    cols = w.shape[2] // 4 * 3

    def body(e, a, b, c, d, _, qkv, att, __):
        attention_body(count, e, a, b, c, d, qkv, att)

    return kernel(
        body, (ends, n1, w, cos, sin, passed),
        [SMEM, tiles(tok, width), VMEM, tiles(tok, HEAD_DIM), tiles(tok, HEAD_DIM), ANY],
        (shaped((rows, cols)), shaped((rows, cols // 3)), shaped(passed.shape)),
        (tiles(tok, cols), tiles(tok, cols // 3), ANY), 20, "attention", grid=(rows // tok,), aliases={5: 2},
    )


def attention_back_body(count, ends, b, branch, wo, qkv, cos, sin, low):
    zn, dz, span = wo.shape
    tok = branch.shape[0]
    heads = span // HEAD_DIM
    acc = dot(branch[:, 0:dz], wo[0])
    for k in range(1, zn):
        acc = acc + dot(branch[:, k * dz : (k + 1) * dz], wo[k])
    same = same_protein(ends, b, tok, count)
    scale = HEAD_DIM ** (-0.5)
    for h in range(heads):
        lo = h * HEAD_DIM
        ag = acc[:, lo : lo + HEAD_DIM].astype(BF)
        q = qkv[:, lo : lo + HEAD_DIM]
        k = qkv[:, span + lo : span + lo + HEAD_DIM]
        v = qkv[:, 2 * span + lo : 2 * span + lo + HEAD_DIM]
        s = jnp.where(same, dot_nt(q, k) * scale, -1e30)
        e = jnp.exp(s - jnp.max(s, axis=-1, keepdims=True))
        p = e / jnp.sum(e, axis=-1, keepdims=True)
        pg = dot_nt(ag, v)
        vg = dot_tn(p.astype(BF), ag)
        rd = jnp.sum(p * pg, axis=-1, keepdims=True)
        sg = (p * (pg - rd)).astype(BF)
        qg = dot(sg, k) * scale
        kg = dot_tn(sg, q) * scale
        low[:, lo : lo + HEAD_DIM] = turn(qg, cos[...], -sin[...]).astype(BF)
        low[:, span + lo : span + lo + HEAD_DIM] = turn(kg, cos[...], -sin[...]).astype(BF)
        low[:, 2 * span + lo : 2 * span + lo + HEAD_DIM] = vg.astype(BF)


def attention_back_kernel(jobs, count, parts, *refs):
    lens, branch, att, wa, qkv, cos, sin, n1, g0, got0, got1, pair, last, middle, *refs = refs
    hids, zin, refs = refs[:parts], refs[parts:][: len(jobs.ins)], refs[parts + len(jobs.ins) :]
    low, grads, keep, theirs, layer_out, *refs = refs
    zout, refs = refs[: len(jobs.outs)], refs[len(jobs.outs) :]
    red, refs = refs[:8], refs[8:]
    bv, wo, ob, yb, load, yl, ls, ss, rs, *talk = refs
    rows, width = bv.shape
    zn, dz, span = wo.shape
    tok = rows // 4
    one = hids[0].shape[1]
    micro, sub, _ = middle.shape
    at = Place()
    cols = low.shape[1]
    downs, chunks = [], chunk_refs(pair, last)
    for k in range(parts):
        place = pl.ds(k * one, one)
        downs.append(pltpu.make_async_copy(hids[k], low.at[:, place], load.at[9 + k]))
        downs.append(
            pltpu.make_async_copy(chunks[k].at[:, :, pl.ds(2 * one, one)], grads.at[:, :, place], load.at[9 + parts + k])
        )
    for copy in downs:
        copy.start()
    weights = pltpu.make_async_copy(wa.at[:, :, pl.ds(cols, span)], wo, load.at[8])
    weights.start()

    def bring(b):
        here = pl.ds(b * tok, tok)
        return (
            pltpu.make_async_copy(branch.at[here], bv.at[here], load.at[b]),
            pltpu.make_async_copy(n1.at[here], red[0].at[b // 2, b % 2], load.at[4 + b]),
        )

    for b in range(4):
        bring(b)[0].start()
    meet(z_partners(zn) + [at.sib, at.xn, at.yn, at.xs])
    wire = Wire(ss, rs)
    host = jobs.host(wire, zin, zout, talk)
    settle = Settle(wire, at, zn, g0, (got0, got1), keep, theirs, yb, yl)
    host.begin()
    for copy in downs:
        copy.wait()
    lows = [low.at[:, pl.ds(k * one, one)] for k in range(parts)]
    total = Reduce(wire, at, red, nt_compute(red[0], lows, [grads] * parts, 0, one))
    for m in range(micro):
        total.cores(m)
        total.diagonal(m)
    settle.go()
    weights.wait()

    def block(b):
        bring(b)[0].wait()
        here = pl.ds(b * tok, tok)
        attention_back_body(
            count, lens, b, bv.at[here], wo, qkv.at[here], cos.at[here], sin.at[here], low.at[here]
        )

    block(0)
    for m in range(micro):
        total.sides(m)
        total.release(m)
    for b in range(4):
        bring(b)[1].start()
    block(1)
    host.next()
    block(2)
    block(3)
    host.next()
    for b in range(4):
        bring(b)[1].wait()

    def weights_of(k, carry):
        here = pl.ds(pl.multiple_of(k * dz, dz), dz)
        acc = 0.0
        for b in range(4):
            acc = acc + dot_tn(red[0][b // 2, b % 2, :, here], low[pl.ds(b * tok, tok), :])
        grads[k, :, :cols] = acc.astype(BF)
        grads[k, :, cols:] = dot_tn(bv[:, here], att[...]).astype(BF)
        return carry

    lax.fori_loop(0, zn, weights_of, 0)
    deals, step = [], sub // 2
    for m in range(micro):
        total.arrived(m)
        for lo in range(0, sub, step):
            ob[m, lo : lo + step, :] = (middle[m, lo : lo + step, :] + total.total(m, lo, step)).astype(BF)
        deals.append(Deal(wire, at, ob, layer_out, m, ls, m))
        deals[-1].begin()
    host.next()
    settle.wait()
    for deal in deals:
        deal.end()
    host.end()
    wire.finish()


def attention_back(count, lens, branch, att, wa, qkv, cos, sin, n1, g0, got, pair, last, middle, hids, plan, zn):
    rows, width = branch.shape
    cols, span, parts = qkv.shape[1], att.shape[1], len(hids)
    micro, sub, _ = middle.shape
    tok = rows // 4
    dz = width // zn
    jobs = Jobs(plan, zn)
    half = shaped((dz // 2, g0.shape[1]))
    links = 2 * jobs.steps + 1 + (REDUCE + 3) * micro
    return kernel(
        functools.partial(attention_back_kernel, jobs, count, parts),
        (lens, branch, att, wa, qkv, cos, sin, n1, g0, *got, pair, last, middle, *hids, *jobs.ins),
        [SMEM, ANY, VMEM, ANY, VMEM, VMEM, VMEM, ANY] + [ANY] * 5 + [VMEM] + [ANY] * (parts + len(jobs.ins)),
        (shaped((rows, cols)), shaped((zn, dz, cols + span)), half, half, shaped((micro, tok, width // 4)), *jobs.outs),
        (VMEM, VMEM) + (ANY,) * (3 + len(jobs.outs)), 70, "attention_back",
        reduce_scratch(micro, tok, sub, width)
        + [pltpu.VMEM((rows, width), BF), pltpu.VMEM((zn, dz, span), BF), pltpu.VMEM((micro, sub, width), BF)]
        + [pltpu.VMEM((3, dz, g0.shape[1]), BF)]
        + sems(9 + 2 * parts, 4, micro, links, links) + jobs.scratch,
        talk=9,
    )


def chunk_body(jobs, c, n2, dy, w, mask, *refs):
    zin, (low, hidden, grad), refs = refs[: len(jobs.ins)], refs[len(jobs.ins) :][:3], refs[len(jobs.ins) + 3 :]
    zout, (nv, dv, wv, load, *talk) = refs[: len(jobs.outs)], refs[len(jobs.outs) :]
    zn, dz, cols = wv.shape
    one = cols // 3
    steps = load.shape[1] - 1
    tile = nv.shape[0] // steps
    whole = pltpu.make_async_copy(w if c is None else w.at[:, c], wv, load.at[0, steps])
    whole.start()

    def bring(t):
        at = pl.ds(pl.multiple_of(t * tile, tile), tile)
        return (
            pltpu.make_async_copy(n2.at[at], nv.at[at], load.at[0, t]),
            pltpu.make_async_copy(dy.at[at], dv.at[at], load.at[1, t]),
        )

    for t in range(steps):
        for copy in bring(t):
            copy.start()
    if talk:
        ss, rs, *talk = talk
        meet(z_partners(jobs.zn))
        host = jobs.host(Wire(ss, rs), zin, zout, talk)
        host.begin()
    whole.wait()

    def forward(t, carry):
        for copy in bring(t):
            copy.wait()
        at = pl.ds(pl.multiple_of(t * tile, tile), tile)
        acc = hg = 0.0
        for k in range(zn):
            acc = acc + dot(nv[at, k * dz : (k + 1) * dz], wv[k, :, : 2 * one])
            hg = hg + dot(dv[at, k * dz : (k + 1) * dz], wv[k, :, 2 * one :])
        hg = hg * mask[...]
        g, u = acc[:, :one], acc[:, one:]
        phi = 0.5 * (1.0 + lax.erf(g * (0.5**0.5)))
        slope = phi + g * jnp.exp(-0.5 * g * g) * 0.3989422804014327
        act = g * phi
        hidden[at, :] = (act * u * mask[...]).astype(BF)
        low[at, :one] = (hg * u * slope).astype(BF)
        low[at, one:] = (hg * act).astype(BF)
        return carry

    lax.fori_loop(0, steps, forward, 0)

    def weights(k, carry):
        at = pl.ds(pl.multiple_of(k * dz, dz), dz)
        grad[at, : 2 * one] = dot_tn(nv[:, at], low[...]).astype(BF)
        grad[at, 2 * one :] = dot_tn(dv[:, at], hidden[...]).astype(BF)
        return carry

    lax.fori_loop(0, zn, weights, 0)
    if jobs.steps:
        host.end()


def chunk(n2, dy, w, c, mask, plan, zn, talk, first):
    rows, width = n2.shape
    cols = w.shape[-1]
    one = cols // 3
    jobs = Jobs(plan, zn)
    return kernel(
        functools.partial(chunk_body, jobs, c), (n2, dy, w, mask, *jobs.ins), [ANY, ANY, ANY, VMEM] + [ANY] * len(jobs.ins),
        (shaped((rows, 2 * one)), shaped((rows, one)), shaped((width, cols)), *jobs.outs),
        (VMEM,) * 3 + (ANY,) * len(jobs.outs), 22, "ffn_chunk",
        [pltpu.VMEM((rows, width), BF)] * 2 + [pltpu.VMEM((zn, width // zn, cols), BF), pltpu.SemaphoreType.DMA((2, 5))]
        + (sems(2 * jobs.steps, 2 * jobs.steps) + jobs.scratch if jobs.steps else []),
        first, talk=talk if jobs.steps else None,
    )


def weight_grad_body(a, b, out):
    out[...] = dot_tn(a[...], b[...]).astype(BF)


def weight_grad(a, b, first=()):
    rows, width = a.shape
    cols = b.shape[1]
    tile = 512
    return kernel(
        weight_grad_body, (a, b), [pl.BlockSpec((rows, tile), lambda i: (0, i)), VMEM],
        shaped((width, cols)), tiles(tile, cols), 10, "weight_grad", first=first, grid=(width // tile,),
    )


def ordered(y, keep, got, axis):
    return jnp.concatenate([jnp.where(y == 0, keep, got), jnp.where(y == 0, got, keep)], axis=axis)


CHUNKS = 3


def on_device(inputs, lengths, counts, w_qkv, w_out, w_gu, w_down, g1, b1, g2, b2, dy_in):
    z = lax.axis_index("z")
    y = lax.axis_index("y")
    n = lax.axis_index("n")
    zn = lax.axis_size("z")
    micro, tok, feat = inputs.shape
    width = feat * lax.axis_size("n")
    rows = micro * 2 * tok
    depth = w_qkv.shape[1]
    half_slots = w_gu.shape[2] // 2
    one = half_slots // CHUNKS

    def gather_z(w):
        return lax.all_gather(w, "z", axis=0, tiled=False)

    own_attn = swap_attn(w_qkv, w_out)
    wa = gather_z(own_attn)
    vecs = jnp.stack([g1, b1, g2, b2]).astype(F32)
    vecs = jnp.pad(vecs, ((0, 4), (0, 0)))
    count = lengths.shape[2]
    lens = jnp.pad(lengths[:, 0], ((0, 8 - micro), (0, 128 - count)))
    half_dim = HEAD_DIM // 2
    freq = 10000.0 ** (-(jnp.arange(HEAD_DIM) % half_dim).astype(F32) / half_dim)
    x_all, norms, lens, cos, sin, own_01 = gather_x(
        inputs, vecs, lens, freq[None], w_gu, w_down, zn, (0, 1), one, count, (own_attn,)
    )
    norms = norms.transpose(2, 0, 1, 3).reshape(8, width)
    gain1, shift1, gain2, shift2 = (norms[i : i + 1] for i in range(4))
    own = jnp.sum(jnp.where(jnp.arange(counts.shape[0]) == n, counts, 0))
    mask = (y * half_slots + jnp.arange(half_slots) < own).astype(F32)[None]

    d_all, n1, own_2 = gather_d(dy_in, x_all, gain1, shift1, w_gu, w_down, (2,), one)
    dy = d_all.reshape(rows, width)
    qkv, att, own_2 = attention(count, lens, n1, wa, cos, sin, own_2, tok)
    w_01, w_2 = gather_z(own_01), gather_z(own_2)
    middle, n2 = attn_out(att, wa, x_all, gain2, shift2)
    n2 = n2.reshape(rows, width)

    def own_mask(c):
        return mask[:, c * one : (c + 1) * one]

    low0, hid0, g0 = chunk(n2, dy, w_01, 0, own_mask(0), [], zn, None, ())
    low1, hid1, grad1 = chunk(n2, dy, w_01, 1, own_mask(1), [], zn, None, (g0,))
    low2, hid2, grad2, *p = chunk(n2, dy, w_2, None, own_mask(2), [(g0, None, 0, 1)], zn, 7, (grad1,))
    mid_grad, branch, vec2, *q = ffn_back(
        [low0, low1, low2], w_01, w_2, d_all, middle, gain2, [(g0, p, 1, zn - 2), (grad1, None, 0, zn - 2)], zn, ()
    )
    got0, got1 = q[2 * zn - 6 : 2 * zn - 4], q[-2:]
    branch = branch.reshape(rows, width)
    low, attn_g, keep0, theirs0, layer_out, *r = attention_back(
        count, lens, branch, att, wa, qkv, cos, sin, n1, g0, got0, w_01, w_2, middle, [hid0, hid1, hid2],
        [(grad1, got1, zn - 2, 1), (grad2, None, 0, zn - 2)], zn,
    )
    in_grad, sums, keep1, theirs1, keep2, theirs2, keep, attn_theirs, *_ = last_sums(
        low, wa, x_all, mid_grad, gain1, vec2, grad1, r[0:2],
        [(grad2, r[-2:], zn - 2, 1), (attn_g.reshape(width, -1), None, 0, zn - 1)], zn,
    )
    pairs = [(keep0, theirs0), (keep1, theirs1), (keep2, theirs2)]

    def joined(k):
        mine, theirs = (jnp.concatenate([p[i][:, k * one : (k + 1) * one] for p in pairs], axis=1) for i in (0, 1))
        return ordered(y, mine, theirs, 1)

    gu_grad = jnp.stack([joined(0), joined(1)]).astype(F32)
    down_grad = joined(2).T.astype(F32)
    cols = 3 * att.shape[1]
    mine, theirs = (v[:, :cols].reshape(depth, 3, -1) for v in (keep, attn_theirs))
    qkv_grad = ordered(y, mine, theirs, 2).transpose(1, 0, 2).astype(F32)
    out_grad = ordered(y, keep[:, cols:].T, attn_theirs[:, cols:].T, 0).astype(F32)

    mine = lax.dynamic_slice_in_dim(sums, (z * 2 + y) * g1.shape[0], g1.shape[0], 1)
    return (
        layer_out,
        in_grad,
        qkv_grad,
        out_grad,
        gu_grad,
        down_grad,
        mine[0],
        mine[1],
        mine[2],
        mine[3],
    )


def solution(mesh):
    wide, narrow = mesh.shape["wide"], mesh.shape["narrow"]
    grid = Mesh(mesh.devices.reshape(wide // 2, 2, narrow), ("z", "y", "n"))
    w = ("z", "y")
    tokens, depth, lines, vector = P(None, w, "n"), P(None, w, "n"), P("n", w), P(w)
    return jax.shard_map(
        on_device,
        mesh=grid,
        in_specs=(
            tokens, P(None, w, None), P(), depth, lines, depth, lines,
            vector, vector, vector, vector, tokens,
        ),
        out_specs=(
            tokens, tokens, depth, lines, depth, lines, vector, vector, vector, vector,
        ),
        check_vma=False,
    )
```

```python
import functools

import jax
import jax.numpy as jnp
from jax import lax
from jax.experimental import pallas as pl
from jax.experimental.pallas import tpu as pltpu
from jax.sharding import Mesh
from jax.sharding import PartitionSpec as P

HEAD_DIM = 128
EPS = 1e-05
BF = jnp.bfloat16
F32 = jnp.float32
MESH = pl.DeviceIdType.MESH
VMEM_BYTES = 60 * 2**20
SWAP = [(0, 1), (1, 0)]
ANY = pl.BlockSpec(memory_space=pl.ANY)
VMEM = pl.BlockSpec(memory_space=pltpu.VMEM)
SMEM = pl.BlockSpec(memory_space=pltpu.SMEM)


def dot(a, b):
    return jnp.dot(a, b, preferred_element_type=F32)


def dot_nt(a, b):
    return lax.dot_general(a, b, (((1,), (1,)), ((), ())), preferred_element_type=F32)


def dot_tn(a, b):
    return lax.dot_general(a, b, (((0,), (0,)), ((), ())), preferred_element_type=F32)


def normalise(v):
    centred = v - jnp.mean(v, axis=-1, keepdims=True)
    rstd = lax.rsqrt(jnp.mean(centred * centred, axis=-1, keepdims=True) + EPS)
    return centred * rstd, rstd


def norm_back(xhat, rstd, grad, gain):
    dx = grad * gain
    a = jnp.mean(dx, axis=-1, keepdims=True)
    b = jnp.mean(dx * xhat, axis=-1, keepdims=True)
    return rstd * (dx - a - xhat * b)


def cost(us, sent=0):
    return pl.CostEstimate(flops=int(us * 1e9), bytes_accessed=int(us * 3.2e6), transcendentals=0)


def without(body, ins, extra):
    def run(*refs):
        return body(*refs[:ins], *refs[ins + extra :])

    return run


def kernel(body, ins, in_specs, outs, out_specs, us, name, scratch=(), first=(), grid=(), talk=None, aliases=None):
    extra = len(first)
    return pl.pallas_call(
        without(body, len(ins), extra),
        grid=grid,
        in_specs=list(in_specs) + [ANY] * extra,
        out_specs=out_specs,
        out_shape=outs,
        scratch_shapes=list(scratch),
        input_output_aliases=aliases or {},
        compiler_params=pltpu.CompilerParams(
            vmem_limit_bytes=VMEM_BYTES, collective_id=talk, has_side_effects=talk is not None
        ),
        cost_estimate=cost(us),
        name=name,
    )(*ins, *first)


def sems(*counts):
    return [pltpu.SemaphoreType.DMA((k,)) for k in counts]


def shaped(shape, dtype=BF):
    return jax.ShapeDtypeStruct(tuple(shape), dtype)


class Place:
    def __init__(self):
        self.y = lax.axis_index("y")
        self.n = lax.axis_index("n")
        self.x = self.n // 2
        self.c = self.n % 2
        self.ns = self.n + 1 - 2 * self.c
        self.nx = (self.n + 2) % 4
        self.nd = (self.ns + 2) % 4
        self.sib = {"n": self.ns}
        self.xn = {"n": self.nx}
        self.yn = {"y": 1 - self.y}
        self.xs = {"n": self.nd}


def meet(devices):
    barrier = pltpu.get_barrier_semaphore()
    for d in devices:
        pl.semaphore_signal(barrier, inc=1, device_id=d, device_id_type=MESH)
    pl.semaphore_wait(barrier, len(devices))


class Wire:
    def __init__(self, send_sems, recv_sems, first=0):
        self.ss, self.rs, self.at, self.sent = send_sems, recv_sems, first, []

    def make(self, src, dst, device, keep=True, again=False):
        self.at += not again
        k = self.at - 1
        copy = pltpu.make_async_remote_copy(
            src_ref=src, dst_ref=dst, send_sem=self.ss.at[k], recv_sem=self.rs.at[k],
            device_id=device, device_id_type=MESH,
        )
        if keep:
            self.sent.append(copy)
        return copy

    def finish(self):
        for copy in self.sent:
            copy.wait_send()


SPREAD = 9


class Spread:
    def __init__(self, wire, at, src, slot):
        y, n, nx = at.y, at.n, at.nx
        self.first = [
            wire.make(src, slot(y, n, None), at.xn),
            wire.make(src, slot(y, n, None), at.yn),
            wire.make(src, slot(y, n, None), at.sib),
        ]
        self.on_x = [
            wire.make(slot(y, nx, 0), slot(y, nx, 0), at.yn),
            wire.make(slot(y, nx, None), slot(y, nx, None), at.sib),
        ]
        self.on_y = [
            wire.make(slot(1 - y, n, 1), slot(1 - y, n, 1), at.xn),
            wire.make(slot(1 - y, n, None), slot(1 - y, n, None), at.sib),
        ]
        self.last = [
            wire.make(slot(1 - y, nx, 0), slot(1 - y, nx, 0), at.sib),
            wire.make(slot(1 - y, nx, 1), slot(1 - y, nx, 1), at.sib),
        ]

    def begin(self):
        for copy in self.first:
            copy.start()

    def forward(self):
        self.first[0].wait_recv()
        for copy in self.on_x:
            copy.start()
        self.first[1].wait_recv()
        for copy in self.on_y:
            copy.start()

    def forward_last(self):
        self.on_x[0].wait_recv()
        self.last[0].start()
        self.on_y[0].wait_recv()
        self.last[1].start()

    def end(self):
        self.first[2].wait_recv()
        self.on_x[1].wait_recv()
        self.on_y[1].wait_recv()
        self.last[0].wait_recv()
        self.last[1].wait_recv()


REDUCE = 10


def reduce_scratch(micro, tok, sub, width):
    half = sub // 2
    return [
        pltpu.VMEM((micro, 2, tok, width), BF),
        pltpu.VMEM((micro, 2, 2, sub, width), BF),
        pltpu.VMEM((micro, sub, width), BF),
        pltpu.VMEM((micro, sub, width), BF),
        pltpu.VMEM((micro, sub, width), BF),
        pltpu.VMEM((micro, 2, half, width), BF),
        pltpu.VMEM((micro, sub, width), BF),
        pltpu.VMEM((micro, sub, width), BF),
    ]


class Reduce:
    def __init__(self, wire, at, scratch, compute):
        self.part, self.ra, self.sb, self.sx, self.sy, self.rb, self.rcx, self.rcy = scratch
        self.wire, self.at, self.compute = wire, at, compute
        self.micro, self.sub = self.sb.shape[0], self.sb.shape[1]
        self.a, self.b, self.d = {}, {}, {}
        self.released = False

    def rows(self, core, xx, lo=0, size=None):
        return pl.ds(pl.multiple_of((2 * xx + core) * self.sub, self.sub) + lo, size or self.sub)

    def summed(self, m, yy, xx, lo, size):
        mine = self.part[m, yy, self.rows(self.at.c, xx, lo, size), :].astype(F32)
        return mine + self.ra[m, yy, xx, lo : lo + size, :].astype(F32)

    def cores(self, m):
        at = self.at
        for yk, yy in ((1, 1 - at.y), (0, at.y)):
            self.compute(m, yy)
            for xk, xx in ((1, 1 - at.x), (0, at.x)):
                copy = self.wire.make(self.part.at[m, yy, self.rows(1 - at.c, xx)], self.ra.at[m, yy, xx], at.sib)
                copy.start()
                self.a[m, yk, xk] = copy

    def diagonal(self, m):
        at, sub, half = self.at, self.sub, self.sub // 2
        self.a[m, 1, 1].wait_recv()
        self.sb[m] = self.summed(m, 1 - at.y, 1 - at.x, 0, sub).astype(BF)
        self.b[m, 0] = self.wire.make(self.sb.at[m, 0:half], self.rb.at[m, 0], at.xn)
        self.b[m, 1] = self.wire.make(self.sb.at[m, half:sub], self.rb.at[m, 1], at.yn)
        self.b[m, 0].start()
        self.b[m, 1].start()

    def sides(self, m):
        at, sub, half = self.at, self.sub, self.sub // 2
        sx, sy, rb, rcx, rcy = self.sx, self.sy, self.rb, self.rcx, self.rcy
        self.a[m, 1, 0].wait_recv()
        sy[m, half:sub] = self.summed(m, 1 - at.y, at.x, half, half).astype(BF)
        self.d[m, 0] = self.wire.make(sy.at[m, half:sub], rcy.at[m, half:sub], at.yn)
        self.d[m, 0].start()
        self.a[m, 0, 1].wait_recv()
        sx[m, 0:half] = self.summed(m, at.y, 1 - at.x, 0, half).astype(BF)
        self.d[m, 1] = self.wire.make(sx.at[m, 0:half], rcx.at[m, 0:half], at.xn)
        self.d[m, 1].start()
        self.b[m, 0].wait_recv()
        sy[m, 0:half] = (self.summed(m, 1 - at.y, at.x, 0, half) + rb[m, 0].astype(F32)).astype(BF)
        self.d[m, 2] = self.wire.make(sy.at[m, 0:half], rcy.at[m, 0:half], at.yn)
        self.d[m, 2].start()
        self.b[m, 1].wait_recv()
        sx[m, half:sub] = (self.summed(m, at.y, 1 - at.x, half, half) + rb[m, 1].astype(F32)).astype(BF)
        self.d[m, 3] = self.wire.make(sx.at[m, half:sub], rcx.at[m, half:sub], at.xn)
        self.d[m, 3].start()

    def release(self, m):
        at = self.at
        self.a[m, 0, 0].wait_recv()
        self.ra[m, at.y, at.x] = self.summed(m, at.y, at.x, 0, self.sub).astype(BF)
        for yk in (1, 0):
            for xk in (1, 0):
                copy = self.a[m, yk, xk]
                copy.wait_send()
                self.wire.sent = [other for other in self.wire.sent if other is not copy]
        self.released = True

    def arrived(self, m):
        if not self.released:
            self.a[m, 0, 0].wait_recv()
        for k in range(4):
            self.d[m, k].wait_recv()

    def total(self, m, lo, size):
        if self.released:
            own = self.ra[m, self.at.y, self.at.x, lo : lo + size, :].astype(F32)
        else:
            own = self.summed(m, self.at.y, self.at.x, lo, size)
        return own + self.rcx[m, lo : lo + size, :].astype(F32) + self.rcy[m, lo : lo + size, :].astype(F32)


def nothing():
    pass


def reduce_rows(wire, at, scratch, compute, finish, tick=nothing):
    red = Reduce(wire, at, scratch, compute)
    for m in range(red.micro):
        red.cores(m)
        red.diagonal(m)
    tick()
    for m in range(red.micro):
        red.sides(m)
    for m in range(red.micro):
        red.arrived(m)
        finish(m, lambda lo, size, m=m: red.total(m, lo, size))
        tick()


class Step:
    def __init__(self, wire, z, zn, s, g, prev, got, bufs, load, k):
        rows, cols = got[0].shape
        far, cap = zn - 1 - s, min(s, zn - 2)
        self.bufs, self.cols, self.ways = bufs, cols, []
        for d, (place, sign) in enumerate(((z, 1), (zn - 1 - z, -1))):
            group = (z + sign * far + zn) % zn
            here = bufs.at[d, 0, :, pl.ds(0, cols)]
            own = pltpu.make_async_copy(
                g.at[pl.ds(pl.multiple_of(group * rows, rows), rows)], here, load.at[k + 2 * d]
            )
            came = bufs.at[d, 1, :, pl.ds(0, cols)]
            carry = pltpu.make_async_copy(prev[d], came, load.at[k + 2 * d + 1]) if s else None
            peer = {"z": (z + sign + zn) % zn}
            away = wire.make(here, got[d], peer, keep=False)
            last = d * (zn - 1 - far) + (1 - d) * far
            straight = wire.make(g.at[pl.ds(last * rows, rows)], got[d], peer, keep=False, again=True)
            gets = jnp.logical_and(place >= 1, place <= cap + 1)
            adds = jnp.logical_and(place <= cap, place >= 1)
            self.ways.append((place <= cap, adds, gets, own, carry, away, place == 0, straight))

    def begin(self):
        for *_, end, straight in self.ways:
            pl.when(end)(straight.start)

    def go(self):
        for _, adds, _, own, carry, *_ in self.ways:
            if carry is not None:
                pl.when(adds)(own.start)
                pl.when(adds)(carry.start)
        for d, (_, adds, _, own, carry, away, *_) in enumerate(self.ways):
            if carry is not None:

                def add(d=d, own=own, carry=carry, away=away):
                    own.wait()
                    carry.wait()
                    cols = pl.ds(0, self.cols)
                    both = self.bufs[d, 0, :, cols].astype(F32) + self.bufs[d, 1, :, cols].astype(F32)
                    self.bufs[d, 0, :, cols] = both.astype(BF)
                    away.start()

                pl.when(adds)(add)

    def wait(self):
        for sends, _, gets, _, _, away, *_ in self.ways:
            pl.when(gets)(away.wait_recv)
            pl.when(sends)(away.wait_send)


class Host:
    def __init__(self, wire, zn, jobs, bufs, load):
        z = lax.axis_index("z")
        self.steps, self.now, self.count, self.then, k = [], None, 0, {}, 0
        self.chains, self.sizes = [], []
        for g, prev, first, outs in jobs:
            for i in range(len(outs) // 2):
                got = outs[2 * i : 2 * i + 2]
                self.steps.append(Step(wire, z, zn, first + i, g, prev, got, bufs, load, k))
                self.chains.append(len(self.sizes))
                prev = got
                k += 4
            self.sizes.append(len(outs) // 2)
        self.all = list(self.steps)

    def begin(self, chains=None):
        for step, chain in zip(self.all, self.chains):
            if chains is None or chain in chains:
                step.begin()
        if self.now is None:
            self.next()

    def next(self):
        if self.now is not None:
            self.now.wait()
            self.count += 1
            done, self.now = self.then.pop(self.count, None), None
            if self.steps:
                self.now = self.steps.pop(0)
                self.now.go()
            if done is not None:
                done()
        elif self.steps:
            self.now = self.steps.pop(0)
            self.now.go()

    def end(self):
        while self.steps or self.now is not None:
            self.next()


class Settle:
    def __init__(self, wire, at, zn, g, got, keep, theirs, bufs, load):
        z = lax.axis_index("z")
        _, self.rows, self.cols = bufs.shape[0], keep.shape[0] * 2, keep.shape[1]
        rows, half = self.rows, keep.shape[0]
        self.bufs, self.has = bufs, (None, z >= 1, z <= zn - 2)
        view = [bufs.at[k, :, pl.ds(0, self.cols)] for k in range(3)]
        mine = g.at[pl.ds(pl.multiple_of(z * rows, rows), rows)]
        self.loads = [pltpu.make_async_copy(src, view[k], load.at[k]) for k, src in enumerate((mine, got[0], got[1]))]

        def part(i):
            return bufs.at[0, pl.ds(pl.multiple_of(i * half, half), half), pl.ds(0, self.cols)]

        self.away = wire.make(part(1 - at.y), theirs, at.yn, keep=False)
        self.here = pltpu.make_async_copy(part(at.y), keep, load.at[3])

    def go(self):
        cols = pl.ds(0, self.cols)
        self.loads[0].start()
        for k in (1, 2):
            pl.when(self.has[k])(self.loads[k].start)
        self.loads[0].wait()
        for k in (1, 2):
            pl.when(self.has[k])(self.loads[k].wait)

            def none(k=k):
                self.bufs[k, :, cols] = jnp.zeros((self.rows, self.cols), BF)

            pl.when(jnp.logical_not(self.has[k]))(none)
        total = self.bufs[0, :, cols].astype(F32)
        for k in (1, 2):
            total = total + self.bufs[k, :, cols].astype(F32)
        self.bufs[0, :, cols] = total.astype(BF)
        self.away.start()
        self.here.start()

    def wait(self):
        self.away.wait_recv()
        self.away.wait_send()
        self.here.wait()


def z_partners(zn):
    z = lax.axis_index("z")
    return [{"z": (z + 1) % zn}, {"z": (z + zn - 1) % zn}]


class Jobs:
    def __init__(self, plan, zn):
        self.plan, self.zn = plan, zn
        self.ins, self.outs = [], []
        for g, prev, first, steps in plan:
            self.ins += [g] + (list(prev) if prev is not None else [])
            self.outs += [shaped((g.shape[0] // zn, g.shape[1]))] * (2 * steps)
        self.steps = sum(p[3] for p in plan)
        wide = max([p[0].shape[1] for p in plan], default=0)
        rows = plan[0][0].shape[0] // zn if plan else 0
        self.scratch = [pltpu.VMEM((2, 2, rows, wide), BF)] + sems(4 * self.steps) if plan else []

    def host(self, wire, ins, outs, scratch):
        jobs, i, o = [], 0, 0
        for _, prev, first, steps in self.plan:
            took = 1 if prev is None else 3
            jobs.append((ins[i], None if prev is None else ins[i + 1 : i + 3], first, outs[o : o + 2 * steps]))
            i, o = i + took, o + 2 * steps
        return Host(wire, self.zn, jobs, *scratch)


def blockwise(part, m, yy, fn, tile=256):
    tok = part.shape[2]

    def step(i, carry):
        lo = pl.multiple_of(i * tile, tile)
        fn(lo, tile)
        return carry

    lax.fori_loop(0, tok // tile, step, 0)


def token_spreads(wire, at, src, out, sem, first, cut):
    micro, tok, feat = src.shape
    spreads, local = [], []
    for m in range(micro):

        def slot(yy, nn, part, m=m):
            lo, size = {None: (0, tok), 0: (0, cut), 1: (cut, tok - cut)}[part]
            return out.at[m, yy, pl.ds(lo, size), pl.ds(pl.multiple_of(nn * feat, feat), feat)]

        spreads.append(Spread(wire, at, src.at[m], slot))
        local.append(pltpu.make_async_copy(src.at[m], slot(at.y, at.n, None), sem.at[first + m]))
    return spreads, local


def attn_cut(w_qkv, w_out, i, buf):
    parts, _, cols = w_qkv.shape
    half = cols // 2
    at = pl.ds(pl.multiple_of(i * half, half), half)
    for p in range(parts):
        buf[:, p * half : (p + 1) * half] = w_qkv[p, :, at]
    buf[:, parts * half :] = w_out[at, :].astype(F32).T.astype(BF)


def chunk_cut(w_gu, w_down, i, c, one, buf):
    half = w_gu.shape[2] // 2
    at = pl.ds(pl.multiple_of(i * half, half) + c * one, one)
    buf[:, :one] = w_gu[0, :, at]
    buf[:, one : 2 * one] = w_gu[1, :, at]
    buf[:, 2 * one :] = w_down[at, :].astype(F32).T.astype(BF)


class Swap:
    def __init__(self, wire, at, bufs, out, sem):
        depth = bufs.shape[1]
        place = out.at[pl.ds(pl.multiple_of(at.y * depth, depth), depth)]
        self.away = wire.make(bufs.at[0], place, at.yn)
        self.here = pltpu.make_async_copy(bufs.at[1], place, sem)

    def end(self):
        self.away.wait_recv()
        self.here.wait()


def swap_attn_kernel(w_qkv, w_out, out, bufs, ss, rs, ls):
    at = Place()
    meet([at.yn])
    wire = Wire(ss, rs)
    swap = Swap(wire, at, bufs, out, ls.at[0])
    attn_cut(w_qkv, w_out, 1 - at.y, bufs.at[0])
    swap.away.start()
    attn_cut(w_qkv, w_out, at.y, bufs.at[1])
    swap.here.start()
    swap.end()
    wire.finish()


def swap_attn(w_qkv, w_out):
    parts, depth, cols = w_qkv.shape
    size = (parts + 1) * cols // 2
    return kernel(
        swap_attn_kernel, (w_qkv, w_out), [VMEM, VMEM], shaped((2 * depth, size)), ANY, 14, "swap_attn",
        [pltpu.VMEM((2, depth, size), BF)] + sems(1, 1, 1), talk=6,
    )


def swap_chunks(wire, at, w_gu, w_down, which, one, bufs, outs, ls):
    swaps = []
    for k, (c, out) in enumerate(zip(which, outs)):
        swap = Swap(wire, at, bufs.at[k], out, ls.at[k])
        chunk_cut(w_gu, w_down, 1 - at.y, c, one, bufs.at[k, 0])
        swap.away.start()
        chunk_cut(w_gu, w_down, at.y, c, one, bufs.at[k, 1])
        swap.here.start()
        swaps.append(swap)
    return swaps


def gather_x_kernel(zn, which, count, x_in, v_in, lens, freq, w_gu, w_down, x_out, v_out, lens_all, cos, sin, own, *scratch):
    bufs, ss, rs, ls = scratch
    at = Place()
    z = lax.axis_index("z")
    one = own.shape[2] // 3
    ring = [(dz, dy) for dz in range(zn) for dy in range(2) if dz or dy]
    others = [{"z": (z + dz) % zn, "y": (at.y + dy) % 2} for dz, dy in ring]
    meet([at.sib, at.xn] + others)
    wire = Wire(ss, rs)
    there = wire.make(lens, lens_all.at[at.y], at.yn)
    there.start()
    spreads, local = token_spreads(wire, at, x_in, x_out, ls, len(which) + 1, x_in.shape[1] // 8)
    local.append(pltpu.make_async_copy(v_in, v_out.at[z, at.y], ls.at[len(which)]))
    small = [wire.make(v_in, v_out.at[z, at.y], d) for d in others]
    for s in spreads:
        s.begin()
    for copy in small + local:
        copy.start()
    swaps = swap_chunks(wire, at, w_gu, w_down, which, one, bufs, [own.at[k] for k in range(len(which))], ls)
    lens_all[at.y] = lens[...]
    there.wait_recv()
    tok = x_in.shape[1]
    row = lax.broadcasted_iota(jnp.int32, (tok, 1), 0)
    flip = jnp.where(lax.broadcasted_iota(jnp.int32, (1, HEAD_DIM), 1) < HEAD_DIM // 2, -1.0, 1.0)

    def table(b, carry):
        m, yy = b // 2, b % 2
        line = lens_all[yy, pl.ds(m, 1), :]
        end = jnp.zeros((1, 1), jnp.int32)
        start = jnp.zeros_like(row)
        for k in range(count):
            end = end + line[:, k : k + 1]
            start = jnp.where(row >= end, end, start)
        angle = (row - start).astype(F32) * freq[...]
        place = pl.ds(pl.multiple_of(b * tok, tok), tok)
        cos[place, :] = jnp.cos(angle)
        sin[place, :] = jnp.sin(angle) * flip
        return carry

    lax.fori_loop(0, x_in.shape[0] * 2, table, 0)
    run_spreads(spreads, local)
    for copy in small:
        copy.wait_recv()
    for swap in swaps:
        swap.end()
    wire.finish()


def gather_x(x, v, lens, freq, w_gu, w_down, zn, which, one, count, first):
    micro, tok, feat = x.shape
    depth = w_gu.shape[1]
    rows = micro * 2 * tok
    links = SPREAD * micro + 2 * zn - 1 + len(which) + 1
    return kernel(
        functools.partial(gather_x_kernel, zn, which, count), (x, v, lens, freq, w_gu, w_down),
        [ANY, ANY, VMEM, VMEM, VMEM, VMEM],
        (
            shaped((micro, 2, tok, 4 * feat)), shaped((zn, 2) + v.shape, F32), shaped((2,) + lens.shape, jnp.int32),
            shaped((rows, HEAD_DIM), F32), shaped((rows, HEAD_DIM), F32), shaped((len(which), 2 * depth, 3 * one)),
        ),
        (ANY, ANY, VMEM, VMEM, VMEM, ANY), 48, "gather_x",
        [pltpu.VMEM((len(which), 2, depth, 3 * one), BF)] + sems(links, links, micro + 1 + len(which)),
        first, talk=0,
    )


def gather_d_kernel(which, one, d_in, x_all, gain, shift, w_gu, w_down, d_out, n1, *refs):
    outs, (bufs, xin, nout, ss, rs, ls, load) = refs[: len(which)], refs[len(which) :]
    at = Place()
    micro, _, tok, _ = x_all.shape
    meet([at.sib, at.xn, at.yn])
    wire = Wire(ss, rs)
    spreads, local = token_spreads(wire, at, d_in, d_out, ls, len(which), d_in.shape[1] // 16 * 5)

    def bring(b):
        return pltpu.make_async_copy(x_all.at[b // 2, b % 2], xin.at[b % 2], load.at[b])

    def put(b):
        return pltpu.make_async_copy(nout.at[b % 2], n1.at[pl.ds(b * tok, tok)], load.at[2 * micro + b])

    bring(0).start()
    bring(1).start()
    for s in spreads:
        s.begin()
    for copy in local:
        copy.start()
    swaps = swap_chunks(wire, at, w_gu, w_down, which, one, bufs, outs, ls)
    for b in range(2 * micro):
        bring(b).wait()
        if b >= 2:
            put(b - 2).wait()

        def tile(i, carry, b=b):
            place = pl.ds(pl.multiple_of(i * 128, 128), 128)
            xhat, _ = normalise(xin[b % 2, place, :].astype(F32))
            nout[b % 2, place, :] = (xhat * gain[...] + shift[...]).astype(BF)
            return carry

        lax.fori_loop(0, tok // 128, tile, 0)
        put(b).start()
        if b + 2 < 2 * micro:
            bring(b + 2).start()
        if b % 2:
            spreads[b // 2].forward()
    put(2 * micro - 2).wait()
    put(2 * micro - 1).wait()
    for s in spreads:
        s.forward_last()
    for s in spreads:
        s.end()
    for copy in local:
        copy.wait()
    for swap in swaps:
        swap.end()
    wire.finish()


def gather_d(d, x_all, gain, shift, w_gu, w_down, which, one):
    micro, tok, feat = d.shape
    depth = w_gu.shape[1]
    count = SPREAD * micro + len(which)
    return kernel(
        functools.partial(gather_d_kernel, which, one), (d, x_all, gain, shift, w_gu, w_down),
        [ANY, ANY, VMEM, VMEM, VMEM, VMEM],
        (shaped((micro, 2, tok, 4 * feat)), shaped((micro * 2 * tok, 4 * feat))) + (shaped((2 * depth, 3 * one)),) * len(which),
        (ANY,) * (2 + len(which)), 48, "gather_d",
        [pltpu.VMEM((len(which), 2, depth, 3 * one), BF)] + [pltpu.VMEM((2, tok, 4 * feat), BF)] * 2
        + sems(count, count, micro + len(which), 4 * micro),
        talk=5,
    )


def row_slot(out, m, sub):
    half = sub // 2

    def slot(yy, nn, part):
        ref = out.at[m, yy, nn]
        return ref if part is None else ref.at[pl.ds(part * half, half)]

    return slot


def run_spreads(spreads, local, tick=nothing):
    for s in spreads:
        s.forward()
    tick()
    for s in spreads:
        s.forward_last()
    for s in spreads:
        s.end()
    for copy in local:
        copy.wait()


def attn_out_kernel(att, wo, x_all, gain, shift, middle, n2, *scratch):
    *red, xb, nb, ss, rs, ls = scratch
    at = Place()
    micro, sub, width = middle.shape
    zn, dz, cols = wo.shape
    span = att.shape[1]
    tok = red[0].shape[2]
    meet([at.sib, at.xn, at.yn])
    wire = Wire(ss, rs)
    own = [pltpu.make_async_copy(x_all.at[m, at.y, pl.ds(at.n * sub, sub)], xb.at[m], ls.at[m]) for m in range(micro)]
    for copy in own:
        copy.start()

    def compute(m, yy):
        def tile(lo, size):
            a = att[pl.ds(pl.multiple_of((m * 2 + yy) * tok, tok) + lo, size), :]
            for k in range(zn):
                red[0][m, yy, pl.ds(lo, size), k * dz : (k + 1) * dz] = dot_nt(a, wo[k, :, cols - span :]).astype(BF)

        blockwise(red[0], m, yy, tile)

    spreads, local = [], []

    def finish(m, total):
        own[m].wait()
        step = sub // 2
        for lo in range(0, sub, step):
            mid = xb[m, lo : lo + step, :].astype(F32) + total(lo, step)
            middle[m, lo : lo + step, :] = mid
            xhat, _ = normalise(mid)
            nb[m, lo : lo + step, :] = (xhat * gain[...] + shift[...]).astype(BF)
        slot = row_slot(n2, m, sub)
        spreads.append(Spread(wire, at, nb.at[m], slot))
        spreads[-1].begin()
        local.append(pltpu.make_async_copy(nb.at[m], slot(at.y, at.n, None), ls.at[micro + m]))
        local[-1].start()

    reduce_rows(wire, at, red, compute, finish)
    run_spreads(spreads, local)
    wire.finish()


def attn_out(att, wo, x_all, gain, shift):
    micro, _, tok, width = x_all.shape
    sub = tok // 4
    count = (REDUCE + SPREAD) * micro
    return kernel(
        attn_out_kernel, (att, wo, x_all, gain, shift), [VMEM, VMEM, ANY, VMEM, VMEM],
        (shaped((micro, sub, width), F32), shaped((micro, 2, 4, sub, width))), (VMEM, ANY), 85, "attn_out",
        reduce_scratch(micro, tok, sub, width) + [pltpu.VMEM((micro, sub, width), BF)] * 2 + sems(count, count, 2 * micro),
        talk=1,
    )


def nt_compute(part, lows, ws, first, each=0):
    zn, dz, _ = ws[0].shape
    tok = part.shape[2]
    span = lows[0].shape[1]

    def compute(m, yy):
        def tile(lo, size):
            at = pl.multiple_of((m * 2 + yy) * tok, tok) + lo
            for k in range(zn):
                acc = None
                for i, (low, w) in enumerate(zip(lows, ws)):
                    lo_col = first + i * each
                    term = dot_nt(low[pl.ds(at, size), :], w[k, :, lo_col : lo_col + span])
                    acc = term if acc is None else acc + term
                part[m, yy, pl.ds(lo, size), k * dz : (k + 1) * dz] = acc.astype(BF)

        blockwise(part, m, yy, tile)

    return compute


class Columns:
    def __init__(self, groups, cols, bufs, load):
        self.copies = [
            pltpu.make_async_copy(src.at[:, :, cols], bufs.at[k], load.at[k]) for k, src in enumerate(groups)
        ]
        for copy in self.copies:
            copy.start()

    def wait(self):
        for copy in self.copies:
            copy.wait()


def chunk_refs(pair, last):
    return [pair.at[:, k] for k in range(pair.shape[1])] + [last]


def ffn_back_kernel(jobs, parts, *refs):
    guls = refs[:parts]
    pair, last, d_all, middle, gain, *refs = refs[parts:]
    zin, (mid_grad, branch, vec), refs = refs[: len(jobs.ins)], refs[len(jobs.ins) :][:3], refs[len(jobs.ins) + 3 :]
    zout, refs = refs[: len(jobs.outs)], refs[len(jobs.outs) :]
    *red, db, nb, wv, ss, rs, ls, lw, zb, zl = refs
    at = Place()
    micro, sub, width = middle.shape
    span = guls[0].shape[1]
    weights = Columns(chunk_refs(pair, last), pl.ds(0, span), wv, lw)
    own = [pltpu.make_async_copy(d_all.at[m, at.y, pl.ds(at.n * sub, sub)], db.at[m], ls.at[m]) for m in range(micro)]
    for copy in own:
        copy.start()
    meet([at.sib, at.xn, at.yn] + z_partners(jobs.zn))
    wire = Wire(ss, rs)
    host = jobs.host(wire, zin, zout, (zb, zl))
    host.begin()
    vec[...] = jnp.zeros_like(vec)
    spreads, local = [], []

    def finish(m, total):
        own[m].wait()
        step = sub // 2
        for lo in range(0, sub, step):
            grad = total(lo, step)
            xhat, rstd = normalise(middle[m, lo : lo + step, :])
            vec[0:1, :] += jnp.sum(grad * xhat, axis=0, keepdims=True)
            vec[1:2, :] += jnp.sum(grad, axis=0, keepdims=True)
            mg = db[m, lo : lo + step, :].astype(F32) + norm_back(xhat, rstd, grad, gain[...])
            mid_grad[m, lo : lo + step, :] = mg
            nb[m, lo : lo + step, :] = mg.astype(BF)
        slot = row_slot(branch, m, sub)
        spreads.append(Spread(wire, at, nb.at[m], slot))
        spreads[-1].begin()
        local.append(pltpu.make_async_copy(nb.at[m], slot(at.y, at.n, None), ls.at[micro + m]))
        local[-1].start()

    weights.wait()
    reduce_rows(wire, at, red, nt_compute(red[0], guls, [wv.at[k] for k in range(parts)], 0), finish, host.next)
    run_spreads(spreads, local, host.next)
    host.end()
    wire.finish()


def ffn_back(guls, pair, last, d_all, middle, gain, plan, zn, first):
    parts = len(guls)
    micro, _, tok, width = d_all.shape
    sub = tok // 4
    jobs = Jobs(plan, zn)
    count = (REDUCE + SPREAD) * micro + 2 * jobs.steps
    span = guls[0].shape[1]
    return kernel(
        functools.partial(ffn_back_kernel, jobs, parts), (*guls, pair, last, d_all, middle, gain, *jobs.ins),
        [VMEM] * parts + [ANY, ANY, ANY, VMEM, VMEM] + [ANY] * len(jobs.ins),
        (shaped((micro, sub, width), F32), shaped((micro, 2, 4, sub, width)), shaped((8, width), F32), *jobs.outs),
        (VMEM, ANY, VMEM) + (ANY,) * len(jobs.outs), 90, "ffn_back",
        reduce_scratch(micro, tok, sub, width) + [pltpu.VMEM((micro, sub, width), BF)] * 2
        + [pltpu.VMEM((parts, zn, width // zn, span), BF)] + sems(count, count, 2 * micro, parts) + jobs.scratch,
        first, talk=2,
    )


def host_kernel(jobs, *refs):
    zin, zout, (ss, rs, zb, zl) = refs[: len(jobs.ins)], refs[len(jobs.ins) :][: len(jobs.outs)], refs[-4:]
    meet(z_partners(jobs.zn))
    host = jobs.host(Wire(ss, rs), zin, zout, (zb, zl))
    host.begin()
    host.end()


def host_only(plan, zn, first):
    jobs = Jobs(plan, zn)
    return kernel(
        functools.partial(host_kernel, jobs), jobs.ins, [ANY] * len(jobs.ins), tuple(jobs.outs), (ANY,) * len(jobs.outs),
        20 * jobs.steps, "along_z", sems(2 * jobs.steps, 2 * jobs.steps) + jobs.scratch, first, talk=8,
    )


class Deal:
    def __init__(self, wire, at, rows, out, m, sems, k):
        sub, width = rows.shape[1], rows.shape[2]
        feat = width // 4

        def cols(nn):
            return rows.at[m, :, pl.ds(pl.multiple_of(nn * feat, feat), feat)]

        place = out.at[m, pl.ds(pl.multiple_of(at.n * sub, sub), sub)]
        self.local = pltpu.make_async_copy(cols(at.n), place, sems.at[k])
        self.copies = [
            wire.make(cols(at.nx), place, at.xn),
            wire.make(cols(at.nd), place, at.xs),
            wire.make(cols(at.ns), place, at.sib),
        ]

    def begin(self):
        for copy in self.copies:
            copy.start()
        self.local.start()

    def end(self):
        for copy in self.copies:
            copy.wait_recv()
        self.local.wait()


def last_kernel(jobs, zn, *refs):
    low, wa, x_all, mid_grad, gain, vec2, g2, got2, got3, out_g, gout2, gout3, *refs = refs
    zin, refs = refs[: len(jobs.ins)], refs[len(jobs.ins) :]
    in_grad, sums, *refs = refs
    settled, zout, refs = refs[:6], refs[6:][: len(jobs.outs)], refs[6 + len(jobs.outs) :]
    red, refs = refs[:8], refs[8:]
    xb, ob, w1, mine, plane, summed, lines, yb2, ybo, ybq, yl2, ylo, ylq, ss, rs, ls, *talk = refs
    at = Place()
    z = lax.axis_index("z")
    micro, sub, width = mid_grad.shape
    qkv = pltpu.make_async_copy(wa.at[:, :, pl.ds(0, low.shape[1])], w1, ls.at[2 * micro])
    qkv.start()
    own = [pltpu.make_async_copy(x_all.at[m, at.y, pl.ds(at.n * sub, sub)], xb.at[m], ls.at[m]) for m in range(micro)]
    for copy in own:
        copy.start()
    flips = [(dy, dn) for dy in range(2) for dn in range(4) if dy or dn]
    peers = [{"y": (at.y + dy) % 2, "n": (at.n + dn) % 4} for dy, dn in flips]
    along = [{"z": (z + dz) % zn} for dz in range(1, zn)]
    meet(peers + along)
    wire = Wire(ss, rs)
    host = jobs.host(wire, zin, zout, talk)
    host.begin()
    settles = [
        Settle(wire, at, zn, g2, (got2, got3), settled[0], settled[1], yb2, yl2),
        Settle(wire, at, zn, out_g, (gout2, gout3), settled[2], settled[3], ybo, ylo),
        Settle(wire, at, zn, zin[0], zout[-2:], settled[4], settled[5], ybq, ylq),
    ]
    host.then = {zn - 1: settles[2].go}
    mine[...] = jnp.zeros_like(mine)
    mine[2:4] = vec2[0:2]
    qkv.wait()
    total = Reduce(wire, at, red, nt_compute(red[0], [low], [w1], 0))
    for m in range(micro):
        total.cores(m)
        total.diagonal(m)
    for m in range(micro):
        total.sides(m)
    settles[0].go()
    settles[1].go()
    host.next()
    step = sub // 2
    deals = []
    for m in range(micro):
        total.arrived(m)
        own[m].wait()
        for lo in range(0, sub, step):
            grad = total.total(m, lo, step)
            xhat, rstd = normalise(xb[m, lo : lo + step, :].astype(F32))
            mine[0:1, :] += jnp.sum(grad * xhat, axis=0, keepdims=True)
            mine[1:2, :] += jnp.sum(grad, axis=0, keepdims=True)
            back = norm_back(xhat, rstd, grad, gain[...])
            ob[m, lo : lo + step, :] = (mid_grad[m, lo : lo + step, :] + back).astype(BF)
        deals.append(Deal(wire, at, ob, in_grad, m, ls, micro + m))
        deals[-1].begin()
    near = [wire.make(mine, plane.at[k], d) for k, d in enumerate(peers)]
    for copy in near:
        copy.start()
    host.next()
    for copy in near:
        copy.wait_recv()
    both = mine[...]
    for k in range(len(peers)):
        both = both + plane[k]
    summed[...] = both
    far = [wire.make(summed, lines.at[k], d) for k, d in enumerate(along)]
    for copy in far:
        copy.start()
    host.next()
    for copy in far:
        copy.wait_recv()
    both = summed[...]
    for k in range(len(along)):
        both = both + lines[k]
    sums[...] = both
    for deal in deals:
        deal.end()
    host.end()
    for settle in settles:
        settle.wait()
    wire.finish()


def last_sums(low, wa, x_all, mid_grad, gain, vec2, g2, got2, out_g, gout, qkv_g, zn):
    micro, _, tok, width = x_all.shape
    sub = tok // 4
    dz, cols = width // zn, low.shape[1]
    jobs = Jobs([(qkv_g, None, 0, zn - 1)], zn)
    count = (REDUCE + 3) * micro + 7 + zn - 1 + 2 * jobs.steps + 3
    size = vec2.shape
    rows = pltpu.VMEM((micro, sub, width), BF)
    sizes = (g2.shape[1], out_g.shape[1], cols)
    halves = [shaped((dz // 2, k)) for k in sizes for _ in range(2)]
    return kernel(
        functools.partial(last_kernel, jobs, zn),
        (low, wa, x_all, mid_grad, gain, vec2, g2, *got2, out_g, *gout, *jobs.ins),
        [VMEM, ANY, ANY, VMEM, VMEM, VMEM] + [ANY] * (6 + len(jobs.ins)),
        (shaped((micro, tok, width // 4)), shaped(size, F32), *halves, *jobs.outs),
        (ANY, VMEM) + (ANY,) * (6 + len(jobs.outs)), 100, "last_sums",
        reduce_scratch(micro, tok, sub, width) + [rows] * 2 + [pltpu.VMEM((zn, dz, cols), BF)]
        + [pltpu.VMEM(size, F32), pltpu.VMEM((7,) + size, F32), pltpu.VMEM(size, F32), pltpu.VMEM((zn - 1,) + size, F32)]
        + [pltpu.VMEM((3, dz, k), BF) for k in sizes] + sems(4, 4, 4, count, count, 2 * micro + 1) + jobs.scratch,
        talk=3,
    )


def tiles(rows, cols):
    return pl.BlockSpec((rows, cols), lambda i: (i, 0))


def same_protein(lens, b, tok, count):
    col = lax.broadcasted_iota(jnp.int32, (tok, 1), 0)
    row = lax.broadcasted_iota(jnp.int32, (1, tok), 1)
    pc, pr = jnp.zeros_like(col), jnp.zeros_like(row)
    end = jnp.int32(0)
    for k in range(count):
        end = end + lens[b % 2, b // 2, k]
        pc = pc + (col >= end).astype(jnp.int32)
        pr = pr + (row >= end).astype(jnp.int32)
    return pc == pr


def turn(v, cos, sin):
    return v * cos + pltpu.roll(v, HEAD_DIM // 2, 1) * sin


def attention_body(count, ends, n1, w, cos, sin, qkv, att):
    zn, dz, _ = w.shape
    cols = qkv.shape[1]
    tok = n1.shape[0]
    heads = cols // 3 // HEAD_DIM
    span = heads * HEAD_DIM
    acc = dot(n1[:, 0:dz], w[0, :, :cols])
    for k in range(1, zn):
        acc = acc + dot(n1[:, k * dz : (k + 1) * dz], w[k, :, :cols])
    same = same_protein(ends, pl.program_id(0), tok, count)
    scale = HEAD_DIM ** (-0.5)
    for h in range(heads):
        lo = h * HEAD_DIM
        q = turn(acc[:, lo : lo + HEAD_DIM], cos[...], sin[...]).astype(BF)
        k = turn(acc[:, span + lo : span + lo + HEAD_DIM], cos[...], sin[...]).astype(BF)
        v = acc[:, 2 * span + lo : 2 * span + lo + HEAD_DIM].astype(BF)
        qkv[:, lo : lo + HEAD_DIM] = q
        qkv[:, span + lo : span + lo + HEAD_DIM] = k
        qkv[:, 2 * span + lo : 2 * span + lo + HEAD_DIM] = v
        s = jnp.where(same, dot_nt(q, k) * scale, -1e30)
        e = jnp.exp(s - jnp.max(s, axis=-1, keepdims=True))
        p = (e / jnp.sum(e, axis=-1, keepdims=True)).astype(BF)
        att[:, lo : lo + HEAD_DIM] = dot(p, v).astype(BF)


def attention(count, ends, n1, w, cos, sin, passed, tok):
    rows, width = n1.shape
    cols = w.shape[2] // 4 * 3

    def body(e, a, b, c, d, _, qkv, att, __):
        attention_body(count, e, a, b, c, d, qkv, att)

    return kernel(
        body, (ends, n1, w, cos, sin, passed),
        [SMEM, tiles(tok, width), VMEM, tiles(tok, HEAD_DIM), tiles(tok, HEAD_DIM), ANY],
        (shaped((rows, cols)), shaped((rows, cols // 3)), shaped(passed.shape)),
        (tiles(tok, cols), tiles(tok, cols // 3), ANY), 20, "attention", grid=(rows // tok,), aliases={5: 2},
    )


def attention_back_body(count, ends, b, branch, wo, qkv, cos, sin, low):
    zn, dz, span = wo.shape
    tok = branch.shape[0]
    heads = span // HEAD_DIM
    acc = dot(branch[:, 0:dz], wo[0])
    for k in range(1, zn):
        acc = acc + dot(branch[:, k * dz : (k + 1) * dz], wo[k])
    same = same_protein(ends, b, tok, count)
    scale = HEAD_DIM ** (-0.5)
    for h in range(heads):
        lo = h * HEAD_DIM
        ag = acc[:, lo : lo + HEAD_DIM].astype(BF)
        q = qkv[:, lo : lo + HEAD_DIM]
        k = qkv[:, span + lo : span + lo + HEAD_DIM]
        v = qkv[:, 2 * span + lo : 2 * span + lo + HEAD_DIM]
        s = jnp.where(same, dot_nt(q, k) * scale, -1e30)
        e = jnp.exp(s - jnp.max(s, axis=-1, keepdims=True))
        p = e / jnp.sum(e, axis=-1, keepdims=True)
        pg = dot_nt(ag, v)
        vg = dot_tn(p.astype(BF), ag)
        rd = jnp.sum(p * pg, axis=-1, keepdims=True)
        sg = (p * (pg - rd)).astype(BF)
        qg = dot(sg, k) * scale
        kg = dot_tn(sg, q) * scale
        low[:, lo : lo + HEAD_DIM] = turn(qg, cos[...], -sin[...]).astype(BF)
        low[:, span + lo : span + lo + HEAD_DIM] = turn(kg, cos[...], -sin[...]).astype(BF)
        low[:, 2 * span + lo : 2 * span + lo + HEAD_DIM] = vg.astype(BF)


def attention_back_kernel(jobs, count, parts, *refs):
    lens, branch, att, wa, qkv, cos, sin, n1, g0, got0, got1, g1, got2, got3, pair, last, middle, *refs = refs
    hids, zin, refs = refs[:parts], refs[parts:][: len(jobs.ins)], refs[parts + len(jobs.ins) :]
    low, grads, out_g, *refs = refs
    settled, layer_out, refs = refs[:4], refs[4], refs[5:]
    zout, refs = refs[: len(jobs.outs)], refs[len(jobs.outs) :]
    zout, gout = zout[: -2 * (jobs.zn - 1)], zout[-2 * (jobs.zn - 1) :]
    red, refs = refs[:8], refs[8:]
    bv, wo, ob, yb, load, yl, ls, ss, rs, *talk = refs
    rows, width = bv.shape
    zn, dz, span = wo.shape
    tok = rows // 4
    one = hids[0].shape[1]
    micro, sub, _ = middle.shape
    at = Place()
    cols = low.shape[1]
    downs, chunks = [], chunk_refs(pair, last)
    for k in range(parts):
        place = pl.ds(k * one, one)
        downs.append(pltpu.make_async_copy(hids[k], low.at[:, place], load.at[9 + k]))
        downs.append(
            pltpu.make_async_copy(chunks[k].at[:, :, pl.ds(2 * one, one)], grads.at[:, :, place], load.at[9 + parts + k])
        )
    for copy in downs:
        copy.start()
    weights = pltpu.make_async_copy(wa.at[:, :, pl.ds(cols, span)], wo, load.at[8])
    weights.start()

    def bring(b):
        here = pl.ds(b * tok, tok)
        return (
            pltpu.make_async_copy(branch.at[here], bv.at[here], load.at[b]),
            pltpu.make_async_copy(n1.at[here], red[0].at[b // 2, b % 2], load.at[4 + b]),
        )

    for b in range(4):
        bring(b)[0].start()
    meet(z_partners(zn) + [at.sib, at.xn, at.yn, at.xs])
    wire = Wire(ss, rs)
    host = Host(wire, zn, [(zin[0], None, 0, zout), (out_g, None, 0, gout)], *talk)
    settles = [
        Settle(wire, at, zn, g0, (got0, got1), settled[0], settled[1], yb, yl),
        Settle(wire, at, zn, g1, (got2, got3), settled[2], settled[3], yb, yl),
    ]
    host.begin((0,))
    for copy in downs:
        copy.wait()
    lows = [low.at[:, pl.ds(k * one, one)] for k in range(parts)]
    total = Reduce(wire, at, red, nt_compute(red[0], lows, [grads] * parts, 0, one))
    for m in range(micro):
        total.cores(m)
        total.diagonal(m)
    settles[0].go()
    weights.wait()
    for b in range(4):
        bring(b)[0].wait()

    def output(k, carry):
        here = pl.ds(pl.multiple_of(k * dz, dz), dz)
        out_g[here, :] = dot_tn(bv[:, here], att[...]).astype(BF)
        return carry

    lax.fori_loop(0, zn, output, 0)
    host.begin((1,))
    host.next()

    def block(b):
        here = pl.ds(b * tok, tok)
        attention_back_body(
            count, lens, b, bv.at[here], wo, qkv.at[here], cos.at[here], sin.at[here], low.at[here]
        )

    block(0)
    for m in range(micro):
        total.sides(m)
        total.release(m)
    for b in range(4):
        bring(b)[1].start()
    block(1)
    settles[0].wait()
    settles[1].go()
    host.next()
    block(2)
    block(3)
    host.next()
    for b in range(4):
        bring(b)[1].wait()

    def weights_of(k, carry):
        here = pl.ds(pl.multiple_of(k * dz, dz), dz)
        acc = 0.0
        for b in range(4):
            acc = acc + dot_tn(red[0][b // 2, b % 2, :, here], low[pl.ds(b * tok, tok), :])
        grads[k] = acc.astype(BF)
        return carry

    lax.fori_loop(0, zn, weights_of, 0)
    deals, step = [], sub // 2
    for m in range(micro):
        total.arrived(m)
        for lo in range(0, sub, step):
            ob[m, lo : lo + step, :] = (middle[m, lo : lo + step, :] + total.total(m, lo, step)).astype(BF)
        deals.append(Deal(wire, at, ob, layer_out, m, ls, m))
        deals[-1].begin()
    host.next()
    settles[1].wait()
    for deal in deals:
        deal.end()
    host.end()
    wire.finish()


def attention_back(count, lens, branch, att, wa, qkv, cos, sin, n1, g0, got0, g1, got1, pair, last, middle, hids, g2, zn):
    rows, width = branch.shape
    cols, span, parts = qkv.shape[1], att.shape[1], len(hids)
    micro, sub, _ = middle.shape
    tok = rows // 4
    dz = width // zn
    out_g = shaped((width, span))
    jobs = Jobs([(g2, None, 0, zn - 1), (out_g, None, 0, zn - 1)], zn)
    jobs.ins = [g2]
    half = shaped((dz // 2, g0.shape[1]))
    links = 2 * jobs.steps + 2 + (REDUCE + 3) * micro
    return kernel(
        functools.partial(attention_back_kernel, jobs, count, parts),
        (lens, branch, att, wa, qkv, cos, sin, n1, g0, *got0, g1, *got1, pair, last, middle, *hids, *jobs.ins),
        [SMEM, ANY, VMEM, ANY, VMEM, VMEM, VMEM, ANY] + [ANY] * 8 + [VMEM] + [ANY] * (parts + len(jobs.ins)),
        (shaped((rows, cols)), shaped((zn, dz, cols)), out_g, *(half,) * 4, shaped((micro, tok, width // 4)), *jobs.outs),
        (VMEM, VMEM, VMEM) + (ANY,) * (5 + len(jobs.outs)), 70, "attention_back",
        reduce_scratch(micro, tok, sub, width)
        + [pltpu.VMEM((rows, width), BF), pltpu.VMEM((zn, dz, span), BF), pltpu.VMEM((micro, sub, width), BF)]
        + [pltpu.VMEM((3, dz, g0.shape[1]), BF)]
        + sems(9 + 2 * parts, 4, micro, links, links) + jobs.scratch,
        talk=9,
    )


def chunk_body(jobs, c, n2, dy, w, mask, *refs):
    zin, (low, hidden, grad), refs = refs[: len(jobs.ins)], refs[len(jobs.ins) :][:3], refs[len(jobs.ins) + 3 :]
    zout, (nv, dv, wv, load, *talk) = refs[: len(jobs.outs)], refs[len(jobs.outs) :]
    zn, dz, cols = wv.shape
    one = cols // 3
    steps = load.shape[1] - 1
    tile = nv.shape[0] // steps
    whole = pltpu.make_async_copy(w if c is None else w.at[:, c], wv, load.at[0, steps])
    whole.start()

    def bring(t):
        at = pl.ds(pl.multiple_of(t * tile, tile), tile)
        return (
            pltpu.make_async_copy(n2.at[at], nv.at[at], load.at[0, t]),
            pltpu.make_async_copy(dy.at[at], dv.at[at], load.at[1, t]),
        )

    for t in range(steps):
        for copy in bring(t):
            copy.start()
    if talk:
        ss, rs, *talk = talk
        meet(z_partners(jobs.zn))
        host = jobs.host(Wire(ss, rs), zin, zout, talk)
        host.begin()
    whole.wait()

    def forward(t, carry):
        for copy in bring(t):
            copy.wait()
        at = pl.ds(pl.multiple_of(t * tile, tile), tile)
        acc = hg = 0.0
        for k in range(zn):
            acc = acc + dot(nv[at, k * dz : (k + 1) * dz], wv[k, :, : 2 * one])
            hg = hg + dot(dv[at, k * dz : (k + 1) * dz], wv[k, :, 2 * one :])
        hg = hg * mask[...]
        g, u = acc[:, :one], acc[:, one:]
        phi = 0.5 * (1.0 + lax.erf(g * (0.5**0.5)))
        slope = phi + g * jnp.exp(-0.5 * g * g) * 0.3989422804014327
        act = g * phi
        hidden[at, :] = (act * u * mask[...]).astype(BF)
        low[at, :one] = (hg * u * slope).astype(BF)
        low[at, one:] = (hg * act).astype(BF)
        return carry

    lax.fori_loop(0, steps, forward, 0)

    def weights(k, carry):
        at = pl.ds(pl.multiple_of(k * dz, dz), dz)
        grad[at, : 2 * one] = dot_tn(nv[:, at], low[...]).astype(BF)
        grad[at, 2 * one :] = dot_tn(dv[:, at], hidden[...]).astype(BF)
        return carry

    lax.fori_loop(0, zn, weights, 0)
    if jobs.steps:
        host.end()


def chunk(n2, dy, w, c, mask, plan, zn, talk, first):
    rows, width = n2.shape
    cols = w.shape[-1]
    one = cols // 3
    jobs = Jobs(plan, zn)
    return kernel(
        functools.partial(chunk_body, jobs, c), (n2, dy, w, mask, *jobs.ins), [ANY, ANY, ANY, VMEM] + [ANY] * len(jobs.ins),
        (shaped((rows, 2 * one)), shaped((rows, one)), shaped((width, cols)), *jobs.outs),
        (VMEM,) * 3 + (ANY,) * len(jobs.outs), 22, "ffn_chunk",
        [pltpu.VMEM((rows, width), BF)] * 2 + [pltpu.VMEM((zn, width // zn, cols), BF), pltpu.SemaphoreType.DMA((2, 5))]
        + (sems(2 * jobs.steps, 2 * jobs.steps) + jobs.scratch if jobs.steps else []),
        first, talk=talk if jobs.steps else None,
    )


def form_body(parts, *refs):
    halves, (gu, down, qkv, out) = refs[: 2 * parts + 4], refs[2 * parts + 4 :]
    y = lax.axis_index("y")
    one = halves[0].shape[1] // 3

    def pair(k):
        keep, theirs = halves[2 * k][...].astype(F32), halves[2 * k + 1][...].astype(F32)
        return jnp.where(y == 0, keep, theirs), jnp.where(y == 0, theirs, keep)

    half = parts * one
    for k in range(parts):
        for i, v in enumerate(pair(k)):
            lo = i * half + k * one
            gu[0, :, lo : lo + one] = v[:, :one]
            gu[1, :, lo : lo + one] = v[:, one : 2 * one]
            down[lo : lo + one, :] = v[:, 2 * one :].T
    for i, v in enumerate(pair(parts)):
        span = v.shape[1]
        out[i * span : (i + 1) * span, :] = v.T
    for i, v in enumerate(pair(parts + 1)):
        span = v.shape[1] // 3
        for p in range(3):
            qkv[p, :, i * span : (i + 1) * span] = v[:, p * span : (p + 1) * span]


def form(halves, w_gu, w_down, w_qkv, w_out):
    parts = (len(halves) - 4) // 2
    return kernel(
        functools.partial(form_body, parts), halves, [VMEM] * len(halves),
        tuple(shaped(w.shape, F32) for w in (w_gu, w_down, w_qkv, w_out)),
        (VMEM,) * 4, 8, "form",
    )


CHUNKS = 3


def on_device(inputs, lengths, counts, w_qkv, w_out, w_gu, w_down, g1, b1, g2, b2, dy_in):
    z = lax.axis_index("z")
    y = lax.axis_index("y")
    n = lax.axis_index("n")
    zn = lax.axis_size("z")
    micro, tok, feat = inputs.shape
    width = feat * lax.axis_size("n")
    rows = micro * 2 * tok
    depth = w_qkv.shape[1]
    half_slots = w_gu.shape[2] // 2
    one = half_slots // CHUNKS

    def gather_z(w):
        return lax.all_gather(w, "z", axis=0, tiled=False)

    own_attn = swap_attn(w_qkv, w_out)
    wa = gather_z(own_attn)
    vecs = jnp.stack([g1, b1, g2, b2]).astype(F32)
    vecs = jnp.pad(vecs, ((0, 4), (0, 0)))
    count = lengths.shape[2]
    lens = jnp.pad(lengths[:, 0], ((0, 8 - micro), (0, 128 - count)))
    half_dim = HEAD_DIM // 2
    freq = 10000.0 ** (-(jnp.arange(HEAD_DIM) % half_dim).astype(F32) / half_dim)
    x_all, norms, lens, cos, sin, own_01 = gather_x(
        inputs, vecs, lens, freq[None], w_gu, w_down, zn, (0, 1), one, count, (own_attn,)
    )
    norms = norms.transpose(2, 0, 1, 3).reshape(8, width)
    gain1, shift1, gain2, shift2 = (norms[i : i + 1] for i in range(4))
    own = jnp.sum(jnp.where(jnp.arange(counts.shape[0]) == n, counts, 0))
    mask = (y * half_slots + jnp.arange(half_slots) < own).astype(F32)[None]

    d_all, n1, own_2 = gather_d(dy_in, x_all, gain1, shift1, w_gu, w_down, (2,), one)
    dy = d_all.reshape(rows, width)
    qkv, att, own_2 = attention(count, lens, n1, wa, cos, sin, own_2, tok)
    w_01, w_2 = gather_z(own_01), gather_z(own_2)
    middle, n2 = attn_out(att, wa, x_all, gain2, shift2)
    n2 = n2.reshape(rows, width)

    def own_mask(c):
        return mask[:, c * one : (c + 1) * one]

    low0, hid0, g0 = chunk(n2, dy, w_01, 0, own_mask(0), [], zn, None, ())
    low1, hid1, grad1 = chunk(n2, dy, w_01, 1, own_mask(1), [], zn, None, (g0,))
    low2, hid2, grad2, *p = chunk(n2, dy, w_2, None, own_mask(2), [(g0, None, 0, 1)], zn, 7, (grad1,))
    mid_grad, branch, vec2, *q = ffn_back(
        [low0, low1, low2], w_01, w_2, d_all, middle, gain2, [(g0, p, 1, zn - 2), (grad1, None, 0, zn - 1)], zn, ()
    )
    got0, got1 = q[2 * zn - 6 : 2 * zn - 4], q[-2:]
    branch = branch.reshape(rows, width)
    low, qkv_g, out_g, *r = attention_back(
        count, lens, branch, att, wa, qkv, cos, sin, n1, g0, got0, grad1, got1, w_01, w_2, middle, [hid0, hid1, hid2], grad2, zn
    )
    first, layer_out, got2, gout = r[:4], r[4], r[2 * zn + 1 : 2 * zn + 3], r[-2:]
    in_grad, sums, *r = last_sums(
        low, wa, x_all, mid_grad, gain1, vec2, grad2, got2, out_g, gout, qkv_g.reshape(width, -1), zn
    )
    gu_grad, down_grad, qkv_grad, out_grad = form(
        [*first, *r[:6]], w_gu, w_down, w_qkv, w_out
    )

    mine = lax.dynamic_slice_in_dim(sums, (z * 2 + y) * g1.shape[0], g1.shape[0], 1)
    return (
        layer_out,
        in_grad,
        qkv_grad,
        out_grad,
        gu_grad,
        down_grad,
        mine[0],
        mine[1],
        mine[2],
        mine[3],
    )


def solution(mesh):
    wide, narrow = mesh.shape["wide"], mesh.shape["narrow"]
    grid = Mesh(mesh.devices.reshape(wide // 2, 2, narrow), ("z", "y", "n"))
    w = ("z", "y")
    tokens, depth, lines, vector = P(None, w, "n"), P(None, w, "n"), P("n", w), P(w)
    return jax.shard_map(
        on_device,
        mesh=grid,
        in_specs=(
            tokens, P(None, w, None), P(), depth, lines, depth, lines,
            vector, vector, vector, vector, tokens,
        ),
        out_specs=(
            tokens, tokens, depth, lines, depth, lines, vector, vector, vector, vector,
        ),
        check_vma=False,
    )
```

```python
import functools

import jax
import jax.numpy as jnp
from jax import lax
from jax.experimental import pallas as pl
from jax.experimental.pallas import tpu as pltpu
from jax.sharding import Mesh
from jax.sharding import PartitionSpec as P

HEAD_DIM = 128
EPS = 1e-05
BF = jnp.bfloat16
F32 = jnp.float32
MESH = pl.DeviceIdType.MESH
VMEM_BYTES = 60 * 2**20
SWAP = [(0, 1), (1, 0)]
ANY = pl.BlockSpec(memory_space=pl.ANY)
VMEM = pl.BlockSpec(memory_space=pltpu.VMEM)
SMEM = pl.BlockSpec(memory_space=pltpu.SMEM)


def dot(a, b):
    return jnp.dot(a, b, preferred_element_type=F32)


def dot_nt(a, b):
    return lax.dot_general(a, b, (((1,), (1,)), ((), ())), preferred_element_type=F32)


def dot_tn(a, b):
    return lax.dot_general(a, b, (((0,), (0,)), ((), ())), preferred_element_type=F32)


def normalise(v):
    centred = v - jnp.mean(v, axis=-1, keepdims=True)
    rstd = lax.rsqrt(jnp.mean(centred * centred, axis=-1, keepdims=True) + EPS)
    return centred * rstd, rstd


def norm_back(xhat, rstd, grad, gain):
    dx = grad * gain
    a = jnp.mean(dx, axis=-1, keepdims=True)
    b = jnp.mean(dx * xhat, axis=-1, keepdims=True)
    return rstd * (dx - a - xhat * b)


def cost(us, sent=0):
    return pl.CostEstimate(flops=int(us * 1e9), bytes_accessed=int(us * 3.2e6), transcendentals=0)


def without(body, ins, extra):
    def run(*refs):
        return body(*refs[:ins], *refs[ins + extra :])

    return run


def kernel(body, ins, in_specs, outs, out_specs, us, name, scratch=(), first=(), grid=(), talk=None, aliases=None):
    extra = len(first)
    return pl.pallas_call(
        without(body, len(ins), extra),
        grid=grid,
        in_specs=list(in_specs) + [ANY] * extra,
        out_specs=out_specs,
        out_shape=outs,
        scratch_shapes=list(scratch),
        input_output_aliases=aliases or {},
        compiler_params=pltpu.CompilerParams(
            vmem_limit_bytes=VMEM_BYTES, collective_id=talk, has_side_effects=talk is not None
        ),
        cost_estimate=cost(us),
        name=name,
    )(*ins, *first)


def sems(*counts):
    return [pltpu.SemaphoreType.DMA((k,)) for k in counts]


def shaped(shape, dtype=BF):
    return jax.ShapeDtypeStruct(tuple(shape), dtype)


class Place:
    def __init__(self):
        self.y = lax.axis_index("y")
        self.n = lax.axis_index("n")
        self.x = self.n // 2
        self.c = self.n % 2
        self.ns = self.n + 1 - 2 * self.c
        self.nx = (self.n + 2) % 4
        self.nd = (self.ns + 2) % 4
        self.sib = {"n": self.ns}
        self.xn = {"n": self.nx}
        self.yn = {"y": 1 - self.y}
        self.xs = {"n": self.nd}


def meet(devices):
    barrier = pltpu.get_barrier_semaphore()
    for d in devices:
        pl.semaphore_signal(barrier, inc=1, device_id=d, device_id_type=MESH)
    pl.semaphore_wait(barrier, len(devices))


class Wire:
    def __init__(self, send_sems, recv_sems, first=0):
        self.ss, self.rs, self.at, self.sent = send_sems, recv_sems, first, []

    def make(self, src, dst, device, keep=True, again=False):
        self.at += not again
        k = self.at - 1
        copy = pltpu.make_async_remote_copy(
            src_ref=src, dst_ref=dst, send_sem=self.ss.at[k], recv_sem=self.rs.at[k],
            device_id=device, device_id_type=MESH,
        )
        if keep:
            self.sent.append(copy)
        return copy

    def finish(self):
        for copy in self.sent:
            copy.wait_send()


SPREAD = 9


class Spread:
    def __init__(self, wire, at, src, slot):
        y, n, nx = at.y, at.n, at.nx
        self.first = [
            wire.make(src, slot(y, n, None), at.xn),
            wire.make(src, slot(y, n, None), at.yn),
            wire.make(src, slot(y, n, None), at.sib),
        ]
        self.on_x = [
            wire.make(slot(y, nx, 0), slot(y, nx, 0), at.yn),
            wire.make(slot(y, nx, None), slot(y, nx, None), at.sib),
        ]
        self.on_y = [
            wire.make(slot(1 - y, n, 1), slot(1 - y, n, 1), at.xn),
            wire.make(slot(1 - y, n, None), slot(1 - y, n, None), at.sib),
        ]
        self.last = [
            wire.make(slot(1 - y, nx, 0), slot(1 - y, nx, 0), at.sib),
            wire.make(slot(1 - y, nx, 1), slot(1 - y, nx, 1), at.sib),
        ]

    def begin(self):
        for copy in self.first:
            copy.start()

    def forward(self):
        self.first[0].wait_recv()
        for copy in self.on_x:
            copy.start()
        self.first[1].wait_recv()
        for copy in self.on_y:
            copy.start()

    def forward_last(self):
        self.on_x[0].wait_recv()
        self.last[0].start()
        self.on_y[0].wait_recv()
        self.last[1].start()

    def end(self):
        self.first[2].wait_recv()
        self.on_x[1].wait_recv()
        self.on_y[1].wait_recv()
        self.last[0].wait_recv()
        self.last[1].wait_recv()


REDUCE = 10


def reduce_scratch(micro, tok, sub, width):
    half = sub // 2
    return [
        pltpu.VMEM((micro, 2, tok, width), BF),
        pltpu.VMEM((micro, 2, 2, sub, width), BF),
        pltpu.VMEM((micro, sub, width), BF),
        pltpu.VMEM((micro, sub, width), BF),
        pltpu.VMEM((micro, sub, width), BF),
        pltpu.VMEM((micro, 2, half, width), BF),
        pltpu.VMEM((micro, sub, width), BF),
        pltpu.VMEM((micro, sub, width), BF),
    ]


class Reduce:
    def __init__(self, wire, at, scratch, compute):
        self.part, self.ra, self.sb, self.sx, self.sy, self.rb, self.rcx, self.rcy = scratch
        self.wire, self.at, self.compute = wire, at, compute
        self.micro, self.sub = self.sb.shape[0], self.sb.shape[1]
        self.a, self.b, self.d = {}, {}, {}
        self.released = False

    def rows(self, core, xx, lo=0, size=None):
        return pl.ds(pl.multiple_of((2 * xx + core) * self.sub, self.sub) + lo, size or self.sub)

    def summed(self, m, yy, xx, lo, size):
        mine = self.part[m, yy, self.rows(self.at.c, xx, lo, size), :].astype(F32)
        return mine + self.ra[m, yy, xx, lo : lo + size, :].astype(F32)

    def cores(self, m):
        at = self.at
        for yk, yy in ((1, 1 - at.y), (0, at.y)):
            self.compute(m, yy)
            for xk, xx in ((1, 1 - at.x), (0, at.x)):
                copy = self.wire.make(self.part.at[m, yy, self.rows(1 - at.c, xx)], self.ra.at[m, yy, xx], at.sib)
                copy.start()
                self.a[m, yk, xk] = copy

    def diagonal(self, m):
        at, sub, half = self.at, self.sub, self.sub // 2
        self.a[m, 1, 1].wait_recv()
        self.sb[m] = self.summed(m, 1 - at.y, 1 - at.x, 0, sub).astype(BF)
        self.b[m, 0] = self.wire.make(self.sb.at[m, 0:half], self.rb.at[m, 0], at.xn)
        self.b[m, 1] = self.wire.make(self.sb.at[m, half:sub], self.rb.at[m, 1], at.yn)
        self.b[m, 0].start()
        self.b[m, 1].start()

    def sides(self, m):
        at, sub, half = self.at, self.sub, self.sub // 2
        sx, sy, rb, rcx, rcy = self.sx, self.sy, self.rb, self.rcx, self.rcy
        self.a[m, 1, 0].wait_recv()
        sy[m, half:sub] = self.summed(m, 1 - at.y, at.x, half, half).astype(BF)
        self.d[m, 0] = self.wire.make(sy.at[m, half:sub], rcy.at[m, half:sub], at.yn)
        self.d[m, 0].start()
        self.a[m, 0, 1].wait_recv()
        sx[m, 0:half] = self.summed(m, at.y, 1 - at.x, 0, half).astype(BF)
        self.d[m, 1] = self.wire.make(sx.at[m, 0:half], rcx.at[m, 0:half], at.xn)
        self.d[m, 1].start()
        self.b[m, 0].wait_recv()
        sy[m, 0:half] = (self.summed(m, 1 - at.y, at.x, 0, half) + rb[m, 0].astype(F32)).astype(BF)
        self.d[m, 2] = self.wire.make(sy.at[m, 0:half], rcy.at[m, 0:half], at.yn)
        self.d[m, 2].start()
        self.b[m, 1].wait_recv()
        sx[m, half:sub] = (self.summed(m, at.y, 1 - at.x, half, half) + rb[m, 1].astype(F32)).astype(BF)
        self.d[m, 3] = self.wire.make(sx.at[m, half:sub], rcx.at[m, half:sub], at.xn)
        self.d[m, 3].start()

    def release(self, m):
        at = self.at
        self.a[m, 0, 0].wait_recv()
        self.ra[m, at.y, at.x] = self.summed(m, at.y, at.x, 0, self.sub).astype(BF)
        for yk in (1, 0):
            for xk in (1, 0):
                copy = self.a[m, yk, xk]
                copy.wait_send()
                self.wire.sent = [other for other in self.wire.sent if other is not copy]
        self.released = True

    def arrived(self, m):
        if not self.released:
            self.a[m, 0, 0].wait_recv()
        for k in range(4):
            self.d[m, k].wait_recv()

    def total(self, m, lo, size):
        if self.released:
            own = self.ra[m, self.at.y, self.at.x, lo : lo + size, :].astype(F32)
        else:
            own = self.summed(m, self.at.y, self.at.x, lo, size)
        return own + self.rcx[m, lo : lo + size, :].astype(F32) + self.rcy[m, lo : lo + size, :].astype(F32)


def nothing():
    pass


def reduce_rows(wire, at, scratch, compute, finish, tick=nothing):
    red = Reduce(wire, at, scratch, compute)
    for m in range(red.micro):
        red.cores(m)
        red.diagonal(m)
    tick()
    for m in range(red.micro):
        red.sides(m)
    for m in range(red.micro):
        red.arrived(m)
        finish(m, lambda lo, size, m=m: red.total(m, lo, size))
        tick()


LINE = (
    (0, 3, 1, -1, 0),
    (3, 0, 2, -1, 0),
    (1, 0, 0, 2, 0),
    (2, 3, 3, 2, 0),
    (1, 2, 2, 2, 0),
    (2, 1, 1, 2, 0),
    (0, 2, 2, 0, 1),
    (3, 1, 1, 0, 1),
    (0, 1, 1, 1, 1),
    (3, 2, 2, 1, 1),
)


def chain_results(zn, parts, rows, cols):
    count = 2 * len(parts) if zn == 4 else (zn - 1 if 0 in parts else 0)
    return [shaped((rows, cols))] * count


def chain_links(zn, parts):
    return sum(t[4] in parts for t in LINE) + (1 in parts) if zn == 4 else (zn - 1 if 0 in parts else 0)


class Chain:
    def __init__(self, wire, zn, parts, g, first, second, bufs, load, k):
        z = lax.axis_index("z")
        rows, cols = (first or second)[0].shape
        self.moves, self.bufs, self.cols, self.joins = [], bufs, cols, zn == 4 and 1 in parts
        self.over = False

        def group(i):
            return g.at[pl.ds(pl.multiple_of(i * rows, rows), rows)]

        if zn == 4:
            places = {2: first[0], -1: first[1]}
            if second:
                places.update({0: second[0], 1: second[1]})
            for src, i, dst, place, part in LINE:
                if part in parts:
                    copy = wire.make(group(i), places[place], {"z": dst}, keep=False)
                    self.moves.append((z == src, z == dst, copy, place < 0))
        elif 0 in parts:
            for dz in range(1, zn):
                to = (z + dz) % zn
                self.moves.append((None, None, wire.make(group(to), first[dz - 1], {"z": to}, keep=False), False))
        if self.joins:
            far = 3 * (1 - z // 2)
            here, there = bufs.at[0, :, pl.ds(0, cols)], bufs.at[1, :, pl.ds(0, cols)]
            self.own = pltpu.make_async_copy(group(far), here, load.at[k])
            self.came = pltpu.make_async_copy(first[1], there, load.at[k + 1])
            self.on = wire.make(here, second[1], {"z": far}, keep=False)
            self.inner = jnp.logical_and(z >= 1, z <= 2)
            self.outer = jnp.logical_not(self.inner)

    def begin(self):
        for sends, _, copy, _ in self.moves:
            if sends is None:
                copy.start()
            else:
                pl.when(sends)(copy.start)

    def join(self):
        if not self.joins:
            return

        def run():
            self.own.start()
            self.came.start()
            self.own.wait()
            self.came.wait()
            cols = pl.ds(0, self.cols)
            both = self.bufs[0, :, cols].astype(F32) + self.bufs[1, :, cols].astype(F32)
            self.bufs[0, :, cols] = both.astype(BF)
            self.on.start()

        for _, gets, copy, middle in self.moves:
            if middle:
                pl.when(gets)(copy.wait_recv)
        pl.when(self.inner)(run)

    def settle_sent(self):
        if self.joins:
            pl.when(self.inner)(self.on.wait_send)

    def wait(self):
        self.over = True
        for sends, gets, copy, middle in self.moves:
            if sends is None:
                copy.wait_recv()
                copy.wait_send()
                continue
            if not (middle and self.joins):
                pl.when(gets)(copy.wait_recv)
            pl.when(sends)(copy.wait_send)
        if self.joins:
            pl.when(self.outer)(self.on.wait_recv)


class Host:
    def __init__(self, chains):
        self.chains, self.todo, self.last = chains, list(chains), None

    def begin(self, which=None):
        for k, chain in enumerate(self.chains):
            if which is None or k == which:
                chain.begin()

    def next(self):
        if self.todo:
            if self.last is not None:
                self.last.settle_sent()
            self.last = self.todo.pop(0)
            self.last.join()

    def end(self):
        while self.todo:
            self.next()
        self.last.settle_sent()
        for chain in self.chains:
            if not chain.over:
                chain.wait()


class Settle:
    def __init__(self, wire, at, zn, g, first, second, keep, theirs, bufs, load):
        z = lax.axis_index("z")
        self.rows, self.cols = keep.shape[0] * 2, keep.shape[1]
        rows, half = self.rows, keep.shape[0]
        came = [first[0], second[1], second[0]] if zn == 4 else list(first)
        self.bufs, self.partly = bufs, jnp.logical_and(z >= 1, z <= 2) if zn == 4 else None
        mine = g.at[pl.ds(pl.multiple_of(z * rows, rows), rows)]
        self.loads = [pltpu.make_async_copy(src, bufs.at[k], load.at[k]) for k, src in enumerate([mine] + came)]

        def part(i):
            return bufs.at[0, pl.ds(pl.multiple_of(i * half, half), half)]

        self.away = wire.make(part(1 - at.y), theirs, at.yn, keep=False)
        self.here = pltpu.make_async_copy(part(at.y), keep, load.at[len(self.loads)])

    def go(self):
        always = self.loads if self.partly is None else self.loads[:-1]
        for copy in always:
            copy.start()
        if self.partly is not None:
            k = len(always)
            pl.when(self.partly)(self.loads[k].start)
            pl.when(self.partly)(self.loads[k].wait)

            def none():
                self.bufs[k] = jnp.zeros((self.rows, self.cols), BF)

            pl.when(jnp.logical_not(self.partly))(none)
        for copy in always:
            copy.wait()
        total = self.bufs[0].astype(F32)
        for k in range(1, len(self.loads)):
            total = total + self.bufs[k].astype(F32)
        self.bufs[0] = total.astype(BF)
        self.away.start()
        self.here.start()

    def wait(self):
        self.away.wait_recv()
        self.away.wait_send()
        self.here.wait()


def settle_scratch(zn, rows, cols):
    return [pltpu.VMEM((zn, rows, cols), BF)] + sems(zn + 1)


def z_partners(zn):
    z = lax.axis_index("z")
    return [{"z": (z + dz) % zn} for dz in range(1, zn)]


class Jobs:
    def __init__(self, plan, zn):
        self.plan, self.zn = plan, zn
        self.ins, self.outs, self.links = [], [], 0
        for g, parts, given in plan:
            self.ins += [g] + list(given)
            self.outs += chain_results(zn, parts, g.shape[0] // zn, g.shape[1])
            self.links += chain_links(zn, parts)
        wide = max([p[0].shape[1] for p in plan], default=0)
        rows = plan[0][0].shape[0] // zn if plan else 0
        self.scratch = [pltpu.VMEM((2, rows, wide), BF)] + sems(2 * len(plan)) if plan else []

    def host(self, wire, ins, outs, scratch):
        chains, i, o = [], 0, 0
        for k, (g, parts, given) in enumerate(self.plan):
            count = len(chain_results(self.zn, parts, 8, 128))
            made = outs[o : o + count]
            first = ins[i + 1 : i + 1 + len(given)] if given else (made if 1 not in parts or self.zn != 4 else made[:2])
            second = [] if 1 not in parts or self.zn != 4 else made[-2:]
            chains.append(Chain(wire, self.zn, parts, ins[i], first, second, *scratch, 2 * k))
            i, o = i + 1 + len(given), o + count
        return Host(chains)


def blockwise(part, m, yy, fn, tile=256):
    tok = part.shape[2]

    def step(i, carry):
        lo = pl.multiple_of(i * tile, tile)
        fn(lo, tile)
        return carry

    lax.fori_loop(0, tok // tile, step, 0)


def token_spreads(wire, at, src, out, sem, first, cut):
    micro, tok, feat = src.shape
    spreads, local = [], []
    for m in range(micro):

        def slot(yy, nn, part, m=m):
            lo, size = {None: (0, tok), 0: (0, cut), 1: (cut, tok - cut)}[part]
            return out.at[m, yy, pl.ds(lo, size), pl.ds(pl.multiple_of(nn * feat, feat), feat)]

        spreads.append(Spread(wire, at, src.at[m], slot))
        local.append(pltpu.make_async_copy(src.at[m], slot(at.y, at.n, None), sem.at[first + m]))
    return spreads, local


def attn_cut(w_qkv, w_out, i, buf):
    parts, _, cols = w_qkv.shape
    half = cols // 2
    at = pl.ds(pl.multiple_of(i * half, half), half)
    for p in range(parts):
        buf[:, p * half : (p + 1) * half] = w_qkv[p, :, at]
    buf[:, parts * half :] = w_out[at, :].astype(F32).T.astype(BF)


def chunk_cut(w_gu, w_down, i, c, one, buf):
    half = w_gu.shape[2] // 2
    at = pl.ds(pl.multiple_of(i * half, half) + c * one, one)
    buf[:, :one] = w_gu[0, :, at]
    buf[:, one : 2 * one] = w_gu[1, :, at]
    buf[:, 2 * one :] = w_down[at, :].astype(F32).T.astype(BF)


class Swap:
    def __init__(self, wire, at, bufs, out, sem):
        depth = bufs.shape[1]
        place = out.at[pl.ds(pl.multiple_of(at.y * depth, depth), depth)]
        self.away = wire.make(bufs.at[0], place, at.yn)
        self.here = pltpu.make_async_copy(bufs.at[1], place, sem)

    def end(self):
        self.away.wait_recv()
        self.here.wait()


def swap_attn_kernel(w_qkv, w_out, out, bufs, ss, rs, ls):
    at = Place()
    meet([at.yn])
    wire = Wire(ss, rs)
    swap = Swap(wire, at, bufs, out, ls.at[0])
    attn_cut(w_qkv, w_out, 1 - at.y, bufs.at[0])
    swap.away.start()
    attn_cut(w_qkv, w_out, at.y, bufs.at[1])
    swap.here.start()
    swap.end()
    wire.finish()


def swap_attn(w_qkv, w_out):
    parts, depth, cols = w_qkv.shape
    size = (parts + 1) * cols // 2
    return kernel(
        swap_attn_kernel, (w_qkv, w_out), [VMEM, VMEM], shaped((2 * depth, size)), ANY, 14, "swap_attn",
        [pltpu.VMEM((2, depth, size), BF)] + sems(1, 1, 1), talk=6,
    )


def swap_chunks(wire, at, w_gu, w_down, which, one, bufs, outs, ls):
    swaps = []
    for k, (c, out) in enumerate(zip(which, outs)):
        swap = Swap(wire, at, bufs.at[k], out, ls.at[k])
        chunk_cut(w_gu, w_down, 1 - at.y, c, one, bufs.at[k, 0])
        swap.away.start()
        chunk_cut(w_gu, w_down, at.y, c, one, bufs.at[k, 1])
        swap.here.start()
        swaps.append(swap)
    return swaps


def gather_x_kernel(zn, which, count, x_in, v_in, lens, freq, w_gu, w_down, x_out, v_out, lens_all, cos, sin, own, *scratch):
    bufs, ss, rs, ls = scratch
    at = Place()
    z = lax.axis_index("z")
    one = own.shape[2] // 3
    ring = [(dz, dy) for dz in range(zn) for dy in range(2) if dz or dy]
    others = [{"z": (z + dz) % zn, "y": (at.y + dy) % 2} for dz, dy in ring]
    meet([at.sib, at.xn] + others)
    wire = Wire(ss, rs)
    there = wire.make(lens, lens_all.at[at.y], at.yn)
    there.start()
    spreads, local = token_spreads(wire, at, x_in, x_out, ls, len(which) + 1, x_in.shape[1] // 8)
    local.append(pltpu.make_async_copy(v_in, v_out.at[z, at.y], ls.at[len(which)]))
    small = [wire.make(v_in, v_out.at[z, at.y], d) for d in others]
    for s in spreads:
        s.begin()
    for copy in small + local:
        copy.start()
    swaps = swap_chunks(wire, at, w_gu, w_down, which, one, bufs, [own.at[k] for k in range(len(which))], ls)
    lens_all[at.y] = lens[...]
    there.wait_recv()
    tok = x_in.shape[1]
    row = lax.broadcasted_iota(jnp.int32, (tok, 1), 0)
    flip = jnp.where(lax.broadcasted_iota(jnp.int32, (1, HEAD_DIM), 1) < HEAD_DIM // 2, -1.0, 1.0)

    def table(b, carry):
        m, yy = b // 2, b % 2
        line = lens_all[yy, pl.ds(m, 1), :]
        end = jnp.zeros((1, 1), jnp.int32)
        start = jnp.zeros_like(row)
        for k in range(count):
            end = end + line[:, k : k + 1]
            start = jnp.where(row >= end, end, start)
        angle = (row - start).astype(F32) * freq[...]
        place = pl.ds(pl.multiple_of(b * tok, tok), tok)
        cos[place, :] = jnp.cos(angle)
        sin[place, :] = jnp.sin(angle) * flip
        return carry

    lax.fori_loop(0, x_in.shape[0] * 2, table, 0)
    run_spreads(spreads, local)
    for copy in small:
        copy.wait_recv()
    for swap in swaps:
        swap.end()
    wire.finish()


def gather_x(x, v, lens, freq, w_gu, w_down, zn, which, one, count, first):
    micro, tok, feat = x.shape
    depth = w_gu.shape[1]
    rows = micro * 2 * tok
    links = SPREAD * micro + 2 * zn - 1 + len(which) + 1
    return kernel(
        functools.partial(gather_x_kernel, zn, which, count), (x, v, lens, freq, w_gu, w_down),
        [ANY, ANY, VMEM, VMEM, VMEM, VMEM],
        (
            shaped((micro, 2, tok, 4 * feat)), shaped((zn, 2) + v.shape, F32), shaped((2,) + lens.shape, jnp.int32),
            shaped((rows, HEAD_DIM), F32), shaped((rows, HEAD_DIM), F32), shaped((len(which), 2 * depth, 3 * one)),
        ),
        (ANY, ANY, VMEM, VMEM, VMEM, ANY), 48, "gather_x",
        [pltpu.VMEM((len(which), 2, depth, 3 * one), BF)] + sems(links, links, micro + 1 + len(which)),
        first, talk=0,
    )


def gather_d_kernel(which, one, d_in, x_all, gain, shift, w_gu, w_down, d_out, n1, *refs):
    outs, (bufs, xin, nout, ss, rs, ls, load) = refs[: len(which)], refs[len(which) :]
    at = Place()
    micro, _, tok, _ = x_all.shape
    meet([at.sib, at.xn, at.yn])
    wire = Wire(ss, rs)
    spreads, local = token_spreads(wire, at, d_in, d_out, ls, len(which), d_in.shape[1] // 16 * 5)

    def bring(b):
        return pltpu.make_async_copy(x_all.at[b // 2, b % 2], xin.at[b % 2], load.at[b])

    def put(b):
        return pltpu.make_async_copy(nout.at[b % 2], n1.at[pl.ds(b * tok, tok)], load.at[2 * micro + b])

    bring(0).start()
    bring(1).start()
    for s in spreads:
        s.begin()
    for copy in local:
        copy.start()
    swaps = swap_chunks(wire, at, w_gu, w_down, which, one, bufs, outs, ls)
    for b in range(2 * micro):
        bring(b).wait()
        if b >= 2:
            put(b - 2).wait()

        def tile(i, carry, b=b):
            place = pl.ds(pl.multiple_of(i * 128, 128), 128)
            xhat, _ = normalise(xin[b % 2, place, :].astype(F32))
            nout[b % 2, place, :] = (xhat * gain[...] + shift[...]).astype(BF)
            return carry

        lax.fori_loop(0, tok // 128, tile, 0)
        put(b).start()
        if b + 2 < 2 * micro:
            bring(b + 2).start()
        if b % 2:
            spreads[b // 2].forward()
    put(2 * micro - 2).wait()
    put(2 * micro - 1).wait()
    for s in spreads:
        s.forward_last()
    for s in spreads:
        s.end()
    for copy in local:
        copy.wait()
    for swap in swaps:
        swap.end()
    wire.finish()


def gather_d(d, x_all, gain, shift, w_gu, w_down, which, one):
    micro, tok, feat = d.shape
    depth = w_gu.shape[1]
    count = SPREAD * micro + len(which)
    return kernel(
        functools.partial(gather_d_kernel, which, one), (d, x_all, gain, shift, w_gu, w_down),
        [ANY, ANY, VMEM, VMEM, VMEM, VMEM],
        (shaped((micro, 2, tok, 4 * feat)), shaped((micro * 2 * tok, 4 * feat))) + (shaped((2 * depth, 3 * one)),) * len(which),
        (ANY,) * (2 + len(which)), 48, "gather_d",
        [pltpu.VMEM((len(which), 2, depth, 3 * one), BF)] + [pltpu.VMEM((2, tok, 4 * feat), BF)] * 2
        + sems(count, count, micro + len(which), 4 * micro),
        talk=5,
    )


def row_slot(out, m, sub):
    half = sub // 2

    def slot(yy, nn, part):
        ref = out.at[m, yy, nn]
        return ref if part is None else ref.at[pl.ds(part * half, half)]

    return slot


def run_spreads(spreads, local, tick=nothing):
    for s in spreads:
        s.forward()
    tick()
    for s in spreads:
        s.forward_last()
    for s in spreads:
        s.end()
    for copy in local:
        copy.wait()


def attn_out_kernel(att, wo, x_all, gain, shift, middle, n2, *scratch):
    *red, xb, nb, ss, rs, ls = scratch
    at = Place()
    micro, sub, width = middle.shape
    zn, dz, cols = wo.shape
    span = att.shape[1]
    tok = red[0].shape[2]
    meet([at.sib, at.xn, at.yn])
    wire = Wire(ss, rs)
    own = [pltpu.make_async_copy(x_all.at[m, at.y, pl.ds(at.n * sub, sub)], xb.at[m], ls.at[m]) for m in range(micro)]
    for copy in own:
        copy.start()

    def compute(m, yy):
        def tile(lo, size):
            a = att[pl.ds(pl.multiple_of((m * 2 + yy) * tok, tok) + lo, size), :]
            for k in range(zn):
                red[0][m, yy, pl.ds(lo, size), k * dz : (k + 1) * dz] = dot_nt(a, wo[k, :, cols - span :]).astype(BF)

        blockwise(red[0], m, yy, tile)

    spreads, local = [], []

    def finish(m, total):
        own[m].wait()
        step = sub // 2
        for lo in range(0, sub, step):
            mid = xb[m, lo : lo + step, :].astype(F32) + total(lo, step)
            middle[m, lo : lo + step, :] = mid
            xhat, _ = normalise(mid)
            nb[m, lo : lo + step, :] = (xhat * gain[...] + shift[...]).astype(BF)
        slot = row_slot(n2, m, sub)
        spreads.append(Spread(wire, at, nb.at[m], slot))
        spreads[-1].begin()
        local.append(pltpu.make_async_copy(nb.at[m], slot(at.y, at.n, None), ls.at[micro + m]))
        local[-1].start()

    reduce_rows(wire, at, red, compute, finish)
    run_spreads(spreads, local)
    wire.finish()


def attn_out(att, wo, x_all, gain, shift):
    micro, _, tok, width = x_all.shape
    sub = tok // 4
    count = (REDUCE + SPREAD) * micro
    return kernel(
        attn_out_kernel, (att, wo, x_all, gain, shift), [VMEM, VMEM, ANY, VMEM, VMEM],
        (shaped((micro, sub, width), F32), shaped((micro, 2, 4, sub, width))), (VMEM, ANY), 85, "attn_out",
        reduce_scratch(micro, tok, sub, width) + [pltpu.VMEM((micro, sub, width), BF)] * 2 + sems(count, count, 2 * micro),
        talk=1,
    )


def nt_compute(part, lows, ws, first, each=0):
    zn, dz, _ = ws[0].shape
    tok = part.shape[2]
    span = lows[0].shape[1]

    def compute(m, yy):
        def tile(lo, size):
            at = pl.multiple_of((m * 2 + yy) * tok, tok) + lo
            for k in range(zn):
                acc = None
                for i, (low, w) in enumerate(zip(lows, ws)):
                    lo_col = first + i * each
                    term = dot_nt(low[pl.ds(at, size), :], w[k, :, lo_col : lo_col + span])
                    acc = term if acc is None else acc + term
                part[m, yy, pl.ds(lo, size), k * dz : (k + 1) * dz] = acc.astype(BF)

        blockwise(part, m, yy, tile)

    return compute


class Columns:
    def __init__(self, groups, cols, bufs, load):
        self.copies = [
            pltpu.make_async_copy(src.at[:, :, cols], bufs.at[k], load.at[k]) for k, src in enumerate(groups)
        ]
        for copy in self.copies:
            copy.start()

    def wait(self):
        for copy in self.copies:
            copy.wait()


def chunk_refs(pair, last):
    return [pair.at[:, k] for k in range(pair.shape[1])] + [last]


def ffn_back_kernel(jobs, parts, *refs):
    guls = refs[:parts]
    pair, last, d_all, middle, gain, *refs = refs[parts:]
    zin, (mid_grad, branch, vec), refs = refs[: len(jobs.ins)], refs[len(jobs.ins) :][:3], refs[len(jobs.ins) + 3 :]
    zout, refs = refs[: len(jobs.outs)], refs[len(jobs.outs) :]
    *red, db, nb, wv, ss, rs, ls, lw, zb, zl = refs
    at = Place()
    micro, sub, width = middle.shape
    span = guls[0].shape[1]
    weights = Columns(chunk_refs(pair, last), pl.ds(0, span), wv, lw)
    own = [pltpu.make_async_copy(d_all.at[m, at.y, pl.ds(at.n * sub, sub)], db.at[m], ls.at[m]) for m in range(micro)]
    for copy in own:
        copy.start()
    meet([at.sib, at.xn, at.yn] + z_partners(jobs.zn))
    wire = Wire(ss, rs)
    host = jobs.host(wire, zin, zout, (zb, zl))
    host.begin()
    vec[...] = jnp.zeros_like(vec)
    spreads, local = [], []

    def finish(m, total):
        own[m].wait()
        step = sub // 2
        for lo in range(0, sub, step):
            grad = total(lo, step)
            xhat, rstd = normalise(middle[m, lo : lo + step, :])
            vec[0:1, :] += jnp.sum(grad * xhat, axis=0, keepdims=True)
            vec[1:2, :] += jnp.sum(grad, axis=0, keepdims=True)
            mg = db[m, lo : lo + step, :].astype(F32) + norm_back(xhat, rstd, grad, gain[...])
            mid_grad[m, lo : lo + step, :] = mg
            nb[m, lo : lo + step, :] = mg.astype(BF)
        slot = row_slot(branch, m, sub)
        spreads.append(Spread(wire, at, nb.at[m], slot))
        spreads[-1].begin()
        local.append(pltpu.make_async_copy(nb.at[m], slot(at.y, at.n, None), ls.at[micro + m]))
        local[-1].start()

    weights.wait()
    reduce_rows(wire, at, red, nt_compute(red[0], guls, [wv.at[k] for k in range(parts)], 0), finish, host.next)
    run_spreads(spreads, local, host.next)
    host.end()
    wire.finish()


def ffn_back(guls, pair, last, d_all, middle, gain, plan, zn, first):
    parts = len(guls)
    micro, _, tok, width = d_all.shape
    sub = tok // 4
    jobs = Jobs(plan, zn)
    count = (REDUCE + SPREAD) * micro + jobs.links
    span = guls[0].shape[1]
    return kernel(
        functools.partial(ffn_back_kernel, jobs, parts), (*guls, pair, last, d_all, middle, gain, *jobs.ins),
        [VMEM] * parts + [ANY, ANY, ANY, VMEM, VMEM] + [ANY] * len(jobs.ins),
        (shaped((micro, sub, width), F32), shaped((micro, 2, 4, sub, width)), shaped((8, width), F32), *jobs.outs),
        (VMEM, ANY, VMEM) + (ANY,) * len(jobs.outs), 90, "ffn_back",
        reduce_scratch(micro, tok, sub, width) + [pltpu.VMEM((micro, sub, width), BF)] * 2
        + [pltpu.VMEM((parts, zn, width // zn, span), BF)] + sems(count, count, 2 * micro, parts) + jobs.scratch,
        first, talk=2,
    )


def host_kernel(jobs, *refs):
    zin, zout, (ss, rs, zb, zl) = refs[: len(jobs.ins)], refs[len(jobs.ins) :][: len(jobs.outs)], refs[-4:]
    meet(z_partners(jobs.zn))
    host = jobs.host(Wire(ss, rs), zin, zout, (zb, zl))
    host.begin()
    host.end()


def host_only(plan, zn, first):
    jobs = Jobs(plan, zn)
    return kernel(
        functools.partial(host_kernel, jobs), jobs.ins, [ANY] * len(jobs.ins), tuple(jobs.outs), (ANY,) * len(jobs.outs),
        20 * jobs.steps, "along_z", sems(2 * jobs.steps, 2 * jobs.steps) + jobs.scratch, first, talk=8,
    )


class Deal:
    def __init__(self, wire, at, rows, out, m, sems, k):
        sub, width = rows.shape[1], rows.shape[2]
        feat = width // 4

        def cols(nn):
            return rows.at[m, :, pl.ds(pl.multiple_of(nn * feat, feat), feat)]

        place = out.at[m, pl.ds(pl.multiple_of(at.n * sub, sub), sub)]
        self.local = pltpu.make_async_copy(cols(at.n), place, sems.at[k])
        self.copies = [
            wire.make(cols(at.nx), place, at.xn),
            wire.make(cols(at.nd), place, at.xs),
            wire.make(cols(at.ns), place, at.sib),
        ]

    def begin(self):
        for copy in self.copies:
            copy.start()
        self.local.start()

    def end(self):
        for copy in self.copies:
            copy.wait_recv()
        self.local.wait()


def last_kernel(jobs, zn, marks, *refs):
    low, wa, x_all, mid_grad, gain, vec2, *refs = refs
    g2, came2, refs = refs[0], refs[1 : 1 + marks], refs[1 + marks :]
    zin, refs = refs[: len(jobs.ins)], refs[len(jobs.ins) :]
    in_grad, sums, *refs = refs
    settled, zout, refs = refs[:6], refs[6:][: len(jobs.outs)], refs[6 + len(jobs.outs) :]
    red, refs = refs[:8], refs[8:]
    xb, ob, w1, mine, plane, summed, lines, yb2, ybo, ybq, yl2, ylo, ylq, ss, rs, ls, *talk = refs
    at = Place()
    z = lax.axis_index("z")
    micro, sub, width = mid_grad.shape
    qkv = pltpu.make_async_copy(wa.at[:, :, pl.ds(0, low.shape[1])], w1, ls.at[2 * micro])
    qkv.start()
    own = [pltpu.make_async_copy(x_all.at[m, at.y, pl.ds(at.n * sub, sub)], xb.at[m], ls.at[m]) for m in range(micro)]
    for copy in own:
        copy.start()
    flips = [(dy, dn) for dy in range(2) for dn in range(4) if dy or dn]
    peers = [{"y": (at.y + dy) % 2, "n": (at.n + dn) % 4} for dy, dn in flips]
    along = [{"z": (z + dz) % zn} for dz in range(1, zn)]
    meet(peers + along)
    wire = Wire(ss, rs)
    host = jobs.host(wire, zin, zout, talk)
    host.begin()
    split = len(chain_results(zn, (0,), 8, 128))
    settles = [
        Settle(wire, at, zn, g2, came2[:split], came2[split:], settled[0], settled[1], yb2, yl2),
        Settle(wire, at, zn, zin[1], zout[marks : marks + split], zout[marks + split :], settled[2], settled[3], ybo, ylo),
        Settle(wire, at, zn, zin[0], zout[:split], zout[split:marks], settled[4], settled[5], ybq, ylq),
    ]
    mine[...] = jnp.zeros_like(mine)
    mine[2:4] = vec2[0:2]
    qkv.wait()
    total = Reduce(wire, at, red, nt_compute(red[0], [low], [w1], 0))
    for m in range(micro):
        total.cores(m)
        total.diagonal(m)
    for m in range(micro):
        total.sides(m)
    host.next()
    step = sub // 2
    deals = []
    for m in range(micro):
        total.arrived(m)
        own[m].wait()
        for lo in range(0, sub, step):
            grad = total.total(m, lo, step)
            xhat, rstd = normalise(xb[m, lo : lo + step, :].astype(F32))
            mine[0:1, :] += jnp.sum(grad * xhat, axis=0, keepdims=True)
            mine[1:2, :] += jnp.sum(grad, axis=0, keepdims=True)
            back = norm_back(xhat, rstd, grad, gain[...])
            ob[m, lo : lo + step, :] = (mid_grad[m, lo : lo + step, :] + back).astype(BF)
        deals.append(Deal(wire, at, ob, in_grad, m, ls, micro + m))
        deals[-1].begin()
        if m == 0:
            settles[0].go()
    near = [wire.make(mine, plane.at[k], d) for k, d in enumerate(peers)]
    for copy in near:
        copy.start()
    for copy in near:
        copy.wait_recv()
    both = mine[...]
    for k in range(len(peers)):
        both = both + plane[k]
    summed[...] = both
    far = [wire.make(summed, lines.at[k], d) for k, d in enumerate(along)]
    for copy in far:
        copy.start()
    host.next()
    host.chains[0].wait()
    settles[2].go()
    host.end()
    settles[1].go()
    for copy in far:
        copy.wait_recv()
    both = summed[...]
    for k in range(len(along)):
        both = both + lines[k]
    sums[...] = both
    for deal in deals:
        deal.end()
    for settle in settles:
        settle.wait()
    wire.finish()


def last_sums(low, wa, x_all, mid_grad, gain, vec2, g2, got2, out_g, qkv_g, zn):
    micro, _, tok, width = x_all.shape
    sub = tok // 4
    dz, cols = width // zn, low.shape[1]
    jobs = Jobs([(qkv_g, (0, 1), ()), (out_g, (0, 1), ())], zn)
    count = (REDUCE + 3) * micro + 7 + zn - 1 + jobs.links + 3
    size = vec2.shape
    rows = pltpu.VMEM((micro, sub, width), BF)
    sizes = (g2.shape[1], out_g.shape[1], cols)
    halves = [shaped((dz // 2, k)) for k in sizes for _ in range(2)]
    return kernel(
        functools.partial(last_kernel, jobs, zn, len(got2)),
        (low, wa, x_all, mid_grad, gain, vec2, g2, *got2, *jobs.ins),
        [VMEM, ANY, ANY, VMEM, VMEM, VMEM] + [ANY] * (1 + len(got2) + len(jobs.ins)),
        (shaped((micro, tok, width // 4)), shaped(size, F32), *halves, *jobs.outs),
        (ANY, VMEM) + (ANY,) * (6 + len(jobs.outs)), 100, "last_sums",
        reduce_scratch(micro, tok, sub, width) + [rows] * 2 + [pltpu.VMEM((zn, dz, cols), BF)]
        + [pltpu.VMEM(size, F32), pltpu.VMEM((7,) + size, F32), pltpu.VMEM(size, F32), pltpu.VMEM((zn - 1,) + size, F32)]
        + [pltpu.VMEM((zn, dz, k), BF) for k in sizes] + sems(zn + 1, zn + 1, zn + 1, count, count, 2 * micro + 1) + jobs.scratch,
        talk=3,
    )


def tiles(rows, cols):
    return pl.BlockSpec((rows, cols), lambda i: (i, 0))


def same_protein(lens, b, tok, count):
    col = lax.broadcasted_iota(jnp.int32, (tok, 1), 0)
    row = lax.broadcasted_iota(jnp.int32, (1, tok), 1)
    pc, pr = jnp.zeros_like(col), jnp.zeros_like(row)
    end = jnp.int32(0)
    for k in range(count):
        end = end + lens[b % 2, b // 2, k]
        pc = pc + (col >= end).astype(jnp.int32)
        pr = pr + (row >= end).astype(jnp.int32)
    return pc == pr


def turn(v, cos, sin):
    return v * cos + pltpu.roll(v, HEAD_DIM // 2, 1) * sin


def attention_body(count, ends, n1, w, cos, sin, qkv, att):
    zn, dz, _ = w.shape
    cols = qkv.shape[1]
    tok = n1.shape[0]
    heads = cols // 3 // HEAD_DIM
    span = heads * HEAD_DIM
    acc = dot(n1[:, 0:dz], w[0, :, :cols])
    for k in range(1, zn):
        acc = acc + dot(n1[:, k * dz : (k + 1) * dz], w[k, :, :cols])
    same = same_protein(ends, pl.program_id(0), tok, count)
    scale = HEAD_DIM ** (-0.5)
    for h in range(heads):
        lo = h * HEAD_DIM
        q = turn(acc[:, lo : lo + HEAD_DIM], cos[...], sin[...]).astype(BF)
        k = turn(acc[:, span + lo : span + lo + HEAD_DIM], cos[...], sin[...]).astype(BF)
        v = acc[:, 2 * span + lo : 2 * span + lo + HEAD_DIM].astype(BF)
        qkv[:, lo : lo + HEAD_DIM] = q
        qkv[:, span + lo : span + lo + HEAD_DIM] = k
        qkv[:, 2 * span + lo : 2 * span + lo + HEAD_DIM] = v
        s = jnp.where(same, dot_nt(q, k) * scale, -1e30)
        e = jnp.exp(s - jnp.max(s, axis=-1, keepdims=True))
        p = (e / jnp.sum(e, axis=-1, keepdims=True)).astype(BF)
        att[:, lo : lo + HEAD_DIM] = dot(p, v).astype(BF)


def attention(count, ends, n1, w, cos, sin, passed, tok):
    rows, width = n1.shape
    cols = w.shape[2] // 4 * 3

    def body(e, a, b, c, d, _, qkv, att, __):
        attention_body(count, e, a, b, c, d, qkv, att)

    return kernel(
        body, (ends, n1, w, cos, sin, passed),
        [SMEM, tiles(tok, width), VMEM, tiles(tok, HEAD_DIM), tiles(tok, HEAD_DIM), ANY],
        (shaped((rows, cols)), shaped((rows, cols // 3)), shaped(passed.shape)),
        (tiles(tok, cols), tiles(tok, cols // 3), ANY), 20, "attention", grid=(rows // tok,), aliases={5: 2},
    )


def attention_back_body(count, ends, b, branch, wo, qkv, cos, sin, low):
    zn, dz, span = wo.shape
    tok = branch.shape[0]
    heads = span // HEAD_DIM
    acc = dot(branch[:, 0:dz], wo[0])
    for k in range(1, zn):
        acc = acc + dot(branch[:, k * dz : (k + 1) * dz], wo[k])
    same = same_protein(ends, b, tok, count)
    scale = HEAD_DIM ** (-0.5)
    for h in range(heads):
        lo = h * HEAD_DIM
        ag = acc[:, lo : lo + HEAD_DIM].astype(BF)
        q = qkv[:, lo : lo + HEAD_DIM]
        k = qkv[:, span + lo : span + lo + HEAD_DIM]
        v = qkv[:, 2 * span + lo : 2 * span + lo + HEAD_DIM]
        s = jnp.where(same, dot_nt(q, k) * scale, -1e30)
        e = jnp.exp(s - jnp.max(s, axis=-1, keepdims=True))
        p = e / jnp.sum(e, axis=-1, keepdims=True)
        pg = dot_nt(ag, v)
        vg = dot_tn(p.astype(BF), ag)
        rd = jnp.sum(p * pg, axis=-1, keepdims=True)
        sg = (p * (pg - rd)).astype(BF)
        qg = dot(sg, k) * scale
        kg = dot_tn(sg, q) * scale
        low[:, lo : lo + HEAD_DIM] = turn(qg, cos[...], -sin[...]).astype(BF)
        low[:, span + lo : span + lo + HEAD_DIM] = turn(kg, cos[...], -sin[...]).astype(BF)
        low[:, 2 * span + lo : 2 * span + lo + HEAD_DIM] = vg.astype(BF)


def attention_back_kernel(jobs, count, parts, marks, *refs):
    lens, branch, att, wa, qkv, cos, sin, n1, *refs = refs
    n0, n1s = marks
    g0, came0, g1, came1, refs = refs[0], refs[1 : 1 + n0], refs[1 + n0], refs[2 + n0 : 2 + n0 + n1s], refs[2 + n0 + n1s :]
    pair, last, middle, *refs = refs
    hids, zin, refs = refs[:parts], refs[parts:][: len(jobs.ins)], refs[parts + len(jobs.ins) :]
    low, grads, out_g, *refs = refs
    settled, layer_out, refs = refs[:4], refs[4], refs[5:]
    zout, refs = refs[: len(jobs.outs)], refs[len(jobs.outs) :]
    red, refs = refs[:8], refs[8:]
    bv, wo, ob, yb, load, yl, ls, ss, rs, *talk = refs
    rows, width = bv.shape
    zn, dz, span = wo.shape
    tok = rows // 4
    one = hids[0].shape[1]
    micro, sub, _ = middle.shape
    at = Place()
    cols = low.shape[1]
    downs, chunks = [], chunk_refs(pair, last)
    for k in range(parts):
        place = pl.ds(k * one, one)
        downs.append(pltpu.make_async_copy(hids[k], low.at[:, place], load.at[9 + k]))
        downs.append(
            pltpu.make_async_copy(chunks[k].at[:, :, pl.ds(2 * one, one)], grads.at[:, :, place], load.at[9 + parts + k])
        )
    for copy in downs:
        copy.start()
    weights = pltpu.make_async_copy(wa.at[:, :, pl.ds(cols, span)], wo, load.at[8])
    weights.start()

    def bring(b):
        here = pl.ds(b * tok, tok)
        return (
            pltpu.make_async_copy(branch.at[here], bv.at[here], load.at[b]),
            pltpu.make_async_copy(n1.at[here], red[0].at[b // 2, b % 2], load.at[4 + b]),
        )

    for b in range(4):
        bring(b)[0].start()
    meet(z_partners(zn) + [at.sib, at.xn, at.yn, at.xs])
    wire = Wire(ss, rs)
    host = jobs.host(wire, zin, zout, talk)
    split = len(chain_results(zn, (0,), 8, 128))
    settles = [
        Settle(wire, at, zn, g0, came0[:split], came0[split:], settled[0], settled[1], yb, yl),
        Settle(wire, at, zn, g1, came1[:split], came1[split:], settled[2], settled[3], yb, yl),
    ]
    host.begin()
    for copy in downs:
        copy.wait()
    lows = [low.at[:, pl.ds(k * one, one)] for k in range(parts)]
    total = Reduce(wire, at, red, nt_compute(red[0], lows, [grads] * parts, 0, one))
    for m in range(micro):
        total.cores(m)
        total.diagonal(m)
    settles[0].go()
    weights.wait()

    def block(b):
        bring(b)[0].wait()
        here = pl.ds(b * tok, tok)
        attention_back_body(
            count, lens, b, bv.at[here], wo, qkv.at[here], cos.at[here], sin.at[here], low.at[here]
        )

    block(0)
    for m in range(micro):
        total.sides(m)
        total.release(m)
    host.next()
    for b in range(4):
        bring(b)[1].start()
    block(1)
    settles[0].wait()
    settles[1].go()
    block(2)
    block(3)
    for b in range(4):
        bring(b)[1].wait()

    def weights_of(k, carry):
        here = pl.ds(pl.multiple_of(k * dz, dz), dz)
        acc = 0.0
        for b in range(4):
            acc = acc + dot_tn(red[0][b // 2, b % 2, :, here], low[pl.ds(b * tok, tok), :])
        grads[k] = acc.astype(BF)
        out_g[here, :] = dot_tn(bv[:, here], att[...]).astype(BF)
        return carry

    lax.fori_loop(0, zn, weights_of, 0)
    deals, step = [], sub // 2
    for m in range(micro):
        total.arrived(m)
        for lo in range(0, sub, step):
            ob[m, lo : lo + step, :] = (middle[m, lo : lo + step, :] + total.total(m, lo, step)).astype(BF)
        deals.append(Deal(wire, at, ob, layer_out, m, ls, m))
        deals[-1].begin()
    settles[1].wait()
    for deal in deals:
        deal.end()
    host.end()
    wire.finish()


def attention_back(count, lens, branch, att, wa, qkv, cos, sin, n1, g0, got0, g1, got1, pair, last, middle, hids, g2, zn):
    rows, width = branch.shape
    cols, span, parts = qkv.shape[1], att.shape[1], len(hids)
    micro, sub, _ = middle.shape
    tok = rows // 4
    dz = width // zn
    out_g = shaped((width, span))
    jobs = Jobs([(g2, (0, 1), ())], zn)
    half = shaped((dz // 2, g0.shape[1]))
    links = jobs.links + 2 + (REDUCE + 3) * micro
    return kernel(
        functools.partial(attention_back_kernel, jobs, count, parts, (len(got0), len(got1))),
        (lens, branch, att, wa, qkv, cos, sin, n1, g0, *got0, g1, *got1, pair, last, middle, *hids, *jobs.ins),
        [SMEM, ANY, VMEM, ANY, VMEM, VMEM, VMEM, ANY] + [ANY] * (4 + len(got0) + len(got1)) + [VMEM] + [ANY] * (parts + len(jobs.ins)),
        (shaped((rows, cols)), shaped((zn, dz, cols)), out_g, *(half,) * 4, shaped((micro, tok, width // 4)), *jobs.outs),
        (VMEM, VMEM, VMEM) + (ANY,) * (5 + len(jobs.outs)), 70, "attention_back",
        reduce_scratch(micro, tok, sub, width)
        + [pltpu.VMEM((rows, width), BF), pltpu.VMEM((zn, dz, span), BF), pltpu.VMEM((micro, sub, width), BF)]
        + settle_scratch(zn, dz, g0.shape[1])[:1]
        + sems(9 + 2 * parts, zn + 1, micro, links, links) + jobs.scratch,
        talk=9,
    )


def chunk_body(jobs, c, n2, dy, w, mask, *refs):
    zin, (low, hidden, grad), refs = refs[: len(jobs.ins)], refs[len(jobs.ins) :][:3], refs[len(jobs.ins) + 3 :]
    zout, (nv, dv, wv, load, *talk) = refs[: len(jobs.outs)], refs[len(jobs.outs) :]
    zn, dz, cols = wv.shape
    one = cols // 3
    steps = load.shape[1] - 1
    tile = nv.shape[0] // steps
    whole = pltpu.make_async_copy(w if c is None else w.at[:, c], wv, load.at[0, steps])
    whole.start()

    def bring(t):
        at = pl.ds(pl.multiple_of(t * tile, tile), tile)
        return (
            pltpu.make_async_copy(n2.at[at], nv.at[at], load.at[0, t]),
            pltpu.make_async_copy(dy.at[at], dv.at[at], load.at[1, t]),
        )

    for t in range(steps):
        for copy in bring(t):
            copy.start()
    if talk:
        ss, rs, *talk = talk
        meet(z_partners(jobs.zn))
        host = jobs.host(Wire(ss, rs), zin, zout, talk)
        host.begin()
    whole.wait()

    def forward(t, carry):
        for copy in bring(t):
            copy.wait()
        at = pl.ds(pl.multiple_of(t * tile, tile), tile)
        acc = hg = 0.0
        for k in range(zn):
            acc = acc + dot(nv[at, k * dz : (k + 1) * dz], wv[k, :, : 2 * one])
            hg = hg + dot(dv[at, k * dz : (k + 1) * dz], wv[k, :, 2 * one :])
        hg = hg * mask[...]
        g, u = acc[:, :one], acc[:, one:]
        phi = 0.5 * (1.0 + lax.erf(g * (0.5**0.5)))
        slope = phi + g * jnp.exp(-0.5 * g * g) * 0.3989422804014327
        act = g * phi
        hidden[at, :] = (act * u * mask[...]).astype(BF)
        low[at, :one] = (hg * u * slope).astype(BF)
        low[at, one:] = (hg * act).astype(BF)
        return carry

    lax.fori_loop(0, steps, forward, 0)

    def weights(k, carry):
        at = pl.ds(pl.multiple_of(k * dz, dz), dz)
        grad[at, : 2 * one] = dot_tn(nv[:, at], low[...]).astype(BF)
        grad[at, 2 * one :] = dot_tn(dv[:, at], hidden[...]).astype(BF)
        return carry

    lax.fori_loop(0, zn, weights, 0)
    if jobs.links:
        host.end()


def chunk(n2, dy, w, c, mask, plan, zn, talk, first):
    rows, width = n2.shape
    cols = w.shape[-1]
    one = cols // 3
    jobs = Jobs(plan, zn)
    return kernel(
        functools.partial(chunk_body, jobs, c), (n2, dy, w, mask, *jobs.ins), [ANY, ANY, ANY, VMEM] + [ANY] * len(jobs.ins),
        (shaped((rows, 2 * one)), shaped((rows, one)), shaped((width, cols)), *jobs.outs),
        (VMEM,) * 3 + (ANY,) * len(jobs.outs), 22, "ffn_chunk",
        [pltpu.VMEM((rows, width), BF)] * 2 + [pltpu.VMEM((zn, width // zn, cols), BF), pltpu.SemaphoreType.DMA((2, 5))]
        + (sems(jobs.links, jobs.links) + jobs.scratch if jobs.links else []),
        first, talk=talk if jobs.links else None,
    )


def form_body(parts, *refs):
    halves, (gu, down, qkv, out) = refs[: 2 * parts + 4], refs[2 * parts + 4 :]
    y = lax.axis_index("y")
    one = halves[0].shape[1] // 3

    def pair(k):
        keep, theirs = halves[2 * k][...].astype(F32), halves[2 * k + 1][...].astype(F32)
        return jnp.where(y == 0, keep, theirs), jnp.where(y == 0, theirs, keep)

    half = parts * one
    for k in range(parts):
        for i, v in enumerate(pair(k)):
            lo = i * half + k * one
            gu[0, :, lo : lo + one] = v[:, :one]
            gu[1, :, lo : lo + one] = v[:, one : 2 * one]
            down[lo : lo + one, :] = v[:, 2 * one :].T
    for i, v in enumerate(pair(parts)):
        span = v.shape[1]
        out[i * span : (i + 1) * span, :] = v.T
    for i, v in enumerate(pair(parts + 1)):
        span = v.shape[1] // 3
        for p in range(3):
            qkv[p, :, i * span : (i + 1) * span] = v[:, p * span : (p + 1) * span]


def form(halves, w_gu, w_down, w_qkv, w_out):
    parts = (len(halves) - 4) // 2
    return kernel(
        functools.partial(form_body, parts), halves, [VMEM] * len(halves),
        tuple(shaped(w.shape, F32) for w in (w_gu, w_down, w_qkv, w_out)),
        (VMEM,) * 4, 8, "form",
    )


CHUNKS = 3


def on_device(inputs, lengths, counts, w_qkv, w_out, w_gu, w_down, g1, b1, g2, b2, dy_in):
    z = lax.axis_index("z")
    y = lax.axis_index("y")
    n = lax.axis_index("n")
    zn = lax.axis_size("z")
    micro, tok, feat = inputs.shape
    width = feat * lax.axis_size("n")
    rows = micro * 2 * tok
    depth = w_qkv.shape[1]
    half_slots = w_gu.shape[2] // 2
    one = half_slots // CHUNKS

    def gather_z(w):
        return lax.all_gather(w, "z", axis=0, tiled=False)

    own_attn = swap_attn(w_qkv, w_out)
    wa = gather_z(own_attn)
    vecs = jnp.stack([g1, b1, g2, b2]).astype(F32)
    vecs = jnp.pad(vecs, ((0, 4), (0, 0)))
    count = lengths.shape[2]
    lens = jnp.pad(lengths[:, 0], ((0, 8 - micro), (0, 128 - count)))
    half_dim = HEAD_DIM // 2
    freq = 10000.0 ** (-(jnp.arange(HEAD_DIM) % half_dim).astype(F32) / half_dim)
    x_all, norms, lens, cos, sin, own_01 = gather_x(
        inputs, vecs, lens, freq[None], w_gu, w_down, zn, (0, 1), one, count, (own_attn,)
    )
    norms = norms.transpose(2, 0, 1, 3).reshape(8, width)
    gain1, shift1, gain2, shift2 = (norms[i : i + 1] for i in range(4))
    own = jnp.sum(jnp.where(jnp.arange(counts.shape[0]) == n, counts, 0))
    mask = (y * half_slots + jnp.arange(half_slots) < own).astype(F32)[None]

    d_all, n1, own_2 = gather_d(dy_in, x_all, gain1, shift1, w_gu, w_down, (2,), one)
    dy = d_all.reshape(rows, width)
    qkv, att, own_2 = attention(count, lens, n1, wa, cos, sin, own_2, tok)
    w_01, w_2 = gather_z(own_01), gather_z(own_2)
    middle, n2 = attn_out(att, wa, x_all, gain2, shift2)
    n2 = n2.reshape(rows, width)

    def own_mask(c):
        return mask[:, c * one : (c + 1) * one]

    low0, hid0, g0 = chunk(n2, dy, w_01, 0, own_mask(0), [], zn, None, ())
    low1, hid1, grad1 = chunk(n2, dy, w_01, 1, own_mask(1), [], zn, None, (g0,))
    low2, hid2, grad2, *p = chunk(n2, dy, w_2, None, own_mask(2), [(g0, (0,), ())], zn, 7, (grad1,))
    mid_grad, branch, vec2, *q = ffn_back(
        [low0, low1, low2], w_01, w_2, d_all, middle, gain2, [(grad1, (0, 1), ()), (g0, (1,), p)], zn, ()
    )
    many = len(chain_results(zn, (0, 1), 8, 128))
    got1, got0 = q[:many], p + q[many:]
    branch = branch.reshape(rows, width)
    low, qkv_g, out_g, *r = attention_back(
        count, lens, branch, att, wa, qkv, cos, sin, n1, g0, got0, grad1, got1, w_01, w_2, middle, [hid0, hid1, hid2], grad2, zn
    )
    first, layer_out, got2 = r[:4], r[4], r[5:]
    in_grad, sums, *r = last_sums(
        low, wa, x_all, mid_grad, gain1, vec2, grad2, got2, out_g, qkv_g.reshape(width, -1), zn
    )
    gu_grad, down_grad, qkv_grad, out_grad = form(
        [*first, *r[:6]], w_gu, w_down, w_qkv, w_out
    )

    mine = lax.dynamic_slice_in_dim(sums, (z * 2 + y) * g1.shape[0], g1.shape[0], 1)
    return (
        layer_out,
        in_grad,
        qkv_grad,
        out_grad,
        gu_grad,
        down_grad,
        mine[0],
        mine[1],
        mine[2],
        mine[3],
    )


def solution(mesh):
    wide, narrow = mesh.shape["wide"], mesh.shape["narrow"]
    grid = Mesh(mesh.devices.reshape(wide // 2, 2, narrow), ("z", "y", "n"))
    w = ("z", "y")
    tokens, depth, lines, vector = P(None, w, "n"), P(None, w, "n"), P("n", w), P(w)
    return jax.shard_map(
        on_device,
        mesh=grid,
        in_specs=(
            tokens, P(None, w, None), P(), depth, lines, depth, lines,
            vector, vector, vector, vector, tokens,
        ),
        out_specs=(
            tokens, tokens, depth, lines, depth, lines, vector, vector, vector, vector,
        ),
        check_vma=False,
    )
```

```python
import functools

import jax
import jax.numpy as jnp
from jax import lax
from jax.experimental import pallas as pl
from jax.experimental.pallas import tpu as pltpu
from jax.sharding import Mesh
from jax.sharding import PartitionSpec as P

HEAD_DIM = 128
EPS = 1e-05
BF = jnp.bfloat16
F32 = jnp.float32
MESH = pl.DeviceIdType.MESH
VMEM_BYTES = 60 * 2**20
SWAP = [(0, 1), (1, 0)]
ANY = pl.BlockSpec(memory_space=pl.ANY)
VMEM = pl.BlockSpec(memory_space=pltpu.VMEM)
SMEM = pl.BlockSpec(memory_space=pltpu.SMEM)


def dot(a, b):
    return jnp.dot(a, b, preferred_element_type=F32)


def dot_nt(a, b):
    return lax.dot_general(a, b, (((1,), (1,)), ((), ())), preferred_element_type=F32)


def dot_tn(a, b):
    return lax.dot_general(a, b, (((0,), (0,)), ((), ())), preferred_element_type=F32)


def normalise(v):
    centred = v - jnp.mean(v, axis=-1, keepdims=True)
    rstd = lax.rsqrt(jnp.mean(centred * centred, axis=-1, keepdims=True) + EPS)
    return centred * rstd, rstd


def norm_back(xhat, rstd, grad, gain):
    dx = grad * gain
    a = jnp.mean(dx, axis=-1, keepdims=True)
    b = jnp.mean(dx * xhat, axis=-1, keepdims=True)
    return rstd * (dx - a - xhat * b)


def cost(us, sent=0):
    return pl.CostEstimate(flops=int(us * 1e9), bytes_accessed=int(us * 3.2e6), transcendentals=0)


def without(body, ins, extra):
    def run(*refs):
        return body(*refs[:ins], *refs[ins + extra :])

    return run


def staged_body(body, ins, staged):
    def run(*refs):
        bufs, sem = refs[-len(staged) - 1 : -1], refs[-1]
        refs = list(refs[: -len(staged) - 1])
        copies = []
        for k, i in enumerate(staged):
            copies.append(pltpu.make_async_copy(refs[i], bufs[k], sem.at[k]))
            copies[-1].start()
            refs[i] = bufs[k]

        def ready():
            for copy in copies:
                copy.wait()

        return body(ready, *refs)

    return run


def kernel(body, ins, in_specs, outs, out_specs, us, name, scratch=(), first=(), grid=(), talk=None, aliases=None, staged=()):
    extra = len(first)
    in_specs, scratch = list(in_specs), list(scratch)
    if staged:
        body = staged_body(body, len(ins), staged)
        for i in staged:
            in_specs[i] = ANY
            scratch.append(pltpu.VMEM(ins[i].shape, ins[i].dtype))
        scratch += sems(len(staged))
    return pl.pallas_call(
        without(body, len(ins), extra),
        grid=grid,
        in_specs=in_specs + [ANY] * extra,
        out_specs=out_specs,
        out_shape=outs,
        scratch_shapes=scratch,
        input_output_aliases=aliases or {},
        compiler_params=pltpu.CompilerParams(
            vmem_limit_bytes=VMEM_BYTES, collective_id=talk, has_side_effects=talk is not None
        ),
        cost_estimate=cost(us),
        name=name,
    )(*ins, *first)


def sems(*counts):
    return [pltpu.SemaphoreType.DMA((k,)) for k in counts]


def shaped(shape, dtype=BF):
    return jax.ShapeDtypeStruct(tuple(shape), dtype)


class Place:
    def __init__(self):
        self.y = lax.axis_index("y")
        self.n = lax.axis_index("n")
        self.x = self.n // 2
        self.c = self.n % 2
        self.ns = self.n + 1 - 2 * self.c
        self.nx = (self.n + 2) % 4
        self.nd = (self.ns + 2) % 4
        self.sib = {"n": self.ns}
        self.xn = {"n": self.nx}
        self.yn = {"y": 1 - self.y}
        self.xs = {"n": self.nd}


def meet(devices):
    barrier = pltpu.get_barrier_semaphore()
    for d in devices:
        pl.semaphore_signal(barrier, inc=1, device_id=d, device_id_type=MESH)
    pl.semaphore_wait(barrier, len(devices))


class Wire:
    def __init__(self, send_sems, recv_sems, first=0):
        self.ss, self.rs, self.at, self.sent = send_sems, recv_sems, first, []

    def make(self, src, dst, device, keep=True, again=False):
        self.at += not again
        k = self.at - 1
        copy = pltpu.make_async_remote_copy(
            src_ref=src, dst_ref=dst, send_sem=self.ss.at[k], recv_sem=self.rs.at[k],
            device_id=device, device_id_type=MESH,
        )
        if keep:
            self.sent.append(copy)
        return copy

    def finish(self):
        for copy in self.sent:
            copy.wait_send()


SPREAD = 9


class Spread:
    def __init__(self, wire, at, src, slot):
        y, n, nx = at.y, at.n, at.nx
        self.first = [
            wire.make(src, slot(y, n, None), at.xn),
            wire.make(src, slot(y, n, None), at.yn),
            wire.make(src, slot(y, n, None), at.sib),
        ]
        self.on_x = [
            wire.make(slot(y, nx, 0), slot(y, nx, 0), at.yn),
            wire.make(slot(y, nx, None), slot(y, nx, None), at.sib),
        ]
        self.on_y = [
            wire.make(slot(1 - y, n, 1), slot(1 - y, n, 1), at.xn),
            wire.make(slot(1 - y, n, None), slot(1 - y, n, None), at.sib),
        ]
        self.last = [
            wire.make(slot(1 - y, nx, 0), slot(1 - y, nx, 0), at.sib),
            wire.make(slot(1 - y, nx, 1), slot(1 - y, nx, 1), at.sib),
        ]

    def begin(self):
        for copy in self.first:
            copy.start()

    def forward(self):
        self.first[0].wait_recv()
        for copy in self.on_x:
            copy.start()
        self.first[1].wait_recv()
        for copy in self.on_y:
            copy.start()

    def forward_last(self):
        self.on_x[0].wait_recv()
        self.last[0].start()
        self.on_y[0].wait_recv()
        self.last[1].start()

    def end(self):
        self.first[2].wait_recv()
        self.on_x[1].wait_recv()
        self.on_y[1].wait_recv()
        self.last[0].wait_recv()
        self.last[1].wait_recv()


REDUCE = 10


def reduce_scratch(micro, tok, sub, width):
    half = sub // 2
    return [
        pltpu.VMEM((micro, 2, tok, width), BF),
        pltpu.VMEM((micro, 2, 2, sub, width), BF),
        pltpu.VMEM((micro, sub, width), BF),
        pltpu.VMEM((micro, sub, width), BF),
        pltpu.VMEM((micro, sub, width), BF),
        pltpu.VMEM((micro, 2, half, width), BF),
        pltpu.VMEM((micro, sub, width), BF),
        pltpu.VMEM((micro, sub, width), BF),
    ]


class Reduce:
    def __init__(self, wire, at, scratch, compute):
        self.part, self.ra, self.sb, self.sx, self.sy, self.rb, self.rcx, self.rcy = scratch
        self.wire, self.at, self.compute = wire, at, compute
        self.micro, self.sub = self.sb.shape[0], self.sb.shape[1]
        self.a, self.b, self.d = {}, {}, {}
        self.released = False

    def rows(self, core, xx, lo=0, size=None):
        return pl.ds(pl.multiple_of((2 * xx + core) * self.sub, self.sub) + lo, size or self.sub)

    def summed(self, m, yy, xx, lo, size):
        mine = self.part[m, yy, self.rows(self.at.c, xx, lo, size), :].astype(F32)
        return mine + self.ra[m, yy, xx, lo : lo + size, :].astype(F32)

    def cores(self, m):
        at = self.at
        for yk, yy in ((1, 1 - at.y), (0, at.y)):
            self.compute(m, yy)
            for xk, xx in ((1, 1 - at.x), (0, at.x)):
                copy = self.wire.make(self.part.at[m, yy, self.rows(1 - at.c, xx)], self.ra.at[m, yy, xx], at.sib)
                copy.start()
                self.a[m, yk, xk] = copy

    def diagonal(self, m):
        at, sub, half = self.at, self.sub, self.sub // 2
        self.a[m, 1, 1].wait_recv()
        self.sb[m] = self.summed(m, 1 - at.y, 1 - at.x, 0, sub).astype(BF)
        self.b[m, 0] = self.wire.make(self.sb.at[m, 0:half], self.rb.at[m, 0], at.xn)
        self.b[m, 1] = self.wire.make(self.sb.at[m, half:sub], self.rb.at[m, 1], at.yn)
        self.b[m, 0].start()
        self.b[m, 1].start()

    def sides(self, m):
        at, sub, half = self.at, self.sub, self.sub // 2
        sx, sy, rb, rcx, rcy = self.sx, self.sy, self.rb, self.rcx, self.rcy
        self.a[m, 1, 0].wait_recv()
        sy[m, half:sub] = self.summed(m, 1 - at.y, at.x, half, half).astype(BF)
        self.d[m, 0] = self.wire.make(sy.at[m, half:sub], rcy.at[m, half:sub], at.yn)
        self.d[m, 0].start()
        self.a[m, 0, 1].wait_recv()
        sx[m, 0:half] = self.summed(m, at.y, 1 - at.x, 0, half).astype(BF)
        self.d[m, 1] = self.wire.make(sx.at[m, 0:half], rcx.at[m, 0:half], at.xn)
        self.d[m, 1].start()
        self.b[m, 0].wait_recv()
        sy[m, 0:half] = (self.summed(m, 1 - at.y, at.x, 0, half) + rb[m, 0].astype(F32)).astype(BF)
        self.d[m, 2] = self.wire.make(sy.at[m, 0:half], rcy.at[m, 0:half], at.yn)
        self.d[m, 2].start()
        self.b[m, 1].wait_recv()
        sx[m, half:sub] = (self.summed(m, at.y, 1 - at.x, half, half) + rb[m, 1].astype(F32)).astype(BF)
        self.d[m, 3] = self.wire.make(sx.at[m, half:sub], rcx.at[m, half:sub], at.xn)
        self.d[m, 3].start()

    def release(self, m):
        at = self.at
        self.a[m, 0, 0].wait_recv()
        self.ra[m, at.y, at.x] = self.summed(m, at.y, at.x, 0, self.sub).astype(BF)
        for yk in (1, 0):
            for xk in (1, 0):
                copy = self.a[m, yk, xk]
                copy.wait_send()
                self.wire.sent = [other for other in self.wire.sent if other is not copy]
        self.released = True

    def arrived(self, m):
        if not self.released:
            self.a[m, 0, 0].wait_recv()
        for k in range(4):
            self.d[m, k].wait_recv()

    def total(self, m, lo, size):
        if self.released:
            own = self.ra[m, self.at.y, self.at.x, lo : lo + size, :].astype(F32)
        else:
            own = self.summed(m, self.at.y, self.at.x, lo, size)
        return own + self.rcx[m, lo : lo + size, :].astype(F32) + self.rcy[m, lo : lo + size, :].astype(F32)


def nothing():
    pass


def reduce_rows(wire, at, scratch, compute, finish, tick=nothing):
    red = Reduce(wire, at, scratch, compute)
    for m in range(red.micro):
        red.cores(m)
        red.diagonal(m)
    tick()
    for m in range(red.micro):
        red.sides(m)
    for m in range(red.micro):
        red.arrived(m)
        finish(m, lambda lo, size, m=m: red.total(m, lo, size))
        tick()


LINE = (
    (0, 3, 1, -1, 0),
    (3, 0, 2, -1, 0),
    (1, 0, 0, 2, 0),
    (2, 3, 3, 2, 0),
    (1, 2, 2, 2, 0),
    (2, 1, 1, 2, 0),
    (0, 2, 2, 0, 1),
    (3, 1, 1, 0, 1),
    (0, 1, 1, 1, 1),
    (3, 2, 2, 1, 1),
)


def chain_results(zn, parts, rows, cols):
    count = 2 * len(parts) if zn == 4 else (zn - 1 if 0 in parts else 0)
    return [shaped((rows, cols))] * count


def chain_links(zn, parts):
    return sum(t[4] in parts for t in LINE) + (1 in parts) if zn == 4 else (zn - 1 if 0 in parts else 0)


class Chain:
    def __init__(self, wire, zn, parts, g, first, second, bufs, load, k):
        z = lax.axis_index("z")
        rows, cols = (first or second)[0].shape
        self.moves, self.bufs, self.cols, self.joins = [], bufs, cols, zn == 4 and 1 in parts
        self.over = False

        def group(i):
            return g.at[pl.ds(pl.multiple_of(i * rows, rows), rows)]

        if zn == 4:
            places = {2: first[0], -1: first[1]}
            if second:
                places.update({0: second[0], 1: second[1]})
            for src, i, dst, place, part in LINE:
                if part in parts:
                    copy = wire.make(group(i), places[place], {"z": dst}, keep=False)
                    self.moves.append((z == src, z == dst, copy, place < 0))
        elif 0 in parts:
            for dz in range(1, zn):
                to = (z + dz) % zn
                self.moves.append((None, None, wire.make(group(to), first[dz - 1], {"z": to}, keep=False), False))
        if self.joins:
            far = 3 * (1 - z // 2)
            here, there = bufs.at[0, :, pl.ds(0, cols)], bufs.at[1, :, pl.ds(0, cols)]
            self.own = pltpu.make_async_copy(group(far), here, load.at[k])
            self.came = pltpu.make_async_copy(first[1], there, load.at[k + 1])
            self.on = wire.make(here, second[1], {"z": far}, keep=False)
            self.inner = jnp.logical_and(z >= 1, z <= 2)
            self.outer = jnp.logical_not(self.inner)

    def begin(self):
        for sends, _, copy, _ in self.moves:
            if sends is None:
                copy.start()
            else:
                pl.when(sends)(copy.start)

    def join(self):
        if not self.joins:
            return

        def run():
            self.own.start()
            self.came.start()
            self.own.wait()
            self.came.wait()
            cols = pl.ds(0, self.cols)
            both = self.bufs[0, :, cols].astype(F32) + self.bufs[1, :, cols].astype(F32)
            self.bufs[0, :, cols] = both.astype(BF)
            self.on.start()

        for _, gets, copy, middle in self.moves:
            if middle:
                pl.when(gets)(copy.wait_recv)
        pl.when(self.inner)(run)

    def settle_sent(self):
        if self.joins:
            pl.when(self.inner)(self.on.wait_send)

    def wait(self):
        self.over = True
        for sends, gets, copy, middle in self.moves:
            if sends is None:
                copy.wait_recv()
                copy.wait_send()
                continue
            if not (middle and self.joins):
                pl.when(gets)(copy.wait_recv)
            pl.when(sends)(copy.wait_send)
        if self.joins:
            pl.when(self.outer)(self.on.wait_recv)


class Host:
    def __init__(self, chains):
        self.chains, self.todo, self.last = chains, list(chains), None

    def begin(self, which=None):
        for k, chain in enumerate(self.chains):
            if which is None or k == which:
                chain.begin()

    def next(self):
        if self.todo:
            if self.last is not None:
                self.last.settle_sent()
            self.last = self.todo.pop(0)
            self.last.join()

    def end(self):
        while self.todo:
            self.next()
        self.last.settle_sent()
        for chain in self.chains:
            if not chain.over:
                chain.wait()


class Settle:
    def __init__(self, wire, at, zn, g, first, second, keep, theirs, bufs, load):
        z = lax.axis_index("z")
        self.rows, self.cols = keep.shape[0] * 2, keep.shape[1]
        rows, half = self.rows, keep.shape[0]
        came = [first[0], second[1], second[0]] if zn == 4 else list(first)
        self.bufs, self.partly = bufs, jnp.logical_and(z >= 1, z <= 2) if zn == 4 else None
        mine = g.at[pl.ds(pl.multiple_of(z * rows, rows), rows)]
        self.loads = [pltpu.make_async_copy(src, bufs.at[k], load.at[k]) for k, src in enumerate([mine] + came)]

        def part(i):
            return bufs.at[0, pl.ds(pl.multiple_of(i * half, half), half)]

        self.away = wire.make(part(1 - at.y), theirs, at.yn, keep=False)
        self.here = pltpu.make_async_copy(part(at.y), keep, load.at[len(self.loads)])

    def go(self):
        always = self.loads if self.partly is None else self.loads[:-1]
        for copy in always:
            copy.start()
        if self.partly is not None:
            k = len(always)
            pl.when(self.partly)(self.loads[k].start)
            pl.when(self.partly)(self.loads[k].wait)

            def none():
                self.bufs[k] = jnp.zeros((self.rows, self.cols), BF)

            pl.when(jnp.logical_not(self.partly))(none)
        for copy in always:
            copy.wait()
        total = self.bufs[0].astype(F32)
        for k in range(1, len(self.loads)):
            total = total + self.bufs[k].astype(F32)
        self.bufs[0] = total.astype(BF)
        self.away.start()
        self.here.start()

    def wait(self):
        self.away.wait_recv()
        self.away.wait_send()
        self.here.wait()


def settle_scratch(zn, rows, cols):
    return [pltpu.VMEM((zn, rows, cols), BF)] + sems(zn + 1)


def z_partners(zn):
    z = lax.axis_index("z")
    return [{"z": (z + dz) % zn} for dz in range(1, zn)]


class Jobs:
    def __init__(self, plan, zn):
        self.plan, self.zn = plan, zn
        self.ins, self.outs, self.links = [], [], 0
        for g, parts, given in plan:
            self.ins += [g] + list(given)
            self.outs += chain_results(zn, parts, g.shape[0] // zn, g.shape[1])
            self.links += chain_links(zn, parts)
        wide = max([p[0].shape[1] for p in plan], default=0)
        rows = plan[0][0].shape[0] // zn if plan else 0
        self.scratch = [pltpu.VMEM((2, rows, wide), BF)] + sems(2 * len(plan)) if plan else []

    def host(self, wire, ins, outs, scratch):
        chains, i, o = [], 0, 0
        for k, (g, parts, given) in enumerate(self.plan):
            count = len(chain_results(self.zn, parts, 8, 128))
            made = outs[o : o + count]
            first = ins[i + 1 : i + 1 + len(given)] if given else (made if 1 not in parts or self.zn != 4 else made[:2])
            second = [] if 1 not in parts or self.zn != 4 else made[-2:]
            chains.append(Chain(wire, self.zn, parts, ins[i], first, second, *scratch, 2 * k))
            i, o = i + 1 + len(given), o + count
        return Host(chains)


def blockwise(part, m, yy, fn, tile=256):
    tok = part.shape[2]

    def step(i, carry):
        lo = pl.multiple_of(i * tile, tile)
        fn(lo, tile)
        return carry

    lax.fori_loop(0, tok // tile, step, 0)


def token_spreads(wire, at, src, out, sem, first, cut):
    micro, tok, feat = src.shape
    spreads, local = [], []
    for m in range(micro):

        def slot(yy, nn, part, m=m):
            lo, size = {None: (0, tok), 0: (0, cut), 1: (cut, tok - cut)}[part]
            return out.at[m, yy, pl.ds(lo, size), pl.ds(pl.multiple_of(nn * feat, feat), feat)]

        spreads.append(Spread(wire, at, src.at[m], slot))
        local.append(pltpu.make_async_copy(src.at[m], slot(at.y, at.n, None), sem.at[first + m]))
    return spreads, local


def attn_cut(w_qkv, w_out, i, buf):
    parts, _, cols = w_qkv.shape
    half = cols // 2
    at = pl.ds(pl.multiple_of(i * half, half), half)
    for p in range(parts):
        buf[:, p * half : (p + 1) * half] = w_qkv[p, :, at]
    buf[:, parts * half :] = w_out[at, :].astype(F32).T.astype(BF)


def chunk_cut(w_gu, w_down, i, c, one, buf):
    half = w_gu.shape[2] // 2
    at = pl.ds(pl.multiple_of(i * half, half) + c * one, one)
    buf[:, :one] = w_gu[0, :, at]
    buf[:, one : 2 * one] = w_gu[1, :, at]
    buf[:, 2 * one :] = w_down[at, :].astype(F32).T.astype(BF)


class Swap:
    def __init__(self, wire, at, bufs, out, sem):
        depth = bufs.shape[1]
        place = out.at[pl.ds(pl.multiple_of(at.y * depth, depth), depth)]
        self.away = wire.make(bufs.at[0], place, at.yn)
        self.here = pltpu.make_async_copy(bufs.at[1], place, sem)

    def end(self):
        self.away.wait_recv()
        self.here.wait()


def swap_attn_kernel(w_qkv, w_out, out, bufs, ss, rs, ls):
    at = Place()
    meet([at.yn])
    wire = Wire(ss, rs)
    swap = Swap(wire, at, bufs, out, ls.at[0])
    attn_cut(w_qkv, w_out, 1 - at.y, bufs.at[0])
    swap.away.start()
    attn_cut(w_qkv, w_out, at.y, bufs.at[1])
    swap.here.start()
    swap.end()
    wire.finish()


def swap_attn(w_qkv, w_out):
    parts, depth, cols = w_qkv.shape
    size = (parts + 1) * cols // 2
    return kernel(
        swap_attn_kernel, (w_qkv, w_out), [VMEM, VMEM], shaped((2 * depth, size)), ANY, 14, "swap_attn",
        [pltpu.VMEM((2, depth, size), BF)] + sems(1, 1, 1), talk=6,
    )


def swap_chunks(wire, at, w_gu, w_down, which, one, bufs, outs, ls):
    swaps = []
    for k, (c, out) in enumerate(zip(which, outs)):
        swap = Swap(wire, at, bufs.at[k], out, ls.at[k])
        chunk_cut(w_gu, w_down, 1 - at.y, c, one, bufs.at[k, 0])
        swap.away.start()
        chunk_cut(w_gu, w_down, at.y, c, one, bufs.at[k, 1])
        swap.here.start()
        swaps.append(swap)
    return swaps


def gather_x_kernel(zn, which, count, x_in, v_in, lens, freq, w_gu, w_down, x_out, v_out, lens_all, cos, sin, own, *scratch):
    bufs, ss, rs, ls = scratch
    at = Place()
    z = lax.axis_index("z")
    one = own.shape[2] // 3
    ring = [(dz, dy) for dz in range(zn) for dy in range(2) if dz or dy]
    others = [{"z": (z + dz) % zn, "y": (at.y + dy) % 2} for dz, dy in ring]
    meet([at.sib, at.xn] + others)
    wire = Wire(ss, rs)
    there = wire.make(lens, lens_all.at[at.y], at.yn)
    there.start()
    spreads, local = token_spreads(wire, at, x_in, x_out, ls, len(which) + 1, x_in.shape[1] // 8)
    local.append(pltpu.make_async_copy(v_in, v_out.at[z, at.y], ls.at[len(which)]))
    small = [wire.make(v_in, v_out.at[z, at.y], d) for d in others]
    for s in spreads:
        s.begin()
    for copy in small + local:
        copy.start()
    swaps = swap_chunks(wire, at, w_gu, w_down, which, one, bufs, [own.at[k] for k in range(len(which))], ls)
    lens_all[at.y] = lens[...]
    there.wait_recv()
    tok = x_in.shape[1]
    row = lax.broadcasted_iota(jnp.int32, (tok, 1), 0)
    flip = jnp.where(lax.broadcasted_iota(jnp.int32, (1, HEAD_DIM), 1) < HEAD_DIM // 2, -1.0, 1.0)

    def table(b, carry):
        m, yy = b // 2, b % 2
        line = lens_all[yy, pl.ds(m, 1), :]
        end = jnp.zeros((1, 1), jnp.int32)
        start = jnp.zeros_like(row)
        for k in range(count):
            end = end + line[:, k : k + 1]
            start = jnp.where(row >= end, end, start)
        angle = (row - start).astype(F32) * freq[...]
        place = pl.ds(pl.multiple_of(b * tok, tok), tok)
        cos[place, :] = jnp.cos(angle)
        sin[place, :] = jnp.sin(angle) * flip
        return carry

    lax.fori_loop(0, x_in.shape[0] * 2, table, 0)
    run_spreads(spreads, local)
    for copy in small:
        copy.wait_recv()
    for swap in swaps:
        swap.end()
    wire.finish()


def gather_x(x, v, lens, freq, w_gu, w_down, zn, which, one, count, first):
    micro, tok, feat = x.shape
    depth = w_gu.shape[1]
    rows = micro * 2 * tok
    links = SPREAD * micro + 2 * zn - 1 + len(which) + 1
    return kernel(
        functools.partial(gather_x_kernel, zn, which, count), (x, v, lens, freq, w_gu, w_down),
        [ANY, ANY, VMEM, VMEM, VMEM, VMEM],
        (
            shaped((micro, 2, tok, 4 * feat)), shaped((zn, 2) + v.shape, F32), shaped((2,) + lens.shape, jnp.int32),
            shaped((rows, HEAD_DIM), F32), shaped((rows, HEAD_DIM), F32), shaped((len(which), 2 * depth, 3 * one)),
        ),
        (ANY, ANY, VMEM, VMEM, VMEM, ANY), 48, "gather_x",
        [pltpu.VMEM((len(which), 2, depth, 3 * one), BF)] + sems(links, links, micro + 1 + len(which)),
        first, talk=0,
    )


def gather_d_kernel(which, one, d_in, x_all, gain, shift, w_gu, w_down, d_out, n1, *refs):
    outs, (bufs, xin, nout, ss, rs, ls, load) = refs[: len(which)], refs[len(which) :]
    at = Place()
    micro, _, tok, _ = x_all.shape
    meet([at.sib, at.xn, at.yn])
    wire = Wire(ss, rs)
    spreads, local = token_spreads(wire, at, d_in, d_out, ls, len(which), d_in.shape[1] // 16 * 5)

    def bring(b):
        return pltpu.make_async_copy(x_all.at[b // 2, b % 2], xin.at[b % 2], load.at[b])

    def put(b):
        return pltpu.make_async_copy(nout.at[b % 2], n1.at[pl.ds(b * tok, tok)], load.at[2 * micro + b])

    bring(0).start()
    bring(1).start()
    for s in spreads:
        s.begin()
    for copy in local:
        copy.start()
    swaps = swap_chunks(wire, at, w_gu, w_down, which, one, bufs, outs, ls)
    for b in range(2 * micro):
        bring(b).wait()
        if b >= 2:
            put(b - 2).wait()

        def tile(i, carry, b=b):
            place = pl.ds(pl.multiple_of(i * 128, 128), 128)
            xhat, _ = normalise(xin[b % 2, place, :].astype(F32))
            nout[b % 2, place, :] = (xhat * gain[...] + shift[...]).astype(BF)
            return carry

        lax.fori_loop(0, tok // 128, tile, 0)
        put(b).start()
        if b + 2 < 2 * micro:
            bring(b + 2).start()
        if b % 2:
            spreads[b // 2].forward()
    put(2 * micro - 2).wait()
    put(2 * micro - 1).wait()
    for s in spreads:
        s.forward_last()
    for s in spreads:
        s.end()
    for copy in local:
        copy.wait()
    for swap in swaps:
        swap.end()
    wire.finish()


def gather_d(d, x_all, gain, shift, w_gu, w_down, which, one):
    micro, tok, feat = d.shape
    depth = w_gu.shape[1]
    count = SPREAD * micro + len(which)
    return kernel(
        functools.partial(gather_d_kernel, which, one), (d, x_all, gain, shift, w_gu, w_down),
        [ANY, ANY, VMEM, VMEM, VMEM, VMEM],
        (shaped((micro, 2, tok, 4 * feat)), shaped((micro * 2 * tok, 4 * feat))) + (shaped((2 * depth, 3 * one)),) * len(which),
        (ANY,) * (2 + len(which)), 48, "gather_d",
        [pltpu.VMEM((len(which), 2, depth, 3 * one), BF)] + [pltpu.VMEM((2, tok, 4 * feat), BF)] * 2
        + sems(count, count, micro + len(which), 4 * micro),
        talk=5,
    )


def row_slot(out, m, sub):
    half = sub // 2

    def slot(yy, nn, part):
        ref = out.at[m, yy, nn]
        return ref if part is None else ref.at[pl.ds(part * half, half)]

    return slot


def run_spreads(spreads, local, tick=nothing):
    for s in spreads:
        s.forward()
    tick()
    for s in spreads:
        s.forward_last()
    for s in spreads:
        s.end()
    for copy in local:
        copy.wait()


def attn_out_kernel(att, wo, x_all, gain, shift, middle, n2, *scratch):
    *red, xb, nb, ss, rs, ls = scratch
    at = Place()
    micro, sub, width = middle.shape
    zn, dz, cols = wo.shape
    span = att.shape[1]
    tok = red[0].shape[2]
    meet([at.sib, at.xn, at.yn])
    wire = Wire(ss, rs)
    own = [pltpu.make_async_copy(x_all.at[m, at.y, pl.ds(at.n * sub, sub)], xb.at[m], ls.at[m]) for m in range(micro)]
    for copy in own:
        copy.start()

    def compute(m, yy):
        def tile(lo, size):
            a = att[pl.ds(pl.multiple_of((m * 2 + yy) * tok, tok) + lo, size), :]
            for k in range(zn):
                red[0][m, yy, pl.ds(lo, size), k * dz : (k + 1) * dz] = dot_nt(a, wo[k, :, cols - span :]).astype(BF)

        blockwise(red[0], m, yy, tile)

    spreads, local = [], []

    def finish(m, total):
        own[m].wait()
        step = sub // 2
        for lo in range(0, sub, step):
            mid = xb[m, lo : lo + step, :].astype(F32) + total(lo, step)
            middle[m, lo : lo + step, :] = mid
            xhat, _ = normalise(mid)
            nb[m, lo : lo + step, :] = (xhat * gain[...] + shift[...]).astype(BF)
        slot = row_slot(n2, m, sub)
        spreads.append(Spread(wire, at, nb.at[m], slot))
        spreads[-1].begin()
        local.append(pltpu.make_async_copy(nb.at[m], slot(at.y, at.n, None), ls.at[micro + m]))
        local[-1].start()

    reduce_rows(wire, at, red, compute, finish)
    run_spreads(spreads, local)
    wire.finish()


def attn_out(att, wo, x_all, gain, shift):
    micro, _, tok, width = x_all.shape
    sub = tok // 4
    count = (REDUCE + SPREAD) * micro
    return kernel(
        attn_out_kernel, (att, wo, x_all, gain, shift), [VMEM, VMEM, ANY, VMEM, VMEM],
        (shaped((micro, sub, width), F32), shaped((micro, 2, 4, sub, width))), (VMEM, ANY), 85, "attn_out",
        reduce_scratch(micro, tok, sub, width) + [pltpu.VMEM((micro, sub, width), BF)] * 2 + sems(count, count, 2 * micro),
        talk=1,
    )


def nt_compute(part, lows, ws, first, each=0):
    zn, dz, _ = ws[0].shape
    tok = part.shape[2]
    span = lows[0].shape[1]

    def compute(m, yy):
        def tile(lo, size):
            at = pl.multiple_of((m * 2 + yy) * tok, tok) + lo
            for k in range(zn):
                acc = None
                for i, (low, w) in enumerate(zip(lows, ws)):
                    lo_col = first + i * each
                    term = dot_nt(low[pl.ds(at, size), :], w[k, :, lo_col : lo_col + span])
                    acc = term if acc is None else acc + term
                part[m, yy, pl.ds(lo, size), k * dz : (k + 1) * dz] = acc.astype(BF)

        blockwise(part, m, yy, tile)

    return compute


class Columns:
    def __init__(self, groups, cols, bufs, load):
        self.copies = [
            pltpu.make_async_copy(src.at[:, :, cols], bufs.at[k], load.at[k]) for k, src in enumerate(groups)
        ]
        for copy in self.copies:
            copy.start()

    def wait(self):
        for copy in self.copies:
            copy.wait()


def chunk_refs(pair, last):
    return [pair.at[:, k] for k in range(pair.shape[1])] + [last]


def ffn_back_kernel(jobs, parts, ready, *refs):
    guls = refs[:parts]
    pair, last, d_all, middle, gain, *refs = refs[parts:]
    zin, (mid_grad, branch, vec), refs = refs[: len(jobs.ins)], refs[len(jobs.ins) :][:3], refs[len(jobs.ins) + 3 :]
    zout, refs = refs[: len(jobs.outs)], refs[len(jobs.outs) :]
    *red, db, nb, wv, ss, rs, ls, lw, zb, zl = refs
    at = Place()
    micro, sub, width = middle.shape
    span = guls[0].shape[1]
    weights = Columns(chunk_refs(pair, last), pl.ds(0, span), wv, lw)
    own = [pltpu.make_async_copy(d_all.at[m, at.y, pl.ds(at.n * sub, sub)], db.at[m], ls.at[m]) for m in range(micro)]
    for copy in own:
        copy.start()
    meet([at.sib, at.xn, at.yn] + z_partners(jobs.zn))
    wire = Wire(ss, rs)
    host = jobs.host(wire, zin, zout, (zb, zl))
    host.begin()
    vec[...] = jnp.zeros_like(vec)
    spreads, local = [], []

    def finish(m, total):
        own[m].wait()
        step = sub // 2
        for lo in range(0, sub, step):
            grad = total(lo, step)
            xhat, rstd = normalise(middle[m, lo : lo + step, :])
            vec[0:1, :] += jnp.sum(grad * xhat, axis=0, keepdims=True)
            vec[1:2, :] += jnp.sum(grad, axis=0, keepdims=True)
            mg = db[m, lo : lo + step, :].astype(F32) + norm_back(xhat, rstd, grad, gain[...])
            mid_grad[m, lo : lo + step, :] = mg
            nb[m, lo : lo + step, :] = mg.astype(BF)
        slot = row_slot(branch, m, sub)
        spreads.append(Spread(wire, at, nb.at[m], slot))
        spreads[-1].begin()
        local.append(pltpu.make_async_copy(nb.at[m], slot(at.y, at.n, None), ls.at[micro + m]))
        local[-1].start()

    weights.wait()
    ready()
    reduce_rows(wire, at, red, nt_compute(red[0], guls, [wv.at[k] for k in range(parts)], 0), finish, host.next)
    run_spreads(spreads, local, host.next)
    host.end()
    wire.finish()


def ffn_back(guls, pair, last, d_all, middle, gain, plan, zn, first):
    parts = len(guls)
    micro, _, tok, width = d_all.shape
    sub = tok // 4
    jobs = Jobs(plan, zn)
    count = (REDUCE + SPREAD) * micro + jobs.links
    span = guls[0].shape[1]
    return kernel(
        functools.partial(ffn_back_kernel, jobs, parts), (*guls, pair, last, d_all, middle, gain, *jobs.ins),
        [VMEM] * parts + [ANY, ANY, ANY, VMEM, VMEM] + [ANY] * len(jobs.ins),
        (shaped((micro, sub, width), F32), shaped((micro, 2, 4, sub, width)), shaped((8, width), F32), *jobs.outs),
        (VMEM, ANY, VMEM) + (ANY,) * len(jobs.outs), 90, "ffn_back",
        reduce_scratch(micro, tok, sub, width) + [pltpu.VMEM((micro, sub, width), BF)] * 2
        + [pltpu.VMEM((parts, zn, width // zn, span), BF)] + sems(count, count, 2 * micro, parts) + jobs.scratch,
        first, talk=2, staged=(*range(parts), parts + 3),
    )


def host_kernel(jobs, *refs):
    zin, zout, (ss, rs, zb, zl) = refs[: len(jobs.ins)], refs[len(jobs.ins) :][: len(jobs.outs)], refs[-4:]
    meet(z_partners(jobs.zn))
    host = jobs.host(Wire(ss, rs), zin, zout, (zb, zl))
    host.begin()
    host.end()


def host_only(plan, zn, first):
    jobs = Jobs(plan, zn)
    return kernel(
        functools.partial(host_kernel, jobs), jobs.ins, [ANY] * len(jobs.ins), tuple(jobs.outs), (ANY,) * len(jobs.outs),
        20 * jobs.steps, "along_z", sems(2 * jobs.steps, 2 * jobs.steps) + jobs.scratch, first, talk=8,
    )


class Deal:
    def __init__(self, wire, at, rows, out, m, sems, k):
        sub, width = rows.shape[1], rows.shape[2]
        feat = width // 4

        def cols(nn):
            return rows.at[m, :, pl.ds(pl.multiple_of(nn * feat, feat), feat)]

        place = out.at[m, pl.ds(pl.multiple_of(at.n * sub, sub), sub)]
        self.local = pltpu.make_async_copy(cols(at.n), place, sems.at[k])
        self.copies = [
            wire.make(cols(at.nx), place, at.xn),
            wire.make(cols(at.nd), place, at.xs),
            wire.make(cols(at.ns), place, at.sib),
        ]

    def begin(self):
        for copy in self.copies:
            copy.start()
        self.local.start()

    def end(self):
        for copy in self.copies:
            copy.wait_recv()
        self.local.wait()


def last_kernel(jobs, zn, marks, ready, *refs):
    low, wa, x_all, mid_grad, gain, vec2, *refs = refs
    g2, came2, refs = refs[0], refs[1 : 1 + marks], refs[1 + marks :]
    zin, refs = refs[: len(jobs.ins)], refs[len(jobs.ins) :]
    in_grad, sums, *refs = refs
    settled, zout, refs = refs[:6], refs[6:][: len(jobs.outs)], refs[6 + len(jobs.outs) :]
    red, refs = refs[:8], refs[8:]
    xb, ob, w1, mine, plane, summed, lines, yb2, ybo, ybq, yl2, ylo, ylq, ss, rs, ls, *talk = refs
    at = Place()
    z = lax.axis_index("z")
    micro, sub, width = mid_grad.shape
    qkv = pltpu.make_async_copy(wa.at[:, :, pl.ds(0, low.shape[1])], w1, ls.at[2 * micro])
    qkv.start()
    own = [pltpu.make_async_copy(x_all.at[m, at.y, pl.ds(at.n * sub, sub)], xb.at[m], ls.at[m]) for m in range(micro)]
    for copy in own:
        copy.start()
    flips = [(dy, dn) for dy in range(2) for dn in range(4) if dy or dn]
    peers = [{"y": (at.y + dy) % 2, "n": (at.n + dn) % 4} for dy, dn in flips]
    along = [{"z": (z + dz) % zn} for dz in range(1, zn)]
    meet(peers + along)
    wire = Wire(ss, rs)
    host = jobs.host(wire, zin, zout, talk)
    host.begin()
    split = len(chain_results(zn, (0,), 8, 128))
    settles = [
        Settle(wire, at, zn, g2, came2[:split], came2[split:], settled[0], settled[1], yb2, yl2),
        Settle(wire, at, zn, zin[1], zin[2:], zout[marks:], settled[2], settled[3], ybo, ylo),
        Settle(wire, at, zn, zin[0], zout[:split], zout[split:marks], settled[4], settled[5], ybq, ylq),
    ]
    mine[...] = jnp.zeros_like(mine)
    mine[2:4] = vec2[0:2]
    qkv.wait()
    ready()
    total = Reduce(wire, at, red, nt_compute(red[0], [low], [w1], 0))
    for m in range(micro):
        total.cores(m)
        total.diagonal(m)
    for m in range(micro):
        total.sides(m)
    host.next()
    step = sub // 2
    deals = []
    for m in range(micro):
        total.arrived(m)
        own[m].wait()
        for lo in range(0, sub, step):
            grad = total.total(m, lo, step)
            xhat, rstd = normalise(xb[m, lo : lo + step, :].astype(F32))
            mine[0:1, :] += jnp.sum(grad * xhat, axis=0, keepdims=True)
            mine[1:2, :] += jnp.sum(grad, axis=0, keepdims=True)
            back = norm_back(xhat, rstd, grad, gain[...])
            ob[m, lo : lo + step, :] = (mid_grad[m, lo : lo + step, :] + back).astype(BF)
        deals.append(Deal(wire, at, ob, in_grad, m, ls, micro + m))
        deals[-1].begin()
        if m == 0:
            settles[0].go()
    near = [wire.make(mine, plane.at[k], d) for k, d in enumerate(peers)]
    for copy in near:
        copy.start()
    for copy in near:
        copy.wait_recv()
    both = mine[...]
    for k in range(len(peers)):
        both = both + plane[k]
    summed[...] = both
    far = [wire.make(summed, lines.at[k], d) for k, d in enumerate(along)]
    for copy in far:
        copy.start()
    host.next()
    host.chains[0].wait()
    settles[2].go()
    host.end()
    settles[1].go()
    for copy in far:
        copy.wait_recv()
    both = summed[...]
    for k in range(len(along)):
        both = both + lines[k]
    sums[...] = both
    for deal in deals:
        deal.end()
    for settle in settles:
        settle.wait()
    wire.finish()


def last_sums(low, wa, x_all, mid_grad, gain, vec2, g2, got2, out_g, gout, qkv_g, zn):
    micro, _, tok, width = x_all.shape
    sub = tok // 4
    dz, cols = width // zn, low.shape[1]
    jobs = Jobs([(qkv_g, (0, 1), ()), (out_g, (1,), gout)], zn)
    count = (REDUCE + 3) * micro + 7 + zn - 1 + jobs.links + 3
    size = vec2.shape
    rows = pltpu.VMEM((micro, sub, width), BF)
    sizes = (g2.shape[1], out_g.shape[1], cols)
    halves = [shaped((dz // 2, k)) for k in sizes for _ in range(2)]
    return kernel(
        functools.partial(last_kernel, jobs, zn, len(got2)),
        (low, wa, x_all, mid_grad, gain, vec2, g2, *got2, *jobs.ins),
        [VMEM, ANY, ANY, VMEM, VMEM, VMEM] + [ANY] * (1 + len(got2) + len(jobs.ins)),
        (shaped((micro, tok, width // 4)), shaped(size, F32), *halves, *jobs.outs),
        (ANY, VMEM) + (ANY,) * (6 + len(jobs.outs)), 100, "last_sums",
        reduce_scratch(micro, tok, sub, width) + [rows] * 2 + [pltpu.VMEM((zn, dz, cols), BF)]
        + [pltpu.VMEM(size, F32), pltpu.VMEM((7,) + size, F32), pltpu.VMEM(size, F32), pltpu.VMEM((zn - 1,) + size, F32)]
        + [pltpu.VMEM((zn, dz, k), BF) for k in sizes] + sems(zn + 1, zn + 1, zn + 1, count, count, 2 * micro + 1) + jobs.scratch,
        talk=3, staged=(0, 3),
    )


def tiles(rows, cols):
    return pl.BlockSpec((rows, cols), lambda i: (i, 0))


def same_protein(lens, b, tok, count):
    col = lax.broadcasted_iota(jnp.int32, (tok, 1), 0)
    row = lax.broadcasted_iota(jnp.int32, (1, tok), 1)
    pc, pr = jnp.zeros_like(col), jnp.zeros_like(row)
    end = jnp.int32(0)
    for k in range(count):
        end = end + lens[b % 2, b // 2, k]
        pc = pc + (col >= end).astype(jnp.int32)
        pr = pr + (row >= end).astype(jnp.int32)
    return pc == pr


def turn(v, cos, sin):
    return v * cos + pltpu.roll(v, HEAD_DIM // 2, 1) * sin


def attention_body(count, ends, n1, w, cos, sin, qkv, att):
    zn, dz, _ = w.shape
    cols = qkv.shape[1]
    tok = n1.shape[0]
    heads = cols // 3 // HEAD_DIM
    span = heads * HEAD_DIM
    acc = dot(n1[:, 0:dz], w[0, :, :cols])
    for k in range(1, zn):
        acc = acc + dot(n1[:, k * dz : (k + 1) * dz], w[k, :, :cols])
    same = same_protein(ends, pl.program_id(0), tok, count)
    scale = HEAD_DIM ** (-0.5)
    for h in range(heads):
        lo = h * HEAD_DIM
        q = turn(acc[:, lo : lo + HEAD_DIM], cos[...], sin[...]).astype(BF)
        k = turn(acc[:, span + lo : span + lo + HEAD_DIM], cos[...], sin[...]).astype(BF)
        v = acc[:, 2 * span + lo : 2 * span + lo + HEAD_DIM].astype(BF)
        qkv[:, lo : lo + HEAD_DIM] = q
        qkv[:, span + lo : span + lo + HEAD_DIM] = k
        qkv[:, 2 * span + lo : 2 * span + lo + HEAD_DIM] = v
        s = jnp.where(same, dot_nt(q, k) * scale, -1e30)
        e = jnp.exp(s - jnp.max(s, axis=-1, keepdims=True))
        p = (e / jnp.sum(e, axis=-1, keepdims=True)).astype(BF)
        att[:, lo : lo + HEAD_DIM] = dot(p, v).astype(BF)


def attention(count, ends, n1, w, cos, sin, passed, tok):
    rows, width = n1.shape
    cols = w.shape[2] // 4 * 3

    def body(e, a, b, c, d, _, qkv, att, __):
        attention_body(count, e, a, b, c, d, qkv, att)

    return kernel(
        body, (ends, n1, w, cos, sin, passed),
        [SMEM, tiles(tok, width), VMEM, tiles(tok, HEAD_DIM), tiles(tok, HEAD_DIM), ANY],
        (shaped((rows, cols)), shaped((rows, cols // 3)), shaped(passed.shape)),
        (tiles(tok, cols), tiles(tok, cols // 3), ANY), 20, "attention", grid=(rows // tok,), aliases={5: 2},
    )


def attention_back_body(count, ends, b, branch, wo, qkv, cos, sin, low):
    zn, dz, span = wo.shape
    tok = branch.shape[0]
    heads = span // HEAD_DIM
    acc = dot(branch[:, 0:dz], wo[0])
    for k in range(1, zn):
        acc = acc + dot(branch[:, k * dz : (k + 1) * dz], wo[k])
    same = same_protein(ends, b, tok, count)
    scale = HEAD_DIM ** (-0.5)
    for h in range(heads):
        lo = h * HEAD_DIM
        ag = acc[:, lo : lo + HEAD_DIM].astype(BF)
        q = qkv[:, lo : lo + HEAD_DIM]
        k = qkv[:, span + lo : span + lo + HEAD_DIM]
        v = qkv[:, 2 * span + lo : 2 * span + lo + HEAD_DIM]
        s = jnp.where(same, dot_nt(q, k) * scale, -1e30)
        e = jnp.exp(s - jnp.max(s, axis=-1, keepdims=True))
        p = e / jnp.sum(e, axis=-1, keepdims=True)
        pg = dot_nt(ag, v)
        vg = dot_tn(p.astype(BF), ag)
        rd = jnp.sum(p * pg, axis=-1, keepdims=True)
        sg = (p * (pg - rd)).astype(BF)
        qg = dot(sg, k) * scale
        kg = dot_tn(sg, q) * scale
        low[:, lo : lo + HEAD_DIM] = turn(qg, cos[...], -sin[...]).astype(BF)
        low[:, span + lo : span + lo + HEAD_DIM] = turn(kg, cos[...], -sin[...]).astype(BF)
        low[:, 2 * span + lo : 2 * span + lo + HEAD_DIM] = vg.astype(BF)


def attention_back_kernel(jobs, count, parts, marks, ready, *refs):
    lens, branch, att, wa, qkv, cos, sin, n1, *refs = refs
    n0, n1s = marks
    g0, came0, g1, came1, refs = refs[0], refs[1 : 1 + n0], refs[1 + n0], refs[2 + n0 : 2 + n0 + n1s], refs[2 + n0 + n1s :]
    pair, last, middle, *refs = refs
    hids, zin, refs = refs[:parts], refs[parts:][: len(jobs.ins)], refs[parts + len(jobs.ins) :]
    low, grads, out_g, *refs = refs
    settled, layer_out, refs = refs[:4], refs[4], refs[5:]
    zout, refs = refs[: len(jobs.outs)], refs[len(jobs.outs) :]
    red, refs = refs[:8], refs[8:]
    bv, wo, ob, yb, load, yl, ls, ss, rs, *talk = refs
    rows, width = bv.shape
    zn, dz, span = wo.shape
    tok = rows // 4
    one = hids[0].shape[1]
    micro, sub, _ = middle.shape
    at = Place()
    cols = low.shape[1]
    downs, chunks = [], chunk_refs(pair, last)
    for k in range(parts):
        place = pl.ds(k * one, one)
        downs.append(pltpu.make_async_copy(hids[k], low.at[:, place], load.at[9 + k]))
        downs.append(
            pltpu.make_async_copy(chunks[k].at[:, :, pl.ds(2 * one, one)], grads.at[:, :, place], load.at[9 + parts + k])
        )
    for copy in downs:
        copy.start()
    weights = pltpu.make_async_copy(wa.at[:, :, pl.ds(cols, span)], wo, load.at[8])
    weights.start()

    def bring(b):
        here = pl.ds(b * tok, tok)
        return (
            pltpu.make_async_copy(branch.at[here], bv.at[here], load.at[b]),
            pltpu.make_async_copy(n1.at[here], red[0].at[b // 2, b % 2], load.at[4 + b]),
        )

    for b in range(4):
        bring(b)[0].start()
    meet(z_partners(zn) + [at.sib, at.xn, at.yn, at.xs])
    wire = Wire(ss, rs)
    host = jobs.host(wire, [zin[0], out_g], zout, talk)
    split = len(chain_results(zn, (0,), 8, 128))
    settles = [
        Settle(wire, at, zn, g0, came0[:split], came0[split:], settled[0], settled[1], yb, yl),
        Settle(wire, at, zn, g1, came1[:split], came1[split:], settled[2], settled[3], yb, yl),
    ]
    host.begin(0)
    for copy in downs:
        copy.wait()
    lows = [low.at[:, pl.ds(k * one, one)] for k in range(parts)]
    total = Reduce(wire, at, red, nt_compute(red[0], lows, [grads] * parts, 0, one))
    for m in range(micro):
        total.cores(m)
        total.diagonal(m)
    settles[0].go()
    weights.wait()
    ready()

    def block(b):
        if b < 2:
            bring(b)[0].wait()
        here = pl.ds(b * tok, tok)
        attention_back_body(
            count, lens, b, bv.at[here], wo, qkv.at[here], cos.at[here], sin.at[here], low.at[here]
        )

    block(0)
    for m in range(micro):
        total.sides(m)
        total.release(m)
    host.next()
    for b in range(4):
        bring(b)[1].start()
    block(1)
    settles[0].wait()
    settles[1].go()
    for b in (2, 3):
        bring(b)[0].wait()

    def output(k, carry):
        here = pl.ds(pl.multiple_of(k * dz, dz), dz)
        out_g[here, :] = dot_tn(bv[:, here], att[...]).astype(BF)
        return carry

    lax.fori_loop(0, zn, output, 0)
    host.begin(1)
    block(2)
    block(3)
    for b in range(4):
        bring(b)[1].wait()

    def weights_of(k, carry):
        here = pl.ds(pl.multiple_of(k * dz, dz), dz)
        acc = 0.0
        for b in range(4):
            acc = acc + dot_tn(red[0][b // 2, b % 2, :, here], low[pl.ds(b * tok, tok), :])
        grads[k] = acc.astype(BF)
        return carry

    lax.fori_loop(0, zn, weights_of, 0)
    deals, step = [], sub // 2
    for m in range(micro):
        total.arrived(m)
        for lo in range(0, sub, step):
            ob[m, lo : lo + step, :] = (middle[m, lo : lo + step, :] + total.total(m, lo, step)).astype(BF)
        deals.append(Deal(wire, at, ob, layer_out, m, ls, m))
        deals[-1].begin()
    settles[1].wait()
    for deal in deals:
        deal.end()
    host.end()
    wire.finish()


def attention_back(count, lens, branch, att, wa, qkv, cos, sin, n1, g0, got0, g1, got1, pair, last, middle, hids, g2, zn):
    rows, width = branch.shape
    cols, span, parts = qkv.shape[1], att.shape[1], len(hids)
    micro, sub, _ = middle.shape
    tok = rows // 4
    dz = width // zn
    out_g = shaped((width, span))
    jobs = Jobs([(g2, (0, 1), ()), (out_g, (0,), ())], zn)
    jobs.ins = [g2]
    half = shaped((dz // 2, g0.shape[1]))
    links = jobs.links + 2 + (REDUCE + 3) * micro
    return kernel(
        functools.partial(attention_back_kernel, jobs, count, parts, (len(got0), len(got1))),
        (lens, branch, att, wa, qkv, cos, sin, n1, g0, *got0, g1, *got1, pair, last, middle, *hids, *jobs.ins),
        [SMEM, ANY, VMEM, ANY, VMEM, VMEM, VMEM, ANY] + [ANY] * (4 + len(got0) + len(got1)) + [VMEM] + [ANY] * (parts + len(jobs.ins)),
        (shaped((rows, cols)), shaped((zn, dz, cols)), out_g, *(half,) * 4, shaped((micro, tok, width // 4)), *jobs.outs),
        (VMEM, VMEM, VMEM) + (ANY,) * (5 + len(jobs.outs)), 70, "attention_back",
        reduce_scratch(micro, tok, sub, width)
        + [pltpu.VMEM((rows, width), BF), pltpu.VMEM((zn, dz, span), BF), pltpu.VMEM((micro, sub, width), BF)]
        + settle_scratch(zn, dz, g0.shape[1])[:1]
        + sems(9 + 2 * parts, zn + 1, micro, links, links) + jobs.scratch,
        talk=9, staged=(2, 4, 5, 6, 12 + len(got0) + len(got1)),
    )


def chunk_body(jobs, c, n2, dy, w, mask, *refs):
    zin, (low, hidden, grad), refs = refs[: len(jobs.ins)], refs[len(jobs.ins) :][:3], refs[len(jobs.ins) + 3 :]
    zout, (nv, dv, wv, load, *talk) = refs[: len(jobs.outs)], refs[len(jobs.outs) :]
    zn, dz, cols = wv.shape
    one = cols // 3
    steps = load.shape[1] - 1
    tile = nv.shape[0] // steps
    whole = pltpu.make_async_copy(w if c is None else w.at[:, c], wv, load.at[0, steps])
    whole.start()

    def bring(t):
        at = pl.ds(pl.multiple_of(t * tile, tile), tile)
        return (
            pltpu.make_async_copy(n2.at[at], nv.at[at], load.at[0, t]),
            pltpu.make_async_copy(dy.at[at], dv.at[at], load.at[1, t]),
        )

    for t in range(steps):
        for copy in bring(t):
            copy.start()
    if talk:
        ss, rs, *talk = talk
        meet(z_partners(jobs.zn))
        host = jobs.host(Wire(ss, rs), zin, zout, talk)
        host.begin()
    whole.wait()

    def forward(t, carry):
        for copy in bring(t):
            copy.wait()
        at = pl.ds(pl.multiple_of(t * tile, tile), tile)
        acc = hg = 0.0
        for k in range(zn):
            acc = acc + dot(nv[at, k * dz : (k + 1) * dz], wv[k, :, : 2 * one])
            hg = hg + dot(dv[at, k * dz : (k + 1) * dz], wv[k, :, 2 * one :])
        hg = hg * mask[...]
        g, u = acc[:, :one], acc[:, one:]
        phi = 0.5 * (1.0 + lax.erf(g * (0.5**0.5)))
        slope = phi + g * jnp.exp(-0.5 * g * g) * 0.3989422804014327
        act = g * phi
        hidden[at, :] = (act * u * mask[...]).astype(BF)
        low[at, :one] = (hg * u * slope).astype(BF)
        low[at, one:] = (hg * act).astype(BF)
        return carry

    lax.fori_loop(0, steps, forward, 0)

    def weights(k, carry):
        at = pl.ds(pl.multiple_of(k * dz, dz), dz)
        grad[at, : 2 * one] = dot_tn(nv[:, at], low[...]).astype(BF)
        grad[at, 2 * one :] = dot_tn(dv[:, at], hidden[...]).astype(BF)
        return carry

    lax.fori_loop(0, zn, weights, 0)
    if jobs.links:
        host.end()


def chunk(n2, dy, w, c, mask, plan, zn, talk, first):
    rows, width = n2.shape
    cols = w.shape[-1]
    one = cols // 3
    jobs = Jobs(plan, zn)
    return kernel(
        functools.partial(chunk_body, jobs, c), (n2, dy, w, mask, *jobs.ins), [ANY, ANY, ANY, VMEM] + [ANY] * len(jobs.ins),
        (shaped((rows, 2 * one)), shaped((rows, one)), shaped((width, cols)), *jobs.outs),
        (VMEM,) * 3 + (ANY,) * len(jobs.outs), 22, "ffn_chunk",
        [pltpu.VMEM((rows, width), BF)] * 2 + [pltpu.VMEM((zn, width // zn, cols), BF), pltpu.SemaphoreType.DMA((2, 5))]
        + (sems(jobs.links, jobs.links) + jobs.scratch if jobs.links else []),
        first, talk=talk if jobs.links else None,
    )


def form_body(parts, *refs):
    halves, (gu, down, qkv, out) = refs[: 2 * parts + 4], refs[2 * parts + 4 :]
    y = lax.axis_index("y")
    one = halves[0].shape[1] // 3

    def pair(k):
        keep, theirs = halves[2 * k][...].astype(F32), halves[2 * k + 1][...].astype(F32)
        return jnp.where(y == 0, keep, theirs), jnp.where(y == 0, theirs, keep)

    half = parts * one
    for k in range(parts):
        for i, v in enumerate(pair(k)):
            lo = i * half + k * one
            gu[0, :, lo : lo + one] = v[:, :one]
            gu[1, :, lo : lo + one] = v[:, one : 2 * one]
            down[lo : lo + one, :] = v[:, 2 * one :].T
    for i, v in enumerate(pair(parts)):
        span = v.shape[1]
        out[i * span : (i + 1) * span, :] = v.T
    for i, v in enumerate(pair(parts + 1)):
        span = v.shape[1] // 3
        for p in range(3):
            qkv[p, :, i * span : (i + 1) * span] = v[:, p * span : (p + 1) * span]


def form(halves, w_gu, w_down, w_qkv, w_out):
    parts = (len(halves) - 4) // 2
    return kernel(
        functools.partial(form_body, parts), halves, [VMEM] * len(halves),
        tuple(shaped(w.shape, F32) for w in (w_gu, w_down, w_qkv, w_out)),
        (VMEM,) * 4, 8, "form",
    )


CHUNKS = 3


def on_device(inputs, lengths, counts, w_qkv, w_out, w_gu, w_down, g1, b1, g2, b2, dy_in):
    z = lax.axis_index("z")
    y = lax.axis_index("y")
    n = lax.axis_index("n")
    zn = lax.axis_size("z")
    micro, tok, feat = inputs.shape
    width = feat * lax.axis_size("n")
    rows = micro * 2 * tok
    depth = w_qkv.shape[1]
    half_slots = w_gu.shape[2] // 2
    one = half_slots // CHUNKS

    def gather_z(w):
        return lax.all_gather(w, "z", axis=0, tiled=False)

    own_attn = swap_attn(w_qkv, w_out)
    wa = gather_z(own_attn)
    vecs = jnp.stack([g1, b1, g2, b2]).astype(F32)
    vecs = jnp.pad(vecs, ((0, 4), (0, 0)))
    count = lengths.shape[2]
    lens = jnp.pad(lengths[:, 0], ((0, 8 - micro), (0, 128 - count)))
    half_dim = HEAD_DIM // 2
    freq = 10000.0 ** (-(jnp.arange(HEAD_DIM) % half_dim).astype(F32) / half_dim)
    x_all, norms, lens, cos, sin, own_01 = gather_x(
        inputs, vecs, lens, freq[None], w_gu, w_down, zn, (0, 1), one, count, (own_attn,)
    )
    norms = norms.transpose(2, 0, 1, 3).reshape(8, width)
    gain1, shift1, gain2, shift2 = (norms[i : i + 1] for i in range(4))
    own = jnp.sum(jnp.where(jnp.arange(counts.shape[0]) == n, counts, 0))
    mask = (y * half_slots + jnp.arange(half_slots) < own).astype(F32)[None]

    d_all, n1, own_2 = gather_d(dy_in, x_all, gain1, shift1, w_gu, w_down, (2,), one)
    dy = d_all.reshape(rows, width)
    qkv, att, own_2 = attention(count, lens, n1, wa, cos, sin, own_2, tok)
    w_01, w_2 = gather_z(own_01), gather_z(own_2)
    middle, n2 = attn_out(att, wa, x_all, gain2, shift2)
    n2 = n2.reshape(rows, width)

    def own_mask(c):
        return mask[:, c * one : (c + 1) * one]

    low0, hid0, g0 = chunk(n2, dy, w_01, 0, own_mask(0), [], zn, None, ())
    low1, hid1, grad1 = chunk(n2, dy, w_01, 1, own_mask(1), [], zn, None, (g0,))
    low2, hid2, grad2, *p = chunk(n2, dy, w_2, None, own_mask(2), [(g0, (0,), ())], zn, 7, (grad1,))
    mid_grad, branch, vec2, *q = ffn_back(
        [low0, low1, low2], w_01, w_2, d_all, middle, gain2, [(grad1, (0, 1), ()), (g0, (1,), p)], zn, ()
    )
    many = len(chain_results(zn, (0, 1), 8, 128))
    got1, got0 = q[:many], p + q[many:]
    branch = branch.reshape(rows, width)
    low, qkv_g, out_g, *r = attention_back(
        count, lens, branch, att, wa, qkv, cos, sin, n1, g0, got0, grad1, got1, w_01, w_2, middle, [hid0, hid1, hid2], grad2, zn
    )
    first, layer_out, got2, gout = r[:4], r[4], r[5 : 5 + many], r[5 + many :]
    in_grad, sums, *r = last_sums(
        low, wa, x_all, mid_grad, gain1, vec2, grad2, got2, out_g, gout, qkv_g.reshape(width, -1), zn
    )
    gu_grad, down_grad, qkv_grad, out_grad = form(
        [*first, *r[:6]], w_gu, w_down, w_qkv, w_out
    )

    mine = lax.dynamic_slice_in_dim(sums, (z * 2 + y) * g1.shape[0], g1.shape[0], 1)
    return (
        layer_out,
        in_grad,
        qkv_grad,
        out_grad,
        gu_grad,
        down_grad,
        mine[0],
        mine[1],
        mine[2],
        mine[3],
    )


def solution(mesh):
    wide, narrow = mesh.shape["wide"], mesh.shape["narrow"]
    grid = Mesh(mesh.devices.reshape(wide // 2, 2, narrow), ("z", "y", "n"))
    w = ("z", "y")
    tokens, depth, lines, vector = P(None, w, "n"), P(None, w, "n"), P("n", w), P(w)
    return jax.shard_map(
        on_device,
        mesh=grid,
        in_specs=(
            tokens, P(None, w, None), P(), depth, lines, depth, lines,
            vector, vector, vector, vector, tokens,
        ),
        out_specs=(
            tokens, tokens, depth, lines, depth, lines, vector, vector, vector, vector,
        ),
        check_vma=False,
    )
```

```python
import functools

import jax
import jax.numpy as jnp
from jax import lax
from jax.experimental import pallas as pl
from jax.experimental.pallas import tpu as pltpu
from jax.sharding import Mesh
from jax.sharding import PartitionSpec as P

HEAD_DIM = 128
EPS = 1e-05
BF = jnp.bfloat16
F32 = jnp.float32
MESH = pl.DeviceIdType.MESH
VMEM_BYTES = 60 * 2**20
SWAP = [(0, 1), (1, 0)]
ANY = pl.BlockSpec(memory_space=pl.ANY)
VMEM = pl.BlockSpec(memory_space=pltpu.VMEM)
SMEM = pl.BlockSpec(memory_space=pltpu.SMEM)


def dot(a, b):
    return jnp.dot(a, b, preferred_element_type=F32)


def dot_nt(a, b):
    return lax.dot_general(a, b, (((1,), (1,)), ((), ())), preferred_element_type=F32)


def dot_tn(a, b):
    return lax.dot_general(a, b, (((0,), (0,)), ((), ())), preferred_element_type=F32)


def normalise(v):
    centred = v - jnp.mean(v, axis=-1, keepdims=True)
    rstd = lax.rsqrt(jnp.mean(centred * centred, axis=-1, keepdims=True) + EPS)
    return centred * rstd, rstd


def norm_back(xhat, rstd, grad, gain):
    dx = grad * gain
    a = jnp.mean(dx, axis=-1, keepdims=True)
    b = jnp.mean(dx * xhat, axis=-1, keepdims=True)
    return rstd * (dx - a - xhat * b)


def cost(us, sent=0):
    return pl.CostEstimate(flops=int(us * 1e9), bytes_accessed=int(us * 3.2e6), transcendentals=0)


def without(body, ins, extra):
    def run(*refs):
        return body(*refs[:ins], *refs[ins + extra :])

    return run


def staged_body(body, ins, staged):
    def run(*refs):
        bufs, sem = refs[-len(staged) - 1 : -1], refs[-1]
        refs = list(refs[: -len(staged) - 1])
        copies = []
        for k, i in enumerate(staged):
            copies.append(pltpu.make_async_copy(refs[i], bufs[k], sem.at[k]))
            copies[-1].start()
            refs[i] = bufs[k]

        def ready():
            for copy in copies:
                copy.wait()

        return body(ready, *refs)

    return run


def kernel(body, ins, in_specs, outs, out_specs, us, name, scratch=(), first=(), grid=(), talk=None, aliases=None, staged=()):
    extra = len(first)
    in_specs, scratch = list(in_specs), list(scratch)
    if staged:
        body = staged_body(body, len(ins), staged)
        for i in staged:
            in_specs[i] = ANY
            scratch.append(pltpu.VMEM(ins[i].shape, ins[i].dtype))
        scratch += sems(len(staged))
    return pl.pallas_call(
        without(body, len(ins), extra),
        grid=grid,
        in_specs=in_specs + [ANY] * extra,
        out_specs=out_specs,
        out_shape=outs,
        scratch_shapes=scratch,
        input_output_aliases=aliases or {},
        compiler_params=pltpu.CompilerParams(
            vmem_limit_bytes=VMEM_BYTES, collective_id=talk, has_side_effects=talk is not None
        ),
        cost_estimate=cost(us),
        name=name,
    )(*ins, *first)


def sems(*counts):
    return [pltpu.SemaphoreType.DMA((k,)) for k in counts]


def shaped(shape, dtype=BF):
    return jax.ShapeDtypeStruct(tuple(shape), dtype)


class Place:
    def __init__(self):
        self.y = lax.axis_index("y")
        self.n = lax.axis_index("n")
        self.x = self.n // 2
        self.c = self.n % 2
        self.ns = self.n + 1 - 2 * self.c
        self.nx = (self.n + 2) % 4
        self.nd = (self.ns + 2) % 4
        self.sib = {"n": self.ns}
        self.xn = {"n": self.nx}
        self.yn = {"y": 1 - self.y}
        self.xs = {"n": self.nd}


def meet(devices):
    barrier = pltpu.get_barrier_semaphore()
    for d in devices:
        pl.semaphore_signal(barrier, inc=1, device_id=d, device_id_type=MESH)
    pl.semaphore_wait(barrier, len(devices))


class Wire:
    def __init__(self, send_sems, recv_sems, first=0):
        self.ss, self.rs, self.at, self.sent = send_sems, recv_sems, first, []

    def make(self, src, dst, device, keep=True, again=False):
        self.at += not again
        k = self.at - 1
        copy = pltpu.make_async_remote_copy(
            src_ref=src, dst_ref=dst, send_sem=self.ss.at[k], recv_sem=self.rs.at[k],
            device_id=device, device_id_type=MESH,
        )
        if keep:
            self.sent.append(copy)
        return copy

    def finish(self):
        for copy in self.sent:
            copy.wait_send()


SPREAD = 9


class Spread:
    def __init__(self, wire, at, src, slot):
        y, n, nx = at.y, at.n, at.nx
        self.first = [
            wire.make(src, slot(y, n, None), at.xn),
            wire.make(src, slot(y, n, None), at.yn),
            wire.make(src, slot(y, n, None), at.sib),
        ]
        self.on_x = [
            wire.make(slot(y, nx, 0), slot(y, nx, 0), at.yn),
            wire.make(slot(y, nx, None), slot(y, nx, None), at.sib),
        ]
        self.on_y = [
            wire.make(slot(1 - y, n, 1), slot(1 - y, n, 1), at.xn),
            wire.make(slot(1 - y, n, None), slot(1 - y, n, None), at.sib),
        ]
        self.last = [
            wire.make(slot(1 - y, nx, 0), slot(1 - y, nx, 0), at.sib),
            wire.make(slot(1 - y, nx, 1), slot(1 - y, nx, 1), at.sib),
        ]

    def begin(self):
        for copy in self.first:
            copy.start()

    def forward(self):
        self.first[0].wait_recv()
        for copy in self.on_x:
            copy.start()
        self.first[1].wait_recv()
        for copy in self.on_y:
            copy.start()

    def forward_last(self):
        self.on_x[0].wait_recv()
        self.last[0].start()
        self.on_y[0].wait_recv()
        self.last[1].start()

    def end(self):
        self.first[2].wait_recv()
        self.on_x[1].wait_recv()
        self.on_y[1].wait_recv()
        self.last[0].wait_recv()
        self.last[1].wait_recv()


REDUCE = 10


def reduce_scratch(micro, tok, sub, width):
    half = sub // 2
    return [
        pltpu.VMEM((micro, 2, tok, width), BF),
        pltpu.VMEM((micro, 2, 2, sub, width), BF),
        pltpu.VMEM((micro, sub, width), BF),
        pltpu.VMEM((micro, sub, width), BF),
        pltpu.VMEM((micro, sub, width), BF),
        pltpu.VMEM((micro, 2, half, width), BF),
        pltpu.VMEM((micro, sub, width), BF),
        pltpu.VMEM((micro, sub, width), BF),
    ]


class Reduce:
    def __init__(self, wire, at, scratch, compute):
        self.part, self.ra, self.sb, self.sx, self.sy, self.rb, self.rcx, self.rcy = scratch
        self.wire, self.at, self.compute = wire, at, compute
        self.micro, self.sub = self.sb.shape[0], self.sb.shape[1]
        self.a, self.b, self.d = {}, {}, {}
        self.released = False

    def rows(self, core, xx, lo=0, size=None):
        return pl.ds(pl.multiple_of((2 * xx + core) * self.sub, self.sub) + lo, size or self.sub)

    def summed(self, m, yy, xx, lo, size):
        mine = self.part[m, yy, self.rows(self.at.c, xx, lo, size), :].astype(F32)
        return mine + self.ra[m, yy, xx, lo : lo + size, :].astype(F32)

    def cores(self, m):
        at = self.at
        for yk, yy in ((1, 1 - at.y), (0, at.y)):
            self.compute(m, yy)
            for xk, xx in ((1, 1 - at.x), (0, at.x)):
                copy = self.wire.make(self.part.at[m, yy, self.rows(1 - at.c, xx)], self.ra.at[m, yy, xx], at.sib)
                copy.start()
                self.a[m, yk, xk] = copy

    def diagonal(self, m):
        at, sub, half = self.at, self.sub, self.sub // 2
        self.a[m, 1, 1].wait_recv()
        self.sb[m] = self.summed(m, 1 - at.y, 1 - at.x, 0, sub).astype(BF)
        self.b[m, 0] = self.wire.make(self.sb.at[m, 0:half], self.rb.at[m, 0], at.xn)
        self.b[m, 1] = self.wire.make(self.sb.at[m, half:sub], self.rb.at[m, 1], at.yn)
        self.b[m, 0].start()
        self.b[m, 1].start()

    def sides(self, m):
        at, sub, half = self.at, self.sub, self.sub // 2
        sx, sy, rb, rcx, rcy = self.sx, self.sy, self.rb, self.rcx, self.rcy
        self.a[m, 1, 0].wait_recv()
        sy[m, half:sub] = self.summed(m, 1 - at.y, at.x, half, half).astype(BF)
        self.d[m, 0] = self.wire.make(sy.at[m, half:sub], rcy.at[m, half:sub], at.yn)
        self.d[m, 0].start()
        self.a[m, 0, 1].wait_recv()
        sx[m, 0:half] = self.summed(m, at.y, 1 - at.x, 0, half).astype(BF)
        self.d[m, 1] = self.wire.make(sx.at[m, 0:half], rcx.at[m, 0:half], at.xn)
        self.d[m, 1].start()
        self.b[m, 0].wait_recv()
        sy[m, 0:half] = (self.summed(m, 1 - at.y, at.x, 0, half) + rb[m, 0].astype(F32)).astype(BF)
        self.d[m, 2] = self.wire.make(sy.at[m, 0:half], rcy.at[m, 0:half], at.yn)
        self.d[m, 2].start()
        self.b[m, 1].wait_recv()
        sx[m, half:sub] = (self.summed(m, at.y, 1 - at.x, half, half) + rb[m, 1].astype(F32)).astype(BF)
        self.d[m, 3] = self.wire.make(sx.at[m, half:sub], rcx.at[m, half:sub], at.xn)
        self.d[m, 3].start()

    def release(self, m):
        at = self.at
        self.a[m, 0, 0].wait_recv()
        self.ra[m, at.y, at.x] = self.summed(m, at.y, at.x, 0, self.sub).astype(BF)
        for yk in (1, 0):
            for xk in (1, 0):
                copy = self.a[m, yk, xk]
                copy.wait_send()
                self.wire.sent = [other for other in self.wire.sent if other is not copy]
        self.released = True

    def arrived(self, m):
        if not self.released:
            self.a[m, 0, 0].wait_recv()
        for k in range(4):
            self.d[m, k].wait_recv()

    def total(self, m, lo, size):
        if self.released:
            own = self.ra[m, self.at.y, self.at.x, lo : lo + size, :].astype(F32)
        else:
            own = self.summed(m, self.at.y, self.at.x, lo, size)
        return own + self.rcx[m, lo : lo + size, :].astype(F32) + self.rcy[m, lo : lo + size, :].astype(F32)


def nothing():
    pass


def reduce_rows(wire, at, scratch, compute, finish, tick=nothing):
    red = Reduce(wire, at, scratch, compute)
    for m in range(red.micro):
        red.cores(m)
        red.diagonal(m)
    tick()
    for m in range(red.micro):
        red.sides(m)
    for m in range(red.micro):
        red.arrived(m)
        finish(m, lambda lo, size, m=m: red.total(m, lo, size))
        tick()


LINE = (
    (0, 3, 1, -1, 0),
    (3, 0, 2, -1, 0),
    (1, 0, 0, 2, 0),
    (2, 3, 3, 2, 0),
    (1, 2, 2, 2, 0),
    (2, 1, 1, 2, 0),
    (0, 2, 2, 0, 1),
    (3, 1, 1, 0, 1),
    (0, 1, 1, 1, 1),
    (3, 2, 2, 1, 1),
)


def chain_results(zn, parts, rows, cols):
    count = 2 * len(parts) if zn == 4 else (zn - 1 if 0 in parts else 0)
    return [shaped((rows, cols))] * count


def chain_links(zn, parts):
    return sum(t[4] in parts for t in LINE) + (1 in parts) if zn == 4 else (zn - 1 if 0 in parts else 0)


class Chain:
    def __init__(self, wire, zn, parts, g, first, second, bufs, load, k):
        z = lax.axis_index("z")
        rows, cols = (first or second)[0].shape
        self.moves, self.bufs, self.cols, self.joins = [], bufs, cols, zn == 4 and 1 in parts
        self.over = False

        def group(i):
            return g.at[pl.ds(pl.multiple_of(i * rows, rows), rows)]

        if zn == 4:
            places = {2: first[0], -1: first[1]}
            if second:
                places.update({0: second[0], 1: second[1]})
            for src, i, dst, place, part in LINE:
                if part in parts:
                    copy = wire.make(group(i), places[place], {"z": dst}, keep=False)
                    self.moves.append((z == src, z == dst, copy, place < 0))
        elif 0 in parts:
            for dz in range(1, zn):
                to = (z + dz) % zn
                self.moves.append((None, None, wire.make(group(to), first[dz - 1], {"z": to}, keep=False), False))
        if self.joins:
            far = 3 * (1 - z // 2)
            here, there = bufs.at[0, :, pl.ds(0, cols)], bufs.at[1, :, pl.ds(0, cols)]
            self.own = pltpu.make_async_copy(group(far), here, load.at[k])
            self.came = pltpu.make_async_copy(first[1], there, load.at[k + 1])
            self.on = wire.make(here, second[1], {"z": far}, keep=False)
            self.inner = jnp.logical_and(z >= 1, z <= 2)
            self.outer = jnp.logical_not(self.inner)

    def begin(self):
        for sends, _, copy, _ in self.moves:
            if sends is None:
                copy.start()
            else:
                pl.when(sends)(copy.start)

    def join(self):
        if not self.joins:
            return

        def run():
            self.own.start()
            self.came.start()
            self.own.wait()
            self.came.wait()
            cols = pl.ds(0, self.cols)
            both = self.bufs[0, :, cols].astype(F32) + self.bufs[1, :, cols].astype(F32)
            self.bufs[0, :, cols] = both.astype(BF)
            self.on.start()

        for _, gets, copy, middle in self.moves:
            if middle:
                pl.when(gets)(copy.wait_recv)
        pl.when(self.inner)(run)

    def settle_sent(self):
        if self.joins:
            pl.when(self.inner)(self.on.wait_send)

    def wait(self):
        self.over = True
        for sends, gets, copy, middle in self.moves:
            if sends is None:
                copy.wait_recv()
                copy.wait_send()
                continue
            if not (middle and self.joins):
                pl.when(gets)(copy.wait_recv)
            pl.when(sends)(copy.wait_send)
        if self.joins:
            pl.when(self.outer)(self.on.wait_recv)


class Host:
    def __init__(self, chains):
        self.chains, self.todo, self.last = chains, list(chains), None

    def begin(self, which=None):
        for k, chain in enumerate(self.chains):
            if which is None or k == which:
                chain.begin()

    def next(self):
        if self.todo:
            if self.last is not None:
                self.last.settle_sent()
            self.last = self.todo.pop(0)
            self.last.join()

    def end(self):
        while self.todo:
            self.next()
        self.last.settle_sent()
        for chain in self.chains:
            if not chain.over:
                chain.wait()


class Settle:
    def __init__(self, wire, at, zn, g, first, second, keep, theirs, bufs, load):
        z = lax.axis_index("z")
        self.rows, self.cols = keep.shape[0] * 2, keep.shape[1]
        rows, half = self.rows, keep.shape[0]
        came = [first[0], second[1], second[0]] if zn == 4 else list(first)
        self.bufs, self.partly = bufs, jnp.logical_and(z >= 1, z <= 2) if zn == 4 else None
        mine = g.at[pl.ds(pl.multiple_of(z * rows, rows), rows)]
        self.loads = [pltpu.make_async_copy(src, bufs.at[k], load.at[k]) for k, src in enumerate([mine] + came)]

        def part(i):
            return bufs.at[0, pl.ds(pl.multiple_of(i * half, half), half)]

        self.away = wire.make(part(1 - at.y), theirs, at.yn, keep=False)
        self.here = pltpu.make_async_copy(part(at.y), keep, load.at[len(self.loads)])

    def go(self):
        always = self.loads if self.partly is None else self.loads[:-1]
        for copy in always:
            copy.start()
        if self.partly is not None:
            k = len(always)
            pl.when(self.partly)(self.loads[k].start)
            pl.when(self.partly)(self.loads[k].wait)

            def none():
                self.bufs[k] = jnp.zeros((self.rows, self.cols), BF)

            pl.when(jnp.logical_not(self.partly))(none)
        for copy in always:
            copy.wait()
        total = self.bufs[0].astype(F32)
        for k in range(1, len(self.loads)):
            total = total + self.bufs[k].astype(F32)
        self.bufs[0] = total.astype(BF)
        self.away.start()
        self.here.start()

    def wait(self):
        self.away.wait_recv()
        self.away.wait_send()
        self.here.wait()


def settle_scratch(zn, rows, cols):
    return [pltpu.VMEM((zn, rows, cols), BF)] + sems(zn + 1)


def z_partners(zn):
    z = lax.axis_index("z")
    return [{"z": (z + dz) % zn} for dz in range(1, zn)]


class Jobs:
    def __init__(self, plan, zn):
        self.plan, self.zn = plan, zn
        self.ins, self.outs, self.links = [], [], 0
        for g, parts, given in plan:
            self.ins += [g] + list(given)
            self.outs += chain_results(zn, parts, g.shape[0] // zn, g.shape[1])
            self.links += chain_links(zn, parts)
        wide = max([p[0].shape[1] for p in plan], default=0)
        rows = plan[0][0].shape[0] // zn if plan else 0
        self.scratch = [pltpu.VMEM((2, rows, wide), BF)] + sems(2 * len(plan)) if plan else []

    def host(self, wire, ins, outs, scratch):
        chains, i, o = [], 0, 0
        for k, (g, parts, given) in enumerate(self.plan):
            count = len(chain_results(self.zn, parts, 8, 128))
            made = outs[o : o + count]
            first = ins[i + 1 : i + 1 + len(given)] if given else (made if 1 not in parts or self.zn != 4 else made[:2])
            second = [] if 1 not in parts or self.zn != 4 else made[-2:]
            chains.append(Chain(wire, self.zn, parts, ins[i], first, second, *scratch, 2 * k))
            i, o = i + 1 + len(given), o + count
        return Host(chains)


def blockwise(part, m, yy, fn, tile=256):
    tok = part.shape[2]

    def step(i, carry):
        lo = pl.multiple_of(i * tile, tile)
        fn(lo, tile)
        return carry

    lax.fori_loop(0, tok // tile, step, 0)


def token_spreads(wire, at, src, out, sem, first, cut):
    micro, tok, feat = src.shape
    spreads, local = [], []
    for m in range(micro):

        def slot(yy, nn, part, m=m):
            lo, size = {None: (0, tok), 0: (0, cut), 1: (cut, tok - cut)}[part]
            return out.at[m, yy, pl.ds(lo, size), pl.ds(pl.multiple_of(nn * feat, feat), feat)]

        spreads.append(Spread(wire, at, src.at[m], slot))
        local.append(pltpu.make_async_copy(src.at[m], slot(at.y, at.n, None), sem.at[first + m]))
    return spreads, local


def attn_cut(w_qkv, w_out, i, buf):
    parts, _, cols = w_qkv.shape
    half = cols // 2
    at = pl.ds(pl.multiple_of(i * half, half), half)
    for p in range(parts):
        buf[:, p * half : (p + 1) * half] = w_qkv[p, :, at]
    buf[:, parts * half :] = w_out[at, :].astype(F32).T.astype(BF)


def chunk_cut(w_gu, w_down, i, c, one, buf):
    half = w_gu.shape[2] // 2
    at = pl.ds(pl.multiple_of(i * half, half) + c * one, one)
    buf[:, :one] = w_gu[0, :, at]
    buf[:, one : 2 * one] = w_gu[1, :, at]
    buf[:, 2 * one :] = w_down[at, :].astype(F32).T.astype(BF)


class Swap:
    def __init__(self, wire, at, bufs, out, sem):
        depth = bufs.shape[1]
        place = out.at[pl.ds(pl.multiple_of(at.y * depth, depth), depth)]
        self.away = wire.make(bufs.at[0], place, at.yn)
        self.here = pltpu.make_async_copy(bufs.at[1], place, sem)

    def end(self):
        self.away.wait_recv()
        self.here.wait()


def swap_attn_kernel(w_qkv, w_out, out, bufs, ss, rs, ls):
    at = Place()
    meet([at.yn])
    wire = Wire(ss, rs)
    swap = Swap(wire, at, bufs, out, ls.at[0])
    attn_cut(w_qkv, w_out, 1 - at.y, bufs.at[0])
    swap.away.start()
    attn_cut(w_qkv, w_out, at.y, bufs.at[1])
    swap.here.start()
    swap.end()
    wire.finish()


def swap_attn(w_qkv, w_out):
    parts, depth, cols = w_qkv.shape
    size = (parts + 1) * cols // 2
    return kernel(
        swap_attn_kernel, (w_qkv, w_out), [VMEM, VMEM], shaped((2 * depth, size)), ANY, 14, "swap_attn",
        [pltpu.VMEM((2, depth, size), BF)] + sems(1, 1, 1), talk=6,
    )


def swap_chunks(wire, at, w_gu, w_down, which, one, bufs, outs, ls):
    swaps = []
    for k, (c, out) in enumerate(zip(which, outs)):
        swap = Swap(wire, at, bufs.at[k], out, ls.at[k])
        chunk_cut(w_gu, w_down, 1 - at.y, c, one, bufs.at[k, 0])
        swap.away.start()
        chunk_cut(w_gu, w_down, at.y, c, one, bufs.at[k, 1])
        swap.here.start()
        swaps.append(swap)
    return swaps


def gather_x_kernel(zn, which, count, x_in, v_in, lens, freq, w_gu, w_down, x_out, v_out, lens_all, cos, sin, own, *scratch):
    bufs, ss, rs, ls = scratch
    at = Place()
    z = lax.axis_index("z")
    one = own.shape[2] // 3
    ring = [(dz, dy) for dz in range(zn) for dy in range(2) if dz or dy]
    others = [{"z": (z + dz) % zn, "y": (at.y + dy) % 2} for dz, dy in ring]
    meet([at.sib, at.xn] + others)
    wire = Wire(ss, rs)
    there = wire.make(lens, lens_all.at[at.y], at.yn)
    there.start()
    spreads, local = token_spreads(wire, at, x_in, x_out, ls, len(which) + 1, x_in.shape[1] // 8)
    local.append(pltpu.make_async_copy(v_in, v_out.at[z, at.y], ls.at[len(which)]))
    small = [wire.make(v_in, v_out.at[z, at.y], d) for d in others]
    for s in spreads:
        s.begin()
    for copy in small + local:
        copy.start()
    swaps = swap_chunks(wire, at, w_gu, w_down, which, one, bufs, [own.at[k] for k in range(len(which))], ls)
    lens_all[at.y] = lens[...]
    there.wait_recv()
    tok = x_in.shape[1]
    row = lax.broadcasted_iota(jnp.int32, (tok, 1), 0)
    flip = jnp.where(lax.broadcasted_iota(jnp.int32, (1, HEAD_DIM), 1) < HEAD_DIM // 2, -1.0, 1.0)

    def table(b, carry):
        m, yy = b // 2, b % 2
        line = lens_all[yy, pl.ds(m, 1), :]
        end = jnp.zeros((1, 1), jnp.int32)
        start = jnp.zeros_like(row)
        for k in range(count):
            end = end + line[:, k : k + 1]
            start = jnp.where(row >= end, end, start)
        angle = (row - start).astype(F32) * freq[...]
        place = pl.ds(pl.multiple_of(b * tok, tok), tok)
        cos[place, :] = jnp.cos(angle)
        sin[place, :] = jnp.sin(angle) * flip
        return carry

    lax.fori_loop(0, x_in.shape[0] * 2, table, 0)
    run_spreads(spreads, local)
    for copy in small:
        copy.wait_recv()
    for swap in swaps:
        swap.end()
    wire.finish()


def gather_x(x, v, lens, freq, w_gu, w_down, zn, which, one, count, first):
    micro, tok, feat = x.shape
    depth = w_gu.shape[1]
    rows = micro * 2 * tok
    links = SPREAD * micro + 2 * zn - 1 + len(which) + 1
    return kernel(
        functools.partial(gather_x_kernel, zn, which, count), (x, v, lens, freq, w_gu, w_down),
        [ANY, ANY, VMEM, VMEM, VMEM, VMEM],
        (
            shaped((micro, 2, tok, 4 * feat)), shaped((zn, 2) + v.shape, F32), shaped((2,) + lens.shape, jnp.int32),
            shaped((rows, HEAD_DIM), F32), shaped((rows, HEAD_DIM), F32), shaped((len(which), 2 * depth, 3 * one)),
        ),
        (ANY, ANY, VMEM, VMEM, VMEM, ANY), 48, "gather_x",
        [pltpu.VMEM((len(which), 2, depth, 3 * one), BF)] + sems(links, links, micro + 1 + len(which)),
        first, talk=0,
    )


def gather_d_kernel(which, one, d_in, x_all, gain, shift, w_gu, w_down, d_out, n1, *refs):
    outs, (bufs, xin, nout, ss, rs, ls, load) = refs[: len(which)], refs[len(which) :]
    at = Place()
    micro, _, tok, _ = x_all.shape
    meet([at.sib, at.xn, at.yn])
    wire = Wire(ss, rs)
    spreads, local = token_spreads(wire, at, d_in, d_out, ls, len(which), d_in.shape[1] // 16 * 5)

    def bring(b):
        return pltpu.make_async_copy(x_all.at[b // 2, b % 2], xin.at[b % 2], load.at[b])

    def put(b):
        return pltpu.make_async_copy(nout.at[b % 2], n1.at[pl.ds(b * tok, tok)], load.at[2 * micro + b])

    bring(0).start()
    bring(1).start()
    for s in spreads:
        s.begin()
    for copy in local:
        copy.start()
    swaps = swap_chunks(wire, at, w_gu, w_down, which, one, bufs, outs, ls)
    for b in range(2 * micro):
        bring(b).wait()
        if b >= 2:
            put(b - 2).wait()

        def tile(i, carry, b=b):
            place = pl.ds(pl.multiple_of(i * 128, 128), 128)
            xhat, _ = normalise(xin[b % 2, place, :].astype(F32))
            nout[b % 2, place, :] = (xhat * gain[...] + shift[...]).astype(BF)
            return carry

        lax.fori_loop(0, tok // 128, tile, 0)
        put(b).start()
        if b + 2 < 2 * micro:
            bring(b + 2).start()
        if b % 2:
            spreads[b // 2].forward()
    put(2 * micro - 2).wait()
    put(2 * micro - 1).wait()
    for s in spreads:
        s.forward_last()
    for s in spreads:
        s.end()
    for copy in local:
        copy.wait()
    for swap in swaps:
        swap.end()
    wire.finish()


def gather_d(d, x_all, gain, shift, w_gu, w_down, which, one):
    micro, tok, feat = d.shape
    depth = w_gu.shape[1]
    count = SPREAD * micro + len(which)
    return kernel(
        functools.partial(gather_d_kernel, which, one), (d, x_all, gain, shift, w_gu, w_down),
        [ANY, ANY, VMEM, VMEM, VMEM, VMEM],
        (shaped((micro, 2, tok, 4 * feat)), shaped((micro * 2 * tok, 4 * feat))) + (shaped((2 * depth, 3 * one)),) * len(which),
        (ANY,) * (2 + len(which)), 48, "gather_d",
        [pltpu.VMEM((len(which), 2, depth, 3 * one), BF)] + [pltpu.VMEM((2, tok, 4 * feat), BF)] * 2
        + sems(count, count, micro + len(which), 4 * micro),
        talk=5,
    )


def row_slot(out, m, sub):
    half = sub // 2

    def slot(yy, nn, part):
        ref = out.at[m, yy, nn]
        return ref if part is None else ref.at[pl.ds(part * half, half)]

    return slot


def run_spreads(spreads, local, tick=nothing):
    for s in spreads:
        s.forward()
    tick()
    for s in spreads:
        s.forward_last()
    for s in spreads:
        s.end()
    for copy in local:
        copy.wait()


def attn_out_kernel(att, wo, x_all, gain, shift, middle, n2, *scratch):
    *red, xb, nb, ss, rs, ls = scratch
    at = Place()
    micro, sub, width = middle.shape
    zn, dz, cols = wo.shape
    span = att.shape[1]
    tok = red[0].shape[2]
    meet([at.sib, at.xn, at.yn])
    wire = Wire(ss, rs)
    own = [pltpu.make_async_copy(x_all.at[m, at.y, pl.ds(at.n * sub, sub)], xb.at[m], ls.at[m]) for m in range(micro)]
    for copy in own:
        copy.start()

    def compute(m, yy):
        def tile(lo, size):
            a = att[pl.ds(pl.multiple_of((m * 2 + yy) * tok, tok) + lo, size), :]
            for k in range(zn):
                red[0][m, yy, pl.ds(lo, size), k * dz : (k + 1) * dz] = dot_nt(a, wo[k, :, cols - span :]).astype(BF)

        blockwise(red[0], m, yy, tile)

    spreads, local = [], []

    def finish(m, total):
        own[m].wait()
        step = sub // 2
        for lo in range(0, sub, step):
            mid = xb[m, lo : lo + step, :].astype(F32) + total(lo, step)
            middle[m, lo : lo + step, :] = mid
            xhat, _ = normalise(mid)
            nb[m, lo : lo + step, :] = (xhat * gain[...] + shift[...]).astype(BF)
        slot = row_slot(n2, m, sub)
        spreads.append(Spread(wire, at, nb.at[m], slot))
        spreads[-1].begin()
        local.append(pltpu.make_async_copy(nb.at[m], slot(at.y, at.n, None), ls.at[micro + m]))
        local[-1].start()

    reduce_rows(wire, at, red, compute, finish)
    run_spreads(spreads, local)
    wire.finish()


def attn_out(att, wo, x_all, gain, shift):
    micro, _, tok, width = x_all.shape
    sub = tok // 4
    count = (REDUCE + SPREAD) * micro
    return kernel(
        attn_out_kernel, (att, wo, x_all, gain, shift), [VMEM, VMEM, ANY, VMEM, VMEM],
        (shaped((micro, sub, width), F32), shaped((micro, 2, 4, sub, width))), (VMEM, ANY), 85, "attn_out",
        reduce_scratch(micro, tok, sub, width) + [pltpu.VMEM((micro, sub, width), BF)] * 2 + sems(count, count, 2 * micro),
        talk=1,
    )


def nt_compute(part, lows, ws, first, each=0):
    zn, dz, _ = ws[0].shape
    tok = part.shape[2]
    span = lows[0].shape[1]

    def compute(m, yy):
        def tile(lo, size):
            at = pl.multiple_of((m * 2 + yy) * tok, tok) + lo
            for k in range(zn):
                acc = None
                for i, (low, w) in enumerate(zip(lows, ws)):
                    lo_col = first + i * each
                    term = dot_nt(low[pl.ds(at, size), :], w[k, :, lo_col : lo_col + span])
                    acc = term if acc is None else acc + term
                part[m, yy, pl.ds(lo, size), k * dz : (k + 1) * dz] = acc.astype(BF)

        blockwise(part, m, yy, tile)

    return compute


class Columns:
    def __init__(self, groups, cols, bufs, load):
        self.copies = [
            pltpu.make_async_copy(src.at[:, :, cols], bufs.at[k], load.at[k]) for k, src in enumerate(groups)
        ]
        for copy in self.copies:
            copy.start()

    def wait(self):
        for copy in self.copies:
            copy.wait()


def chunk_refs(pair, last):
    return [pair.at[:, k] for k in range(pair.shape[1])] + [last]


def ffn_back_kernel(jobs, parts, ready, *refs):
    guls = refs[:parts]
    pair, last, d_all, middle, gain, *refs = refs[parts:]
    zin, (mid_grad, branch, vec), refs = refs[: len(jobs.ins)], refs[len(jobs.ins) :][:3], refs[len(jobs.ins) + 3 :]
    zout, refs = refs[: len(jobs.outs)], refs[len(jobs.outs) :]
    *red, db, nb, wv, ss, rs, ls, lw, zb, zl = refs
    at = Place()
    micro, sub, width = middle.shape
    span = guls[0].shape[1]
    weights = Columns(chunk_refs(pair, last), pl.ds(0, span), wv, lw)
    own = [pltpu.make_async_copy(d_all.at[m, at.y, pl.ds(at.n * sub, sub)], db.at[m], ls.at[m]) for m in range(micro)]
    for copy in own:
        copy.start()
    meet([at.sib, at.xn, at.yn] + z_partners(jobs.zn))
    wire = Wire(ss, rs)
    host = jobs.host(wire, zin, zout, (zb, zl))
    host.begin()
    vec[...] = jnp.zeros_like(vec)
    spreads, local = [], []

    def finish(m, total):
        own[m].wait()
        step = sub // 2
        for lo in range(0, sub, step):
            grad = total(lo, step)
            xhat, rstd = normalise(middle[m, lo : lo + step, :])
            vec[0:1, :] += jnp.sum(grad * xhat, axis=0, keepdims=True)
            vec[1:2, :] += jnp.sum(grad, axis=0, keepdims=True)
            mg = db[m, lo : lo + step, :].astype(F32) + norm_back(xhat, rstd, grad, gain[...])
            mid_grad[m, lo : lo + step, :] = mg
            nb[m, lo : lo + step, :] = mg.astype(BF)
        slot = row_slot(branch, m, sub)
        spreads.append(Spread(wire, at, nb.at[m], slot))
        spreads[-1].begin()
        local.append(pltpu.make_async_copy(nb.at[m], slot(at.y, at.n, None), ls.at[micro + m]))
        local[-1].start()

    weights.wait()
    ready()
    reduce_rows(wire, at, red, nt_compute(red[0], guls, [wv.at[k] for k in range(parts)], 0), finish, host.next)
    run_spreads(spreads, local, host.next)
    host.end()
    wire.finish()


def ffn_back(guls, pair, last, d_all, middle, gain, plan, zn, first):
    parts = len(guls)
    micro, _, tok, width = d_all.shape
    sub = tok // 4
    jobs = Jobs(plan, zn)
    count = (REDUCE + SPREAD) * micro + jobs.links
    span = guls[0].shape[1]
    return kernel(
        functools.partial(ffn_back_kernel, jobs, parts), (*guls, pair, last, d_all, middle, gain, *jobs.ins),
        [VMEM] * parts + [ANY, ANY, ANY, VMEM, VMEM] + [ANY] * len(jobs.ins),
        (shaped((micro, sub, width), F32), shaped((micro, 2, 4, sub, width)), shaped((8, width), F32), *jobs.outs),
        (VMEM, ANY, VMEM) + (ANY,) * len(jobs.outs), 90, "ffn_back",
        reduce_scratch(micro, tok, sub, width) + [pltpu.VMEM((micro, sub, width), BF)] * 2
        + [pltpu.VMEM((parts, zn, width // zn, span), BF)] + sems(count, count, 2 * micro, parts) + jobs.scratch,
        first, talk=2, staged=(*range(parts), parts + 3),
    )


def host_kernel(jobs, *refs):
    zin, zout, (ss, rs, zb, zl) = refs[: len(jobs.ins)], refs[len(jobs.ins) :][: len(jobs.outs)], refs[-4:]
    meet(z_partners(jobs.zn))
    host = jobs.host(Wire(ss, rs), zin, zout, (zb, zl))
    host.begin()
    host.end()


def host_only(plan, zn, first):
    jobs = Jobs(plan, zn)
    return kernel(
        functools.partial(host_kernel, jobs), jobs.ins, [ANY] * len(jobs.ins), tuple(jobs.outs), (ANY,) * len(jobs.outs),
        20 * jobs.steps, "along_z", sems(2 * jobs.steps, 2 * jobs.steps) + jobs.scratch, first, talk=8,
    )


class Deal:
    def __init__(self, wire, at, rows, out, m, sems, k):
        sub, width = rows.shape[1], rows.shape[2]
        feat = width // 4

        def cols(nn):
            return rows.at[m, :, pl.ds(pl.multiple_of(nn * feat, feat), feat)]

        place = out.at[m, pl.ds(pl.multiple_of(at.n * sub, sub), sub)]
        self.local = pltpu.make_async_copy(cols(at.n), place, sems.at[k])
        self.copies = [
            wire.make(cols(at.nx), place, at.xn),
            wire.make(cols(at.nd), place, at.xs),
            wire.make(cols(at.ns), place, at.sib),
        ]

    def begin(self):
        for copy in self.copies:
            copy.start()
        self.local.start()

    def end(self):
        for copy in self.copies:
            copy.wait_recv()
        self.local.wait()


def last_kernel(jobs, zn, marks, ready, *refs):
    low, wa, x_all, mid_grad, gain, vec2, *refs = refs
    g2, came2, refs = refs[0], refs[1 : 1 + marks], refs[1 + marks :]
    zin, refs = refs[: len(jobs.ins)], refs[len(jobs.ins) :]
    in_grad, sums, *refs = refs
    settled, zout, refs = refs[:6], refs[6:][: len(jobs.outs)], refs[6 + len(jobs.outs) :]
    red, refs = refs[:8], refs[8:]
    xb, ob, w1, mine, plane, summed, lines, yb2, ybo, ybq, yl2, ylo, ylq, ss, rs, ls, *talk = refs
    at = Place()
    z = lax.axis_index("z")
    micro, sub, width = mid_grad.shape
    qkv = pltpu.make_async_copy(wa.at[:, :, pl.ds(0, low.shape[1])], w1, ls.at[2 * micro])
    qkv.start()
    own = [pltpu.make_async_copy(x_all.at[m, at.y, pl.ds(at.n * sub, sub)], xb.at[m], ls.at[m]) for m in range(micro)]
    for copy in own:
        copy.start()
    flips = [(dy, dn) for dy in range(2) for dn in range(4) if dy or dn]
    peers = [{"y": (at.y + dy) % 2, "n": (at.n + dn) % 4} for dy, dn in flips]
    along = [{"z": (z + dz) % zn} for dz in range(1, zn)]
    meet(peers + along)
    wire = Wire(ss, rs)
    host = jobs.host(wire, zin, zout, talk)
    host.begin()
    split = len(chain_results(zn, (0,), 8, 128))
    settles = [
        Settle(wire, at, zn, g2, came2[:split], came2[split:], settled[0], settled[1], yb2, yl2),
        Settle(wire, at, zn, zin[1], zin[2:], zout[marks:], settled[2], settled[3], ybo, ylo),
        Settle(wire, at, zn, zin[0], zout[:split], zout[split:marks], settled[4], settled[5], ybq, ylq),
    ]
    mine[...] = jnp.zeros_like(mine)
    mine[2:4] = vec2[0:2]
    qkv.wait()
    ready()
    total = Reduce(wire, at, red, nt_compute(red[0], [low], [w1], 0))
    for m in range(micro):
        total.cores(m)
        total.diagonal(m)
    for m in range(micro):
        total.sides(m)
    host.next()
    step = sub // 2
    deals = []
    for m in range(micro):
        total.arrived(m)
        own[m].wait()
        for lo in range(0, sub, step):
            grad = total.total(m, lo, step)
            xhat, rstd = normalise(xb[m, lo : lo + step, :].astype(F32))
            mine[0:1, :] += jnp.sum(grad * xhat, axis=0, keepdims=True)
            mine[1:2, :] += jnp.sum(grad, axis=0, keepdims=True)
            back = norm_back(xhat, rstd, grad, gain[...])
            ob[m, lo : lo + step, :] = (mid_grad[m, lo : lo + step, :] + back).astype(BF)
        deals.append(Deal(wire, at, ob, in_grad, m, ls, micro + m))
        deals[-1].begin()
        if m == 0:
            settles[0].go()
    host.next()
    near = [wire.make(mine, plane.at[k], d) for k, d in enumerate(peers)]
    for copy in near:
        copy.start()
    host.chains[0].wait()
    settles[2].go()
    for copy in near:
        copy.wait_recv()
    both = mine[...]
    for k in range(len(peers)):
        both = both + plane[k]
    summed[...] = both
    far = [wire.make(summed, lines.at[k], d) for k, d in enumerate(along)]
    for copy in far:
        copy.start()
    host.end()
    settles[1].go()
    for copy in far:
        copy.wait_recv()
    both = summed[...]
    for k in range(len(along)):
        both = both + lines[k]
    sums[...] = both
    for deal in deals:
        deal.end()
    for settle in settles:
        settle.wait()
    wire.finish()


def last_sums(low, wa, x_all, mid_grad, gain, vec2, g2, got2, out_g, gout, qkv_g, zn):
    micro, _, tok, width = x_all.shape
    sub = tok // 4
    dz, cols = width // zn, low.shape[1]
    jobs = Jobs([(qkv_g, (0, 1), ()), (out_g, (1,), gout)], zn)
    count = (REDUCE + 3) * micro + 7 + zn - 1 + jobs.links + 3
    size = vec2.shape
    rows = pltpu.VMEM((micro, sub, width), BF)
    sizes = (g2.shape[1], out_g.shape[1], cols)
    halves = [shaped((dz // 2, k)) for k in sizes for _ in range(2)]
    return kernel(
        functools.partial(last_kernel, jobs, zn, len(got2)),
        (low, wa, x_all, mid_grad, gain, vec2, g2, *got2, *jobs.ins),
        [VMEM, ANY, ANY, VMEM, VMEM, VMEM] + [ANY] * (1 + len(got2) + len(jobs.ins)),
        (shaped((micro, tok, width // 4)), shaped(size, F32), *halves, *jobs.outs),
        (ANY, VMEM) + (ANY,) * (6 + len(jobs.outs)), 100, "last_sums",
        reduce_scratch(micro, tok, sub, width) + [rows] * 2 + [pltpu.VMEM((zn, dz, cols), BF)]
        + [pltpu.VMEM(size, F32), pltpu.VMEM((7,) + size, F32), pltpu.VMEM(size, F32), pltpu.VMEM((zn - 1,) + size, F32)]
        + [pltpu.VMEM((zn, dz, k), BF) for k in sizes] + sems(zn + 1, zn + 1, zn + 1, count, count, 2 * micro + 1) + jobs.scratch,
        talk=3, staged=(0, 3),
    )


def tiles(rows, cols):
    return pl.BlockSpec((rows, cols), lambda i: (i, 0))


def same_protein(lens, b, tok, count):
    col = lax.broadcasted_iota(jnp.int32, (tok, 1), 0)
    row = lax.broadcasted_iota(jnp.int32, (1, tok), 1)
    pc, pr = jnp.zeros_like(col), jnp.zeros_like(row)
    end = jnp.int32(0)
    for k in range(count):
        end = end + lens[b % 2, b // 2, k]
        pc = pc + (col >= end).astype(jnp.int32)
        pr = pr + (row >= end).astype(jnp.int32)
    return pc == pr


def turn(v, cos, sin):
    return v * cos + pltpu.roll(v, HEAD_DIM // 2, 1) * sin


def attention_body(count, ends, n1, w, cos, sin, qkv, att):
    zn, dz, _ = w.shape
    cols = qkv.shape[1]
    tok = n1.shape[0]
    heads = cols // 3 // HEAD_DIM
    span = heads * HEAD_DIM
    acc = dot(n1[:, 0:dz], w[0, :, :cols])
    for k in range(1, zn):
        acc = acc + dot(n1[:, k * dz : (k + 1) * dz], w[k, :, :cols])
    same = same_protein(ends, pl.program_id(0), tok, count)
    scale = HEAD_DIM ** (-0.5)
    for h in range(heads):
        lo = h * HEAD_DIM
        q = turn(acc[:, lo : lo + HEAD_DIM], cos[...], sin[...]).astype(BF)
        k = turn(acc[:, span + lo : span + lo + HEAD_DIM], cos[...], sin[...]).astype(BF)
        v = acc[:, 2 * span + lo : 2 * span + lo + HEAD_DIM].astype(BF)
        qkv[:, lo : lo + HEAD_DIM] = q
        qkv[:, span + lo : span + lo + HEAD_DIM] = k
        qkv[:, 2 * span + lo : 2 * span + lo + HEAD_DIM] = v
        s = jnp.where(same, dot_nt(q, k) * scale, -1e30)
        e = jnp.exp(s - jnp.max(s, axis=-1, keepdims=True))
        p = (e / jnp.sum(e, axis=-1, keepdims=True)).astype(BF)
        att[:, lo : lo + HEAD_DIM] = dot(p, v).astype(BF)


def attention(count, ends, n1, w, cos, sin, passed, tok):
    rows, width = n1.shape
    cols = w.shape[2] // 4 * 3

    def body(e, a, b, c, d, _, qkv, att, __):
        attention_body(count, e, a, b, c, d, qkv, att)

    return kernel(
        body, (ends, n1, w, cos, sin, passed),
        [SMEM, tiles(tok, width), VMEM, tiles(tok, HEAD_DIM), tiles(tok, HEAD_DIM), ANY],
        (shaped((rows, cols)), shaped((rows, cols // 3)), shaped(passed.shape)),
        (tiles(tok, cols), tiles(tok, cols // 3), ANY), 20, "attention", grid=(rows // tok,), aliases={5: 2},
    )


def attention_back_body(count, ends, b, branch, wo, qkv, cos, sin, low):
    zn, dz, span = wo.shape
    tok = branch.shape[0]
    heads = span // HEAD_DIM
    acc = dot(branch[:, 0:dz], wo[0])
    for k in range(1, zn):
        acc = acc + dot(branch[:, k * dz : (k + 1) * dz], wo[k])
    same = same_protein(ends, b, tok, count)
    scale = HEAD_DIM ** (-0.5)
    for h in range(heads):
        lo = h * HEAD_DIM
        ag = acc[:, lo : lo + HEAD_DIM].astype(BF)
        q = qkv[:, lo : lo + HEAD_DIM]
        k = qkv[:, span + lo : span + lo + HEAD_DIM]
        v = qkv[:, 2 * span + lo : 2 * span + lo + HEAD_DIM]
        s = jnp.where(same, dot_nt(q, k) * scale, -1e30)
        e = jnp.exp(s - jnp.max(s, axis=-1, keepdims=True))
        p = e / jnp.sum(e, axis=-1, keepdims=True)
        pg = dot_nt(ag, v)
        vg = dot_tn(p.astype(BF), ag)
        rd = jnp.sum(p * pg, axis=-1, keepdims=True)
        sg = (p * (pg - rd)).astype(BF)
        qg = dot(sg, k) * scale
        kg = dot_tn(sg, q) * scale
        low[:, lo : lo + HEAD_DIM] = turn(qg, cos[...], -sin[...]).astype(BF)
        low[:, span + lo : span + lo + HEAD_DIM] = turn(kg, cos[...], -sin[...]).astype(BF)
        low[:, 2 * span + lo : 2 * span + lo + HEAD_DIM] = vg.astype(BF)


def attention_back_kernel(jobs, count, parts, marks, ready, *refs):
    lens, branch, att, wa, qkv, cos, sin, n1, *refs = refs
    n0, n1s = marks
    g0, came0, g1, came1, refs = refs[0], refs[1 : 1 + n0], refs[1 + n0], refs[2 + n0 : 2 + n0 + n1s], refs[2 + n0 + n1s :]
    pair, last, middle, *refs = refs
    hids, zin, refs = refs[:parts], refs[parts:][: len(jobs.ins)], refs[parts + len(jobs.ins) :]
    low, grads, out_g, *refs = refs
    settled, layer_out, refs = refs[:4], refs[4], refs[5:]
    zout, refs = refs[: len(jobs.outs)], refs[len(jobs.outs) :]
    red, refs = refs[:8], refs[8:]
    bv, wo, ob, yb, load, yl, ls, ss, rs, *talk = refs
    rows, width = bv.shape
    zn, dz, span = wo.shape
    tok = rows // 4
    one = hids[0].shape[1]
    micro, sub, _ = middle.shape
    at = Place()
    cols = low.shape[1]
    downs, chunks = [], chunk_refs(pair, last)
    for k in range(parts):
        place = pl.ds(k * one, one)
        downs.append(pltpu.make_async_copy(hids[k], low.at[:, place], load.at[9 + k]))
        downs.append(
            pltpu.make_async_copy(chunks[k].at[:, :, pl.ds(2 * one, one)], grads.at[:, :, place], load.at[9 + parts + k])
        )
    for copy in downs:
        copy.start()
    weights = pltpu.make_async_copy(wa.at[:, :, pl.ds(cols, span)], wo, load.at[8])
    weights.start()

    def bring(b):
        here = pl.ds(b * tok, tok)
        return (
            pltpu.make_async_copy(branch.at[here], bv.at[here], load.at[b]),
            pltpu.make_async_copy(n1.at[here], red[0].at[b // 2, b % 2], load.at[4 + b]),
        )

    for b in range(4):
        bring(b)[0].start()
    meet(z_partners(zn) + [at.sib, at.xn, at.yn, at.xs])
    wire = Wire(ss, rs)
    host = jobs.host(wire, [zin[0], out_g], zout, talk)
    split = len(chain_results(zn, (0,), 8, 128))
    settles = [
        Settle(wire, at, zn, g0, came0[:split], came0[split:], settled[0], settled[1], yb, yl),
        Settle(wire, at, zn, g1, came1[:split], came1[split:], settled[2], settled[3], yb, yl),
    ]
    host.begin(0)
    for copy in downs:
        copy.wait()
    lows = [low.at[:, pl.ds(k * one, one)] for k in range(parts)]
    total = Reduce(wire, at, red, nt_compute(red[0], lows, [grads] * parts, 0, one))
    for m in range(micro):
        total.cores(m)
        total.diagonal(m)
    settles[0].go()
    weights.wait()
    ready()

    def block(b):
        if b < 2:
            bring(b)[0].wait()
        here = pl.ds(b * tok, tok)
        attention_back_body(
            count, lens, b, bv.at[here], wo, qkv.at[here], cos.at[here], sin.at[here], low.at[here]
        )

    block(0)
    for m in range(micro):
        total.sides(m)
        total.release(m)
    host.next()
    for b in range(4):
        bring(b)[1].start()
    block(1)
    settles[0].wait()
    settles[1].go()
    for b in (2, 3):
        bring(b)[0].wait()

    def output(k, carry):
        here = pl.ds(pl.multiple_of(k * dz, dz), dz)
        out_g[here, :] = dot_tn(bv[:, here], att[...]).astype(BF)
        return carry

    lax.fori_loop(0, zn, output, 0)
    host.begin(1)
    block(2)
    block(3)
    for b in range(4):
        bring(b)[1].wait()

    def weights_of(k, carry):
        here = pl.ds(pl.multiple_of(k * dz, dz), dz)
        acc = 0.0
        for b in range(4):
            acc = acc + dot_tn(red[0][b // 2, b % 2, :, here], low[pl.ds(b * tok, tok), :])
        grads[k] = acc.astype(BF)
        return carry

    lax.fori_loop(0, zn, weights_of, 0)
    deals, step = [], sub // 2
    for m in range(micro):
        total.arrived(m)
        for lo in range(0, sub, step):
            ob[m, lo : lo + step, :] = (middle[m, lo : lo + step, :] + total.total(m, lo, step)).astype(BF)
        deals.append(Deal(wire, at, ob, layer_out, m, ls, m))
        deals[-1].begin()
    settles[1].wait()
    for deal in deals:
        deal.end()
    host.end()
    wire.finish()


def attention_back(count, lens, branch, att, wa, qkv, cos, sin, n1, g0, got0, g1, got1, pair, last, middle, hids, g2, zn):
    rows, width = branch.shape
    cols, span, parts = qkv.shape[1], att.shape[1], len(hids)
    micro, sub, _ = middle.shape
    tok = rows // 4
    dz = width // zn
    out_g = shaped((width, span))
    jobs = Jobs([(g2, (0, 1), ()), (out_g, (0,), ())], zn)
    jobs.ins = [g2]
    half = shaped((dz // 2, g0.shape[1]))
    links = jobs.links + 2 + (REDUCE + 3) * micro
    return kernel(
        functools.partial(attention_back_kernel, jobs, count, parts, (len(got0), len(got1))),
        (lens, branch, att, wa, qkv, cos, sin, n1, g0, *got0, g1, *got1, pair, last, middle, *hids, *jobs.ins),
        [SMEM, ANY, VMEM, ANY, VMEM, VMEM, VMEM, ANY] + [ANY] * (4 + len(got0) + len(got1)) + [VMEM] + [ANY] * (parts + len(jobs.ins)),
        (shaped((rows, cols)), shaped((zn, dz, cols)), out_g, *(half,) * 4, shaped((micro, tok, width // 4)), *jobs.outs),
        (VMEM, VMEM, VMEM) + (ANY,) * (5 + len(jobs.outs)), 70, "attention_back",
        reduce_scratch(micro, tok, sub, width)
        + [pltpu.VMEM((rows, width), BF), pltpu.VMEM((zn, dz, span), BF), pltpu.VMEM((micro, sub, width), BF)]
        + settle_scratch(zn, dz, g0.shape[1])[:1]
        + sems(9 + 2 * parts, zn + 1, micro, links, links) + jobs.scratch,
        talk=9, staged=(2, 4, 5, 6, 12 + len(got0) + len(got1)),
    )


def chunk_body(jobs, c, n2, dy, w, mask, *refs):
    zin, (low, hidden, grad), refs = refs[: len(jobs.ins)], refs[len(jobs.ins) :][:3], refs[len(jobs.ins) + 3 :]
    zout, (nv, dv, wv, load, *talk) = refs[: len(jobs.outs)], refs[len(jobs.outs) :]
    zn, dz, cols = wv.shape
    one = cols // 3
    steps = load.shape[1] - 1
    tile = nv.shape[0] // steps
    whole = pltpu.make_async_copy(w if c is None else w.at[:, c], wv, load.at[0, steps])
    whole.start()

    def bring(t):
        at = pl.ds(pl.multiple_of(t * tile, tile), tile)
        return (
            pltpu.make_async_copy(n2.at[at], nv.at[at], load.at[0, t]),
            pltpu.make_async_copy(dy.at[at], dv.at[at], load.at[1, t]),
        )

    for t in range(steps):
        for copy in bring(t):
            copy.start()
    if talk:
        ss, rs, *talk = talk
        meet(z_partners(jobs.zn))
        host = jobs.host(Wire(ss, rs), zin, zout, talk)
        host.begin()
    whole.wait()

    def forward(t, carry):
        for copy in bring(t):
            copy.wait()
        at = pl.ds(pl.multiple_of(t * tile, tile), tile)
        acc = hg = 0.0
        for k in range(zn):
            acc = acc + dot(nv[at, k * dz : (k + 1) * dz], wv[k, :, : 2 * one])
            hg = hg + dot(dv[at, k * dz : (k + 1) * dz], wv[k, :, 2 * one :])
        hg = hg * mask[...]
        g, u = acc[:, :one], acc[:, one:]
        phi = 0.5 * (1.0 + lax.erf(g * (0.5**0.5)))
        slope = phi + g * jnp.exp(-0.5 * g * g) * 0.3989422804014327
        act = g * phi
        hidden[at, :] = (act * u * mask[...]).astype(BF)
        low[at, :one] = (hg * u * slope).astype(BF)
        low[at, one:] = (hg * act).astype(BF)
        return carry

    lax.fori_loop(0, steps, forward, 0)

    def weights(k, carry):
        at = pl.ds(pl.multiple_of(k * dz, dz), dz)
        grad[at, : 2 * one] = dot_tn(nv[:, at], low[...]).astype(BF)
        grad[at, 2 * one :] = dot_tn(dv[:, at], hidden[...]).astype(BF)
        return carry

    lax.fori_loop(0, zn, weights, 0)
    if jobs.links:
        host.end()


def chunk(n2, dy, w, c, mask, plan, zn, talk, first):
    rows, width = n2.shape
    cols = w.shape[-1]
    one = cols // 3
    jobs = Jobs(plan, zn)
    return kernel(
        functools.partial(chunk_body, jobs, c), (n2, dy, w, mask, *jobs.ins), [ANY, ANY, ANY, VMEM] + [ANY] * len(jobs.ins),
        (shaped((rows, 2 * one)), shaped((rows, one)), shaped((width, cols)), *jobs.outs),
        (VMEM,) * 3 + (ANY,) * len(jobs.outs), 22, "ffn_chunk",
        [pltpu.VMEM((rows, width), BF)] * 2 + [pltpu.VMEM((zn, width // zn, cols), BF), pltpu.SemaphoreType.DMA((2, 5))]
        + (sems(jobs.links, jobs.links) + jobs.scratch if jobs.links else []),
        first, talk=talk if jobs.links else None,
    )


def form_body(parts, *refs):
    halves, (gu, down, qkv, out) = refs[: 2 * parts + 4], refs[2 * parts + 4 :]
    y = lax.axis_index("y")
    one = halves[0].shape[1] // 3

    def pair(k):
        keep, theirs = halves[2 * k][...].astype(F32), halves[2 * k + 1][...].astype(F32)
        return jnp.where(y == 0, keep, theirs), jnp.where(y == 0, theirs, keep)

    half = parts * one
    for k in range(parts):
        for i, v in enumerate(pair(k)):
            lo = i * half + k * one
            gu[0, :, lo : lo + one] = v[:, :one]
            gu[1, :, lo : lo + one] = v[:, one : 2 * one]
            down[lo : lo + one, :] = v[:, 2 * one :].T
    for i, v in enumerate(pair(parts)):
        span = v.shape[1]
        out[i * span : (i + 1) * span, :] = v.T
    for i, v in enumerate(pair(parts + 1)):
        span = v.shape[1] // 3
        for p in range(3):
            qkv[p, :, i * span : (i + 1) * span] = v[:, p * span : (p + 1) * span]


def form(halves, w_gu, w_down, w_qkv, w_out):
    parts = (len(halves) - 4) // 2
    return kernel(
        functools.partial(form_body, parts), halves, [VMEM] * len(halves),
        tuple(shaped(w.shape, F32) for w in (w_gu, w_down, w_qkv, w_out)),
        (VMEM,) * 4, 8, "form",
    )


CHUNKS = 3


def on_device(inputs, lengths, counts, w_qkv, w_out, w_gu, w_down, g1, b1, g2, b2, dy_in):
    z = lax.axis_index("z")
    y = lax.axis_index("y")
    n = lax.axis_index("n")
    zn = lax.axis_size("z")
    micro, tok, feat = inputs.shape
    width = feat * lax.axis_size("n")
    rows = micro * 2 * tok
    depth = w_qkv.shape[1]
    half_slots = w_gu.shape[2] // 2
    one = half_slots // CHUNKS

    def gather_z(w):
        return lax.all_gather(w, "z", axis=0, tiled=False)

    own_attn = swap_attn(w_qkv, w_out)
    wa = gather_z(own_attn)
    vecs = jnp.stack([g1, b1, g2, b2]).astype(F32)
    vecs = jnp.pad(vecs, ((0, 4), (0, 0)))
    count = lengths.shape[2]
    lens = jnp.pad(lengths[:, 0], ((0, 8 - micro), (0, 128 - count)))
    half_dim = HEAD_DIM // 2
    freq = 10000.0 ** (-(jnp.arange(HEAD_DIM) % half_dim).astype(F32) / half_dim)
    x_all, norms, lens, cos, sin, own_01 = gather_x(
        inputs, vecs, lens, freq[None], w_gu, w_down, zn, (0, 1), one, count, (own_attn,)
    )
    norms = norms.transpose(2, 0, 1, 3).reshape(8, width)
    gain1, shift1, gain2, shift2 = (norms[i : i + 1] for i in range(4))
    own = jnp.sum(jnp.where(jnp.arange(counts.shape[0]) == n, counts, 0))
    mask = (y * half_slots + jnp.arange(half_slots) < own).astype(F32)[None]

    d_all, n1, own_2 = gather_d(dy_in, x_all, gain1, shift1, w_gu, w_down, (2,), one)
    dy = d_all.reshape(rows, width)
    qkv, att, own_2 = attention(count, lens, n1, wa, cos, sin, own_2, tok)
    w_01, w_2 = gather_z(own_01), gather_z(own_2)
    middle, n2 = attn_out(att, wa, x_all, gain2, shift2)
    n2 = n2.reshape(rows, width)

    def own_mask(c):
        return mask[:, c * one : (c + 1) * one]

    low0, hid0, g0 = chunk(n2, dy, w_01, 0, own_mask(0), [], zn, None, ())
    low1, hid1, grad1 = chunk(n2, dy, w_01, 1, own_mask(1), [], zn, None, (g0,))
    low2, hid2, grad2, *p = chunk(n2, dy, w_2, None, own_mask(2), [(g0, (0,), ())], zn, 7, (grad1,))
    mid_grad, branch, vec2, *q = ffn_back(
        [low0, low1, low2], w_01, w_2, d_all, middle, gain2, [(grad1, (0, 1), ()), (g0, (1,), p)], zn, ()
    )
    many = len(chain_results(zn, (0, 1), 8, 128))
    got1, got0 = q[:many], p + q[many:]
    branch = branch.reshape(rows, width)
    low, qkv_g, out_g, *r = attention_back(
        count, lens, branch, att, wa, qkv, cos, sin, n1, g0, got0, grad1, got1, w_01, w_2, middle, [hid0, hid1, hid2], grad2, zn
    )
    first, layer_out, got2, gout = r[:4], r[4], r[5 : 5 + many], r[5 + many :]
    in_grad, sums, *r = last_sums(
        low, wa, x_all, mid_grad, gain1, vec2, grad2, got2, out_g, gout, qkv_g.reshape(width, -1), zn
    )
    gu_grad, down_grad, qkv_grad, out_grad = form(
        [*first, *r[:6]], w_gu, w_down, w_qkv, w_out
    )

    mine = lax.dynamic_slice_in_dim(sums, (z * 2 + y) * g1.shape[0], g1.shape[0], 1)
    return (
        layer_out,
        in_grad,
        qkv_grad,
        out_grad,
        gu_grad,
        down_grad,
        mine[0],
        mine[1],
        mine[2],
        mine[3],
    )


def solution(mesh):
    wide, narrow = mesh.shape["wide"], mesh.shape["narrow"]
    grid = Mesh(mesh.devices.reshape(wide // 2, 2, narrow), ("z", "y", "n"))
    w = ("z", "y")
    tokens, depth, lines, vector = P(None, w, "n"), P(None, w, "n"), P("n", w), P(w)
    return jax.shard_map(
        on_device,
        mesh=grid,
        in_specs=(
            tokens, P(None, w, None), P(), depth, lines, depth, lines,
            vector, vector, vector, vector, tokens,
        ),
        out_specs=(
            tokens, tokens, depth, lines, depth, lines, vector, vector, vector, vector,
        ),
        check_vma=False,
    )
```

```python
import functools

import jax
import jax.numpy as jnp
from jax import lax
from jax.experimental import pallas as pl
from jax.experimental.pallas import tpu as pltpu
from jax.sharding import Mesh
from jax.sharding import PartitionSpec as P

HEAD_DIM = 128
EPS = 1e-05
BF = jnp.bfloat16
F32 = jnp.float32
MESH = pl.DeviceIdType.MESH
VMEM_BYTES = 60 * 2**20
SWAP = [(0, 1), (1, 0)]
ANY = pl.BlockSpec(memory_space=pl.ANY)
VMEM = pl.BlockSpec(memory_space=pltpu.VMEM)
SMEM = pl.BlockSpec(memory_space=pltpu.SMEM)


def dot(a, b):
    return jnp.dot(a, b, preferred_element_type=F32)


def dot_nt(a, b):
    return lax.dot_general(a, b, (((1,), (1,)), ((), ())), preferred_element_type=F32)


def dot_tn(a, b):
    return lax.dot_general(a, b, (((0,), (0,)), ((), ())), preferred_element_type=F32)


def normalise(v):
    centred = v - jnp.mean(v, axis=-1, keepdims=True)
    rstd = lax.rsqrt(jnp.mean(centred * centred, axis=-1, keepdims=True) + EPS)
    return centred * rstd, rstd


def norm_back(xhat, rstd, grad, gain):
    dx = grad * gain
    a = jnp.mean(dx, axis=-1, keepdims=True)
    b = jnp.mean(dx * xhat, axis=-1, keepdims=True)
    return rstd * (dx - a - xhat * b)


def cost(us, sent=0):
    return pl.CostEstimate(flops=int(us * 1e9), bytes_accessed=int(us * 3.2e6), transcendentals=0)


def without(body, ins, extra):
    def run(*refs):
        return body(*refs[:ins], *refs[ins + extra :])

    return run


def staged_body(body, ins, staged):
    def run(*refs):
        bufs, sem = refs[-len(staged) - 1 : -1], refs[-1]
        refs = list(refs[: -len(staged) - 1])
        copies = []
        for k, i in enumerate(staged):
            copies.append(pltpu.make_async_copy(refs[i], bufs[k], sem.at[k]))
            copies[-1].start()
            refs[i] = bufs[k]

        def ready():
            for copy in copies:
                copy.wait()

        return body(ready, *refs)

    return run


def kernel(body, ins, in_specs, outs, out_specs, us, name, scratch=(), first=(), grid=(), talk=None, aliases=None, staged=()):
    extra = len(first)
    in_specs, scratch = list(in_specs), list(scratch)
    if staged:
        body = staged_body(body, len(ins), staged)
        for i in staged:
            in_specs[i] = ANY
            scratch.append(pltpu.VMEM(ins[i].shape, ins[i].dtype))
        scratch += sems(len(staged))
    return pl.pallas_call(
        without(body, len(ins), extra),
        grid=grid,
        in_specs=in_specs + [ANY] * extra,
        out_specs=out_specs,
        out_shape=outs,
        scratch_shapes=scratch,
        input_output_aliases=aliases or {},
        compiler_params=pltpu.CompilerParams(
            vmem_limit_bytes=VMEM_BYTES, collective_id=talk, has_side_effects=talk is not None
        ),
        cost_estimate=cost(us),
        name=name,
    )(*ins, *first)


def sems(*counts):
    return [pltpu.SemaphoreType.DMA((k,)) for k in counts]


def shaped(shape, dtype=BF):
    return jax.ShapeDtypeStruct(tuple(shape), dtype)


class Place:
    def __init__(self):
        self.y = lax.axis_index("y")
        self.n = lax.axis_index("n")
        self.x = self.n // 2
        self.c = self.n % 2
        self.ns = self.n + 1 - 2 * self.c
        self.nx = (self.n + 2) % 4
        self.nd = (self.ns + 2) % 4
        self.sib = {"n": self.ns}
        self.xn = {"n": self.nx}
        self.yn = {"y": 1 - self.y}
        self.xs = {"n": self.nd}


def meet(devices):
    barrier = pltpu.get_barrier_semaphore()
    for d in devices:
        pl.semaphore_signal(barrier, inc=1, device_id=d, device_id_type=MESH)
    pl.semaphore_wait(barrier, len(devices))


class Wire:
    def __init__(self, send_sems, recv_sems, first=0):
        self.ss, self.rs, self.at, self.sent = send_sems, recv_sems, first, []

    def make(self, src, dst, device, keep=True, again=False):
        self.at += not again
        k = self.at - 1
        copy = pltpu.make_async_remote_copy(
            src_ref=src, dst_ref=dst, send_sem=self.ss.at[k], recv_sem=self.rs.at[k],
            device_id=device, device_id_type=MESH,
        )
        if keep:
            self.sent.append(copy)
        return copy

    def finish(self):
        for copy in self.sent:
            copy.wait_send()


SPREAD = 9


class Spread:
    def __init__(self, wire, at, src, slot):
        y, n, nx = at.y, at.n, at.nx
        self.first = [
            wire.make(src, slot(y, n, None), at.xn),
            wire.make(src, slot(y, n, None), at.yn),
            wire.make(src, slot(y, n, None), at.sib),
        ]
        self.on_x = [
            wire.make(slot(y, nx, 0), slot(y, nx, 0), at.yn),
            wire.make(slot(y, nx, None), slot(y, nx, None), at.sib),
        ]
        self.on_y = [
            wire.make(slot(1 - y, n, 1), slot(1 - y, n, 1), at.xn),
            wire.make(slot(1 - y, n, None), slot(1 - y, n, None), at.sib),
        ]
        self.last = [
            wire.make(slot(1 - y, nx, 0), slot(1 - y, nx, 0), at.sib),
            wire.make(slot(1 - y, nx, 1), slot(1 - y, nx, 1), at.sib),
        ]

    def begin(self):
        for copy in self.first:
            copy.start()

    def forward(self):
        self.first[0].wait_recv()
        for copy in self.on_x:
            copy.start()
        self.first[1].wait_recv()
        for copy in self.on_y:
            copy.start()

    def forward_last(self):
        self.on_x[0].wait_recv()
        self.last[0].start()
        self.on_y[0].wait_recv()
        self.last[1].start()

    def end(self):
        self.first[2].wait_recv()
        self.on_x[1].wait_recv()
        self.on_y[1].wait_recv()
        self.last[0].wait_recv()
        self.last[1].wait_recv()


REDUCE = 10


def reduce_scratch(micro, tok, sub, width):
    half = sub // 2
    return [
        pltpu.VMEM((micro, 2, tok, width), BF),
        pltpu.VMEM((micro, 2, 2, sub, width), BF),
        pltpu.VMEM((micro, sub, width), BF),
        pltpu.VMEM((micro, sub, width), BF),
        pltpu.VMEM((micro, sub, width), BF),
        pltpu.VMEM((micro, 2, half, width), BF),
        pltpu.VMEM((micro, sub, width), BF),
        pltpu.VMEM((micro, sub, width), BF),
    ]


class Reduce:
    def __init__(self, wire, at, scratch, compute):
        self.part, self.ra, self.sb, self.sx, self.sy, self.rb, self.rcx, self.rcy = scratch
        self.wire, self.at, self.compute = wire, at, compute
        self.micro, self.sub = self.sb.shape[0], self.sb.shape[1]
        self.a, self.b, self.d = {}, {}, {}
        self.released = False

    def rows(self, core, xx, lo=0, size=None):
        return pl.ds(pl.multiple_of((2 * xx + core) * self.sub, self.sub) + lo, size or self.sub)

    def summed(self, m, yy, xx, lo, size):
        mine = self.part[m, yy, self.rows(self.at.c, xx, lo, size), :].astype(F32)
        return mine + self.ra[m, yy, xx, lo : lo + size, :].astype(F32)

    def cores(self, m):
        at = self.at
        for yk, yy in ((1, 1 - at.y), (0, at.y)):
            self.compute(m, yy)
            for xk, xx in ((1, 1 - at.x), (0, at.x)):
                copy = self.wire.make(self.part.at[m, yy, self.rows(1 - at.c, xx)], self.ra.at[m, yy, xx], at.sib)
                copy.start()
                self.a[m, yk, xk] = copy

    def diagonal(self, m):
        at, sub, half = self.at, self.sub, self.sub // 2
        self.a[m, 1, 1].wait_recv()
        self.sb[m] = self.summed(m, 1 - at.y, 1 - at.x, 0, sub).astype(BF)
        self.b[m, 0] = self.wire.make(self.sb.at[m, 0:half], self.rb.at[m, 0], at.xn)
        self.b[m, 1] = self.wire.make(self.sb.at[m, half:sub], self.rb.at[m, 1], at.yn)
        self.b[m, 0].start()
        self.b[m, 1].start()

    def sides(self, m):
        at, sub, half = self.at, self.sub, self.sub // 2
        sx, sy, rb, rcx, rcy = self.sx, self.sy, self.rb, self.rcx, self.rcy
        self.a[m, 1, 0].wait_recv()
        sy[m, half:sub] = self.summed(m, 1 - at.y, at.x, half, half).astype(BF)
        self.d[m, 0] = self.wire.make(sy.at[m, half:sub], rcy.at[m, half:sub], at.yn)
        self.d[m, 0].start()
        self.a[m, 0, 1].wait_recv()
        sx[m, 0:half] = self.summed(m, at.y, 1 - at.x, 0, half).astype(BF)
        self.d[m, 1] = self.wire.make(sx.at[m, 0:half], rcx.at[m, 0:half], at.xn)
        self.d[m, 1].start()
        self.b[m, 0].wait_recv()
        sy[m, 0:half] = (self.summed(m, 1 - at.y, at.x, 0, half) + rb[m, 0].astype(F32)).astype(BF)
        self.d[m, 2] = self.wire.make(sy.at[m, 0:half], rcy.at[m, 0:half], at.yn)
        self.d[m, 2].start()
        self.b[m, 1].wait_recv()
        sx[m, half:sub] = (self.summed(m, at.y, 1 - at.x, half, half) + rb[m, 1].astype(F32)).astype(BF)
        self.d[m, 3] = self.wire.make(sx.at[m, half:sub], rcx.at[m, half:sub], at.xn)
        self.d[m, 3].start()

    def release(self, m):
        at = self.at
        self.a[m, 0, 0].wait_recv()
        self.ra[m, at.y, at.x] = self.summed(m, at.y, at.x, 0, self.sub).astype(BF)
        for yk in (1, 0):
            for xk in (1, 0):
                copy = self.a[m, yk, xk]
                copy.wait_send()
                self.wire.sent = [other for other in self.wire.sent if other is not copy]
        self.released = True

    def arrived(self, m):
        if not self.released:
            self.a[m, 0, 0].wait_recv()
        for k in range(4):
            self.d[m, k].wait_recv()

    def total(self, m, lo, size):
        if self.released:
            own = self.ra[m, self.at.y, self.at.x, lo : lo + size, :].astype(F32)
        else:
            own = self.summed(m, self.at.y, self.at.x, lo, size)
        return own + self.rcx[m, lo : lo + size, :].astype(F32) + self.rcy[m, lo : lo + size, :].astype(F32)


def nothing():
    pass


def reduce_rows(wire, at, scratch, compute, finish, tick=nothing):
    red = Reduce(wire, at, scratch, compute)
    for m in range(red.micro):
        red.cores(m)
        red.diagonal(m)
    tick()
    for m in range(red.micro):
        red.sides(m)
    for m in range(red.micro):
        red.arrived(m)
        finish(m, lambda lo, size, m=m: red.total(m, lo, size))
        tick()


LINE = (
    (0, 3, 1, -1, 0),
    (3, 0, 2, -1, 0),
    (1, 0, 0, 2, 0),
    (2, 3, 3, 2, 0),
    (1, 2, 2, 2, 0),
    (2, 1, 1, 2, 0),
    (0, 2, 2, 0, 1),
    (3, 1, 1, 0, 1),
    (0, 1, 1, 1, 1),
    (3, 2, 2, 1, 1),
)


def chain_results(zn, parts, rows, cols):
    count = 2 * len(parts) if zn == 4 else (zn - 1 if 0 in parts else 0)
    return [shaped((rows, cols))] * count


def chain_links(zn, parts):
    return sum(t[4] in parts for t in LINE) + (1 in parts) if zn == 4 else (zn - 1 if 0 in parts else 0)


class Chain:
    def __init__(self, wire, zn, parts, g, first, second, bufs, load, k):
        z = lax.axis_index("z")
        rows, cols = (first or second)[0].shape
        self.moves, self.bufs, self.cols, self.joins = [], bufs, cols, zn == 4 and 1 in parts
        self.over = False

        def group(i):
            return g.at[pl.ds(pl.multiple_of(i * rows, rows), rows)]

        if zn == 4:
            places = {2: first[0], -1: first[1]}
            if second:
                places.update({0: second[0], 1: second[1]})
            for src, i, dst, place, part in LINE:
                if part in parts:
                    copy = wire.make(group(i), places[place], {"z": dst}, keep=False)
                    self.moves.append((z == src, z == dst, copy, place < 0))
        elif 0 in parts:
            for dz in range(1, zn):
                to = (z + dz) % zn
                self.moves.append((None, None, wire.make(group(to), first[dz - 1], {"z": to}, keep=False), False))
        if self.joins:
            far = 3 * (1 - z // 2)
            here, there = bufs.at[0, :, pl.ds(0, cols)], bufs.at[1, :, pl.ds(0, cols)]
            self.own = pltpu.make_async_copy(group(far), here, load.at[k])
            self.came = pltpu.make_async_copy(first[1], there, load.at[k + 1])
            self.on = wire.make(here, second[1], {"z": far}, keep=False)
            self.inner = jnp.logical_and(z >= 1, z <= 2)
            self.outer = jnp.logical_not(self.inner)

    def begin(self):
        for sends, _, copy, _ in self.moves:
            if sends is None:
                copy.start()
            else:
                pl.when(sends)(copy.start)

    def join(self):
        if not self.joins:
            return

        def run():
            self.own.start()
            self.came.start()
            self.own.wait()
            self.came.wait()
            cols = pl.ds(0, self.cols)
            both = self.bufs[0, :, cols].astype(F32) + self.bufs[1, :, cols].astype(F32)
            self.bufs[0, :, cols] = both.astype(BF)
            self.on.start()

        for _, gets, copy, middle in self.moves:
            if middle:
                pl.when(gets)(copy.wait_recv)
        pl.when(self.inner)(run)

    def settle_sent(self):
        if self.joins:
            pl.when(self.inner)(self.on.wait_send)

    def wait(self):
        self.over = True
        for sends, gets, copy, middle in self.moves:
            if sends is None:
                copy.wait_recv()
                copy.wait_send()
                continue
            if not (middle and self.joins):
                pl.when(gets)(copy.wait_recv)
            pl.when(sends)(copy.wait_send)
        if self.joins:
            pl.when(self.outer)(self.on.wait_recv)


class Host:
    def __init__(self, chains):
        self.chains, self.todo, self.last = chains, list(chains), None

    def begin(self, which=None):
        for k, chain in enumerate(self.chains):
            if which is None or k == which:
                chain.begin()

    def next(self):
        if self.todo:
            if self.last is not None:
                self.last.settle_sent()
            self.last = self.todo.pop(0)
            self.last.join()

    def end(self):
        while self.todo:
            self.next()
        self.last.settle_sent()
        for chain in self.chains:
            if not chain.over:
                chain.wait()


class Settle:
    def __init__(self, wire, at, zn, g, first, second, keep, theirs, bufs, load):
        z = lax.axis_index("z")
        self.rows, self.cols = keep.shape[0] * 2, keep.shape[1]
        rows, half = self.rows, keep.shape[0]
        came = [first[0], second[1], second[0]] if zn == 4 else list(first)
        self.bufs, self.partly = bufs, jnp.logical_and(z >= 1, z <= 2) if zn == 4 else None
        mine = g.at[pl.ds(pl.multiple_of(z * rows, rows), rows)]
        self.loads = [pltpu.make_async_copy(src, bufs.at[k], load.at[k]) for k, src in enumerate([mine] + came)]

        def part(i):
            return bufs.at[0, pl.ds(pl.multiple_of(i * half, half), half)]

        self.away = wire.make(part(1 - at.y), theirs, at.yn, keep=False)
        self.here = pltpu.make_async_copy(part(at.y), keep, load.at[len(self.loads)])

    def go(self):
        always = self.loads if self.partly is None else self.loads[:-1]
        for copy in always:
            copy.start()
        if self.partly is not None:
            k = len(always)
            pl.when(self.partly)(self.loads[k].start)
            pl.when(self.partly)(self.loads[k].wait)

            def none():
                self.bufs[k] = jnp.zeros((self.rows, self.cols), BF)

            pl.when(jnp.logical_not(self.partly))(none)
        for copy in always:
            copy.wait()
        total = self.bufs[0].astype(F32)
        for k in range(1, len(self.loads)):
            total = total + self.bufs[k].astype(F32)
        self.bufs[0] = total.astype(BF)
        self.away.start()
        self.here.start()

    def wait(self):
        self.away.wait_recv()
        self.away.wait_send()
        self.here.wait()


def settle_scratch(zn, rows, cols):
    return [pltpu.VMEM((zn, rows, cols), BF)] + sems(zn + 1)


def z_partners(zn):
    z = lax.axis_index("z")
    return [{"z": (z + dz) % zn} for dz in range(1, zn)]


class Jobs:
    def __init__(self, plan, zn):
        self.plan, self.zn = plan, zn
        self.ins, self.outs, self.links = [], [], 0
        for g, parts, given in plan:
            self.ins += [g] + list(given)
            self.outs += chain_results(zn, parts, g.shape[0] // zn, g.shape[1])
            self.links += chain_links(zn, parts)
        wide = max([p[0].shape[1] for p in plan], default=0)
        rows = plan[0][0].shape[0] // zn if plan else 0
        self.scratch = [pltpu.VMEM((2, rows, wide), BF)] + sems(2 * len(plan)) if plan else []

    def host(self, wire, ins, outs, scratch):
        chains, i, o = [], 0, 0
        for k, (g, parts, given) in enumerate(self.plan):
            count = len(chain_results(self.zn, parts, 8, 128))
            made = outs[o : o + count]
            first = ins[i + 1 : i + 1 + len(given)] if given else (made if 1 not in parts or self.zn != 4 else made[:2])
            second = [] if 1 not in parts or self.zn != 4 else made[-2:]
            chains.append(Chain(wire, self.zn, parts, ins[i], first, second, *scratch, 2 * k))
            i, o = i + 1 + len(given), o + count
        return Host(chains)


def blockwise(part, m, yy, fn, tile=256):
    tok = part.shape[2]

    def step(i, carry):
        lo = pl.multiple_of(i * tile, tile)
        fn(lo, tile)
        return carry

    lax.fori_loop(0, tok // tile, step, 0)


def token_spreads(wire, at, src, out, sem, first, cut):
    micro, tok, feat = src.shape
    spreads, local = [], []
    for m in range(micro):

        def slot(yy, nn, part, m=m):
            lo, size = {None: (0, tok), 0: (0, cut), 1: (cut, tok - cut)}[part]
            return out.at[m, yy, pl.ds(lo, size), pl.ds(pl.multiple_of(nn * feat, feat), feat)]

        spreads.append(Spread(wire, at, src.at[m], slot))
        local.append(pltpu.make_async_copy(src.at[m], slot(at.y, at.n, None), sem.at[first + m]))
    return spreads, local


def attn_cut(w_qkv, w_out, i, buf):
    parts, _, cols = w_qkv.shape
    half = cols // 2
    at = pl.ds(pl.multiple_of(i * half, half), half)
    for p in range(parts):
        buf[:, p * half : (p + 1) * half] = w_qkv[p, :, at]
    buf[:, parts * half :] = w_out[at, :].astype(F32).T.astype(BF)


def chunk_cut(w_gu, w_down, i, c, one, buf):
    half = w_gu.shape[2] // 2
    at = pl.ds(pl.multiple_of(i * half, half) + c * one, one)
    buf[:, :one] = w_gu[0, :, at]
    buf[:, one : 2 * one] = w_gu[1, :, at]
    buf[:, 2 * one :] = w_down[at, :].astype(F32).T.astype(BF)


class Swap:
    def __init__(self, wire, at, bufs, out, sem):
        depth = bufs.shape[1]
        place = out.at[pl.ds(pl.multiple_of(at.y * depth, depth), depth)]
        self.away = wire.make(bufs.at[0], place, at.yn)
        self.here = pltpu.make_async_copy(bufs.at[1], place, sem)

    def end(self):
        self.away.wait_recv()
        self.here.wait()


def swap_attn_kernel(w_qkv, w_out, out, bufs, ss, rs, ls):
    at = Place()
    meet([at.yn])
    wire = Wire(ss, rs)
    swap = Swap(wire, at, bufs, out, ls.at[0])
    attn_cut(w_qkv, w_out, 1 - at.y, bufs.at[0])
    swap.away.start()
    attn_cut(w_qkv, w_out, at.y, bufs.at[1])
    swap.here.start()
    swap.end()
    wire.finish()


def swap_attn(w_qkv, w_out):
    parts, depth, cols = w_qkv.shape
    size = (parts + 1) * cols // 2
    return kernel(
        swap_attn_kernel, (w_qkv, w_out), [VMEM, VMEM], shaped((2 * depth, size)), ANY, 14, "swap_attn",
        [pltpu.VMEM((2, depth, size), BF)] + sems(1, 1, 1), talk=6,
    )


def swap_chunks(wire, at, w_gu, w_down, which, one, bufs, outs, ls):
    swaps = []
    for k, (c, out) in enumerate(zip(which, outs)):
        swap = Swap(wire, at, bufs.at[k], out, ls.at[k])
        chunk_cut(w_gu, w_down, 1 - at.y, c, one, bufs.at[k, 0])
        swap.away.start()
        chunk_cut(w_gu, w_down, at.y, c, one, bufs.at[k, 1])
        swap.here.start()
        swaps.append(swap)
    return swaps


def gather_x_kernel(zn, which, count, x_in, v_in, lens, freq, w_gu, w_down, x_out, v_out, lens_all, cos, sin, own, *scratch):
    bufs, ss, rs, ls = scratch
    at = Place()
    z = lax.axis_index("z")
    one = own.shape[2] // 3
    ring = [(dz, dy) for dz in range(zn) for dy in range(2) if dz or dy]
    others = [{"z": (z + dz) % zn, "y": (at.y + dy) % 2} for dz, dy in ring]
    meet([at.sib, at.xn] + others)
    wire = Wire(ss, rs)
    there = wire.make(lens, lens_all.at[at.y], at.yn)
    there.start()
    spreads, local = token_spreads(wire, at, x_in, x_out, ls, len(which) + 1, x_in.shape[1] // 8)
    local.append(pltpu.make_async_copy(v_in, v_out.at[z, at.y], ls.at[len(which)]))
    small = [wire.make(v_in, v_out.at[z, at.y], d) for d in others]
    for s in spreads:
        s.begin()
    for copy in small + local:
        copy.start()
    swaps = swap_chunks(wire, at, w_gu, w_down, which, one, bufs, [own.at[k] for k in range(len(which))], ls)
    lens_all[at.y] = lens[...]
    there.wait_recv()
    tok = x_in.shape[1]
    row = lax.broadcasted_iota(jnp.int32, (tok, 1), 0)
    flip = jnp.where(lax.broadcasted_iota(jnp.int32, (1, HEAD_DIM), 1) < HEAD_DIM // 2, -1.0, 1.0)

    def table(b, carry):
        m, yy = b // 2, b % 2
        line = lens_all[yy, pl.ds(m, 1), :]
        end = jnp.zeros((1, 1), jnp.int32)
        start = jnp.zeros_like(row)
        for k in range(count):
            end = end + line[:, k : k + 1]
            start = jnp.where(row >= end, end, start)
        angle = (row - start).astype(F32) * freq[...]
        place = pl.ds(pl.multiple_of(b * tok, tok), tok)
        cos[place, :] = jnp.cos(angle)
        sin[place, :] = jnp.sin(angle) * flip
        return carry

    lax.fori_loop(0, x_in.shape[0] * 2, table, 0)
    run_spreads(spreads, local)
    for copy in small:
        copy.wait_recv()
    for swap in swaps:
        swap.end()
    wire.finish()


def gather_x(x, v, lens, freq, w_gu, w_down, zn, which, one, count, first):
    micro, tok, feat = x.shape
    depth = w_gu.shape[1]
    rows = micro * 2 * tok
    links = SPREAD * micro + 2 * zn - 1 + len(which) + 1
    return kernel(
        functools.partial(gather_x_kernel, zn, which, count), (x, v, lens, freq, w_gu, w_down),
        [ANY, ANY, VMEM, VMEM, VMEM, VMEM],
        (
            shaped((micro, 2, tok, 4 * feat)), shaped((zn, 2) + v.shape, F32), shaped((2,) + lens.shape, jnp.int32),
            shaped((rows, HEAD_DIM), F32), shaped((rows, HEAD_DIM), F32), shaped((len(which), 2 * depth, 3 * one)),
        ),
        (ANY, ANY, VMEM, VMEM, VMEM, ANY), 48, "gather_x",
        [pltpu.VMEM((len(which), 2, depth, 3 * one), BF)] + sems(links, links, micro + 1 + len(which)),
        first, talk=0,
    )


def gather_d_kernel(which, one, d_in, x_all, gain, shift, w_gu, w_down, d_out, n1, *refs):
    outs, (bufs, xin, nout, ss, rs, ls, load) = refs[: len(which)], refs[len(which) :]
    at = Place()
    micro, _, tok, _ = x_all.shape
    meet([at.sib, at.xn, at.yn])
    wire = Wire(ss, rs)
    spreads, local = token_spreads(wire, at, d_in, d_out, ls, len(which), d_in.shape[1] // 16 * 5)

    def bring(b):
        return pltpu.make_async_copy(x_all.at[b // 2, b % 2], xin.at[b % 2], load.at[b])

    def put(b):
        return pltpu.make_async_copy(nout.at[b % 2], n1.at[pl.ds(b * tok, tok)], load.at[2 * micro + b])

    bring(0).start()
    bring(1).start()
    for s in spreads:
        s.begin()
    for copy in local:
        copy.start()
    swaps = swap_chunks(wire, at, w_gu, w_down, which, one, bufs, outs, ls)
    for b in range(2 * micro):
        bring(b).wait()
        if b >= 2:
            put(b - 2).wait()

        def tile(i, carry, b=b):
            place = pl.ds(pl.multiple_of(i * 128, 128), 128)
            xhat, _ = normalise(xin[b % 2, place, :].astype(F32))
            nout[b % 2, place, :] = (xhat * gain[...] + shift[...]).astype(BF)
            return carry

        lax.fori_loop(0, tok // 128, tile, 0)
        put(b).start()
        if b + 2 < 2 * micro:
            bring(b + 2).start()
        if b % 2:
            spreads[b // 2].forward()
    put(2 * micro - 2).wait()
    put(2 * micro - 1).wait()
    for s in spreads:
        s.forward_last()
    for s in spreads:
        s.end()
    for copy in local:
        copy.wait()
    for swap in swaps:
        swap.end()
    wire.finish()


def gather_d(d, x_all, gain, shift, w_gu, w_down, which, one):
    micro, tok, feat = d.shape
    depth = w_gu.shape[1]
    count = SPREAD * micro + len(which)
    return kernel(
        functools.partial(gather_d_kernel, which, one), (d, x_all, gain, shift, w_gu, w_down),
        [ANY, ANY, VMEM, VMEM, VMEM, VMEM],
        (shaped((micro, 2, tok, 4 * feat)), shaped((micro * 2 * tok, 4 * feat))) + (shaped((2 * depth, 3 * one)),) * len(which),
        (ANY,) * (2 + len(which)), 48, "gather_d",
        [pltpu.VMEM((len(which), 2, depth, 3 * one), BF)] + [pltpu.VMEM((2, tok, 4 * feat), BF)] * 2
        + sems(count, count, micro + len(which), 4 * micro),
        talk=5,
    )


def row_slot(out, m, sub):
    half = sub // 2

    def slot(yy, nn, part):
        ref = out.at[m, yy, nn]
        return ref if part is None else ref.at[pl.ds(part * half, half)]

    return slot


def run_spreads(spreads, local, tick=nothing):
    for s in spreads:
        s.forward()
    tick()
    for s in spreads:
        s.forward_last()
    for s in spreads:
        s.end()
    for copy in local:
        copy.wait()


def attn_out_kernel(att, wo, x_all, gain, shift, middle, n2, *scratch):
    *red, xb, nb, ss, rs, ls = scratch
    at = Place()
    micro, sub, width = middle.shape
    zn, dz, cols = wo.shape
    span = att.shape[1]
    tok = red[0].shape[2]
    meet([at.sib, at.xn, at.yn])
    wire = Wire(ss, rs)
    own = [pltpu.make_async_copy(x_all.at[m, at.y, pl.ds(at.n * sub, sub)], xb.at[m], ls.at[m]) for m in range(micro)]
    for copy in own:
        copy.start()

    def compute(m, yy):
        def tile(lo, size):
            a = att[pl.ds(pl.multiple_of((m * 2 + yy) * tok, tok) + lo, size), :]
            for k in range(zn):
                red[0][m, yy, pl.ds(lo, size), k * dz : (k + 1) * dz] = dot_nt(a, wo[k, :, cols - span :]).astype(BF)

        blockwise(red[0], m, yy, tile)

    spreads, local = [], []

    def finish(m, total):
        own[m].wait()
        step = sub // 2
        for lo in range(0, sub, step):
            mid = xb[m, lo : lo + step, :].astype(F32) + total(lo, step)
            middle[m, lo : lo + step, :] = mid
            xhat, _ = normalise(mid)
            nb[m, lo : lo + step, :] = (xhat * gain[...] + shift[...]).astype(BF)
        slot = row_slot(n2, m, sub)
        spreads.append(Spread(wire, at, nb.at[m], slot))
        spreads[-1].begin()
        local.append(pltpu.make_async_copy(nb.at[m], slot(at.y, at.n, None), ls.at[micro + m]))
        local[-1].start()

    reduce_rows(wire, at, red, compute, finish)
    run_spreads(spreads, local)
    wire.finish()


def attn_out(att, wo, x_all, gain, shift):
    micro, _, tok, width = x_all.shape
    sub = tok // 4
    count = (REDUCE + SPREAD) * micro
    return kernel(
        attn_out_kernel, (att, wo, x_all, gain, shift), [VMEM, VMEM, ANY, VMEM, VMEM],
        (shaped((micro, sub, width), F32), shaped((micro, 2, 4, sub, width))), (VMEM, ANY), 85, "attn_out",
        reduce_scratch(micro, tok, sub, width) + [pltpu.VMEM((micro, sub, width), BF)] * 2 + sems(count, count, 2 * micro),
        talk=1,
    )


def nt_compute(part, lows, ws, first, each=0):
    zn, dz, _ = ws[0].shape
    tok = part.shape[2]
    span = lows[0].shape[1]

    def compute(m, yy):
        def tile(lo, size):
            at = pl.multiple_of((m * 2 + yy) * tok, tok) + lo
            for k in range(zn):
                acc = None
                for i, (low, w) in enumerate(zip(lows, ws)):
                    lo_col = first + i * each
                    term = dot_nt(low[pl.ds(at, size), :], w[k, :, lo_col : lo_col + span])
                    acc = term if acc is None else acc + term
                part[m, yy, pl.ds(lo, size), k * dz : (k + 1) * dz] = acc.astype(BF)

        blockwise(part, m, yy, tile)

    return compute


class Columns:
    def __init__(self, groups, cols, bufs, load):
        self.copies = [
            pltpu.make_async_copy(src.at[:, :, cols], bufs.at[k], load.at[k]) for k, src in enumerate(groups)
        ]
        for copy in self.copies:
            copy.start()

    def wait(self):
        for copy in self.copies:
            copy.wait()


def chunk_refs(pair, last):
    return [pair.at[:, k] for k in range(pair.shape[1])] + [last]


def ffn_back_kernel(jobs, parts, ready, *refs):
    guls = refs[:parts]
    pair, last, d_all, middle, gain, *refs = refs[parts:]
    zin, (mid_grad, branch, vec), refs = refs[: len(jobs.ins)], refs[len(jobs.ins) :][:3], refs[len(jobs.ins) + 3 :]
    zout, refs = refs[: len(jobs.outs)], refs[len(jobs.outs) :]
    *red, db, nb, wv, ss, rs, ls, lw, zb, zl = refs
    at = Place()
    micro, sub, width = middle.shape
    span = guls[0].shape[1]
    weights = Columns(chunk_refs(pair, last), pl.ds(0, span), wv, lw)
    own = [pltpu.make_async_copy(d_all.at[m, at.y, pl.ds(at.n * sub, sub)], db.at[m], ls.at[m]) for m in range(micro)]
    for copy in own:
        copy.start()
    meet([at.sib, at.xn, at.yn] + z_partners(jobs.zn))
    wire = Wire(ss, rs)
    host = jobs.host(wire, zin, zout, (zb, zl))
    host.begin()
    vec[...] = jnp.zeros_like(vec)
    spreads, local = [], []

    def finish(m, total):
        own[m].wait()
        step = sub // 2
        for lo in range(0, sub, step):
            grad = total(lo, step)
            xhat, rstd = normalise(middle[m, lo : lo + step, :])
            vec[0:1, :] += jnp.sum(grad * xhat, axis=0, keepdims=True)
            vec[1:2, :] += jnp.sum(grad, axis=0, keepdims=True)
            mg = db[m, lo : lo + step, :].astype(F32) + norm_back(xhat, rstd, grad, gain[...])
            mid_grad[m, lo : lo + step, :] = mg
            nb[m, lo : lo + step, :] = mg.astype(BF)
        slot = row_slot(branch, m, sub)
        spreads.append(Spread(wire, at, nb.at[m], slot))
        spreads[-1].begin()
        local.append(pltpu.make_async_copy(nb.at[m], slot(at.y, at.n, None), ls.at[micro + m]))
        local[-1].start()

    weights.wait()
    ready()
    reduce_rows(wire, at, red, nt_compute(red[0], guls, [wv.at[k] for k in range(parts)], 0), finish, host.next)
    run_spreads(spreads, local, host.next)
    host.end()
    wire.finish()


def ffn_back(guls, pair, last, d_all, middle, gain, plan, zn, first):
    parts = len(guls)
    micro, _, tok, width = d_all.shape
    sub = tok // 4
    jobs = Jobs(plan, zn)
    count = (REDUCE + SPREAD) * micro + jobs.links
    span = guls[0].shape[1]
    return kernel(
        functools.partial(ffn_back_kernel, jobs, parts), (*guls, pair, last, d_all, middle, gain, *jobs.ins),
        [VMEM] * parts + [ANY, ANY, ANY, VMEM, VMEM] + [ANY] * len(jobs.ins),
        (shaped((micro, sub, width), F32), shaped((micro, 2, 4, sub, width)), shaped((8, width), F32), *jobs.outs),
        (VMEM, ANY, VMEM) + (ANY,) * len(jobs.outs), 90, "ffn_back",
        reduce_scratch(micro, tok, sub, width) + [pltpu.VMEM((micro, sub, width), BF)] * 2
        + [pltpu.VMEM((parts, zn, width // zn, span), BF)] + sems(count, count, 2 * micro, parts) + jobs.scratch,
        first, talk=2, staged=(*range(parts), parts + 3),
    )


def host_kernel(jobs, *refs):
    zin, zout, (ss, rs, zb, zl) = refs[: len(jobs.ins)], refs[len(jobs.ins) :][: len(jobs.outs)], refs[-4:]
    meet(z_partners(jobs.zn))
    host = jobs.host(Wire(ss, rs), zin, zout, (zb, zl))
    host.begin()
    host.end()


def host_only(plan, zn, first):
    jobs = Jobs(plan, zn)
    return kernel(
        functools.partial(host_kernel, jobs), jobs.ins, [ANY] * len(jobs.ins), tuple(jobs.outs), (ANY,) * len(jobs.outs),
        20 * jobs.steps, "along_z", sems(2 * jobs.steps, 2 * jobs.steps) + jobs.scratch, first, talk=8,
    )


class Deal:
    def __init__(self, wire, at, rows, out, m, sems, k):
        sub, width = rows.shape[1], rows.shape[2]
        feat = width // 4

        def cols(nn):
            return rows.at[m, :, pl.ds(pl.multiple_of(nn * feat, feat), feat)]

        place = out.at[m, pl.ds(pl.multiple_of(at.n * sub, sub), sub)]
        self.local = pltpu.make_async_copy(cols(at.n), place, sems.at[k])
        self.copies = [
            wire.make(cols(at.nx), place, at.xn),
            wire.make(cols(at.nd), place, at.xs),
            wire.make(cols(at.ns), place, at.sib),
        ]

    def begin(self):
        for copy in self.copies:
            copy.start()
        self.local.start()

    def end(self):
        for copy in self.copies:
            copy.wait_recv()
        self.local.wait()


def last_kernel(jobs, zn, marks, ready, *refs):
    low, wa, x_all, mid_grad, gain, vec2, *refs = refs
    g2, came2, refs = refs[0], refs[1 : 1 + marks], refs[1 + marks :]
    zin, refs = refs[: len(jobs.ins)], refs[len(jobs.ins) :]
    in_grad, sums, *refs = refs
    settled, zout, refs = refs[:6], refs[6:][: len(jobs.outs)], refs[6 + len(jobs.outs) :]
    red, refs = refs[:8], refs[8:]
    xb, ob, w1, mine, plane, summed, lines, yb2, ybo, ybq, yl2, ylo, ylq, ss, rs, ls, *talk = refs
    at = Place()
    z = lax.axis_index("z")
    micro, sub, width = mid_grad.shape
    qkv = pltpu.make_async_copy(wa.at[:, :, pl.ds(0, low.shape[1])], w1, ls.at[2 * micro])
    qkv.start()
    own = [pltpu.make_async_copy(x_all.at[m, at.y, pl.ds(at.n * sub, sub)], xb.at[m], ls.at[m]) for m in range(micro)]
    for copy in own:
        copy.start()
    flips = [(dy, dn) for dy in range(2) for dn in range(4) if dy or dn]
    peers = [{"y": (at.y + dy) % 2, "n": (at.n + dn) % 4} for dy, dn in flips]
    along = [{"z": (z + dz) % zn} for dz in range(1, zn)]
    meet(peers + along)
    wire = Wire(ss, rs)
    host = jobs.host(wire, zin, zout, talk)
    host.begin()
    split = len(chain_results(zn, (0,), 8, 128))
    settles = [
        Settle(wire, at, zn, g2, came2[:split], came2[split:], settled[0], settled[1], yb2, yl2),
        Settle(wire, at, zn, zin[1], zin[2:], zout[marks:], settled[2], settled[3], ybo, ylo),
        Settle(wire, at, zn, zin[0], zout[:split], zout[split:marks], settled[4], settled[5], ybq, ylq),
    ]
    mine[...] = jnp.zeros_like(mine)
    mine[2:4] = vec2[0:2]
    qkv.wait()
    ready()
    total = Reduce(wire, at, red, nt_compute(red[0], [low], [w1], 0))
    for m in range(micro):
        total.cores(m)
        total.diagonal(m)
    for m in range(micro):
        total.sides(m)
    host.next()
    step = sub // 2
    deals = []
    for m in range(micro):
        total.arrived(m)
        own[m].wait()
        for lo in range(0, sub, step):
            grad = total.total(m, lo, step)
            xhat, rstd = normalise(xb[m, lo : lo + step, :].astype(F32))
            mine[0:1, :] += jnp.sum(grad * xhat, axis=0, keepdims=True)
            mine[1:2, :] += jnp.sum(grad, axis=0, keepdims=True)
            back = norm_back(xhat, rstd, grad, gain[...])
            ob[m, lo : lo + step, :] = (mid_grad[m, lo : lo + step, :] + back).astype(BF)
        deals.append(Deal(wire, at, ob, in_grad, m, ls, micro + m))
        deals[-1].begin()
        if m == 0:
            settles[0].go()
    host.next()
    near = [wire.make(mine, plane.at[k], d) for k, d in enumerate(peers)]
    for copy in near:
        copy.start()
    host.chains[0].wait()
    settles[2].go()
    for copy in near:
        copy.wait_recv()
    both = mine[...]
    for k in range(len(peers)):
        both = both + plane[k]
    summed[...] = both
    far = [wire.make(summed, lines.at[k], d) for k, d in enumerate(along)]
    for copy in far:
        copy.start()
    host.end()
    settles[1].go()
    for copy in far:
        copy.wait_recv()
    both = summed[...]
    for k in range(len(along)):
        both = both + lines[k]
    sums[...] = both
    for deal in deals:
        deal.end()
    for settle in settles:
        settle.wait()
    wire.finish()


def last_sums(low, wa, x_all, mid_grad, gain, vec2, g2, got2, out_g, gout, qkv_g, zn):
    micro, _, tok, width = x_all.shape
    sub = tok // 4
    dz, cols = width // zn, low.shape[1]
    jobs = Jobs([(qkv_g, (0, 1), ()), (out_g, (1,), gout)], zn)
    count = (REDUCE + 3) * micro + 7 + zn - 1 + jobs.links + 3
    size = vec2.shape
    rows = pltpu.VMEM((micro, sub, width), BF)
    sizes = (g2.shape[1], out_g.shape[1], cols)
    halves = [shaped((dz // 2, k)) for k in sizes for _ in range(2)]
    return kernel(
        functools.partial(last_kernel, jobs, zn, len(got2)),
        (low, wa, x_all, mid_grad, gain, vec2, g2, *got2, *jobs.ins),
        [VMEM, ANY, ANY, VMEM, VMEM, VMEM] + [ANY] * (1 + len(got2) + len(jobs.ins)),
        (shaped((micro, tok, width // 4)), shaped(size, F32), *halves, *jobs.outs),
        (ANY, VMEM) + (ANY,) * (6 + len(jobs.outs)), 100, "last_sums",
        reduce_scratch(micro, tok, sub, width) + [rows] * 2 + [pltpu.VMEM((zn, dz, cols), BF)]
        + [pltpu.VMEM(size, F32), pltpu.VMEM((7,) + size, F32), pltpu.VMEM(size, F32), pltpu.VMEM((zn - 1,) + size, F32)]
        + [pltpu.VMEM((zn, dz, k), BF) for k in sizes] + sems(zn + 1, zn + 1, zn + 1, count, count, 2 * micro + 1) + jobs.scratch,
        talk=3, staged=(0, 3),
    )


def tiles(rows, cols):
    return pl.BlockSpec((rows, cols), lambda i: (i, 0))


def same_protein(lens, b, tok, count):
    col = lax.broadcasted_iota(jnp.int32, (tok, 1), 0)
    row = lax.broadcasted_iota(jnp.int32, (1, tok), 1)
    pc, pr = jnp.zeros_like(col), jnp.zeros_like(row)
    end = jnp.int32(0)
    for k in range(count):
        end = end + lens[b % 2, b // 2, k]
        pc = pc + (col >= end).astype(jnp.int32)
        pr = pr + (row >= end).astype(jnp.int32)
    return pc == pr


def turn(v, cos, sin):
    return v * cos + pltpu.roll(v, HEAD_DIM // 2, 1) * sin


def attention_body(count, ends, n1, w, cos, sin, qkv, att):
    zn, dz, _ = w.shape
    cols = qkv.shape[1]
    tok = n1.shape[0]
    heads = cols // 3 // HEAD_DIM
    span = heads * HEAD_DIM
    acc = dot(n1[:, 0:dz], w[0, :, :cols])
    for k in range(1, zn):
        acc = acc + dot(n1[:, k * dz : (k + 1) * dz], w[k, :, :cols])
    same = same_protein(ends, pl.program_id(0), tok, count)
    scale = HEAD_DIM ** (-0.5)
    for h in range(heads):
        lo = h * HEAD_DIM
        q = turn(acc[:, lo : lo + HEAD_DIM], cos[...], sin[...]).astype(BF)
        k = turn(acc[:, span + lo : span + lo + HEAD_DIM], cos[...], sin[...]).astype(BF)
        v = acc[:, 2 * span + lo : 2 * span + lo + HEAD_DIM].astype(BF)
        qkv[:, lo : lo + HEAD_DIM] = q
        qkv[:, span + lo : span + lo + HEAD_DIM] = k
        qkv[:, 2 * span + lo : 2 * span + lo + HEAD_DIM] = v
        s = jnp.where(same, dot_nt(q, k) * scale, -1e30)
        e = jnp.exp(s - jnp.max(s, axis=-1, keepdims=True))
        p = (e / jnp.sum(e, axis=-1, keepdims=True)).astype(BF)
        att[:, lo : lo + HEAD_DIM] = dot(p, v).astype(BF)


def attention(count, ends, n1, w, cos, sin, passed, tok):
    rows, width = n1.shape
    cols = w.shape[2] // 4 * 3

    def body(e, a, b, c, d, _, qkv, att, __):
        attention_body(count, e, a, b, c, d, qkv, att)

    return kernel(
        body, (ends, n1, w, cos, sin, passed),
        [SMEM, tiles(tok, width), VMEM, tiles(tok, HEAD_DIM), tiles(tok, HEAD_DIM), ANY],
        (shaped((rows, cols)), shaped((rows, cols // 3)), shaped(passed.shape)),
        (tiles(tok, cols), tiles(tok, cols // 3), ANY), 20, "attention", grid=(rows // tok,), aliases={5: 2},
    )


def attention_back_body(count, ends, b, branch, wo, qkv, cos, sin, low):
    zn, dz, span = wo.shape
    tok = branch.shape[0]
    heads = span // HEAD_DIM
    acc = dot(branch[:, 0:dz], wo[0])
    for k in range(1, zn):
        acc = acc + dot(branch[:, k * dz : (k + 1) * dz], wo[k])
    same = same_protein(ends, b, tok, count)
    scale = HEAD_DIM ** (-0.5)
    for h in range(heads):
        lo = h * HEAD_DIM
        ag = acc[:, lo : lo + HEAD_DIM].astype(BF)
        q = qkv[:, lo : lo + HEAD_DIM]
        k = qkv[:, span + lo : span + lo + HEAD_DIM]
        v = qkv[:, 2 * span + lo : 2 * span + lo + HEAD_DIM]
        s = jnp.where(same, dot_nt(q, k) * scale, -1e30)
        e = jnp.exp(s - jnp.max(s, axis=-1, keepdims=True))
        p = e / jnp.sum(e, axis=-1, keepdims=True)
        pg = dot_nt(ag, v)
        vg = dot_tn(p.astype(BF), ag)
        rd = jnp.sum(p * pg, axis=-1, keepdims=True)
        sg = (p * (pg - rd)).astype(BF)
        qg = dot(sg, k) * scale
        kg = dot_tn(sg, q) * scale
        low[:, lo : lo + HEAD_DIM] = turn(qg, cos[...], -sin[...]).astype(BF)
        low[:, span + lo : span + lo + HEAD_DIM] = turn(kg, cos[...], -sin[...]).astype(BF)
        low[:, 2 * span + lo : 2 * span + lo + HEAD_DIM] = vg.astype(BF)


def attention_back_kernel(jobs, count, parts, marks, ready, *refs):
    lens, branch, att, wa, qkv, cos, sin, n1, *refs = refs
    n0, n1s = marks
    g0, came0, g1, came1, refs = refs[0], refs[1 : 1 + n0], refs[1 + n0], refs[2 + n0 : 2 + n0 + n1s], refs[2 + n0 + n1s :]
    pair, last, middle, *refs = refs
    hids, zin, refs = refs[:parts], refs[parts:][: len(jobs.ins)], refs[parts + len(jobs.ins) :]
    low, grads, out_g, *refs = refs
    settled, layer_out, refs = refs[:4], refs[4], refs[5:]
    zout, refs = refs[: len(jobs.outs)], refs[len(jobs.outs) :]
    red, refs = refs[:8], refs[8:]
    bv, wo, ob, yb, load, yl, ls, ss, rs, *talk = refs
    rows, width = bv.shape
    zn, dz, span = wo.shape
    tok = rows // 4
    one = hids[0].shape[1]
    micro, sub, _ = middle.shape
    at = Place()
    cols = low.shape[1]
    downs, chunks = [], chunk_refs(pair, last)
    for k in range(parts):
        place = pl.ds(k * one, one)
        downs.append(pltpu.make_async_copy(hids[k], low.at[:, place], load.at[9 + k]))
        downs.append(
            pltpu.make_async_copy(chunks[k].at[:, :, pl.ds(2 * one, one)], grads.at[:, :, place], load.at[9 + parts + k])
        )
    for copy in downs:
        copy.start()
    weights = pltpu.make_async_copy(wa.at[:, :, pl.ds(cols, span)], wo, load.at[8])
    weights.start()

    def bring(b):
        here = pl.ds(b * tok, tok)
        return (
            pltpu.make_async_copy(branch.at[here], bv.at[here], load.at[b]),
            pltpu.make_async_copy(n1.at[here], red[0].at[b // 2, b % 2], load.at[4 + b]),
        )

    for b in range(4):
        bring(b)[0].start()
    meet(z_partners(zn) + [at.sib, at.xn, at.yn, at.xs])
    wire = Wire(ss, rs)
    host = jobs.host(wire, [zin[0], out_g], zout, talk)
    split = len(chain_results(zn, (0,), 8, 128))
    settles = [
        Settle(wire, at, zn, g0, came0[:split], came0[split:], settled[0], settled[1], yb, yl),
        Settle(wire, at, zn, g1, came1[:split], came1[split:], settled[2], settled[3], yb, yl),
    ]
    host.begin(0)
    for copy in downs:
        copy.wait()
    lows = [low.at[:, pl.ds(k * one, one)] for k in range(parts)]
    total = Reduce(wire, at, red, nt_compute(red[0], lows, [grads] * parts, 0, one))
    for m in range(micro):
        total.cores(m)
        total.diagonal(m)
    settles[0].go()
    weights.wait()
    ready()

    def block(b):
        if b < 2:
            bring(b)[0].wait()
        here = pl.ds(b * tok, tok)
        attention_back_body(
            count, lens, b, bv.at[here], wo, qkv.at[here], cos.at[here], sin.at[here], low.at[here]
        )

    block(0)
    for m in range(micro):
        total.sides(m)
        total.release(m)
    host.next()
    for b in range(4):
        bring(b)[1].start()
    block(1)
    settles[0].wait()
    settles[1].go()
    for b in (2, 3):
        bring(b)[0].wait()

    def output(k, carry):
        here = pl.ds(pl.multiple_of(k * dz, dz), dz)
        out_g[here, :] = dot_tn(bv[:, here], att[...]).astype(BF)
        return carry

    lax.fori_loop(0, zn, output, 0)
    host.begin(1)
    block(2)
    block(3)
    for b in range(4):
        bring(b)[1].wait()

    def weights_of(k, carry):
        here = pl.ds(pl.multiple_of(k * dz, dz), dz)
        acc = 0.0
        for b in range(4):
            acc = acc + dot_tn(red[0][b // 2, b % 2, :, here], low[pl.ds(b * tok, tok), :])
        grads[k] = acc.astype(BF)
        return carry

    lax.fori_loop(0, zn, weights_of, 0)
    deals, step = [], sub // 2
    for m in range(micro):
        total.arrived(m)
        for lo in range(0, sub, step):
            ob[m, lo : lo + step, :] = (middle[m, lo : lo + step, :] + total.total(m, lo, step)).astype(BF)
        deals.append(Deal(wire, at, ob, layer_out, m, ls, m))
        deals[-1].begin()
    settles[1].wait()
    for deal in deals:
        deal.end()
    host.end()
    wire.finish()


def attention_back(count, lens, branch, att, wa, qkv, cos, sin, n1, g0, got0, g1, got1, pair, last, middle, hids, g2, zn):
    rows, width = branch.shape
    cols, span, parts = qkv.shape[1], att.shape[1], len(hids)
    micro, sub, _ = middle.shape
    tok = rows // 4
    dz = width // zn
    out_g = shaped((width, span))
    jobs = Jobs([(g2, (0, 1), ()), (out_g, (0,), ())], zn)
    jobs.ins = [g2]
    half = shaped((dz // 2, g0.shape[1]))
    links = jobs.links + 2 + (REDUCE + 3) * micro
    return kernel(
        functools.partial(attention_back_kernel, jobs, count, parts, (len(got0), len(got1))),
        (lens, branch, att, wa, qkv, cos, sin, n1, g0, *got0, g1, *got1, pair, last, middle, *hids, *jobs.ins),
        [SMEM, ANY, VMEM, ANY, VMEM, VMEM, VMEM, ANY] + [ANY] * (4 + len(got0) + len(got1)) + [VMEM] + [ANY] * (parts + len(jobs.ins)),
        (shaped((rows, cols)), shaped((zn, dz, cols)), out_g, *(half,) * 4, shaped((micro, tok, width // 4)), *jobs.outs),
        (VMEM, VMEM, VMEM) + (ANY,) * (5 + len(jobs.outs)), 70, "attention_back",
        reduce_scratch(micro, tok, sub, width)
        + [pltpu.VMEM((rows, width), BF), pltpu.VMEM((zn, dz, span), BF), pltpu.VMEM((micro, sub, width), BF)]
        + settle_scratch(zn, dz, g0.shape[1])[:1]
        + sems(9 + 2 * parts, zn + 1, micro, links, links) + jobs.scratch,
        talk=9, staged=(2, 4, 5, 6, 12 + len(got0) + len(got1)),
    )


def chunk_body(jobs, c, n2, dy, w, mask, *refs):
    zin, (low, hidden, grad), refs = refs[: len(jobs.ins)], refs[len(jobs.ins) :][:3], refs[len(jobs.ins) + 3 :]
    zout, (nv, dv, wv, load, *talk) = refs[: len(jobs.outs)], refs[len(jobs.outs) :]
    zn, dz, cols = wv.shape
    one = cols // 3
    steps = load.shape[1] - 1
    tile = nv.shape[0] // steps
    whole = pltpu.make_async_copy(w if c is None else w.at[:, c], wv, load.at[0, steps])
    whole.start()

    def bring(t):
        at = pl.ds(pl.multiple_of(t * tile, tile), tile)
        return (
            pltpu.make_async_copy(n2.at[at], nv.at[at], load.at[0, t]),
            pltpu.make_async_copy(dy.at[at], dv.at[at], load.at[1, t]),
        )

    for t in range(steps):
        for copy in bring(t):
            copy.start()
    if talk:
        ss, rs, *talk = talk
        meet(z_partners(jobs.zn))
        host = jobs.host(Wire(ss, rs), zin, zout, talk)
        host.begin()
    whole.wait()

    def forward(t, carry):
        for copy in bring(t):
            copy.wait()
        at = pl.ds(pl.multiple_of(t * tile, tile), tile)
        acc = hg = 0.0
        for k in range(zn):
            acc = acc + dot(nv[at, k * dz : (k + 1) * dz], wv[k, :, : 2 * one])
            hg = hg + dot(dv[at, k * dz : (k + 1) * dz], wv[k, :, 2 * one :])
        hg = hg * mask[...]
        g, u = acc[:, :one], acc[:, one:]
        phi = 0.5 * (1.0 + lax.erf(g * (0.5**0.5)))
        slope = phi + g * jnp.exp(-0.5 * g * g) * 0.3989422804014327
        act = g * phi
        hidden[at, :] = (act * u * mask[...]).astype(BF)
        low[at, :one] = (hg * u * slope).astype(BF)
        low[at, one:] = (hg * act).astype(BF)
        return carry

    lax.fori_loop(0, steps, forward, 0)

    def weights(k, carry):
        at = pl.ds(pl.multiple_of(k * dz, dz), dz)
        grad[at, : 2 * one] = dot_tn(nv[:, at], low[...]).astype(BF)
        grad[at, 2 * one :] = dot_tn(dv[:, at], hidden[...]).astype(BF)
        return carry

    lax.fori_loop(0, zn, weights, 0)
    if jobs.links:
        host.end()


def chunk(n2, dy, w, c, mask, plan, zn, talk, first):
    rows, width = n2.shape
    cols = w.shape[-1]
    one = cols // 3
    jobs = Jobs(plan, zn)
    return kernel(
        functools.partial(chunk_body, jobs, c), (n2, dy, w, mask, *jobs.ins), [ANY, ANY, ANY, VMEM] + [ANY] * len(jobs.ins),
        (shaped((rows, 2 * one)), shaped((rows, one)), shaped((width, cols)), *jobs.outs),
        (VMEM,) * 3 + (ANY,) * len(jobs.outs), 22, "ffn_chunk",
        [pltpu.VMEM((rows, width), BF)] * 2 + [pltpu.VMEM((zn, width // zn, cols), BF), pltpu.SemaphoreType.DMA((2, 5))]
        + (sems(jobs.links, jobs.links) + jobs.scratch if jobs.links else []),
        first, talk=talk if jobs.links else None,
    )


def form_body(parts, *refs):
    halves, (one_in, two_in, gu, down, qkv, out, one_out, two_out) = refs[: 2 * parts + 4], refs[2 * parts + 4 :]
    one_out[...] = one_in[...]
    two_out[...] = two_in[...]
    y = lax.axis_index("y")
    one = halves[0].shape[1] // 3

    def pair(k):
        keep, theirs = halves[2 * k][...].astype(F32), halves[2 * k + 1][...].astype(F32)
        return jnp.where(y == 0, keep, theirs), jnp.where(y == 0, theirs, keep)

    half = parts * one
    for k in range(parts):
        for i, v in enumerate(pair(k)):
            lo = i * half + k * one
            gu[0, :, lo : lo + one] = v[:, :one]
            gu[1, :, lo : lo + one] = v[:, one : 2 * one]
            down[lo : lo + one, :] = v[:, 2 * one :].T
    for i, v in enumerate(pair(parts)):
        span = v.shape[1]
        out[i * span : (i + 1) * span, :] = v.T
    for i, v in enumerate(pair(parts + 1)):
        span = v.shape[1] // 3
        for p in range(3):
            qkv[p, :, i * span : (i + 1) * span] = v[:, p * span : (p + 1) * span]


def form(halves, tokens, w_gu, w_down, w_qkv, w_out):
    parts = (len(halves) - 4) // 2
    return kernel(
        functools.partial(form_body, parts), [*halves, *tokens], [VMEM] * (len(halves) + 2),
        tuple(shaped(w.shape, F32) for w in (w_gu, w_down, w_qkv, w_out)) + tuple(shaped(t.shape) for t in tokens),
        (VMEM,) * 6, 8, "form",
    )


CHUNKS = 3


def on_device(inputs, lengths, counts, w_qkv, w_out, w_gu, w_down, g1, b1, g2, b2, dy_in):
    z = lax.axis_index("z")
    y = lax.axis_index("y")
    n = lax.axis_index("n")
    zn = lax.axis_size("z")
    micro, tok, feat = inputs.shape
    width = feat * lax.axis_size("n")
    rows = micro * 2 * tok
    depth = w_qkv.shape[1]
    half_slots = w_gu.shape[2] // 2
    one = half_slots // CHUNKS

    def gather_z(w):
        return lax.all_gather(w, "z", axis=0, tiled=False)

    own_attn = swap_attn(w_qkv, w_out)
    wa = gather_z(own_attn)
    vecs = jnp.stack([g1, b1, g2, b2]).astype(F32)
    vecs = jnp.pad(vecs, ((0, 4), (0, 0)))
    count = lengths.shape[2]
    lens = jnp.pad(lengths[:, 0], ((0, 8 - micro), (0, 128 - count)))
    half_dim = HEAD_DIM // 2
    freq = 10000.0 ** (-(jnp.arange(HEAD_DIM) % half_dim).astype(F32) / half_dim)
    x_all, norms, lens, cos, sin, own_01 = gather_x(
        inputs, vecs, lens, freq[None], w_gu, w_down, zn, (0, 1), one, count, (own_attn,)
    )
    norms = norms.transpose(2, 0, 1, 3).reshape(8, width)
    gain1, shift1, gain2, shift2 = (norms[i : i + 1] for i in range(4))
    own = jnp.sum(jnp.where(jnp.arange(counts.shape[0]) == n, counts, 0))
    mask = (y * half_slots + jnp.arange(half_slots) < own).astype(F32)[None]

    d_all, n1, own_2 = gather_d(dy_in, x_all, gain1, shift1, w_gu, w_down, (2,), one)
    dy = d_all.reshape(rows, width)
    qkv, att, own_2 = attention(count, lens, n1, wa, cos, sin, own_2, tok)
    w_01, w_2 = gather_z(own_01), gather_z(own_2)
    middle, n2 = attn_out(att, wa, x_all, gain2, shift2)
    n2 = n2.reshape(rows, width)

    def own_mask(c):
        return mask[:, c * one : (c + 1) * one]

    low0, hid0, g0 = chunk(n2, dy, w_01, 0, own_mask(0), [], zn, None, ())
    low1, hid1, grad1 = chunk(n2, dy, w_01, 1, own_mask(1), [], zn, None, (g0,))
    low2, hid2, grad2, *p = chunk(n2, dy, w_2, None, own_mask(2), [(g0, (0,), ())], zn, 7, (grad1,))
    mid_grad, branch, vec2, *q = ffn_back(
        [low0, low1, low2], w_01, w_2, d_all, middle, gain2, [(grad1, (0, 1), ()), (g0, (1,), p)], zn, ()
    )
    many = len(chain_results(zn, (0, 1), 8, 128))
    got1, got0 = q[:many], p + q[many:]
    branch = branch.reshape(rows, width)
    low, qkv_g, out_g, *r = attention_back(
        count, lens, branch, att, wa, qkv, cos, sin, n1, g0, got0, grad1, got1, w_01, w_2, middle, [hid0, hid1, hid2], grad2, zn
    )
    first, layer_out, got2, gout = r[:4], r[4], r[5 : 5 + many], r[5 + many :]
    in_grad, sums, *r = last_sums(
        low, wa, x_all, mid_grad, gain1, vec2, grad2, got2, out_g, gout, qkv_g.reshape(width, -1), zn
    )
    gu_grad, down_grad, qkv_grad, out_grad, layer_out, in_grad = form(
        [*first, *r[:6]], [layer_out, in_grad], w_gu, w_down, w_qkv, w_out
    )

    mine = lax.dynamic_slice_in_dim(sums, (z * 2 + y) * g1.shape[0], g1.shape[0], 1)
    return (
        layer_out,
        in_grad,
        qkv_grad,
        out_grad,
        gu_grad,
        down_grad,
        mine[0],
        mine[1],
        mine[2],
        mine[3],
    )


def solution(mesh):
    wide, narrow = mesh.shape["wide"], mesh.shape["narrow"]
    grid = Mesh(mesh.devices.reshape(wide // 2, 2, narrow), ("z", "y", "n"))
    w = ("z", "y")
    tokens, depth, lines, vector = P(None, w, "n"), P(None, w, "n"), P("n", w), P(w)
    return jax.shard_map(
        on_device,
        mesh=grid,
        in_specs=(
            tokens, P(None, w, None), P(), depth, lines, depth, lines,
            vector, vector, vector, vector, tokens,
        ),
        out_specs=(
            tokens, tokens, depth, lines, depth, lines, vector, vector, vector, vector,
        ),
        check_vma=False,
    )
```
